32 devices in a mesh: dp: 16 (over z, x, core), seq: 2 (over y).
Axes of the slice: x: 2, y: 2, z: 4, core: 2. Of those that a mesh axis runs over, the one named last changes fastest.
Arguments:
- hidden_in: bfloat16 [16, 1024, 1024], P('dp', 'seq'), may hold values from -6 to 6
- condition: bfloat16 [16, 1024], P('dp'), may hold values from -6 to 6
- cotangent: bfloat16 [16, 1024, 1024], P('dp', 'seq'), as said below
- weights_in: float32 [1024, 14336], P('seq', 'dp')
- weights_down: float32 [4096, 1024], P('seq', 'dp'), may hold values from -0.09375 to 0.09375
- biases: float32 [14336], P(('dp', 'seq')), may hold values from -1.8 to 1.8
- moment_in: float32 [1024, 14336], P('seq', 'dp'), as said below
- moment_down: float32 [4096, 1024], P('seq', 'dp'), as said below
- moment_bias: float32 [14336], P(('dp', 'seq')), as said below
- square_in: float32 [1024, 14336], P('seq', 'dp'), as said below
- square_down: float32 [4096, 1024], P('seq', 'dp'), as said below
- square_bias: float32 [14336], P(('dp', 'seq')), as said below
Outputs:
- block_out: bfloat16 [16, 1024, 1024], P('dp', 'seq')
- input_grad: float32 [16, 1024, 1024], P('dp', 'seq')
- cond_grad: float32 [16, 1024], P('dp')
- moments_in: float32 [1024, 14336], P('seq', 'dp')
- moments_down: float32 [4096, 1024], P('seq', 'dp')
- moments_bias: float32 [14336], P(('dp', 'seq'))
- squares_in: float32 [1024, 14336], P('seq', 'dp')
- squares_down: float32 [4096, 1024], P('seq', 'dp')
- squares_bias: float32 [14336], P(('dp', 'seq'))
- master_in: float32 [1024, 14336], P('seq', 'dp')
- master_down: float32 [4096, 1024], P('seq', 'dp')
- master_bias: float32 [14336], P(('dp', 'seq'))
- copy_in: bfloat16 [1024, 14336], P('seq', 'dp')
- copy_down: bfloat16 [4096, 1024], P('seq', 'dp')
- copy_bias: bfloat16 [14336], P(('dp', 'seq'))
The draws below stay inside these ranges and needn't reach their ends.
Inputs may be any that keep to these rules, and one draw needn't show every extreme that they name: A cotangent of order one in every token. `moment_in`: real first moments of both signs. `moment_down`: real first moments of both signs. `moment_bias`: real first moments of both signs. `square_in`: positive second moments. `square_down`: positive second moments. `square_bias`: positive second moments.
All inputs are finite; a program needn't handle non-finite values.
Results may differ from the reference program's by a relative error of at most 0.025.
Values may be sent and summed in bfloat16 or wider, within the bound.
A program may use at most 384 MiB of HBM per device.

```python
import math
import jax
import jax.numpy as jnp
from jax import lax

D = 1024
HEADS = 16
HEAD_DIM = 64
FF = 4096
SEQ_LEN = 1024
STEP = 5
LATENTS = 16
TOKENS = 16384


def flat_scales(layout):
    return jnp.concatenate([jnp.full((width_part,), factor, jnp.float32) for width_part, factor in layout])


def grad_level():
    return 2.0 * math.sqrt(TOKENS)


def input_factors():
    return flat_scales([(6 * D, 1.0), (D, 0.6), (D, 0.6), (D, 3.0), (D, 0.15), (FF, 0.5)])


def bias_factors():
    return flat_scales([(6 * D, 2.0), (D, 1.0), (D, 5.0), (D, 1.0), (FF, 0.4), (D, 0.6)])


def normal_part(key, shape):
    return jax.random.truncated_normal(key, -4.0, 4.0, shape, jnp.float32)


def square_part(key, shape):
    return jnp.exp(jax.random.uniform(key, shape, jnp.float32, 0.0, math.log(4.0)))


def draw_cotangent(key, part):
    key = jax.random.fold_in(key, 11)
    latent_pos = jnp.arange(LATENTS, dtype=jnp.float32)[:, None, None] / max(LATENTS - 1, 1)
    token_pos = jnp.arange(SEQ_LEN, dtype=jnp.float32)[None, :, None] / max(SEQ_LEN - 1, 1)
    base_draw = normal_part(key, (LATENTS, SEQ_LEN, D))
    rising = 1.0 + latent_pos + token_pos
    return (base_draw * rising).astype(jnp.bfloat16)


def draw_weights_in(key, part):
    key = jax.random.fold_in(key, 1)
    out_scale = max(1.0, math.sqrt(SEQ_LEN) / 5.0)
    column = flat_scales([(6 * D, 1.0), (D, 0.9), (D, 0.9), (D, 1.0), (D, out_scale), (FF, 1.0)]) / math.sqrt(D)
    base_draw = normal_part(key, (D, 10 * D + FF))
    return base_draw * column[None, :]


def draw_moment_in(key, part):
    key = jax.random.fold_in(key, 2)
    return normal_part(key, (D, 10 * D + FF)) * (input_factors() * grad_level())[None, :]


def draw_square_in(key, part):
    key = jax.random.fold_in(key, 3)
    level = input_factors() * grad_level()
    return square_part(key, (D, 10 * D + FF)) * (level * level)[None, :]


def draw_moment_down(key, part):
    key = jax.random.fold_in(key, 4)
    return normal_part(key, (FF, D)) * (0.4 * grad_level())


def draw_square_down(key, part):
    key = jax.random.fold_in(key, 5)
    level = 0.4 * grad_level()
    return square_part(key, (FF, D)) * (level * level)


def draw_moment_bias(key, part):
    key = jax.random.fold_in(key, 6)
    return normal_part(key, (10 * D + FF,)) * bias_factors() * grad_level()


def draw_square_bias(key, part):
    key = jax.random.fold_in(key, 7)
    level = bias_factors() * grad_level()
    return square_part(key, (10 * D + FF,)) * level * level


def level_of(rng, extent, shards, least, largest):
    loudness = 1.0
    for axis_at, shards_of in shards:
        steps = jax.random.uniform(jax.random.fold_in(jax.random.fold_in(rng, 6), axis_at), (shards_of,), jnp.float32, least / len(shards), largest / len(shards))
        loudness = loudness * jnp.repeat(jnp.exp(steps), extent[axis_at] // shards_of).reshape((-1,) + (1,) * (len(extent) - 1 - axis_at))
    return loudness


def scatter_about(rng, dims, scale, limit, shards=(), kind=jnp.bfloat16):
    values = jax.random.normal(rng, dims, jnp.float32) * scale
    if len(shards) > 0:
        values = level_of(rng, dims, shards, -0.22, 0.18) * values
    return jnp.clip(values, min=-limit, max=limit).astype(kind)


def setup_inputs(seed: int = 0) -> dict:
    splits = jax.random.split(jax.random.key(seed), 13)
    return {
        "hidden_in": scatter_about(splits[0], (LATENTS, SEQ_LEN, D), 1.0, 6.0, ((0, 16), (1, 2))),
        "condition": scatter_about(splits[1], (LATENTS, D), 1.0, 6.0, ((0, 16),)),
        "cotangent": draw_cotangent(jax.random.fold_in(splits[12], 71), 0),
        "weights_in": draw_weights_in(jax.random.fold_in(splits[12], 71), 0),
        "weights_down": scatter_about(splits[4], (FF, D), FF ** -0.5, 0.09375, ((0, 2), (1, 16)), jnp.float32),
        "biases": scatter_about(splits[5], (10 * D + FF,), 0.3, 1.8, ((0, 32),), jnp.float32),
        "moment_in": draw_moment_in(jax.random.fold_in(splits[12], 71), 0),
        "moment_down": draw_moment_down(jax.random.fold_in(splits[12], 71), 0),
        "moment_bias": draw_moment_bias(jax.random.fold_in(splits[12], 71), 0),
        "square_in": draw_square_in(jax.random.fold_in(splits[12], 71), 0),
        "square_down": draw_square_down(jax.random.fold_in(splits[12], 71), 0),
        "square_bias": draw_square_bias(jax.random.fold_in(splits[12], 71), 0),
    }


@jax.custom_vjp
def low(v):
    return lax.optimization_barrier(v.astype(jnp.bfloat16)).astype(jnp.float32)

@jax.custom_vjp
def low_back(v):
    return v

def low_keep(v):
    return (low(v), None)

def low_pass(kept, grad):
    return (grad,)

def back_keep(v):
    return (v, None)

def back_low(kept, grad):
    return (low(grad),)
low.defvjp(low_keep, low_pass)
low_back.defvjp(back_keep, back_low)
norm_eps = 1e-06
beta_first = 0.5
beta_second = 0.5
adam_eps = 1e-08
weight_decay = 0.01
rate_in = 0.03
rate_down = 0.016
rate_bias = 0.3
highest = lax.Precision.HIGHEST

def rounded(values):
    return low_back(low(values))

def layer_norm(values):
    center = values - lax.optimization_barrier(jnp.mean(values, axis=-1, keepdims=True))
    return center * lax.rsqrt(lax.optimization_barrier(jnp.mean(center * center, axis=-1, keepdims=True)) + norm_eps)

def project(values, matrix):
    return jnp.einsum('nld,de->nle', values, matrix, precision=highest)

def attend(queries, keys_all, values_all):
    length = queries.shape[0]
    block_rows = math.gcd(length, 512)
    heads_query = queries.reshape(length // block_rows, block_rows, HEADS, HEAD_DIM)
    heads_key = keys_all.reshape(length, HEADS, HEAD_DIM)
    heads_value = values_all.reshape(length, HEADS, HEAD_DIM)

    @jax.checkpoint
    def one_block(query_rows):
        scores = low_back(jnp.einsum('qhd,khd->hqk', query_rows, heads_key, precision=highest) * HEAD_DIM ** (-0.5))
        weights = low(jax.nn.softmax(scores, axis=-1))
        return jnp.einsum('hqk,khd->qhd', weights, heads_value, precision=highest)
    return lax.map(one_block, heads_query).reshape(length, HEADS * HEAD_DIM)

def forward_group(hidden, condition, matrix_in, matrix_down, bias_all):
    cond_act = low(jax.nn.silu(condition))
    modulation = low_back(jnp.dot(cond_act, matrix_in[:, :6 * D], precision=highest) + bias_all[:6 * D])
    pieces = [modulation[:, None, part_index * D:(part_index + 1) * D] for part_index in range(6)]
    shift_one, scale_one, gate_one, shift_two, scale_two, gate_two = pieces
    normed_one = layer_norm(hidden)
    input_one = low(normed_one * (1.0 + scale_one) + shift_one)
    qkv_all = project(input_one, matrix_in[:, 6 * D:9 * D])
    queries = rounded(qkv_all[..., :D] + bias_all[6 * D:7 * D])
    keys_all = rounded(qkv_all[..., D:2 * D])
    values_all = rounded(qkv_all[..., 2 * D:] + bias_all[7 * D:8 * D])
    attn_mixed = rounded(lax.map(lambda triple: attend(*triple), (queries, keys_all, values_all)))
    attn_out = low_back(project(attn_mixed, matrix_in[:, 9 * D:10 * D]) + bias_all[8 * D:9 * D])
    middle = hidden + gate_one * attn_out
    normed_two = layer_norm(middle)
    input_two = low(normed_two * (1.0 + scale_two) + shift_two)
    upward = low_back(project(input_two, matrix_in[:, 10 * D:]) + bias_all[9 * D:9 * D + FF])
    activated = low(jax.nn.gelu(upward, approximate=True))
    branch = low_back(project(activated, matrix_down) + bias_all[9 * D + FF:])
    return middle + gate_two * branch

def adamw_step(master, moment, square, gradient, step_rate):
    moment_new = beta_first * moment + (1.0 - beta_first) * gradient
    square_new = beta_second * square + (1.0 - beta_second) * gradient * gradient
    corrected = moment_new / (1.0 - beta_first ** STEP)
    scale_sq = square_new / (1.0 - beta_second ** STEP)
    master_new = master - step_rate * (corrected / (jnp.sqrt(scale_sq) + adam_eps) + weight_decay * master)
    return (moment_new, square_new, master_new)

def reference(hidden_in, condition, cotangent, weights_in, weights_down, biases, moment_in, moment_down, moment_bias, square_in, square_down, square_bias):
    group_size = math.gcd(LATENTS, max(1, 4096 // SEQ_LEN))

    def whole(hidden, cond_all, master_in, master_down, master_bias):
        matrix_in = low(master_in)
        matrix_down = low(master_down)
        bias_all = low(master_bias)
        hidden_groups = hidden.reshape(LATENTS // group_size, group_size, SEQ_LEN, D)
        cond_groups = cond_all.reshape(LATENTS // group_size, group_size, D)
        step_fn = jax.checkpoint(lambda grouped: forward_group(grouped[0], grouped[1], matrix_in, matrix_down, bias_all))
        return lax.map(step_fn, (hidden_groups, cond_groups)).reshape(LATENTS, SEQ_LEN, D)
    block_out, pullback = jax.vjp(whole, hidden_in.astype(jnp.float32), condition.astype(jnp.float32), weights_in, weights_down, biases)
    input_grad, cond_grad, grad_in, grad_down, grad_bias = pullback(cotangent.astype(jnp.float32))
    moments_in, squares_in, master_in = adamw_step(weights_in, moment_in, square_in, grad_in, rate_in)
    moments_down, squares_down, master_down = adamw_step(weights_down, moment_down, square_down, grad_down, rate_down)
    moments_bias, squares_bias, master_bias = adamw_step(biases, moment_bias, square_bias, grad_bias, rate_bias)
    return (block_out.astype(jnp.bfloat16), input_grad, cond_grad, moments_in, moments_down, moments_bias, squares_in, squares_down, squares_bias, master_in, master_down, master_bias, master_in.astype(jnp.bfloat16), master_down.astype(jnp.bfloat16), master_bias.astype(jnp.bfloat16))
```

```python
import math

import jax
import jax.numpy as jnp
from jax import lax
from jax.experimental import pallas as pl
from jax.experimental.pallas import tpu as pltpu
from jax.sharding import PartitionSpec as P

D = 1024
HEADS = 16
HEAD_DIM = 64
FF = 4096
STEP = 5


norm_eps = 1e-06
beta_first = 0.5
beta_second = 0.5
adam_eps = 1e-08
weight_decay = 0.01
rate_in = 0.03
rate_down = 0.016
rate_bias = 0.3


def layer_norm(values):
    center = values - jnp.mean(values, axis=-1, keepdims=True)
    return center * lax.rsqrt(jnp.mean(center * center, axis=-1, keepdims=True) + norm_eps)


def adamw_step(master, moment, square, gradient, step_rate):
    moment_new = beta_first * moment + (1.0 - beta_first) * gradient
    square_new = beta_second * square + (1.0 - beta_second) * gradient * gradient
    corrected = moment_new / (1.0 - beta_first**STEP)
    scale_sq = square_new / (1.0 - beta_second**STEP)
    master_new = master - step_rate * (
        corrected / (jnp.sqrt(scale_sq) + adam_eps) + weight_decay * master
    )
    return (moment_new, square_new, master_new)


def dense_map(values, matrix):
    return jnp.einsum("nld,de->nle", values, matrix, preferred_element_type=jnp.float32)


def dense_back(gradients, matrix):
    return jnp.einsum("nle,de->nld", gradients, matrix, preferred_element_type=jnp.float32)


def outer_sum(values, gradients):
    return jnp.einsum("nld,nle->de", values, gradients, preferred_element_type=jnp.float32)


def total_sum(values):
    return jnp.sum(values.astype(jnp.float32), axis=(0, 1))


def gather_weights(low_in, low_down, low_bias):
    seq_parts = (
        lax.all_gather(low_in, "seq", axis=0, tiled=True),
        lax.all_gather(low_down, "seq", axis=0, tiled=True),
        lax.all_gather(low_bias, "seq", axis=0, tiled=True),
    )
    whole_in, whole_down, bias_row = (
        lax.all_gather(seq_parts[0], "dp", axis=1, tiled=True),
        lax.all_gather(seq_parts[1], "dp", axis=1, tiled=True),
        lax.all_gather(seq_parts[2].reshape(1, -1), "dp", axis=1, tiled=True),
    )
    return (whole_in, whole_down, bias_row[0])


def head_layout():
    heads_here = math.gcd(HEADS, max(1, 128 // HEAD_DIM))
    return (heads_here, heads_here * HEAD_DIM, HEADS // heads_here)


def split_heads(values, lane_start, lane_count, heads_here):
    piece = lax.dynamic_slice_in_dim(values, lane_start, lane_count, 2)
    return piece.reshape(piece.shape[0], piece.shape[1], heads_here, HEAD_DIM)


def join_heads(stacked):
    moved = jnp.moveaxis(stacked, 0, 2)
    return moved.reshape(moved.shape[0], moved.shape[1], moved.shape[2] * moved.shape[3])


def attention_forward(queries, keys_all, values_all):
    heads_here, lane_count, head_steps = head_layout()
    scale_factor = HEAD_DIM ** (-0.5)

    def one_group(group_index):
        lane_start = group_index * lane_count
        query_part = split_heads(queries, lane_start, lane_count, heads_here)
        key_part = split_heads(keys_all, lane_start, lane_count, heads_here)
        value_part = split_heads(values_all, lane_start, lane_count, heads_here)
        scores = (
            jnp.einsum("nqhd,nkhd->nhqk", query_part, key_part, preferred_element_type=jnp.float32)
            * scale_factor
        )
        row_max = jnp.max(scores, axis=-1, keepdims=True)
        exponent = jnp.exp(scores - row_max)
        row_total = jnp.sum(exponent, axis=-1, keepdims=True)
        weights = (exponent / row_total).astype(jnp.bfloat16)
        attn_part = jnp.einsum(
            "nhqk,nkhd->nqhd", weights, value_part, preferred_element_type=jnp.float32
        )
        shaped = attn_part.reshape(attn_part.shape[0], attn_part.shape[1], lane_count)
        return (shaped, (row_max + jnp.log(row_total))[..., 0])

    stacked, log_totals = lax.map(one_group, jnp.arange(head_steps))
    return (join_heads(stacked), log_totals)


def attention_backward(queries, keys_all, values_all, log_totals, grad_mixed):
    heads_here, lane_count, head_steps = head_layout()
    scale_factor = HEAD_DIM ** (-0.5)

    def one_group(carried):
        group_index, log_part = carried
        lane_start = group_index * lane_count
        query_part = split_heads(queries, lane_start, lane_count, heads_here)
        key_part = split_heads(keys_all, lane_start, lane_count, heads_here)
        value_part = split_heads(values_all, lane_start, lane_count, heads_here)
        grad_part = split_heads(grad_mixed, lane_start, lane_count, heads_here)
        scores = (
            jnp.einsum("nqhd,nkhd->nhqk", query_part, key_part, preferred_element_type=jnp.float32)
            * scale_factor
        )
        probability = jnp.exp(scores - log_part[..., None])
        grad_prob = jnp.einsum(
            "nqhd,nkhd->nhqk", grad_part, value_part, preferred_element_type=jnp.float32
        )
        inner_sum = jnp.sum(probability * grad_prob, axis=-1, keepdims=True)
        grad_score = (probability * (grad_prob - inner_sum)).astype(jnp.bfloat16)
        grad_query = (
            jnp.einsum("nhqk,nkhd->nqhd", grad_score, key_part, preferred_element_type=jnp.float32)
            * scale_factor
        )
        grad_key = (
            jnp.einsum(
                "nhqk,nqhd->nkhd", grad_score, query_part, preferred_element_type=jnp.float32
            )
            * scale_factor
        )
        grad_value = jnp.einsum(
            "nhqk,nqhd->nkhd",
            probability.astype(jnp.bfloat16),
            grad_part,
            preferred_element_type=jnp.float32,
        )
        return (
            grad_query.reshape(grad_query.shape[0], grad_query.shape[1], lane_count),
            grad_key.reshape(grad_key.shape[0], grad_key.shape[1], lane_count),
            grad_value.reshape(grad_value.shape[0], grad_value.shape[1], lane_count),
        )

    query_terms, key_terms, value_terms = lax.map(one_group, (jnp.arange(head_steps), log_totals))
    return (join_heads(query_terms), join_heads(key_terms), join_heads(value_terms))


def local_general(
    hidden_in,
    condition,
    cotangent,
    weights_in,
    weights_down,
    biases,
    moment_in,
    moment_down,
    moment_bias,
    square_in,
    square_down,
    square_bias,
):
    low_in = weights_in.astype(jnp.bfloat16)
    low_down = weights_down.astype(jnp.bfloat16)
    low_bias = biases.astype(jnp.bfloat16)
    whole_in, whole_down, bias_all = gather_weights(low_in, low_down, low_bias)
    bias_float = bias_all.astype(jnp.float32)
    hidden = hidden_in.astype(jnp.float32)
    cond_float = condition.astype(jnp.float32)
    cond_act = jax.nn.silu(cond_float).astype(jnp.bfloat16)
    modulation = (
        jnp.dot(cond_act, whole_in[:, : 6 * D], preferred_element_type=jnp.float32)
        + bias_float[: 6 * D]
    )
    pieces = [modulation[:, None, part_index * D : (part_index + 1) * D] for part_index in range(6)]
    shift_one, scale_one, gate_one, shift_two, scale_two, gate_two = pieces
    normed_one = layer_norm(hidden)
    input_one = (normed_one * (1.0 + scale_one) + shift_one).astype(jnp.bfloat16)
    qkv_all = dense_map(input_one, whole_in[:, 6 * D : 9 * D])
    queries = (qkv_all[..., :D] + bias_float[6 * D : 7 * D]).astype(jnp.bfloat16)
    keys_local = qkv_all[..., D : 2 * D].astype(jnp.bfloat16)
    values_local = (qkv_all[..., 2 * D :] + bias_float[7 * D : 8 * D]).astype(jnp.bfloat16)
    keys_all, values_all = (
        lax.all_gather(keys_local, "seq", axis=1, tiled=True),
        lax.all_gather(values_local, "seq", axis=1, tiled=True),
    )
    attn_float, log_totals = attention_forward(queries, keys_all, values_all)
    attn_mixed = attn_float.astype(jnp.bfloat16)
    attn_out = dense_map(attn_mixed, whole_in[:, 9 * D : 10 * D]) + bias_float[8 * D : 9 * D]
    middle = hidden + gate_one * attn_out
    normed_two = layer_norm(middle)
    input_two = (normed_two * (1.0 + scale_two) + shift_two).astype(jnp.bfloat16)
    upward = dense_map(input_two, whole_in[:, 10 * D :]) + bias_float[9 * D : 9 * D + FF]
    activated = jax.nn.gelu(upward, approximate=True).astype(jnp.bfloat16)
    branch = dense_map(activated, whole_down) + bias_float[9 * D + FF :]
    block_out = (middle + gate_two * branch).astype(jnp.bfloat16)
    whole_in, whole_down, bias_all = gather_weights(low_in, low_down, low_bias)
    grad_out = cotangent.astype(jnp.float32)
    grad_branch = (grad_out * gate_two).astype(jnp.bfloat16)
    gate_two_grad = jnp.sum(grad_out * branch, axis=1)
    grad_down = outer_sum(activated, grad_branch)
    bias_down_grad = total_sum(grad_branch)
    grad_act = dense_back(grad_branch, whole_down)
    _, gelu_pull = jax.vjp(lambda inner_value: jax.nn.gelu(inner_value, approximate=True), upward)
    grad_upward = gelu_pull(grad_act)[0].astype(jnp.bfloat16)
    grad_up = outer_sum(input_two, grad_upward)
    bias_up_grad = total_sum(grad_upward)
    grad_input_two = dense_back(grad_upward, whole_in[:, 10 * D :])
    shift_two_grad = jnp.sum(grad_input_two, axis=1)
    scale_two_grad = jnp.sum(grad_input_two * normed_two, axis=1)
    _, norm_pull_two = jax.vjp(layer_norm, middle)
    grad_middle = grad_out + norm_pull_two(grad_input_two * (1.0 + scale_two))[0]
    grad_attn = (grad_middle * gate_one).astype(jnp.bfloat16)
    gate_one_grad = jnp.sum(grad_middle * attn_out, axis=1)
    grad_out_proj = outer_sum(attn_mixed, grad_attn)
    bias_out_grad = total_sum(grad_attn)
    grad_mixed = dense_back(grad_attn, whole_in[:, 9 * D : 10 * D]).astype(jnp.bfloat16)
    grad_query, key_terms, value_terms = attention_backward(
        queries, keys_all, values_all, log_totals, grad_mixed
    )
    key_grad, value_grad = (
        lax.psum_scatter(
            key_terms.astype(jnp.bfloat16), "seq", scatter_dimension=1, tiled=True
        ).astype(jnp.float32),
        lax.psum_scatter(
            value_terms.astype(jnp.bfloat16), "seq", scatter_dimension=1, tiled=True
        ).astype(jnp.float32),
    )
    grad_qkv = jnp.concatenate(
        [
            grad_query.astype(jnp.bfloat16),
            key_grad.astype(jnp.bfloat16),
            value_grad.astype(jnp.bfloat16),
        ],
        axis=-1,
    )
    grad_proj_qkv = outer_sum(input_one, grad_qkv)
    bias_query_grad = total_sum(grad_qkv[..., :D])
    bias_value_grad = total_sum(grad_qkv[..., 2 * D :])
    grad_input_one = dense_back(grad_qkv, whole_in[:, 6 * D : 9 * D])
    shift_one_grad = jnp.sum(grad_input_one, axis=1)
    scale_one_grad = jnp.sum(grad_input_one * normed_one, axis=1)
    _, norm_pull_one = jax.vjp(layer_norm, hidden)
    input_grad = grad_middle + norm_pull_one(grad_input_one * (1.0 + scale_one))[0]
    mod_terms = jnp.concatenate(
        [
            shift_one_grad,
            scale_one_grad,
            gate_one_grad,
            shift_two_grad,
            scale_two_grad,
            gate_two_grad,
        ],
        axis=-1,
    )
    mod_grad = lax.psum(mod_terms, "seq").astype(jnp.bfloat16)
    _, silu_pull = jax.vjp(jax.nn.silu, cond_float)
    cond_grad = silu_pull(
        jnp.einsum("ne,de->nd", mod_grad, whole_in[:, : 6 * D], preferred_element_type=jnp.float32)
    )[0]
    owner_mask = (lax.axis_index("seq") == 0).astype(jnp.float32)
    grad_ada = (
        jnp.einsum("nd,ne->de", cond_act, mod_grad, preferred_element_type=jnp.float32) * owner_mask
    )
    bias_ada_grad = jnp.sum(mod_grad.astype(jnp.float32), axis=0) * owner_mask
    grad_in_all = jnp.zeros((D, 10 * D + FF), jnp.float32)
    grad_in_all = grad_in_all.at[:, : 6 * D].set(grad_ada)
    grad_in_all = grad_in_all.at[:, 6 * D : 9 * D].set(grad_proj_qkv)
    grad_in_all = grad_in_all.at[:, 9 * D : 10 * D].set(grad_out_proj)
    grad_in_all = grad_in_all.at[:, 10 * D :].set(grad_up)
    bias_flat = jnp.concatenate(
        [
            bias_ada_grad,
            bias_query_grad,
            bias_value_grad,
            bias_out_grad,
            bias_up_grad,
            bias_down_grad,
        ]
    )
    summed_in, summed_down, summed_bias = (
        lax.psum_scatter(
            grad_in_all.astype(jnp.bfloat16), "dp", scatter_dimension=1, tiled=True
        ).astype(jnp.float32),
        lax.psum_scatter(
            grad_down.astype(jnp.bfloat16), "dp", scatter_dimension=1, tiled=True
        ).astype(jnp.float32),
        lax.psum_scatter(
            bias_flat.reshape(1, -1).astype(jnp.bfloat16), "dp", scatter_dimension=1, tiled=True
        ).astype(jnp.float32),
    )
    owned_in, owned_down, owned_bias = (
        lax.psum_scatter(
            summed_in.astype(jnp.bfloat16), "seq", scatter_dimension=0, tiled=True
        ).astype(jnp.float32),
        lax.psum_scatter(
            summed_down.astype(jnp.bfloat16), "seq", scatter_dimension=0, tiled=True
        ).astype(jnp.float32),
        lax.psum_scatter(
            summed_bias.reshape(-1).astype(jnp.bfloat16), "seq", scatter_dimension=0, tiled=True
        ).astype(jnp.float32),
    )
    moments_in, squares_in, master_in = adamw_step(
        weights_in, moment_in, square_in, owned_in, rate_in
    )
    moments_down, squares_down, master_down = adamw_step(
        weights_down, moment_down, square_down, owned_down, rate_down
    )
    moments_bias, squares_bias, master_bias = adamw_step(
        biases, moment_bias, square_bias, owned_bias, rate_bias
    )
    return (
        block_out,
        input_grad,
        cond_grad,
        moments_in,
        moments_down,
        moments_bias,
        squares_in,
        squares_down,
        squares_bias,
        master_in,
        master_down,
        master_bias,
        master_in.astype(jnp.bfloat16),
        master_down.astype(jnp.bfloat16),
        master_bias.astype(jnp.bfloat16),
    )


MESH = pl.DeviceIdType.MESH
WIDE = 896
LOW = 6 * D
KEPT = 4 * D + FF
PLANES = 4
HALF = D // 2
TALL = HALF + 16
SUBS = 3
SUB_ROWS = TALL // SUBS
FF_PART = FF // 2
DP = 16


def place():
    dp = lax.axis_index("dp")
    y = lax.axis_index("seq")
    return (dp // 4, lax.rem(dp // 2, 2), lax.rem(dp, 2), y)


def device_at(z, x, c, y):
    return ((z * 2 + x) * 2 + c, y)


def neighbours():
    z, x, c, y = place()
    return {
        "x": device_at(z, 1 - x, c, y),
        "y": device_at(z, x, c, 1 - y),
        "up": device_at(jnp.minimum(z + 1, PLANES - 1), x, c, y),
        "down": device_at(jnp.maximum(z - 1, 0), x, c, y),
        "core": device_at(z, x, 1 - c, y),
        "swap": device_at(z, x, 1 - c, 1 - y),
    }


def repeat(count, body):
    def step(at, carried):
        body(at)
        return carried

    lax.fori_loop(0, count, step, 0)


def greet_all():
    barrier = pltpu.get_barrier_semaphore()
    here = lax.axis_index("dp") * 2 + lax.axis_index("seq")

    def signal(at):
        there = lax.rem(here + at + 1, 2 * DP)
        pl.semaphore_signal(
            barrier, inc=1, device_id=(there // 2, lax.rem(there, 2)), device_id_type=MESH
        )

    repeat(2 * DP - 1, signal)
    pl.semaphore_wait(barrier, 2 * DP - 1)


class Broad:
    height, width, subs, split = SUB_ROWS, WIDE, SUBS, 96
    first, source_column = 0, 0

    @staticmethod
    def holds(zs, xs, cs):
        return (zs * 2 + xs) * 2 + cs >= 7

    @staticmethod
    def view(whole, zs, xs, ys, cs, sub, start=0, rows=SUB_ROWS):
        column = jnp.maximum(((zs * 2 + xs) * 2 + cs) * WIDE - LOW, 128)
        row = pl.multiple_of(sub * SUB_ROWS + start, 16)
        return whole.at[ys, pl.ds(row, rows), pl.ds(pl.multiple_of(column, 128), WIDE)]


class Narrow:
    height, width, subs, split = TALL, 128, 1, 272
    first, source_column = 16 * SUBS, WIDE - 128

    @staticmethod
    def holds(zs, xs, cs):
        return (zs * 2 + xs) * 2 + cs == 6

    @staticmethod
    def view(whole, zs, xs, ys, cs, sub, start=0, rows=TALL):
        return whole.at[ys, pl.ds(start, rows), pl.ds(0, 128)]


class Down:
    height, width, subs, split = 64, FF_PART, 1, 32
    first, source_column = 16 * SUBS + 16, 0

    @staticmethod
    def holds(zs, xs, cs):
        return zs >= 0

    @staticmethod
    def view(whole, zs, xs, ys, cs, sub, start=0, rows=64):
        row = pl.multiple_of(((zs * 2 + xs) * 2 + cs) * 64 + start, 32)
        return whole.at[pl.ds(row, rows), pl.ds(pl.multiple_of(ys * FF_PART, 128), FF_PART)]


SLOTS = 16 * SUBS + 32
RELATIONS = ("own", "x", "y", "xy")
HOPS = {"own": 0, "x": 1, "y": 1, "xy": 2}


def by_plane(z, table):
    picked = table[PLANES - 1]
    for plane in range(PLANES - 2, -1, -1):
        picked = jnp.where(z == plane, table[plane], picked)
    return picked


def forward_block(what, refs, kind, zs, relation, sub, sems, valid):
    whole, mine = refs
    send_sem, recv_sem, core_sem = sems
    z, x, c, y = place()
    near = neighbours()
    xs = 1 - x if "x" in relation else x
    ys = 1 - y if "y" in relation else y
    slot = kind.first + ((zs * 2 + xs) * 2 + ys) * kind.subs + sub
    full, half = recv_sem.at[slot, 0], recv_sem.at[slot, 1]
    parts = ((0, kind.height), (0, kind.split), (kind.split, kind.height - kind.split))

    def copy(part, index, arrival, key, source=None, cs=None):
        target = kind.view(whole, zs, xs, ys, c if cs is None else cs, sub, *parts[part])
        return pltpu.make_async_remote_copy(
            src_ref=target if source is None else source,
            dst_ref=target,
            send_sem=send_sem.at[slot, index],
            recv_sem=arrival,
            device_id=near[key],
            device_id_type=MESH,
        )

    if what == "core":

        @pl.when(valid & kind.holds(zs, xs, 1 - c))
        def _():
            copy(0, 4, core_sem.at[slot], "core", cs=1 - c).wait_recv()

        return
    valid = valid & kind.holds(zs, xs, c)
    if what == "tick":
        arrived = valid & (zs != z) if relation == "own" else valid

        @pl.when(arrived)
        def _():
            if relation == "xy":
                copy(1, 0, full, "x").wait_recv()
                copy(2, 0, half, "x").wait_recv()
            else:
                copy(0, 0, full, "x").wait_recv()

    def act(descriptor):
        if what == "tick":
            descriptor.start()
        else:
            descriptor.wait_send()

    def spread(source, upward, downward):
        @pl.when(upward)
        def _():
            act(copy(0, 0, full, "up", source))

        @pl.when(downward)
        def _():
            act(copy(0, 1, full, "down", source))

        act(copy(0, 2, full, "x", source))
        act(copy(0, 3, full, "y", source))
        act(copy(0, 4, core_sem.at[slot], "core", source))

    if relation == "own":

        @pl.when(valid & (zs == z))
        def _():
            source = mine.at[
                pl.ds(pl.multiple_of(sub * kind.height, 16), kind.height),
                pl.ds(kind.source_column, kind.width),
            ]
            spread(source, z < PLANES - 1, z > 0)

        @pl.when(valid & (zs != z))
        def _():
            spread(None, (zs < z) & (z < PLANES - 1), (zs > z) & (z > 0))

        return

    @pl.when(valid)
    def _():
        if relation == "x":
            act(copy(1, 3, full, "y"))
        if relation == "y":
            act(copy(2, 2, half, "x"))
        act(copy(0, 4, core_sem.at[slot], "core"))


def forward_step(what, refs, plan, sems, at):
    z = place()[0]
    for kind, order, after in plan:
        for position in range(len(order[0])):
            zs = by_plane(z, [row[position] for row in order])
            for relation in RELATIONS:
                sub = at
                if what == "tick":
                    sub = at - (after + position + HOPS[relation])
                forward_block(
                    what,
                    refs[kind.__name__],
                    kind,
                    zs,
                    relation,
                    jnp.clip(sub, 0, kind.subs - 1),
                    sems,
                    (sub >= 0) & (sub < kind.subs),
                )


NEAR_LOW = ((1, 2), (1, 2), (2, 1), (2, 1))
ONLY_ONE = ((1,),) * PLANES
ONLY_LAST = ((3,),) * PLANES
NEAR = ((0, 1, 2, 3), (1, 0, 2, 3), (2, 3, 1, 0), (3, 2, 1, 0))
PLAN_LOW = ((Broad, NEAR_LOW, 0), (Narrow, ONLY_ONE, 0))
PLAN_UP = ((Broad, ONLY_LAST, 3),)
PLAN_DOWN = ((Down, NEAR, 6),)
PLAN_ALL = PLAN_LOW + PLAN_UP + PLAN_DOWN
EARLY_STEPS = 6
LATE_STEPS = 12


BF16 = jnp.bfloat16
F32 = jnp.float32
PLAIN = (((1,), (0,)), ((), ()))
BOTH_LAST = (((1,), (1,)), ((), ()))
BOTH_FIRST = (((0,), (0,)), ((), ()))
LANES = 128
PAIRS = HEADS // 2
TOKENS_HERE = 512


def multiply(left, right, dims=PLAIN):
    return lax.dot_general(left, right, dims, preferred_element_type=F32)


def two_heads(block):
    lanes = lax.broadcasted_iota(jnp.int32, block.shape, 1)
    zero = jnp.zeros_like(block)
    return (jnp.where(lanes < HEAD_DIM, block, zero), jnp.where(lanes < HEAD_DIM, zero, block))


def attend_pair(pair, queries, keys, values, mixed, log_totals):
    columns = pl.ds(pl.multiple_of(pair * LANES, LANES), LANES)
    key_block = keys[:, columns]
    value_flat = values[:, columns].T
    parts = []
    for head, query_block in enumerate(two_heads(queries[:, columns])):
        scores = multiply(key_block, query_block, BOTH_LAST)
        largest = jnp.max(scores, axis=0, keepdims=True)
        weights = jnp.exp((scores - largest) * HEAD_DIM**-0.5)
        total = jnp.sum(weights, axis=0, keepdims=True)
        parts.append(multiply(value_flat, weights.astype(BF16)) * (1.0 / total))
        log_totals[2 * pair + head] = largest * HEAD_DIM**-0.5 + jnp.log(total)
    joined = jnp.concatenate([parts[0][:HEAD_DIM], parts[1][HEAD_DIM:]], axis=0)
    mixed[:, columns] = joined.T.astype(BF16)


def normalize(values):
    center = values - jnp.mean(values, axis=-1, keepdims=True)
    return center * lax.rsqrt(jnp.mean(center * center, axis=-1, keepdims=True) + norm_eps)


def from_weights(left, whole, start, width):
    columns = pl.ds(pl.multiple_of(start, LANES), width)
    return multiply(left[:, :HALF], whole[0, :HALF, columns]) + multiply(
        left[:, HALF:], whole[1, :HALF, columns]
    )


def bias_of(whole, start, width):
    columns = pl.ds(pl.multiple_of(start, LANES), width)
    both = whole[0, HALF:TALL, columns].astype(F32) + whole[1, HALF:TALL, columns].astype(F32)
    return both[:1]


def forward_kernel(
    low_in,
    low_down,
    hidden_in,
    cotangent,
    condition,
    ada_bias,
    whole_in,
    whole_down,
    hidden,
    grad_out,
    cond_all,
    modulation,
    input_one,
    queries,
    keys,
    values,
    mixed,
    log_totals,
    attn_out,
    middle,
    input_two,
    upward,
    grad_branch,
    gate_grad,
    block_out,
    own_in,
    own_down,
    ada_weights,
    ada_part,
    mod_parts,
    up_stage,
    wide,
    active,
    out_stage,
    send_sem,
    recv_sem,
    core_sem,
    local_sem,
    cond_send,
    cond_recv,
    mod_send,
    mod_recv,
    swap_sem,
    pair_sem,
    up_sem,
):
    z, x, c, y = place()
    dp = (z * 2 + x) * 2 + c
    near = neighbours()
    sems = (send_sem, recv_sem, core_sem)
    refs = {"Broad": (own_in, low_in), "Narrow": (own_in, low_in), "Down": (own_down, low_down)}
    at_home = c == y

    def remote(source, target, sent, arrived, device):
        return pltpu.make_async_remote_copy(
            src_ref=source,
            dst_ref=target,
            send_sem=sent,
            recv_sem=arrived,
            device_id=device,
            device_id_type=MESH,
        )

    broad = pltpu.make_async_copy(
        low_in,
        own_in.at[y, :, pl.ds(pl.multiple_of(jnp.maximum(dp, 7) * WIDE - LOW, LANES), WIDE)],
        local_sem.at[0],
    )
    narrow = pltpu.make_async_copy(
        low_in.at[:, pl.ds(WIDE - 128, 128)], own_in.at[y, :, pl.ds(0, 128)], local_sem.at[0]
    )
    down = pltpu.make_async_copy(
        low_down,
        own_down.at[
            pl.ds(pl.multiple_of(dp * 64, 64), 64),
            pl.ds(pl.multiple_of(y * FF_PART, LANES), FF_PART),
        ],
        local_sem.at[1],
    )
    ada = pltpu.make_async_copy(low_in.at[pl.ds(0, HALF)], ada_weights, local_sem.at[2])
    ada.start()
    down.start()

    @pl.when(dp >= 7)
    def _():
        broad.start()

    @pl.when(dp == 6)
    def _():
        narrow.start()

    greet_all()

    cond_all[dp] = condition[...]

    def cond_copy(at):
        there = lax.rem(dp + at + 1, DP)
        return remote(
            condition, cond_all.at[dp], cond_send.at[at], cond_recv.at[dp], (there, y)
        )

    repeat(DP - 1, lambda at: cond_copy(at).start())

    swaps = []
    for index, (source, target) in enumerate(((hidden_in, hidden), (cotangent, grad_out))):
        swaps.append(
            (
                pltpu.make_async_copy(source, target, swap_sem.at[index, 0]),
                remote(
                    source, target, swap_sem.at[index, 1], swap_sem.at[index, 2], near["swap"]
                ),
            )
        )

    def trade(index):
        @pl.when(at_home)
        def _():
            swaps[index][0].start()

        @pl.when(jnp.logical_not(at_home))
        def _():
            swaps[index][1].start()

    def traded(index):
        @pl.when(at_home)
        def _():
            swaps[index][0].wait()

        @pl.when(jnp.logical_not(at_home))
        def _():
            swaps[index][1].wait()

    trade(0)
    repeat(2, lambda at: forward_step("tick", refs, PLAN_LOW, sems, at))

    def cond_arrived(at):
        there = lax.rem(dp + at + 1, DP)
        remote(
            condition, cond_all.at[there], cond_send.at[at], cond_recv.at[there], (there, y)
        ).wait_recv()

    repeat(DP - 1, cond_arrived)
    raw = jnp.concatenate([cond_all[index] for index in range(DP)], axis=0)
    active[...] = (raw / (1.0 + jnp.exp(-raw))).astype(BF16)
    ada.wait()
    partial = (
        multiply(
            active[:, pl.ds(pl.multiple_of(y * HALF, LANES), HALF)],
            ada_weights[...],
        )
        + ada_bias[...]
    )
    for index in range(DP):
        ada_part[index] = partial[index : index + 1]

    def mod_target(at):
        latent, core = at // 2, lax.rem(at, 2)
        return (latent // 2 * 2 + core, lax.rem(latent, 2))

    def mod_copy(at):
        return remote(
            ada_part.at[at // 2],
            mod_parts.at[dp * 2 + y],
            mod_send.at[at],
            mod_recv.at[dp * 2 + y],
            mod_target(at),
        )

    def elsewhere(at):
        there = mod_target(at)
        return (there[0] != dp) | (there[1] != y)

    @pl.when(dp < 7)
    def _():
        def send(at):
            @pl.when(elsewhere(at))
            def _():
                mod_copy(at).start()

            @pl.when(jnp.logical_not(elsewhere(at)))
            def _():
                mod_parts[dp * 2 + y] = ada_part[at // 2]

        repeat(2 * DP, send)

    forward_step("tick", refs, PLAN_LOW, sems, 2)
    trade(1)
    traded(0)

    def mod_arrived(at):
        @pl.when(at != dp * 2 + y)
        def _():
            remote(
                ada_part.at[0], mod_parts.at[at], mod_send.at[0], mod_recv.at[at], near["x"]
            ).wait_recv()

    repeat(14, mod_arrived)
    for index in range(7):
        modulation[:, index * WIDE : (index + 1) * WIDE] = (
            mod_parts[2 * index] + mod_parts[2 * index + 1]
        )

    def vector(index):
        return modulation[:, index * D : (index + 1) * D]

    def shape_one(at):
        rows = pl.ds(pl.multiple_of(at * 128, 128), 128)
        normed = normalize(hidden[rows].astype(F32))
        input_one[rows] = (normed * (1.0 + vector(1)) + vector(0)).astype(BF16)

    repeat(4, shape_one)

    repeat(
        EARLY_STEPS - 3,
        lambda at: forward_step("tick", refs, PLAN_LOW + PLAN_UP, sems, at + 3),
    )
    repeat(SUBS, lambda at: forward_step("core", refs, PLAN_LOW, sems, at))

    @pl.when(dp >= 7)
    def _():
        broad.wait()

    @pl.when(dp == 6)
    def _():
        narrow.wait()

    def project(at):
        columns = pl.ds(pl.multiple_of(at * 256, LANES), 256)
        keys[:HALF, columns] = from_weights(input_one, own_in, D + at * 256, 256).astype(BF16)
        values[:HALF, columns] = (
            from_weights(input_one, own_in, 2 * D + at * 256, 256)
            + bias_of(own_in, D + at * 256, 256)
        ).astype(BF16)

    repeat(D // 256, project)
    mates = [
        remote(
            one.at[:HALF], one.at[HALF:], pair_sem.at[index, 0], pair_sem.at[index, 1], near["core"]
        )
        for index, one in enumerate((keys, values))
    ]
    for mate in mates:
        mate.start()

    def project_queries(at):
        columns = pl.ds(pl.multiple_of(at * 256, LANES), 256)
        queries[:, columns] = (
            from_weights(input_one, own_in, at * 256, 256) + bias_of(own_in, at * 256, 256)
        ).astype(BF16)

    repeat(D // 256, project_queries)
    for mate in mates:
        mate.wait()

    def attention(pair):
        attend_pair(pair, queries, keys, values, mixed, log_totals)

        @pl.when(lax.rem(pair, 4) == 3)
        def _():
            forward_step("tick", refs, PLAN_UP + PLAN_DOWN, sems, EARLY_STEPS + pair // 4)

    repeat(PAIRS, attention)

    def project_out(at):
        columns = pl.ds(pl.multiple_of(at * 256, LANES), 256)
        attn_out[:, columns] = from_weights(mixed, own_in, 3 * D + at * 256, 256) + bias_of(
            own_in, 2 * D + at * 256, 256
        )

    repeat(D // 256, project_out)

    def shape_two(at):
        rows = pl.ds(pl.multiple_of(at * 128, 128), 128)
        mid = hidden[rows].astype(F32) + vector(2) * attn_out[rows]
        middle[rows] = mid
        input_two[rows] = (normalize(mid) * (1.0 + vector(4)) + vector(3)).astype(BF16)

    repeat(4, shape_two)
    repeat(SUBS, lambda at: forward_step("core", refs, PLAN_UP, sems, at))
    whole_copies = [
        pltpu.make_async_copy(
            own_in.at[half, pl.ds(0, HALF)],
            whole_in.at[pl.ds(half * HALF, HALF)],
            local_sem.at[3 + half],
        )
        for half in range(2)
    ]
    for whole_copy in whole_copies:
        whole_copy.start()
    tile = 512

    def up_copy(at, slot):
        return pltpu.make_async_copy(
            up_stage.at[slot],
            upward.at[:, pl.ds(pl.multiple_of(at * tile, LANES), tile)],
            up_sem.at[slot],
        )

    def widen(at):
        slot = lax.rem(at, 2)

        @pl.when(at >= 2)
        def _():
            up_copy(at - 2, slot).wait()

        for side in range(2):
            start = at * tile + side * 256
            value = from_weights(input_two, own_in, 4 * D + start, 256) + bias_of(
                own_in, 3 * D + start, 256
            )
            up_stage[slot, :, side * 256 : (side + 1) * 256] = value
            inner = math.sqrt(2.0 / math.pi) * (value + 0.044715 * (value * value * value))
            wide[:, pl.ds(pl.multiple_of(start, LANES), 256)] = (
                0.5 * value * (1.0 + jnp.tanh(inner))
            ).astype(BF16)
        up_copy(at, slot).start()

        @pl.when(lax.rem(at, 2) == 1)
        def _():
            forward_step("tick", refs, PLAN_DOWN, sems, EARLY_STEPS + 2 + at // 2)

    repeat(FF // tile, widen)
    for at in (FF // tile - 2, FF // tile - 1):
        up_copy(at, at % 2).wait()
    forward_step("core", refs, PLAN_DOWN, sems, 0)
    down.wait()
    down_copy = pltpu.make_async_copy(own_down, whole_down, local_sem.at[5])
    down_copy.start()
    traded(1)

    def narrow_down(at):
        columns = pl.ds(pl.multiple_of(at * 256, LANES), 256)
        value = bias_of(own_in, 7 * D + at * 256, 256)
        for side in range(2):
            value += multiply(
                wide[:, side * FF_PART : (side + 1) * FF_PART],
                own_down[columns, side * FF_PART : (side + 1) * FF_PART],
                BOTH_LAST,
            )
        gate = modulation[:, pl.ds(pl.multiple_of(5 * D + at * 256, LANES), 256)]
        out_stage[:, columns] = (middle[:, columns] + gate * value).astype(BF16)
        towards = grad_out[:, columns].astype(F32)
        gate_grad[:, columns] = jnp.sum(towards * value, axis=0, keepdims=True)
        grad_branch[:, columns] = (towards * gate).astype(BF16)

    repeat(D // 256, narrow_down)
    home = pltpu.make_async_copy(out_stage, block_out, swap_sem.at[2, 0])
    away = remote(out_stage, block_out, swap_sem.at[2, 1], swap_sem.at[2, 2], near["swap"])

    @pl.when(at_home)
    def _():
        home.start()
        home.wait()

    @pl.when(jnp.logical_not(at_home))
    def _():
        away.start()
        away.wait()

    repeat(SUBS, lambda at: forward_step("drain", refs, PLAN_ALL, sems, at))
    repeat(DP - 1, lambda at: cond_copy(at).wait_send())

    @pl.when(dp < 7)
    def _():
        def sent(at):
            @pl.when(elsewhere(at))
            def _():
                mod_copy(at).wait_send()

        repeat(2 * DP, sent)

    for whole_copy in whole_copies:
        whole_copy.wait()
    down_copy.wait()


def run_forward(low_in, low_down, hidden_in, cotangent, condition, ada_bias):
    shape = jax.ShapeDtypeStruct
    rows = TOKENS_HERE
    outs = [
        (shape((D, KEPT), BF16), pl.ANY),
        (shape((D, FF), BF16), pl.ANY),
        (shape((rows, D), BF16), pltpu.VMEM),
        (shape((rows, D), BF16), pltpu.VMEM),
        (shape((DP, 1, D), F32), pltpu.VMEM),
        (shape((1, 7 * WIDE), F32), pltpu.VMEM),
        (shape((rows, D), BF16), pltpu.VMEM),
        (shape((rows, D), BF16), pltpu.VMEM),
        (shape((2 * rows, D), BF16), pltpu.VMEM),
        (shape((2 * rows, D), BF16), pltpu.VMEM),
        (shape((rows, D), BF16), pltpu.VMEM),
        (shape((HEADS, 1, rows), F32), pltpu.VMEM),
        (shape((rows, D), F32), pltpu.VMEM),
        (shape((rows, D), F32), pltpu.VMEM),
        (shape((rows, D), BF16), pltpu.VMEM),
        (shape((rows, FF), F32), pl.ANY),
        (shape((rows, D), BF16), pltpu.VMEM),
        (shape((1, D), F32), pltpu.VMEM),
        (shape((rows, D), BF16), pl.ANY),
    ]
    dma = pltpu.SemaphoreType.DMA
    return pl.pallas_call(
        forward_kernel,
        out_shape=[one for one, _ in outs],
        in_specs=[pl.BlockSpec(memory_space=pl.ANY)] * 4
        + [pl.BlockSpec(memory_space=pltpu.VMEM)] * 2,
        out_specs=[pl.BlockSpec(memory_space=where) for _, where in outs],
        scratch_shapes=[
            pltpu.VMEM((2, TALL, KEPT), BF16),
            pltpu.VMEM((D, FF), BF16),
            pltpu.VMEM((HALF, WIDE), BF16),
            pltpu.VMEM((DP, 1, WIDE), F32),
            pltpu.VMEM((14, 1, WIDE), F32),
            pltpu.VMEM((2, rows, 512), F32),
            pltpu.VMEM((rows, FF), BF16),
            pltpu.VMEM((DP, D), BF16),
            pltpu.VMEM((rows, D), BF16),
            dma((SLOTS, 5)),
            dma((SLOTS, 2)),
            dma((SLOTS,)),
            dma((6,)),
            dma((DP,)),
            dma((DP,)),
            dma((2 * DP,)),
            dma((14,)),
            dma((3, 3)),
            dma((2, 2)),
            dma((2,)),
        ],
        compiler_params=pltpu.CompilerParams(
            collective_id=0, has_side_effects=True, vmem_limit_bytes=62 * 2**20
        ),
        name="forward",
    )(low_in, low_down, hidden_in, cotangent, condition, ada_bias)


GRAD_SUBS = 4
GRAD_ROWS = HALF // GRAD_SUBS


class BroadGrad:
    height, width, subs, source_column = GRAD_ROWS, WIDE, GRAD_SUBS, 0

    @staticmethod
    def holds(zs, xs, cs):
        return (zs * 2 + xs) * 2 + cs >= 7

    @staticmethod
    def corner(zs, xs, ys, cs, sub):
        column = jnp.maximum(((zs * 2 + xs) * 2 + cs) * WIDE - LOW, 128)
        return (
            pl.multiple_of(ys * HALF + sub * GRAD_ROWS, GRAD_ROWS),
            pl.multiple_of(column, 128),
        )


class NarrowGrad:
    height, width, subs, source_column = HALF, 128, 1, WIDE - 128

    @staticmethod
    def holds(zs, xs, cs):
        return (zs * 2 + xs) * 2 + cs == 6

    @staticmethod
    def corner(zs, xs, ys, cs, sub):
        return (pl.multiple_of(ys * HALF, HALF), 0)


def reduce_block(what, refs, kind, zs, plane_at, planes, relation, sub, sems, valid):
    grads, first_column, owned, buffers = refs
    from_core, from_x, from_y, from_low, from_high, half_a, half_b = buffers
    send_sem, recv_sem = sems
    z, x, c, y = place()
    near = neighbours()
    xs = 1 - x if "x" in relation else x
    ys = 1 - y if "y" in relation else y
    flat = plane_at * kind.subs + sub
    count = planes * kind.subs
    kin = RELATIONS.index(relation)
    slot = kin * count + flat
    rows, half_rows = kind.height, kind.height // 2

    def remote(source, target, index, arrival, key):
        return pltpu.make_async_remote_copy(
            src_ref=source,
            dst_ref=target,
            send_sem=send_sem.at[slot, index],
            recv_sem=recv_sem.at[arrival, flat],
            device_id=near[key],
            device_id_type=MESH,
        )

    def share(cs):
        row, column = kind.corner(zs, xs, ys, cs, sub)
        column = jnp.clip(column - first_column, 0, grads.shape[1] - kind.width)
        return (pl.ds(row, rows), pl.ds(pl.multiple_of(column, 128), kind.width))

    total = from_core.at[slot]
    across = remote(grads.at[share(1 - c)], total, 2, kin, "core")
    other = valid & kind.holds(zs, xs, 1 - c)
    if what == "across":
        pl.when(other)(across.start)
        return
    if what == "drain":
        pl.when(other)(across.wait_send)
    valid = valid & kind.holds(zs, xs, c)
    part_a = from_core.at[slot, pl.ds(0, half_rows)]
    part_b = from_core.at[slot, pl.ds(half_rows, half_rows)]
    if relation == "xy":
        sends = [
            (valid, remote(part_a, half_a.at[flat], 0, 4, "y")),
            (valid, remote(part_b, half_b.at[flat], 1, 5, "x")),
        ]
    elif relation == "x":
        sends = [(valid, remote(total, from_x.at[flat], 0, 6, "x"))]
    elif relation == "y":
        sends = [(valid, remote(total, from_y.at[flat], 0, 7, "y"))]
    else:
        sends = [
            (valid & (z < zs), remote(total, from_low.at[flat], 0, 8, "up")),
            (valid & (z > zs), remote(total, from_high.at[flat], 1, 9, "down")),
        ]
    if what == "drain":
        for condition, descriptor in sends:
            pl.when(condition)(descriptor.wait_send)
        return

    @pl.when(valid)
    def _():
        remote(total, total, 2, kin, "core").wait_recv()
        value = from_core[slot].astype(F32) + grads[share(c)].astype(F32)
        if relation == "xy":
            from_core[slot] = value.astype(BF16)
        elif relation == "x":
            remote(half_a.at[flat], half_a.at[flat], 0, 4, "y").wait_recv()
            from_core[slot, pl.ds(half_rows, half_rows)] = value[half_rows:].astype(BF16)
            from_core[slot, pl.ds(0, half_rows)] = (
                value[:half_rows] + half_a[flat].astype(F32)
            ).astype(BF16)
        elif relation == "y":
            remote(half_b.at[flat], half_b.at[flat], 1, 5, "x").wait_recv()
            from_core[slot, pl.ds(0, half_rows)] = value[:half_rows].astype(BF16)
            from_core[slot, pl.ds(half_rows, half_rows)] = (
                value[half_rows:] + half_b[flat].astype(F32)
            ).astype(BF16)
        else:
            remote(from_x.at[flat], from_x.at[flat], 0, 6, "x").wait_recv()
            remote(from_y.at[flat], from_y.at[flat], 0, 7, "y").wait_recv()
            value += from_x[flat].astype(F32) + from_y[flat].astype(F32)

            @pl.when((z <= zs) & (z > 0))
            def _():
                remote(from_low.at[flat], from_low.at[flat], 0, 8, "up").wait_recv()

            @pl.when((z >= zs) & (z < PLANES - 1))
            def _():
                remote(from_high.at[flat], from_high.at[flat], 1, 9, "down").wait_recv()

            def low():
                return jnp.where(z > 0, from_low[flat].astype(F32), 0.0)

            def high():
                return jnp.where(z < PLANES - 1, from_high[flat].astype(F32), 0.0)

            @pl.when(z < zs)
            def _():
                from_core[slot] = (value + low()).astype(BF16)

            @pl.when(z > zs)
            def _():
                from_core[slot] = (value + high()).astype(BF16)

            @pl.when(z == zs)
            def _():
                owned[
                    pl.ds(pl.multiple_of(sub * rows, rows), rows),
                    pl.ds(kind.source_column, kind.width),
                ] = value + low() + high()

    for condition, descriptor in sends:
        pl.when(condition)(descriptor.start)


def reduce_step(what, refs, plan, sems, at):
    z = place()[0]
    for kind, planes in plan:
        name = kind.__name__
        for plane_at, zs in enumerate(planes):
            for relation in ("xy", "x", "y", "own"):
                sub = at
                if what == "tick":
                    depth = 0
                    if relation == "own":
                        depth = by_plane(
                            z,
                            [
                                place_z
                                if place_z < zs
                                else max(place_z, 3 - place_z)
                                if place_z == zs
                                else 3 - place_z
                                for place_z in range(PLANES)
                            ],
                        )
                    sub = at - (2 - HOPS[relation] + depth)
                reduce_block(
                    what,
                    refs[name],
                    kind,
                    zs,
                    plane_at,
                    len(planes),
                    relation,
                    jnp.clip(sub, 0, kind.subs - 1),
                    sems[name],
                    (sub >= 0) & (sub < kind.subs),
                )


def landing(kind, planes):
    count = planes * kind.subs
    full = pltpu.VMEM((count, kind.height, kind.width), BF16)
    half = pltpu.VMEM((count, kind.height // 2, kind.width), BF16)
    return [pltpu.VMEM((4 * count, kind.height, kind.width), BF16)] + [full] * 4 + [half] * 2


def landing_signals(kind, planes):
    count = planes * kind.subs
    return [pltpu.SemaphoreType.DMA((4 * count, 3)), pltpu.SemaphoreType.DMA((10, count))]


def greet_near():
    z, x, c, y = place()
    near = neighbours()
    barrier = pltpu.get_barrier_semaphore()
    for key in ("x", "y", "core"):
        pl.semaphore_signal(barrier, inc=1, device_id=near[key], device_id_type=MESH)

    @pl.when(z < PLANES - 1)
    def _():
        pl.semaphore_signal(barrier, inc=1, device_id=near["up"], device_id_type=MESH)

    @pl.when(z > 0)
    def _():
        pl.semaphore_signal(barrier, inc=1, device_id=near["down"], device_id_type=MESH)

    middle = (z > 0) & (z < PLANES - 1)

    @pl.when(middle)
    def _():
        pl.semaphore_wait(barrier, 5)

    @pl.when(jnp.logical_not(middle))
    def _():
        pl.semaphore_wait(barrier, 4)


REDUCE_HIGH = ((BroadGrad, (3,)),)
REDUCE_LOW = ((BroadGrad, (1, 2)), (NarrowGrad, (1,)))
HIGH_STEPS = GRAD_SUBS + 5
LOW_STEPS = GRAD_SUBS + 5
HIGH_FIRST = FF // 8


def attend_back(
    pair, queries, keys, values, mixed, grad_mixed, log_totals, grad_query, grad_key, grad_value
):
    columns = pl.ds(pl.multiple_of(pair * LANES, LANES), LANES)
    key_block = keys[:, columns]
    value_block = values[:, columns]
    key_flat = key_block.T
    key_sum, value_sum = None, None
    step = 256
    for part in range(TOKENS_HERE // step):
        rows = pl.ds(part * step, step)
        grad_block = grad_mixed[rows, columns]
        product = (grad_block.astype(F32) * mixed[rows, columns].astype(F32)).T
        query_parts = []
        heads = zip(two_heads(queries[rows, columns]), two_heads(grad_block))
        for head, (query_head, grad_head) in enumerate(heads):
            scores = multiply(key_block, query_head, BOTH_LAST)
            weights = jnp.exp(scores * HEAD_DIM**-0.5 - log_totals[2 * pair + head, :, rows])
            grad_weights = multiply(value_block, grad_head, BOTH_LAST)
            inner = jnp.sum(
                product[HEAD_DIM * head : HEAD_DIM * (head + 1)], axis=0, keepdims=True
            )
            grad_scores = (weights * (grad_weights - inner)).astype(BF16)
            value_term = multiply(weights.astype(BF16), grad_head)
            key_term = multiply(grad_scores, query_head)
            value_sum = value_term if value_sum is None else value_sum + value_term
            key_sum = key_term if key_sum is None else key_sum + key_term
            query_parts.append(multiply(key_flat, grad_scores))
        joined = jnp.concatenate([query_parts[0][:HEAD_DIM], query_parts[1][HEAD_DIM:]], axis=0)
        grad_query[rows, columns] = (joined * HEAD_DIM**-0.5).T.astype(BF16)
    grad_key[:, columns] = (key_sum * HEAD_DIM**-0.5).astype(BF16)
    grad_value[:, columns] = value_sum.astype(BF16)


def backward_kernel(
    queries,
    keys,
    values,
    mixed,
    grad_mixed,
    log_totals,
    grads,
    grad_query,
    grad_key,
    grad_value,
    owned,
    key_all,
    value_all,
    key_mate,
    value_mate,
    mate_sem,
    *scratch,
):
    dp = lax.axis_index("dp")
    near = neighbours()
    refs = {"BroadGrad": (grads, 4 * D, owned, scratch[:7])}
    sems = {"BroadGrad": scratch[7:9]}
    greet_near()
    repeat(GRAD_SUBS, lambda at: reduce_step("across", refs, REDUCE_HIGH, sems, at))

    @pl.when(dp < 12)
    def _():
        owned[...] = jnp.zeros_like(owned)

    def mates(pair):
        columns = pl.ds(pl.multiple_of(pair * LANES, LANES), LANES)
        return [
            pltpu.make_async_remote_copy(
                src_ref=source.at[HALF:, columns],
                dst_ref=target.at[:, columns],
                send_sem=mate_sem.at[pair, 2 * index],
                recv_sem=mate_sem.at[pair, 2 * index + 1],
                device_id=near["core"],
                device_id_type=MESH,
            )
            for index, (source, target) in enumerate(((key_all, key_mate), (value_all, value_mate)))
        ]

    def attention(pair):
        reduce_step("tick", refs, REDUCE_HIGH, sems, pair)
        attend_back(
            pair,
            queries,
            keys,
            values,
            mixed,
            grad_mixed,
            log_totals,
            grad_query,
            key_all,
            value_all,
        )
        for mate in mates(pair):
            mate.start()

    repeat(PAIRS, attention)
    for source, target, total, index in (
        (key_all, key_mate, grad_key, 0),
        (value_all, value_mate, grad_value, 1),
    ):
        repeat(PAIRS, lambda pair: mates(pair)[index].wait())
        total[...] = (source[:HALF].astype(F32) + target[...].astype(F32)).astype(BF16)
    repeat(
        HIGH_STEPS - PAIRS, lambda at: reduce_step("tick", refs, REDUCE_HIGH, sems, at + PAIRS)
    )
    repeat(GRAD_SUBS, lambda at: reduce_step("drain", refs, REDUCE_HIGH, sems, at))


def run_backward(queries, keys, values, mixed, grad_mixed, log_totals, grads):
    shape = jax.ShapeDtypeStruct
    rows = TOKENS_HERE
    vmem = pl.BlockSpec(memory_space=pltpu.VMEM)
    return pl.pallas_call(
        backward_kernel,
        out_shape=[shape((rows, D), BF16)] * 3 + [shape((HALF, WIDE), F32)],
        in_specs=[vmem] * 7,
        out_specs=[vmem] * 4,
        scratch_shapes=[pltpu.VMEM((2 * rows, D), BF16)] * 2
        + [pltpu.VMEM((rows, D), BF16)] * 2
        + [pltpu.SemaphoreType.DMA((PAIRS, 4))]
        + landing(BroadGrad, 1)
        + landing_signals(BroadGrad, 1),
        compiler_params=pltpu.CompilerParams(
            collective_id=1, has_side_effects=True, vmem_limit_bytes=60 * 2**20
        ),
        cost_estimate=pl.CostEstimate(
            flops=5 * 2 * 512 * 1024 * 1024 * 2, bytes_accessed=60 * 2**20, transcendentals=2**23
        ),
        name="backward",
    )(queries, keys, values, mixed, grad_mixed, log_totals, grads)


VECTOR = 17 * WIDE


def finish_kernel(
    grad_qkv,
    grad_out_proj,
    grad_up,
    low_in,
    active_rows,
    condition,
    sums,
    input_grad,
    owned_high,
    owned,
    cond_grad,
    bias_parts,
    ada_bias_grad,
    input_swapped,
    grads,
    ada_weights,
    sum_mate,
    sum_pieces,
    ada_in,
    cond_piece,
    cond_in,
    local_sem,
    mate_sem,
    piece_send,
    ada_recv,
    bias_recv,
    cond_send,
    cond_recv,
    swap_sem,
    *scratch,
):
    z, x, c, y = place()
    dp = (z * 2 + x) * 2 + c
    near = neighbours()
    refs = {
        "BroadGrad": (grads, 0, owned, scratch[0:7]),
        "NarrowGrad": (grads, 0, owned, scratch[7:14]),
    }
    sems = {"BroadGrad": scratch[14:16], "NarrowGrad": scratch[16:18]}
    at_home = c == y

    def remote(source, target, sent, arrived, device):
        return pltpu.make_async_remote_copy(
            src_ref=source,
            dst_ref=target,
            send_sem=sent,
            recv_sem=arrived,
            device_id=device,
            device_id_type=MESH,
        )

    loads = [
        pltpu.make_async_copy(grad_qkv, grads.at[:, : 3 * D], local_sem.at[0]),
        pltpu.make_async_copy(grad_out_proj, grads.at[:, 3 * D : 4 * D], local_sem.at[1]),
        pltpu.make_async_copy(
            grad_up.at[:, :HIGH_FIRST], grads.at[:, 4 * D : 4 * D + HIGH_FIRST], local_sem.at[2]
        ),
        pltpu.make_async_copy(low_in.at[pl.ds(0, HALF)], ada_weights, local_sem.at[3]),
    ]
    for load in loads:
        load.start()
    owned[...] = owned_high[...]
    greet_all()
    mate = remote(sums, sum_mate, mate_sem.at[0], mate_sem.at[1], near["core"])
    mate.start()
    away = remote(input_grad, input_swapped, swap_sem.at[0], swap_sem.at[1], near["swap"])

    for load in loads[:3]:
        load.wait()
    repeat(GRAD_SUBS, lambda at: reduce_step("across", refs, REDUCE_LOW, sems, at))

    mate.wait()
    for index in range(17):
        columns = slice(index * WIDE, (index + 1) * WIDE)
        piece = sums[:, columns] + sum_mate[:, columns]
        if index < 7:
            piece = piece.astype(BF16).astype(F32)
        sum_pieces[index] = piece
    latent = (z * 2 + x) * 2 + y

    def piece_target(at):
        return jnp.where(at < 7, at, at - 1)

    def piece_copy(at, target, arrived):
        return remote(
            sum_pieces.at[at], target, piece_send.at[at], arrived, (piece_target(at), c)
        )

    def each_piece(act, keep):
        def go(at):
            mine = (piece_target(at) == dp) & (y == c)

            @pl.when(jnp.logical_not(mine) & (at < 7))
            def _():
                act(piece_copy(at, ada_in.at[latent], ada_recv.at[latent]))

            @pl.when(jnp.logical_not(mine) & (at >= 7))
            def _():
                act(piece_copy(at, bias_parts.at[latent], bias_recv.at[latent]))

            if keep:

                @pl.when(mine & (at < 7))
                def _():
                    ada_in[latent] = sum_pieces[at]

                @pl.when(mine & (at >= 7))
                def _():
                    bias_parts[latent] = sum_pieces[at]

        repeat(17, go)

    each_piece(lambda copy: copy.start(), True)
    repeat(3, lambda at: reduce_step("tick", refs, REDUCE_LOW, sems, at))

    @pl.when(jnp.logical_not(at_home))
    def _():
        away.start()

    def from_latent(at, target, arrived):
        mine = (at // 2 == z * 2 + x) & (lax.rem(at, 2) == y) & (c == y)

        @pl.when(jnp.logical_not(mine))
        def _():
            remote(
                sum_pieces.at[0], target.at[at], piece_send.at[0], arrived.at[at], near["x"]
            ).wait_recv()

    loads[3].wait()

    @pl.when(dp < 7)
    def _():
        repeat(DP, lambda at: from_latent(at, ada_in, ada_recv))
        gathered = jnp.concatenate([ada_in[index] for index in range(DP)], axis=0)
        ada_bias_grad[...] = jnp.sum(gathered, axis=0, keepdims=True)
        narrow = gathered.astype(BF16)
        owned[...] += multiply(active_rows[...], narrow, BOTH_FIRST)
        part = multiply(narrow, ada_weights[...], BOTH_LAST)
        for index in range(DP):
            cond_piece[index] = part[index : index + 1]

    @pl.when(dp >= 7)
    def _():
        ada_bias_grad[...] = jnp.zeros_like(ada_bias_grad)

    def cond_copy(at):
        return remote(
            cond_piece.at[at // 2],
            cond_in.at[dp * 2 + y],
            cond_send.at[at],
            cond_recv.at[dp * 2 + y],
            (at // 2, lax.rem(at, 2)),
        )

    def each_cond(act, keep):
        def go(at):
            mine = at == dp * 2 + y

            @pl.when(jnp.logical_not(mine))
            def _():
                act(cond_copy(at))

            if keep:

                @pl.when(mine)
                def _():
                    cond_in[dp * 2 + y] = cond_piece[at // 2]

        repeat(2 * DP, go)

    @pl.when(dp < 7)
    def _():
        each_cond(lambda copy: copy.start(), True)

    repeat(LOW_STEPS - 3, lambda at: reduce_step("tick", refs, REDUCE_LOW, sems, at + 3))

    def cond_arrived(at):
        @pl.when(at != dp * 2 + y)
        def _():
            remote(
                cond_piece.at[0], cond_in.at[at], cond_send.at[0], cond_recv.at[at], near["x"]
            ).wait_recv()

    repeat(14, cond_arrived)
    sides = []
    for side in range(2):
        total = cond_in[side]
        for index in range(1, 7):
            total = total + cond_in[2 * index + side]
        sides.append(total)
    value = condition[...]
    logistic = 1.0 / (1.0 + jnp.exp(-value))
    cond_grad[...] = jnp.concatenate(sides, axis=1) * (
        logistic * (1.0 + value * (1.0 - logistic))
    )

    @pl.when(dp >= 6)
    def _():
        repeat(DP, lambda at: from_latent(at, bias_parts, bias_recv))

    @pl.when(dp < 6)
    def _():
        bias_parts[...] = jnp.zeros_like(bias_parts)

    @pl.when(jnp.logical_not(at_home))
    def _():
        away.wait()

    each_piece(lambda copy: copy.wait_send(), False)

    @pl.when(dp < 7)
    def _():
        each_cond(lambda copy: copy.wait_send(), False)

    repeat(GRAD_SUBS, lambda at: reduce_step("drain", refs, REDUCE_LOW, sems, at))


def run_finish(
    grad_qkv, grad_out_proj, grad_up, low_in, active_rows, condition, sums, input_grad, owned_high
):
    shape = jax.ShapeDtypeStruct
    dma = pltpu.SemaphoreType.DMA
    vmem = pl.BlockSpec(memory_space=pltpu.VMEM)
    hbm = pl.BlockSpec(memory_space=pl.ANY)
    return pl.pallas_call(
        finish_kernel,
        out_shape=[
            shape((HALF, WIDE), F32),
            shape((1, D), F32),
            shape((DP, 1, WIDE), F32),
            shape((1, WIDE), F32),
            shape((TOKENS_HERE, D), BF16),
        ],
        in_specs=[hbm] * 4 + [vmem] * 3 + [hbm, vmem],
        out_specs=[vmem] * 4 + [hbm],
        scratch_shapes=[
            pltpu.VMEM((D, 4 * D + HIGH_FIRST), BF16),
            pltpu.VMEM((HALF, WIDE), BF16),
            pltpu.VMEM((1, VECTOR), F32),
            pltpu.VMEM((17, 1, WIDE), F32),
            pltpu.VMEM((DP, 1, WIDE), F32),
            pltpu.VMEM((DP, 1, HALF), F32),
            pltpu.VMEM((14, 1, HALF), F32),
            dma((4,)),
            dma((2,)),
            dma((17,)),
            dma((DP,)),
            dma((DP,)),
            dma((2 * DP,)),
            dma((14,)),
            dma((2,)),
        ]
        + landing(BroadGrad, 2)
        + landing(NarrowGrad, 1)
        + landing_signals(BroadGrad, 2)
        + landing_signals(NarrowGrad, 1),
        compiler_params=pltpu.CompilerParams(
            collective_id=2, has_side_effects=True, vmem_limit_bytes=60 * 2**20
        ),
        name="finish",
    )(grad_qkv, grad_out_proj, grad_up, low_in, active_rows, condition, sums, input_grad, owned_high)


def local(
    hidden_in,
    condition,
    cotangent,
    weights_in,
    weights_down,
    biases,
    moment_in,
    moment_down,
    moment_bias,
    square_in,
    square_down,
    square_bias,
):
    dp = lax.axis_index("dp")
    y = lax.axis_index("seq")
    side = WIDE // 2
    bias_row = jnp.pad(biases.astype(BF16)[None], ((0, 15), (0, side)))
    bias_row = jnp.where(y == 0, bias_row, jnp.roll(bias_row, side, axis=1))
    low_in = jnp.concatenate([weights_in.astype(BF16), bias_row], axis=0)
    cond_float = condition.astype(F32)
    (
        whole_in,
        whole_down,
        hidden,
        grad_out,
        cond_all,
        modulation,
        input_one,
        queries,
        keys,
        values,
        mixed,
        log_totals,
        attn_out,
        middle,
        input_two,
        upward,
        grad_branch,
        gate_two_grad,
        block_out,
    ) = run_forward(
        low_in,
        weights_down.astype(BF16).T,
        hidden_in[0],
        cotangent[0],
        cond_float,
        bias_row[:1].astype(F32),
    )
    grad_out = grad_out.astype(F32)
    pieces = [modulation[:, part * D : (part + 1) * D] for part in range(6)]
    shift_one, scale_one, gate_one, shift_two, scale_two, gate_two = pieces

    def back_through(gradients, start, width):
        return lax.dot_general(
            gradients,
            whole_in[:, start : start + width],
            BOTH_LAST,
            preferred_element_type=F32,
        )

    def outer(left, right):
        return lax.dot_general(left, right, BOTH_FIRST, preferred_element_type=F32)

    def down_rows(total):
        return jnp.sum(total.astype(F32), axis=0, keepdims=True)

    activated, gelu_pull = jax.vjp(lambda inner: jax.nn.gelu(inner, approximate=True), upward)
    grad_down = outer(activated.astype(BF16), grad_branch)
    grad_act = jnp.dot(grad_branch, whole_down, preferred_element_type=F32)
    grad_upward = gelu_pull(grad_act)[0].astype(BF16)
    grad_up = outer(input_two, grad_upward).astype(BF16)
    grad_input_two = back_through(grad_upward, 4 * D, FF)
    normed_two, norm_pull_two = jax.vjp(layer_norm, middle)
    shift_two_grad = down_rows(grad_input_two)
    scale_two_grad = down_rows(grad_input_two * normed_two)
    grad_middle = grad_out + norm_pull_two(grad_input_two * (1.0 + scale_two))[0]
    grad_attn = (grad_middle * gate_one).astype(BF16)
    gate_one_grad = down_rows(grad_middle * attn_out)
    grad_out_proj = outer(mixed, grad_attn).astype(BF16)
    grad_mixed = back_through(grad_attn, 3 * D, D).astype(BF16)
    down_sum = lax.psum_scatter(
        grad_down.astype(BF16), "dp", scatter_dimension=1, tiled=True
    )
    grad_query, grad_key, grad_value, owned_high = run_backward(
        queries, keys, values, mixed, grad_mixed, log_totals, grad_up
    )
    grad_qkv = jnp.concatenate([grad_query, grad_key, grad_value], axis=-1)
    grad_proj_qkv = outer(input_one, grad_qkv).astype(BF16)
    grad_input_one = back_through(grad_qkv, 0, 3 * D)
    normed_one, norm_pull_one = jax.vjp(layer_norm, hidden.astype(F32))
    shift_one_grad = down_rows(grad_input_one)
    scale_one_grad = down_rows(grad_input_one * normed_one)
    input_grad = grad_middle + norm_pull_one(grad_input_one * (1.0 + scale_one))[0]
    sums = jnp.concatenate(
        [
            shift_one_grad,
            scale_one_grad,
            gate_one_grad,
            shift_two_grad,
            scale_two_grad,
            gate_two_grad,
            jnp.zeros((1, WIDE), F32),
            down_rows(grad_query),
            down_rows(grad_value),
            down_rows(grad_attn),
            down_rows(grad_upward),
            down_rows(grad_branch),
        ],
        axis=-1,
    )
    active_rows = lax.dynamic_slice_in_dim(
        jax.nn.silu(cond_all[:, 0]).astype(BF16), y * HALF, HALF, 1
    )
    owned_in, cond_grad, bias_parts, ada_bias_grad, input_swapped = run_finish(
        grad_proj_qkv,
        grad_out_proj,
        grad_up,
        low_in,
        active_rows,
        cond_float,
        sums,
        input_grad.astype(BF16),
        owned_high,
    )
    at_home = lax.rem(dp, 2) == y
    input_grad = jnp.where(at_home, input_grad, input_swapped.astype(F32))
    owned_down = lax.psum_scatter(down_sum, "seq", scatter_dimension=0, tiled=True).astype(F32)
    owned_bias = jnp.sum(bias_parts[:, 0], axis=0) + ada_bias_grad[0]
    owned_bias = lax.dynamic_slice_in_dim(owned_bias, y * side, side, 0)
    moments_in, squares_in, master_in = adamw_step(
        weights_in, moment_in, square_in, owned_in, rate_in
    )
    moments_down, squares_down, master_down = adamw_step(
        weights_down, moment_down, square_down, owned_down, rate_down
    )
    moments_bias, squares_bias, master_bias = adamw_step(
        biases, moment_bias, square_bias, owned_bias, rate_bias
    )
    return (
        block_out[None],
        input_grad[None],
        cond_grad,
        moments_in,
        moments_down,
        moments_bias,
        squares_in,
        squares_down,
        squares_bias,
        master_in,
        master_down,
        master_bias,
        master_in.astype(BF16),
        master_down.astype(BF16),
        master_bias.astype(BF16),
    )


def solution(mesh):
    return jax.shard_map(
        local if dict(mesh.shape) == {"dp": 16, "seq": 2} else local_general,
        mesh=mesh,
        in_specs=(
            P("dp", "seq", None),
            P("dp", None),
            P("dp", "seq", None),
            P("seq", "dp"),
            P("seq", "dp"),
            P(("dp", "seq")),
            P("seq", "dp"),
            P("seq", "dp"),
            P(("dp", "seq")),
            P("seq", "dp"),
            P("seq", "dp"),
            P(("dp", "seq")),
        ),
        out_specs=(
            P("dp", "seq", None),
            P("dp", "seq", None),
            P("dp", None),
            P("seq", "dp"),
            P("seq", "dp"),
            P(("dp", "seq")),
            P("seq", "dp"),
            P("seq", "dp"),
            P(("dp", "seq")),
            P("seq", "dp"),
            P("seq", "dp"),
            P(("dp", "seq")),
            P("seq", "dp"),
            P("seq", "dp"),
            P(("dp", "seq")),
        ),
        check_vma=False,
    )
```

```python
import math

import jax
import jax.numpy as jnp
from jax import lax
from jax.experimental import pallas as pl
from jax.experimental.pallas import tpu as pltpu
from jax.sharding import PartitionSpec as P

D = 1024
HEADS = 16
HEAD_DIM = 64
FF = 4096
STEP = 5


norm_eps = 1e-06
beta_first = 0.5
beta_second = 0.5
adam_eps = 1e-08
weight_decay = 0.01
rate_in = 0.03
rate_down = 0.016
rate_bias = 0.3


def layer_norm(values):
    center = values - jnp.mean(values, axis=-1, keepdims=True)
    return center * lax.rsqrt(jnp.mean(center * center, axis=-1, keepdims=True) + norm_eps)


def adamw_step(master, moment, square, gradient, step_rate):
    moment_new = beta_first * moment + (1.0 - beta_first) * gradient
    square_new = beta_second * square + (1.0 - beta_second) * gradient * gradient
    corrected = moment_new / (1.0 - beta_first**STEP)
    scale_sq = square_new / (1.0 - beta_second**STEP)
    master_new = master - step_rate * (
        corrected / (jnp.sqrt(scale_sq) + adam_eps) + weight_decay * master
    )
    return (moment_new, square_new, master_new)


def dense_map(values, matrix):
    return jnp.einsum("nld,de->nle", values, matrix, preferred_element_type=jnp.float32)


def dense_back(gradients, matrix):
    return jnp.einsum("nle,de->nld", gradients, matrix, preferred_element_type=jnp.float32)


def outer_sum(values, gradients):
    return jnp.einsum("nld,nle->de", values, gradients, preferred_element_type=jnp.float32)


def total_sum(values):
    return jnp.sum(values.astype(jnp.float32), axis=(0, 1))


def gather_weights(low_in, low_down, low_bias):
    seq_parts = (
        lax.all_gather(low_in, "seq", axis=0, tiled=True),
        lax.all_gather(low_down, "seq", axis=0, tiled=True),
        lax.all_gather(low_bias, "seq", axis=0, tiled=True),
    )
    whole_in, whole_down, bias_row = (
        lax.all_gather(seq_parts[0], "dp", axis=1, tiled=True),
        lax.all_gather(seq_parts[1], "dp", axis=1, tiled=True),
        lax.all_gather(seq_parts[2].reshape(1, -1), "dp", axis=1, tiled=True),
    )
    return (whole_in, whole_down, bias_row[0])


def head_layout():
    heads_here = math.gcd(HEADS, max(1, 128 // HEAD_DIM))
    return (heads_here, heads_here * HEAD_DIM, HEADS // heads_here)


def split_heads(values, lane_start, lane_count, heads_here):
    piece = lax.dynamic_slice_in_dim(values, lane_start, lane_count, 2)
    return piece.reshape(piece.shape[0], piece.shape[1], heads_here, HEAD_DIM)


def join_heads(stacked):
    moved = jnp.moveaxis(stacked, 0, 2)
    return moved.reshape(moved.shape[0], moved.shape[1], moved.shape[2] * moved.shape[3])


def attention_forward(queries, keys_all, values_all):
    heads_here, lane_count, head_steps = head_layout()
    scale_factor = HEAD_DIM ** (-0.5)

    def one_group(group_index):
        lane_start = group_index * lane_count
        query_part = split_heads(queries, lane_start, lane_count, heads_here)
        key_part = split_heads(keys_all, lane_start, lane_count, heads_here)
        value_part = split_heads(values_all, lane_start, lane_count, heads_here)
        scores = (
            jnp.einsum("nqhd,nkhd->nhqk", query_part, key_part, preferred_element_type=jnp.float32)
            * scale_factor
        )
        row_max = jnp.max(scores, axis=-1, keepdims=True)
        exponent = jnp.exp(scores - row_max)
        row_total = jnp.sum(exponent, axis=-1, keepdims=True)
        weights = (exponent / row_total).astype(jnp.bfloat16)
        attn_part = jnp.einsum(
            "nhqk,nkhd->nqhd", weights, value_part, preferred_element_type=jnp.float32
        )
        shaped = attn_part.reshape(attn_part.shape[0], attn_part.shape[1], lane_count)
        return (shaped, (row_max + jnp.log(row_total))[..., 0])

    stacked, log_totals = lax.map(one_group, jnp.arange(head_steps))
    return (join_heads(stacked), log_totals)


def attention_backward(queries, keys_all, values_all, log_totals, grad_mixed):
    heads_here, lane_count, head_steps = head_layout()
    scale_factor = HEAD_DIM ** (-0.5)

    def one_group(carried):
        group_index, log_part = carried
        lane_start = group_index * lane_count
        query_part = split_heads(queries, lane_start, lane_count, heads_here)
        key_part = split_heads(keys_all, lane_start, lane_count, heads_here)
        value_part = split_heads(values_all, lane_start, lane_count, heads_here)
        grad_part = split_heads(grad_mixed, lane_start, lane_count, heads_here)
        scores = (
            jnp.einsum("nqhd,nkhd->nhqk", query_part, key_part, preferred_element_type=jnp.float32)
            * scale_factor
        )
        probability = jnp.exp(scores - log_part[..., None])
        grad_prob = jnp.einsum(
            "nqhd,nkhd->nhqk", grad_part, value_part, preferred_element_type=jnp.float32
        )
        inner_sum = jnp.sum(probability * grad_prob, axis=-1, keepdims=True)
        grad_score = (probability * (grad_prob - inner_sum)).astype(jnp.bfloat16)
        grad_query = (
            jnp.einsum("nhqk,nkhd->nqhd", grad_score, key_part, preferred_element_type=jnp.float32)
            * scale_factor
        )
        grad_key = (
            jnp.einsum(
                "nhqk,nqhd->nkhd", grad_score, query_part, preferred_element_type=jnp.float32
            )
            * scale_factor
        )
        grad_value = jnp.einsum(
            "nhqk,nqhd->nkhd",
            probability.astype(jnp.bfloat16),
            grad_part,
            preferred_element_type=jnp.float32,
        )
        return (
            grad_query.reshape(grad_query.shape[0], grad_query.shape[1], lane_count),
            grad_key.reshape(grad_key.shape[0], grad_key.shape[1], lane_count),
            grad_value.reshape(grad_value.shape[0], grad_value.shape[1], lane_count),
        )

    query_terms, key_terms, value_terms = lax.map(one_group, (jnp.arange(head_steps), log_totals))
    return (join_heads(query_terms), join_heads(key_terms), join_heads(value_terms))


def local_general(
    hidden_in,
    condition,
    cotangent,
    weights_in,
    weights_down,
    biases,
    moment_in,
    moment_down,
    moment_bias,
    square_in,
    square_down,
    square_bias,
):
    low_in = weights_in.astype(jnp.bfloat16)
    low_down = weights_down.astype(jnp.bfloat16)
    low_bias = biases.astype(jnp.bfloat16)
    whole_in, whole_down, bias_all = gather_weights(low_in, low_down, low_bias)
    bias_float = bias_all.astype(jnp.float32)
    hidden = hidden_in.astype(jnp.float32)
    cond_float = condition.astype(jnp.float32)
    cond_act = jax.nn.silu(cond_float).astype(jnp.bfloat16)
    modulation = (
        jnp.dot(cond_act, whole_in[:, : 6 * D], preferred_element_type=jnp.float32)
        + bias_float[: 6 * D]
    )
    pieces = [modulation[:, None, part_index * D : (part_index + 1) * D] for part_index in range(6)]
    shift_one, scale_one, gate_one, shift_two, scale_two, gate_two = pieces
    normed_one = layer_norm(hidden)
    input_one = (normed_one * (1.0 + scale_one) + shift_one).astype(jnp.bfloat16)
    qkv_all = dense_map(input_one, whole_in[:, 6 * D : 9 * D])
    queries = (qkv_all[..., :D] + bias_float[6 * D : 7 * D]).astype(jnp.bfloat16)
    keys_local = qkv_all[..., D : 2 * D].astype(jnp.bfloat16)
    values_local = (qkv_all[..., 2 * D :] + bias_float[7 * D : 8 * D]).astype(jnp.bfloat16)
    keys_all, values_all = (
        lax.all_gather(keys_local, "seq", axis=1, tiled=True),
        lax.all_gather(values_local, "seq", axis=1, tiled=True),
    )
    attn_float, log_totals = attention_forward(queries, keys_all, values_all)
    attn_mixed = attn_float.astype(jnp.bfloat16)
    attn_out = dense_map(attn_mixed, whole_in[:, 9 * D : 10 * D]) + bias_float[8 * D : 9 * D]
    middle = hidden + gate_one * attn_out
    normed_two = layer_norm(middle)
    input_two = (normed_two * (1.0 + scale_two) + shift_two).astype(jnp.bfloat16)
    upward = dense_map(input_two, whole_in[:, 10 * D :]) + bias_float[9 * D : 9 * D + FF]
    activated = jax.nn.gelu(upward, approximate=True).astype(jnp.bfloat16)
    branch = dense_map(activated, whole_down) + bias_float[9 * D + FF :]
    block_out = (middle + gate_two * branch).astype(jnp.bfloat16)
    whole_in, whole_down, bias_all = gather_weights(low_in, low_down, low_bias)
    grad_out = cotangent.astype(jnp.float32)
    grad_branch = (grad_out * gate_two).astype(jnp.bfloat16)
    gate_two_grad = jnp.sum(grad_out * branch, axis=1)
    grad_down = outer_sum(activated, grad_branch)
    bias_down_grad = total_sum(grad_branch)
    grad_act = dense_back(grad_branch, whole_down)
    _, gelu_pull = jax.vjp(lambda inner_value: jax.nn.gelu(inner_value, approximate=True), upward)
    grad_upward = gelu_pull(grad_act)[0].astype(jnp.bfloat16)
    grad_up = outer_sum(input_two, grad_upward)
    bias_up_grad = total_sum(grad_upward)
    grad_input_two = dense_back(grad_upward, whole_in[:, 10 * D :])
    shift_two_grad = jnp.sum(grad_input_two, axis=1)
    scale_two_grad = jnp.sum(grad_input_two * normed_two, axis=1)
    _, norm_pull_two = jax.vjp(layer_norm, middle)
    grad_middle = grad_out + norm_pull_two(grad_input_two * (1.0 + scale_two))[0]
    grad_attn = (grad_middle * gate_one).astype(jnp.bfloat16)
    gate_one_grad = jnp.sum(grad_middle * attn_out, axis=1)
    grad_out_proj = outer_sum(attn_mixed, grad_attn)
    bias_out_grad = total_sum(grad_attn)
    grad_mixed = dense_back(grad_attn, whole_in[:, 9 * D : 10 * D]).astype(jnp.bfloat16)
    grad_query, key_terms, value_terms = attention_backward(
        queries, keys_all, values_all, log_totals, grad_mixed
    )
    key_grad, value_grad = (
        lax.psum_scatter(
            key_terms.astype(jnp.bfloat16), "seq", scatter_dimension=1, tiled=True
        ).astype(jnp.float32),
        lax.psum_scatter(
            value_terms.astype(jnp.bfloat16), "seq", scatter_dimension=1, tiled=True
        ).astype(jnp.float32),
    )
    grad_qkv = jnp.concatenate(
        [
            grad_query.astype(jnp.bfloat16),
            key_grad.astype(jnp.bfloat16),
            value_grad.astype(jnp.bfloat16),
        ],
        axis=-1,
    )
    grad_proj_qkv = outer_sum(input_one, grad_qkv)
    bias_query_grad = total_sum(grad_qkv[..., :D])
    bias_value_grad = total_sum(grad_qkv[..., 2 * D :])
    grad_input_one = dense_back(grad_qkv, whole_in[:, 6 * D : 9 * D])
    shift_one_grad = jnp.sum(grad_input_one, axis=1)
    scale_one_grad = jnp.sum(grad_input_one * normed_one, axis=1)
    _, norm_pull_one = jax.vjp(layer_norm, hidden)
    input_grad = grad_middle + norm_pull_one(grad_input_one * (1.0 + scale_one))[0]
    mod_terms = jnp.concatenate(
        [
            shift_one_grad,
            scale_one_grad,
            gate_one_grad,
            shift_two_grad,
            scale_two_grad,
            gate_two_grad,
        ],
        axis=-1,
    )
    mod_grad = lax.psum(mod_terms, "seq").astype(jnp.bfloat16)
    _, silu_pull = jax.vjp(jax.nn.silu, cond_float)
    cond_grad = silu_pull(
        jnp.einsum("ne,de->nd", mod_grad, whole_in[:, : 6 * D], preferred_element_type=jnp.float32)
    )[0]
    owner_mask = (lax.axis_index("seq") == 0).astype(jnp.float32)
    grad_ada = (
        jnp.einsum("nd,ne->de", cond_act, mod_grad, preferred_element_type=jnp.float32) * owner_mask
    )
    bias_ada_grad = jnp.sum(mod_grad.astype(jnp.float32), axis=0) * owner_mask
    grad_in_all = jnp.zeros((D, 10 * D + FF), jnp.float32)
    grad_in_all = grad_in_all.at[:, : 6 * D].set(grad_ada)
    grad_in_all = grad_in_all.at[:, 6 * D : 9 * D].set(grad_proj_qkv)
    grad_in_all = grad_in_all.at[:, 9 * D : 10 * D].set(grad_out_proj)
    grad_in_all = grad_in_all.at[:, 10 * D :].set(grad_up)
    bias_flat = jnp.concatenate(
        [
            bias_ada_grad,
            bias_query_grad,
            bias_value_grad,
            bias_out_grad,
            bias_up_grad,
            bias_down_grad,
        ]
    )
    summed_in, summed_down, summed_bias = (
        lax.psum_scatter(
            grad_in_all.astype(jnp.bfloat16), "dp", scatter_dimension=1, tiled=True
        ).astype(jnp.float32),
        lax.psum_scatter(
            grad_down.astype(jnp.bfloat16), "dp", scatter_dimension=1, tiled=True
        ).astype(jnp.float32),
        lax.psum_scatter(
            bias_flat.reshape(1, -1).astype(jnp.bfloat16), "dp", scatter_dimension=1, tiled=True
        ).astype(jnp.float32),
    )
    owned_in, owned_down, owned_bias = (
        lax.psum_scatter(
            summed_in.astype(jnp.bfloat16), "seq", scatter_dimension=0, tiled=True
        ).astype(jnp.float32),
        lax.psum_scatter(
            summed_down.astype(jnp.bfloat16), "seq", scatter_dimension=0, tiled=True
        ).astype(jnp.float32),
        lax.psum_scatter(
            summed_bias.reshape(-1).astype(jnp.bfloat16), "seq", scatter_dimension=0, tiled=True
        ).astype(jnp.float32),
    )
    moments_in, squares_in, master_in = adamw_step(
        weights_in, moment_in, square_in, owned_in, rate_in
    )
    moments_down, squares_down, master_down = adamw_step(
        weights_down, moment_down, square_down, owned_down, rate_down
    )
    moments_bias, squares_bias, master_bias = adamw_step(
        biases, moment_bias, square_bias, owned_bias, rate_bias
    )
    return (
        block_out,
        input_grad,
        cond_grad,
        moments_in,
        moments_down,
        moments_bias,
        squares_in,
        squares_down,
        squares_bias,
        master_in,
        master_down,
        master_bias,
        master_in.astype(jnp.bfloat16),
        master_down.astype(jnp.bfloat16),
        master_bias.astype(jnp.bfloat16),
    )


MESH = pl.DeviceIdType.MESH
WIDE = 896
LOW = 6 * D
KEPT = 4 * D + FF
PLANES = 4
HALF = D // 2
TALL = HALF + 16
SUBS = 3
SUB_ROWS = TALL // SUBS
FF_PART = FF // 2
DP = 16


def place():
    dp = lax.axis_index("dp")
    y = lax.axis_index("seq")
    return (dp // 4, lax.rem(dp // 2, 2), lax.rem(dp, 2), y)


def device_at(z, x, c, y):
    return ((z * 2 + x) * 2 + c, y)


def neighbours():
    z, x, c, y = place()
    return {
        "x": device_at(z, 1 - x, c, y),
        "y": device_at(z, x, c, 1 - y),
        "up": device_at(jnp.minimum(z + 1, PLANES - 1), x, c, y),
        "down": device_at(jnp.maximum(z - 1, 0), x, c, y),
        "core": device_at(z, x, 1 - c, y),
        "swap": device_at(z, x, 1 - c, 1 - y),
    }


def repeat(count, body):
    def step(at, carried):
        body(at)
        return carried

    lax.fori_loop(0, count, step, 0)


def greet_all():
    barrier = pltpu.get_barrier_semaphore()
    here = lax.axis_index("dp") * 2 + lax.axis_index("seq")

    def signal(at):
        there = lax.rem(here + at + 1, 2 * DP)
        pl.semaphore_signal(
            barrier, inc=1, device_id=(there // 2, lax.rem(there, 2)), device_id_type=MESH
        )

    repeat(2 * DP - 1, signal)
    pl.semaphore_wait(barrier, 2 * DP - 1)


class Broad:
    height, width, subs, split = SUB_ROWS, WIDE, SUBS, 96
    first, source_column = 0, 0

    @staticmethod
    def holds(zs, xs, cs):
        return (zs * 2 + xs) * 2 + cs >= 7

    @staticmethod
    def view(whole, zs, xs, ys, cs, sub, start=0, rows=SUB_ROWS):
        column = jnp.maximum(((zs * 2 + xs) * 2 + cs) * WIDE - LOW, 128)
        row = pl.multiple_of(sub * SUB_ROWS + start, 16)
        return whole.at[ys, pl.ds(row, rows), pl.ds(pl.multiple_of(column, 128), WIDE)]


class Narrow:
    height, width, subs, split = TALL, 128, 1, 272
    first, source_column = 16 * SUBS, WIDE - 128

    @staticmethod
    def holds(zs, xs, cs):
        return (zs * 2 + xs) * 2 + cs == 6

    @staticmethod
    def view(whole, zs, xs, ys, cs, sub, start=0, rows=TALL):
        return whole.at[ys, pl.ds(start, rows), pl.ds(0, 128)]


class Down:
    height, width, subs, split = 64, FF_PART, 1, 32
    first, source_column = 16 * SUBS + 16, 0

    @staticmethod
    def holds(zs, xs, cs):
        return zs >= 0

    @staticmethod
    def view(whole, zs, xs, ys, cs, sub, start=0, rows=64):
        row = pl.multiple_of(((zs * 2 + xs) * 2 + cs) * 64 + start, 32)
        return whole.at[pl.ds(row, rows), pl.ds(pl.multiple_of(ys * FF_PART, 128), FF_PART)]


SLOTS = 16 * SUBS + 32
RELATIONS = ("own", "x", "y", "xy")
HOPS = {"own": 0, "x": 1, "y": 1, "xy": 2}


def by_plane(z, table):
    picked = table[PLANES - 1]
    for plane in range(PLANES - 2, -1, -1):
        picked = jnp.where(z == plane, table[plane], picked)
    return picked


def forward_block(what, refs, kind, zs, relation, sub, sems, valid):
    whole, mine = refs
    send_sem, recv_sem, core_sem = sems
    z, x, c, y = place()
    near = neighbours()
    xs = 1 - x if "x" in relation else x
    ys = 1 - y if "y" in relation else y
    slot = kind.first + ((zs * 2 + xs) * 2 + ys) * kind.subs + sub
    full, half = recv_sem.at[slot, 0], recv_sem.at[slot, 1]
    parts = ((0, kind.height), (0, kind.split), (kind.split, kind.height - kind.split))

    def copy(part, index, arrival, key, source=None, cs=None):
        target = kind.view(whole, zs, xs, ys, c if cs is None else cs, sub, *parts[part])
        return pltpu.make_async_remote_copy(
            src_ref=target if source is None else source,
            dst_ref=target,
            send_sem=send_sem.at[slot, index],
            recv_sem=arrival,
            device_id=near[key],
            device_id_type=MESH,
        )

    if what == "core":

        @pl.when(valid & kind.holds(zs, xs, 1 - c))
        def _():
            copy(0, 4, core_sem.at[slot], "core", cs=1 - c).wait_recv()

        return
    valid = valid & kind.holds(zs, xs, c)
    if what == "tick":
        arrived = valid & (zs != z) if relation == "own" else valid

        @pl.when(arrived)
        def _():
            if relation == "xy":
                copy(1, 0, full, "x").wait_recv()
                copy(2, 0, half, "x").wait_recv()
            else:
                copy(0, 0, full, "x").wait_recv()

    def act(descriptor):
        if what == "drain":
            descriptor.wait_send()
        else:
            descriptor.start()

    def spread(source, upward, downward):
        @pl.when(upward)
        def _():
            act(copy(0, 0, full, "up", source))

        @pl.when(downward)
        def _():
            act(copy(0, 1, full, "down", source))

        act(copy(0, 2, full, "x", source))
        act(copy(0, 3, full, "y", source))
        act(copy(0, 4, core_sem.at[slot], "core", source))

    if relation == "own":

        if what != "tick":

            @pl.when(valid & (zs == z))
            def _():
                source = mine.at[
                    pl.ds(pl.multiple_of(sub * kind.height, 16), kind.height),
                    pl.ds(kind.source_column, kind.width),
                ]
                spread(source, z < PLANES - 1, z > 0)

        if what != "launch":

            @pl.when(valid & (zs != z))
            def _():
                spread(None, (zs < z) & (z < PLANES - 1), (zs > z) & (z > 0))

        return

    @pl.when(valid)
    def _():
        if relation == "x":
            act(copy(1, 3, full, "y"))
        if relation == "y":
            act(copy(2, 2, half, "x"))
        act(copy(0, 4, core_sem.at[slot], "core"))


def forward_step(what, refs, plan, relations, sems, sub):
    z = place()[0]
    for kind, order in plan:
        for position in range(len(order[0])):
            zs = by_plane(z, [row[position] for row in order])
            for relation in relations:
                forward_block(
                    what,
                    refs[kind.__name__],
                    kind,
                    zs,
                    relation,
                    jnp.minimum(sub, kind.subs - 1),
                    sems,
                    sub < kind.subs,
                )


def launch(refs, kinds, sems):
    z = place()[0]

    def go(sub):
        for kind in kinds:
            forward_block(
                "launch",
                refs[kind.__name__],
                kind,
                z,
                "own",
                jnp.minimum(sub, kind.subs - 1),
                sems,
                sub < kind.subs,
            )

    repeat(max(kind.subs for kind in kinds), go)


NEAR_LOW = ((1, 2), (1, 2), (2, 1), (2, 1))
ONLY_ONE = ((1,),) * PLANES
ONLY_LAST = ((3,),) * PLANES
NEAR = ((0, 1, 2, 3), (1, 0, 2, 3), (2, 3, 1, 0), (3, 2, 1, 0))
PLAN_LOW = ((Broad, NEAR_LOW), (Narrow, ONLY_ONE))
PLAN_UP = ((Broad, ONLY_LAST),)
PLAN_DOWN = ((Down, NEAR),)
PLAN_ALL = PLAN_LOW + PLAN_UP + PLAN_DOWN


BF16 = jnp.bfloat16
F32 = jnp.float32
PLAIN = (((1,), (0,)), ((), ()))
BOTH_LAST = (((1,), (1,)), ((), ()))
BOTH_FIRST = (((0,), (0,)), ((), ()))
LANES = 128
PAIRS = HEADS // 2
TOKENS_HERE = 512


def multiply(left, right, dims=PLAIN):
    return lax.dot_general(left, right, dims, preferred_element_type=F32)


def two_heads(block):
    lanes = lax.broadcasted_iota(jnp.int32, block.shape, 1)
    zero = jnp.zeros_like(block)
    return (jnp.where(lanes < HEAD_DIM, block, zero), jnp.where(lanes < HEAD_DIM, zero, block))


def attend_pair(pair, queries, keys, values, mixed, log_totals):
    columns = pl.ds(pl.multiple_of(pair * LANES, LANES), LANES)
    key_block = keys[:, columns]
    value_flat = values[:, columns].T
    parts = []
    for head, query_block in enumerate(two_heads(queries[:, columns])):
        scores = multiply(key_block, query_block, BOTH_LAST)
        largest = jnp.max(scores, axis=0, keepdims=True)
        weights = jnp.exp((scores - largest) * HEAD_DIM**-0.5)
        total = jnp.sum(weights, axis=0, keepdims=True)
        parts.append(multiply(value_flat, weights.astype(BF16)) * (1.0 / total))
        log_totals[2 * pair + head] = largest * HEAD_DIM**-0.5 + jnp.log(total)
    joined = jnp.concatenate([parts[0][:HEAD_DIM], parts[1][HEAD_DIM:]], axis=0)
    mixed[:, columns] = joined.T.astype(BF16)


def normalize(values):
    center = values - jnp.mean(values, axis=-1, keepdims=True)
    return center * lax.rsqrt(jnp.mean(center * center, axis=-1, keepdims=True) + norm_eps)


def from_weights(left, whole, start, width):
    columns = pl.ds(pl.multiple_of(start, LANES), width)
    return multiply(left[:, :HALF], whole[0, :HALF, columns]) + multiply(
        left[:, HALF:], whole[1, :HALF, columns]
    )


def bias_of(whole, start, width):
    columns = pl.ds(pl.multiple_of(start, LANES), width)
    both = whole[0, HALF:TALL, columns].astype(F32) + whole[1, HALF:TALL, columns].astype(F32)
    return both[:1]


def forward_kernel(
    low_in,
    low_down,
    hidden_in,
    cotangent,
    condition,
    ada_bias,
    whole_in,
    whole_down,
    hidden,
    grad_out,
    cond_all,
    modulation,
    input_one,
    queries,
    keys,
    values,
    mixed,
    log_totals,
    attn_out,
    middle,
    input_two,
    slope,
    grad_branch,
    gate_grad,
    block_out,
    grad_down,
    own_in,
    own_down,
    ada_weights,
    ada_part,
    mod_parts,
    up_stage,
    wide,
    active,
    flat_branch,
    down_stage,
    send_sem,
    recv_sem,
    core_sem,
    local_sem,
    cond_send,
    cond_recv,
    mod_send,
    mod_recv,
    swap_sem,
    pair_sem,
    up_sem,
    down_sem,
):
    z, x, c, y = place()
    dp = (z * 2 + x) * 2 + c
    near = neighbours()
    sems = (send_sem, recv_sem, core_sem)
    refs = {"Broad": (own_in, low_in), "Narrow": (own_in, low_in), "Down": (own_down, low_down)}
    at_home = c == y

    def remote(source, target, sent, arrived, device):
        return pltpu.make_async_remote_copy(
            src_ref=source,
            dst_ref=target,
            send_sem=sent,
            recv_sem=arrived,
            device_id=device,
            device_id_type=MESH,
        )

    broad = pltpu.make_async_copy(
        low_in,
        own_in.at[y, :, pl.ds(pl.multiple_of(jnp.maximum(dp, 7) * WIDE - LOW, LANES), WIDE)],
        local_sem.at[0],
    )
    narrow = pltpu.make_async_copy(
        low_in.at[:, pl.ds(WIDE - 128, 128)], own_in.at[y, :, pl.ds(0, 128)], local_sem.at[0]
    )
    down = pltpu.make_async_copy(
        low_down,
        own_down.at[
            pl.ds(pl.multiple_of(dp * 64, 64), 64),
            pl.ds(pl.multiple_of(y * FF_PART, LANES), FF_PART),
        ],
        local_sem.at[1],
    )
    ada = pltpu.make_async_copy(low_in.at[pl.ds(0, HALF)], ada_weights, local_sem.at[2])
    ada.start()
    down.start()

    @pl.when(dp >= 7)
    def _():
        broad.start()

    @pl.when(dp == 6)
    def _():
        narrow.start()

    greet_all()

    cond_all[dp] = condition[...]

    def cond_copy(at):
        there = lax.rem(dp + at + 1, DP)
        return remote(
            condition, cond_all.at[dp], cond_send.at[at], cond_recv.at[dp], (there, y)
        )

    repeat(DP - 1, lambda at: cond_copy(at).start())

    swaps = []
    for index, (source, target) in enumerate(((hidden_in, hidden), (cotangent, grad_out))):
        swaps.append(
            (
                pltpu.make_async_copy(source, target, swap_sem.at[index, 0]),
                remote(
                    source, target, swap_sem.at[index, 1], swap_sem.at[index, 2], near["swap"]
                ),
            )
        )

    def trade(index):
        @pl.when(at_home)
        def _():
            swaps[index][0].start()

        @pl.when(jnp.logical_not(at_home))
        def _():
            swaps[index][1].start()

    def traded(index):
        @pl.when(at_home)
        def _():
            swaps[index][0].wait()

        @pl.when(jnp.logical_not(at_home))
        def _():
            swaps[index][1].wait()

    trade(0)
    launch(refs, (Broad, Narrow), sems)

    @pl.when((z == 0) | (z == PLANES - 1))
    def _():
        launch(refs, (Down,), sems)

    def pass_on(plan, relations):
        subs = max(kind.subs for kind, _ in plan)
        repeat(subs, lambda sub: forward_step("tick", refs, plan, relations, sems, sub))

    pass_on(PLAN_LOW, ("own",))

    def cond_arrived(at):
        there = lax.rem(dp + at + 1, DP)
        remote(
            condition, cond_all.at[there], cond_send.at[at], cond_recv.at[there], (there, y)
        ).wait_recv()

    repeat(DP - 1, cond_arrived)
    raw = jnp.concatenate([cond_all[index] for index in range(DP)], axis=0)
    active[...] = (raw / (1.0 + jnp.exp(-raw))).astype(BF16)
    ada.wait()
    partial = (
        multiply(
            active[:, pl.ds(pl.multiple_of(y * HALF, LANES), HALF)],
            ada_weights[...],
        )
        + ada_bias[...]
    )
    for index in range(DP):
        ada_part[index] = partial[index : index + 1]

    def mod_target(at):
        latent, core = at // 2, lax.rem(at, 2)
        return (latent // 2 * 2 + core, lax.rem(latent, 2))

    def mod_copy(at):
        return remote(
            ada_part.at[at // 2],
            mod_parts.at[dp * 2 + y],
            mod_send.at[at],
            mod_recv.at[dp * 2 + y],
            mod_target(at),
        )

    def elsewhere(at):
        there = mod_target(at)
        return (there[0] != dp) | (there[1] != y)

    @pl.when(dp < 7)
    def _():
        def send(at):
            @pl.when(elsewhere(at))
            def _():
                mod_copy(at).start()

            @pl.when(jnp.logical_not(elsewhere(at)))
            def _():
                mod_parts[dp * 2 + y] = ada_part[at // 2]

        repeat(2 * DP, send)

    pass_on(PLAN_LOW, ("x", "y"))

    @pl.when((z > 0) & (z < PLANES - 1))
    def _():
        launch(refs, (Down,), sems)

    pass_on(PLAN_UP, ("own",))
    trade(1)
    traded(0)

    def mod_arrived(at):
        @pl.when(at != dp * 2 + y)
        def _():
            remote(
                ada_part.at[0], mod_parts.at[at], mod_send.at[0], mod_recv.at[at], near["x"]
            ).wait_recv()

    repeat(14, mod_arrived)
    for index in range(7):
        modulation[:, index * WIDE : (index + 1) * WIDE] = (
            mod_parts[2 * index] + mod_parts[2 * index + 1]
        )

    def vector(index):
        return modulation[:, index * D : (index + 1) * D]

    def shape_one(at):
        rows = pl.ds(pl.multiple_of(at * 128, 128), 128)
        normed = normalize(hidden[rows].astype(F32))
        input_one[rows] = (normed * (1.0 + vector(1)) + vector(0)).astype(BF16)

    repeat(4, shape_one)

    pass_on(PLAN_LOW, ("xy",))
    repeat(SUBS, lambda at: forward_step("core", refs, PLAN_LOW, RELATIONS, sems, at))

    @pl.when(dp >= 7)
    def _():
        broad.wait()

    @pl.when(dp == 6)
    def _():
        narrow.wait()

    def project(at):
        columns = pl.ds(pl.multiple_of(at * 256, LANES), 256)
        keys[:HALF, columns] = from_weights(input_one, own_in, D + at * 256, 256).astype(BF16)
        values[:HALF, columns] = (
            from_weights(input_one, own_in, 2 * D + at * 256, 256)
            + bias_of(own_in, D + at * 256, 256)
        ).astype(BF16)

    repeat(D // 256, project)
    mates = [
        remote(
            one.at[:HALF], one.at[HALF:], pair_sem.at[index, 0], pair_sem.at[index, 1], near["core"]
        )
        for index, one in enumerate((keys, values))
    ]
    for mate in mates:
        mate.start()

    def project_queries(at):
        columns = pl.ds(pl.multiple_of(at * 256, LANES), 256)
        queries[:, columns] = (
            from_weights(input_one, own_in, at * 256, 256) + bias_of(own_in, at * 256, 256)
        ).astype(BF16)

    repeat(D // 256, project_queries)
    for mate in mates:
        mate.wait()

    def attention(pair):
        attend_pair(pair, queries, keys, values, mixed, log_totals)

        @pl.when(pair < SUBS)
        def _():
            forward_step("tick", refs, PLAN_UP, ("x", "y"), sems, pair)

        @pl.when(pair == SUBS)
        def _():
            forward_step("tick", refs, PLAN_DOWN, ("own",), sems, 0)

        @pl.when((pair > SUBS) & (pair <= 2 * SUBS))
        def _():
            forward_step("tick", refs, PLAN_UP, ("xy",), sems, pair - SUBS - 1)

        @pl.when(pair == 2 * SUBS + 1)
        def _():
            forward_step("tick", refs, PLAN_DOWN, ("x", "y"), sems, 0)

    repeat(PAIRS, attention)

    def project_out(at):
        columns = pl.ds(pl.multiple_of(at * 256, LANES), 256)
        attn_out[:, columns] = from_weights(mixed, own_in, 3 * D + at * 256, 256) + bias_of(
            own_in, 2 * D + at * 256, 256
        )

    repeat(D // 256, project_out)

    def shape_two(at):
        rows = pl.ds(pl.multiple_of(at * 128, 128), 128)
        mid = hidden[rows].astype(F32) + vector(2) * attn_out[rows]
        middle[rows] = mid
        input_two[rows] = (normalize(mid) * (1.0 + vector(4)) + vector(3)).astype(BF16)

    repeat(4, shape_two)
    repeat(SUBS, lambda at: forward_step("core", refs, PLAN_UP, RELATIONS, sems, at))
    whole_copies = [
        pltpu.make_async_copy(
            own_in.at[half, pl.ds(0, HALF)],
            whole_in.at[pl.ds(half * HALF, HALF)],
            local_sem.at[3 + half],
        )
        for half in range(2)
    ]
    for whole_copy in whole_copies:
        whole_copy.start()
    tile = 512

    def up_copy(at, slot):
        return pltpu.make_async_copy(
            up_stage.at[slot],
            slope.at[:, pl.ds(pl.multiple_of(at * tile, LANES), tile)],
            up_sem.at[slot],
        )

    def down_grad_copy(at, slot):
        return pltpu.make_async_copy(
            down_stage.at[slot],
            grad_down.at[:, pl.ds(pl.multiple_of(at * tile, LANES), tile)],
            down_sem.at[slot],
        )

    traded(1)

    def shape_branch(at):
        columns = pl.ds(pl.multiple_of(at * 256, LANES), 256)
        gate = modulation[:, pl.ds(pl.multiple_of(5 * D + at * 256, LANES), 256)]
        scaled = (grad_out[:, columns].astype(F32) * gate).astype(BF16)
        grad_branch[:, columns] = scaled
        flat_branch[pl.ds(pl.multiple_of(at * 256, 256), 256)] = scaled.T

    repeat(D // 256, shape_branch)

    def widen(at):
        slot = lax.rem(at, 2)

        @pl.when(at >= 2)
        def _():
            up_copy(at - 2, slot).wait()
            down_grad_copy(at - 2, slot).wait()

        factor = math.sqrt(2.0 / math.pi)
        for side in range(2):
            start = at * tile + side * 256
            value = from_weights(input_two, own_in, 4 * D + start, 256) + bias_of(
                own_in, 3 * D + start, 256
            )
            square = value * value
            bent = jnp.tanh(factor * value * (1.0 + 0.044715 * square))
            half_up = 0.5 + 0.5 * bent
            up_stage[slot, :, side * 256 : (side + 1) * 256] = half_up + 0.5 * value * (
                1.0 - bent * bent
            ) * (factor + 3.0 * 0.044715 * factor * square)
            wide[:, pl.ds(pl.multiple_of(start, LANES), 256)] = (value * half_up).astype(BF16)
        up_copy(at, slot).start()
        for side in range(2):
            columns = pl.ds(pl.multiple_of(at * tile + side * 256, LANES), 256)
            down_stage[slot, :, side * 256 : (side + 1) * 256] = multiply(
                flat_branch[...], wide[:, columns]
            ).astype(BF16)
        down_grad_copy(at, slot).start()

        @pl.when(at == 3)
        def _():
            forward_step("tick", refs, PLAN_DOWN, ("xy",), sems, 0)

    repeat(FF // tile, widen)
    for at in (FF // tile - 2, FF // tile - 1):
        up_copy(at, at % 2).wait()
        down_grad_copy(at, at % 2).wait()
    forward_step("core", refs, PLAN_DOWN, RELATIONS, sems, 0)
    down.wait()
    down_copy = pltpu.make_async_copy(own_down, whole_down, local_sem.at[5])
    down_copy.start()

    def narrow_down(at):
        columns = pl.ds(pl.multiple_of(at * 256, LANES), 256)
        value = bias_of(own_in, 7 * D + at * 256, 256)
        for side in range(2):
            value += multiply(
                wide[:, side * FF_PART : (side + 1) * FF_PART],
                own_down[columns, side * FF_PART : (side + 1) * FF_PART],
                BOTH_LAST,
            )
        gate = modulation[:, pl.ds(pl.multiple_of(5 * D + at * 256, LANES), 256)]
        block_out[:, columns] = (middle[:, columns] + gate * value).astype(BF16)
        towards = grad_out[:, columns].astype(F32)
        gate_grad[:, columns] = jnp.sum(towards * value, axis=0, keepdims=True)

    repeat(D // 256, narrow_down)

    repeat(SUBS, lambda at: forward_step("drain", refs, PLAN_ALL, RELATIONS, sems, at))
    repeat(DP - 1, lambda at: cond_copy(at).wait_send())

    @pl.when(dp < 7)
    def _():
        def sent(at):
            @pl.when(elsewhere(at))
            def _():
                mod_copy(at).wait_send()

        repeat(2 * DP, sent)

    for whole_copy in whole_copies:
        whole_copy.wait()
    down_copy.wait()


def run_forward(low_in, low_down, hidden_in, cotangent, condition, ada_bias):
    shape = jax.ShapeDtypeStruct
    rows = TOKENS_HERE
    outs = [
        (shape((D, KEPT), BF16), pl.ANY),
        (shape((D, FF), BF16), pl.ANY),
        (shape((rows, D), BF16), pltpu.VMEM),
        (shape((rows, D), BF16), pltpu.VMEM),
        (shape((DP, 1, D), F32), pltpu.VMEM),
        (shape((1, 7 * WIDE), F32), pltpu.VMEM),
        (shape((rows, D), BF16), pltpu.VMEM),
        (shape((rows, D), BF16), pltpu.VMEM),
        (shape((2 * rows, D), BF16), pltpu.VMEM),
        (shape((2 * rows, D), BF16), pltpu.VMEM),
        (shape((rows, D), BF16), pltpu.VMEM),
        (shape((HEADS, 1, rows), F32), pltpu.VMEM),
        (shape((rows, D), F32), pltpu.VMEM),
        (shape((rows, D), F32), pltpu.VMEM),
        (shape((rows, D), BF16), pltpu.VMEM),
        (shape((rows, FF), F32), pl.ANY),
        (shape((rows, D), BF16), pltpu.VMEM),
        (shape((1, D), F32), pltpu.VMEM),
        (shape((rows, D), BF16), pltpu.VMEM),
        (shape((D, FF), BF16), pl.ANY),
    ]
    dma = pltpu.SemaphoreType.DMA
    return pl.pallas_call(
        forward_kernel,
        out_shape=[one for one, _ in outs],
        in_specs=[pl.BlockSpec(memory_space=pl.ANY)] * 4
        + [pl.BlockSpec(memory_space=pltpu.VMEM)] * 2,
        out_specs=[pl.BlockSpec(memory_space=where) for _, where in outs],
        scratch_shapes=[
            pltpu.VMEM((2, TALL, KEPT), BF16),
            pltpu.VMEM((D, FF), BF16),
            pltpu.VMEM((HALF, WIDE), BF16),
            pltpu.VMEM((DP, 1, WIDE), F32),
            pltpu.VMEM((14, 1, WIDE), F32),
            pltpu.VMEM((2, rows, 512), F32),
            pltpu.VMEM((rows, FF), BF16),
            pltpu.VMEM((DP, D), BF16),
            pltpu.VMEM((D, rows), BF16),
            pltpu.VMEM((2, D, 512), BF16),
            dma((SLOTS, 5)),
            dma((SLOTS, 2)),
            dma((SLOTS,)),
            dma((6,)),
            dma((DP,)),
            dma((DP,)),
            dma((2 * DP,)),
            dma((14,)),
            dma((2, 3)),
            dma((2, 2)),
            dma((2,)),
            dma((2,)),
        ],
        compiler_params=pltpu.CompilerParams(
            collective_id=0, has_side_effects=True, vmem_limit_bytes=62 * 2**20
        ),
        name="forward",
    )(low_in, low_down, hidden_in, cotangent, condition, ada_bias)


GRAD_SUBS = 8
GRAD_ROWS = HALF // GRAD_SUBS


class BroadGrad:
    height, width, subs, source_column = GRAD_ROWS, WIDE, GRAD_SUBS, 0

    @staticmethod
    def holds(zs, xs, cs):
        return (zs * 2 + xs) * 2 + cs >= 7

    @staticmethod
    def corner(zs, xs, ys, cs, sub):
        column = jnp.maximum(((zs * 2 + xs) * 2 + cs) * WIDE - LOW, 128)
        return (
            pl.multiple_of(ys * HALF + sub * GRAD_ROWS, GRAD_ROWS),
            pl.multiple_of(column, 128),
        )


class NarrowGrad:
    height, width, subs, source_column = HALF, 128, 1, WIDE - 128

    @staticmethod
    def holds(zs, xs, cs):
        return (zs * 2 + xs) * 2 + cs == 6

    @staticmethod
    def corner(zs, xs, ys, cs, sub):
        return (pl.multiple_of(ys * HALF, HALF), 0)


def reduce_block(what, refs, kind, zs, plane_at, planes, relation, sub, sems, valid):
    grads, first_column, owned, buffers = refs
    from_core, from_x, from_y, from_low, from_high, half_a, half_b = buffers
    send_sem, recv_sem = sems
    z, x, c, y = place()
    near = neighbours()
    xs = 1 - x if "x" in relation else x
    ys = 1 - y if "y" in relation else y
    flat = plane_at * kind.subs + sub
    count = planes * kind.subs
    kin = RELATIONS.index(relation)
    slot = kin * count + flat
    rows, half_rows = kind.height, kind.height // 2

    def remote(source, target, index, arrival, key):
        return pltpu.make_async_remote_copy(
            src_ref=source,
            dst_ref=target,
            send_sem=send_sem.at[slot, index],
            recv_sem=recv_sem.at[arrival, flat],
            device_id=near[key],
            device_id_type=MESH,
        )

    def share(cs):
        row, column = kind.corner(zs, xs, ys, cs, sub)
        column = jnp.clip(column - first_column, 0, grads.shape[1] - kind.width)
        return (pl.ds(row, rows), pl.ds(pl.multiple_of(column, 128), kind.width))

    total = from_core.at[slot]
    across = remote(grads.at[share(1 - c)], total, 2, kin, "core")
    other = valid & kind.holds(zs, xs, 1 - c)
    if what == "across":
        pl.when(other)(across.start)
        return
    if what == "drain":
        pl.when(other)(across.wait_send)
    valid = valid & kind.holds(zs, xs, c)
    part_a = from_core.at[slot, pl.ds(0, half_rows)]
    part_b = from_core.at[slot, pl.ds(half_rows, half_rows)]
    if relation == "xy":
        sends = [
            (valid, remote(part_a, half_a.at[flat], 0, 4, "y")),
            (valid, remote(part_b, half_b.at[flat], 1, 5, "x")),
        ]
    elif relation == "x":
        sends = [(valid, remote(total, from_x.at[flat], 0, 6, "x"))]
    elif relation == "y":
        sends = [(valid, remote(total, from_y.at[flat], 0, 7, "y"))]
    else:
        sends = [
            (valid & (z < zs), remote(total, from_low.at[flat], 0, 8, "up")),
            (valid & (z > zs), remote(total, from_high.at[flat], 1, 9, "down")),
        ]
    if what == "drain":
        for condition, descriptor in sends:
            pl.when(condition)(descriptor.wait_send)
        return

    @pl.when(valid)
    def _():
        remote(total, total, 2, kin, "core").wait_recv()
        value = from_core[slot].astype(F32) + grads[share(c)].astype(F32)
        if relation == "xy":
            from_core[slot] = value.astype(BF16)
        elif relation == "x":
            remote(half_a.at[flat], half_a.at[flat], 0, 4, "y").wait_recv()
            from_core[slot, pl.ds(half_rows, half_rows)] = value[half_rows:].astype(BF16)
            from_core[slot, pl.ds(0, half_rows)] = (
                value[:half_rows] + half_a[flat].astype(F32)
            ).astype(BF16)
        elif relation == "y":
            remote(half_b.at[flat], half_b.at[flat], 1, 5, "x").wait_recv()
            from_core[slot, pl.ds(0, half_rows)] = value[:half_rows].astype(BF16)
            from_core[slot, pl.ds(half_rows, half_rows)] = (
                value[half_rows:] + half_b[flat].astype(F32)
            ).astype(BF16)
        else:
            remote(from_x.at[flat], from_x.at[flat], 0, 6, "x").wait_recv()
            remote(from_y.at[flat], from_y.at[flat], 0, 7, "y").wait_recv()
            value += from_x[flat].astype(F32) + from_y[flat].astype(F32)

            @pl.when((z <= zs) & (z > 0))
            def _():
                remote(from_low.at[flat], from_low.at[flat], 0, 8, "up").wait_recv()

            @pl.when((z >= zs) & (z < PLANES - 1))
            def _():
                remote(from_high.at[flat], from_high.at[flat], 1, 9, "down").wait_recv()

            def low():
                return jnp.where(z > 0, from_low[flat].astype(F32), 0.0)

            def high():
                return jnp.where(z < PLANES - 1, from_high[flat].astype(F32), 0.0)

            @pl.when(z < zs)
            def _():
                from_core[slot] = (value + low()).astype(BF16)

            @pl.when(z > zs)
            def _():
                from_core[slot] = (value + high()).astype(BF16)

            @pl.when(z == zs)
            def _():
                owned[
                    pl.ds(pl.multiple_of(sub * rows, rows), rows),
                    pl.ds(kind.source_column, kind.width),
                ] = value + low() + high()

    for condition, descriptor in sends:
        pl.when(condition)(descriptor.start)


LAGS = {"xy": 0, "x": 1, "y": 1, "own": 2}
Z_LAG = 1


def reduce_step(what, refs, plan, sems, at):
    z = place()[0]
    for kind, planes in plan:
        name = kind.__name__
        for plane_at, zs in enumerate(planes):
            for relation in ("xy", "x", "y", "own"):
                sub = at
                if what == "tick":
                    depth = 0
                    if relation == "own":
                        depth = by_plane(
                            z,
                            [
                                place_z
                                if place_z < zs
                                else max(place_z, 3 - place_z)
                                if place_z == zs
                                else 3 - place_z
                                for place_z in range(PLANES)
                            ],
                        )
                    sub = at - (LAGS[relation] + Z_LAG * depth)
                reduce_block(
                    what,
                    refs[name],
                    kind,
                    zs,
                    plane_at,
                    len(planes),
                    relation,
                    jnp.clip(sub, 0, kind.subs - 1),
                    sems[name],
                    (sub >= 0) & (sub < kind.subs),
                )


def landing(kind, planes):
    count = planes * kind.subs
    full = pltpu.VMEM((count, kind.height, kind.width), BF16)
    half = pltpu.VMEM((count, kind.height // 2, kind.width), BF16)
    return [pltpu.VMEM((4 * count, kind.height, kind.width), BF16)] + [full] * 4 + [half] * 2


def landing_signals(kind, planes):
    count = planes * kind.subs
    return [pltpu.SemaphoreType.DMA((4 * count, 3)), pltpu.SemaphoreType.DMA((10, count))]


def greet_near():
    z, x, c, y = place()
    near = neighbours()
    barrier = pltpu.get_barrier_semaphore()
    for key in ("x", "y", "core", "swap"):
        pl.semaphore_signal(barrier, inc=1, device_id=near[key], device_id_type=MESH)

    @pl.when(z < PLANES - 1)
    def _():
        pl.semaphore_signal(barrier, inc=1, device_id=near["up"], device_id_type=MESH)

    @pl.when(z > 0)
    def _():
        pl.semaphore_signal(barrier, inc=1, device_id=near["down"], device_id_type=MESH)

    middle = (z > 0) & (z < PLANES - 1)

    @pl.when(middle)
    def _():
        pl.semaphore_wait(barrier, 6)

    @pl.when(jnp.logical_not(middle))
    def _():
        pl.semaphore_wait(barrier, 5)


REDUCE_HIGH = ((BroadGrad, (3,)),)
REDUCE_LOW = ((BroadGrad, (1, 2)), (NarrowGrad, (1,)))
HIGH_STEPS = GRAD_SUBS + 5
LOW_STEPS = GRAD_SUBS + 5
HIGH_FIRST = FF // 8


def attend_back(
    pair, queries, keys, values, mixed, grad_mixed, log_totals, grad_query, grad_key, grad_value
):
    columns = pl.ds(pl.multiple_of(pair * LANES, LANES), LANES)
    key_block = keys[:, columns]
    value_block = values[:, columns]
    key_flat = key_block.T
    key_sum, value_sum = None, None
    step = 256
    for part in range(TOKENS_HERE // step):
        rows = pl.ds(part * step, step)
        grad_block = grad_mixed[rows, columns]
        product = (grad_block.astype(F32) * mixed[rows, columns].astype(F32)).T
        query_parts = []
        heads = zip(two_heads(queries[rows, columns]), two_heads(grad_block))
        for head, (query_head, grad_head) in enumerate(heads):
            scores = multiply(key_block, query_head, BOTH_LAST)
            weights = jnp.exp(scores * HEAD_DIM**-0.5 - log_totals[2 * pair + head, :, rows])
            grad_weights = multiply(value_block, grad_head, BOTH_LAST)
            inner = jnp.sum(
                product[HEAD_DIM * head : HEAD_DIM * (head + 1)], axis=0, keepdims=True
            )
            grad_scores = (weights * (grad_weights - inner)).astype(BF16)
            value_term = multiply(weights.astype(BF16), grad_head)
            key_term = multiply(grad_scores, query_head)
            value_sum = value_term if value_sum is None else value_sum + value_term
            key_sum = key_term if key_sum is None else key_sum + key_term
            query_parts.append(multiply(key_flat, grad_scores))
        joined = jnp.concatenate([query_parts[0][:HEAD_DIM], query_parts[1][HEAD_DIM:]], axis=0)
        grad_query[rows, columns] = (joined * HEAD_DIM**-0.5).T.astype(BF16)
    grad_key[:, columns] = (key_sum * HEAD_DIM**-0.5).astype(BF16)
    grad_value[:, columns] = value_sum.astype(BF16)


def backward_kernel(
    queries,
    keys,
    values,
    mixed,
    grad_mixed,
    log_totals,
    grads,
    block_out,
    grad_query,
    grad_key,
    grad_value,
    owned,
    block_swapped,
    key_all,
    value_all,
    key_mate,
    value_mate,
    mate_sem,
    swap_sem,
    *scratch,
):
    dp = lax.axis_index("dp")
    at_home = lax.rem(dp, 2) == lax.axis_index("seq")
    near = neighbours()
    refs = {"BroadGrad": (grads, 4 * D, owned, scratch[:7])}
    sems = {"BroadGrad": scratch[7:9]}
    greet_near()
    away = pltpu.make_async_remote_copy(
        src_ref=block_out,
        dst_ref=block_swapped,
        send_sem=swap_sem.at[0],
        recv_sem=swap_sem.at[1],
        device_id=near["swap"],
        device_id_type=MESH,
    )

    @pl.when(jnp.logical_not(at_home))
    def _():
        away.start()

    repeat(GRAD_SUBS, lambda at: reduce_step("across", refs, REDUCE_HIGH, sems, at))

    @pl.when(dp < 12)
    def _():
        owned[...] = jnp.zeros_like(owned)

    def mates(pair):
        columns = pl.ds(pl.multiple_of(pair * LANES, LANES), LANES)
        return [
            pltpu.make_async_remote_copy(
                src_ref=source.at[HALF:, columns],
                dst_ref=target.at[:, columns],
                send_sem=mate_sem.at[pair, 2 * index],
                recv_sem=mate_sem.at[pair, 2 * index + 1],
                device_id=near["core"],
                device_id_type=MESH,
            )
            for index, (source, target) in enumerate(((key_all, key_mate), (value_all, value_mate)))
        ]

    def attention(pair):
        reduce_step("tick", refs, REDUCE_HIGH, sems, pair)
        attend_back(
            pair,
            queries,
            keys,
            values,
            mixed,
            grad_mixed,
            log_totals,
            grad_query,
            key_all,
            value_all,
        )
        for mate in mates(pair):
            mate.start()

    repeat(PAIRS, attention)
    for source, target, total, index in (
        (key_all, key_mate, grad_key, 0),
        (value_all, value_mate, grad_value, 1),
    ):
        repeat(PAIRS, lambda pair: mates(pair)[index].wait())
        total[...] = (source[:HALF].astype(F32) + target[...].astype(F32)).astype(BF16)
    repeat(
        HIGH_STEPS - PAIRS, lambda at: reduce_step("tick", refs, REDUCE_HIGH, sems, at + PAIRS)
    )
    repeat(GRAD_SUBS, lambda at: reduce_step("drain", refs, REDUCE_HIGH, sems, at))

    @pl.when(jnp.logical_not(at_home))
    def _():
        away.wait()


def run_backward(queries, keys, values, mixed, grad_mixed, log_totals, grads, block_out):
    shape = jax.ShapeDtypeStruct
    rows = TOKENS_HERE
    vmem = pl.BlockSpec(memory_space=pltpu.VMEM)
    hbm = pl.BlockSpec(memory_space=pl.ANY)
    return pl.pallas_call(
        backward_kernel,
        out_shape=[shape((rows, D), BF16)] * 3
        + [shape((HALF, WIDE), F32), shape((rows, D), BF16)],
        in_specs=[vmem] * 7 + [hbm],
        out_specs=[vmem] * 4 + [hbm],
        scratch_shapes=[pltpu.VMEM((2 * rows, D), BF16)] * 2
        + [pltpu.VMEM((rows, D), BF16)] * 2
        + [pltpu.SemaphoreType.DMA((PAIRS, 4)), pltpu.SemaphoreType.DMA((2,))]
        + landing(BroadGrad, 1)
        + landing_signals(BroadGrad, 1),
        compiler_params=pltpu.CompilerParams(
            collective_id=1, has_side_effects=True, vmem_limit_bytes=60 * 2**20
        ),
        cost_estimate=pl.CostEstimate(
            flops=5 * 2 * 512 * 1024 * 1024 * 2, bytes_accessed=60 * 2**20, transcendentals=2**23
        ),
        name="backward",
    )(queries, keys, values, mixed, grad_mixed, log_totals, grads, block_out)


VECTOR = 17 * WIDE


def finish_kernel(
    grad_qkv,
    grad_out_proj,
    grad_up,
    low_in,
    active_rows,
    condition,
    sums,
    input_grad,
    owned_high,
    down_sum,
    owned,
    cond_grad,
    bias_parts,
    ada_bias_grad,
    owned_down,
    input_swapped,
    grads,
    ada_weights,
    sum_mate,
    sum_pieces,
    ada_in,
    cond_piece,
    cond_in,
    down_mate,
    local_sem,
    mate_sem,
    down_sem,
    piece_send,
    ada_recv,
    bias_recv,
    cond_send,
    cond_recv,
    swap_sem,
    *scratch,
):
    z, x, c, y = place()
    dp = (z * 2 + x) * 2 + c
    near = neighbours()
    refs = {
        "BroadGrad": (grads, 0, owned, scratch[0:7]),
        "NarrowGrad": (grads, 0, owned, scratch[7:14]),
    }
    sems = {"BroadGrad": scratch[14:16], "NarrowGrad": scratch[16:18]}
    at_home = c == y

    def remote(source, target, sent, arrived, device):
        return pltpu.make_async_remote_copy(
            src_ref=source,
            dst_ref=target,
            send_sem=sent,
            recv_sem=arrived,
            device_id=device,
            device_id_type=MESH,
        )

    loads = [
        pltpu.make_async_copy(grad_qkv, grads.at[:, : 3 * D], local_sem.at[0]),
        pltpu.make_async_copy(grad_out_proj, grads.at[:, 3 * D : 4 * D], local_sem.at[1]),
        pltpu.make_async_copy(
            grad_up.at[:, :HIGH_FIRST], grads.at[:, 4 * D : 4 * D + HIGH_FIRST], local_sem.at[2]
        ),
        pltpu.make_async_copy(low_in.at[pl.ds(0, HALF)], ada_weights, local_sem.at[3]),
    ]
    for load in loads:
        load.start()
    owned[...] = owned_high[...]
    greet_all()
    mate = remote(sums, sum_mate, mate_sem.at[0], mate_sem.at[1], near["core"])
    mate.start()
    down_away = remote(
        down_sum.at[:, pl.ds(pl.multiple_of((1 - y) * FF_PART, LANES), FF_PART)],
        down_mate,
        down_sem.at[0],
        down_sem.at[1],
        near["y"],
    )
    down_away.start()
    away = remote(input_grad, input_swapped, swap_sem.at[0], swap_sem.at[1], near["swap"])

    for load in loads[:3]:
        load.wait()
    repeat(GRAD_SUBS, lambda at: reduce_step("across", refs, REDUCE_LOW, sems, at))

    mate.wait()
    for index in range(17):
        columns = slice(index * WIDE, (index + 1) * WIDE)
        piece = sums[:, columns] + sum_mate[:, columns]
        if index < 7:
            piece = piece.astype(BF16).astype(F32)
        sum_pieces[index] = piece
    latent = (z * 2 + x) * 2 + y

    def piece_target(at):
        return jnp.where(at < 7, at, at - 1)

    def piece_copy(at, target, arrived):
        return remote(
            sum_pieces.at[at], target, piece_send.at[at], arrived, (piece_target(at), c)
        )

    def each_piece(act, keep):
        def go(at):
            mine = (piece_target(at) == dp) & (y == c)

            @pl.when(jnp.logical_not(mine) & (at < 7))
            def _():
                act(piece_copy(at, ada_in.at[latent], ada_recv.at[latent]))

            @pl.when(jnp.logical_not(mine) & (at >= 7))
            def _():
                act(piece_copy(at, bias_parts.at[latent], bias_recv.at[latent]))

            if keep:

                @pl.when(mine & (at < 7))
                def _():
                    ada_in[latent] = sum_pieces[at]

                @pl.when(mine & (at >= 7))
                def _():
                    bias_parts[latent] = sum_pieces[at]

        repeat(17, go)

    each_piece(lambda copy: copy.start(), True)
    repeat(3, lambda at: reduce_step("tick", refs, REDUCE_LOW, sems, at))

    @pl.when(jnp.logical_not(at_home))
    def _():
        away.start()

    def from_latent(at, target, arrived):
        mine = (at // 2 == z * 2 + x) & (lax.rem(at, 2) == y) & (c == y)

        @pl.when(jnp.logical_not(mine))
        def _():
            remote(
                sum_pieces.at[0], target.at[at], piece_send.at[0], arrived.at[at], near["x"]
            ).wait_recv()

    loads[3].wait()

    @pl.when(dp < 7)
    def _():
        repeat(DP, lambda at: from_latent(at, ada_in, ada_recv))
        gathered = jnp.concatenate([ada_in[index] for index in range(DP)], axis=0)
        ada_bias_grad[...] = jnp.sum(gathered, axis=0, keepdims=True)
        narrow = gathered.astype(BF16)
        owned[...] += multiply(active_rows[...], narrow, BOTH_FIRST)
        part = multiply(narrow, ada_weights[...], BOTH_LAST)
        for index in range(DP):
            cond_piece[index] = part[index : index + 1]

    @pl.when(dp >= 7)
    def _():
        ada_bias_grad[...] = jnp.zeros_like(ada_bias_grad)

    def cond_copy(at):
        return remote(
            cond_piece.at[at // 2],
            cond_in.at[dp * 2 + y],
            cond_send.at[at],
            cond_recv.at[dp * 2 + y],
            (at // 2, lax.rem(at, 2)),
        )

    def each_cond(act, keep):
        def go(at):
            mine = at == dp * 2 + y

            @pl.when(jnp.logical_not(mine))
            def _():
                act(cond_copy(at))

            if keep:

                @pl.when(mine)
                def _():
                    cond_in[dp * 2 + y] = cond_piece[at // 2]

        repeat(2 * DP, go)

    @pl.when(dp < 7)
    def _():
        each_cond(lambda copy: copy.start(), True)

    repeat(LOW_STEPS - 3, lambda at: reduce_step("tick", refs, REDUCE_LOW, sems, at + 3))

    def cond_arrived(at):
        @pl.when(at != dp * 2 + y)
        def _():
            remote(
                cond_piece.at[0], cond_in.at[at], cond_send.at[0], cond_recv.at[at], near["x"]
            ).wait_recv()

    repeat(14, cond_arrived)
    sides = []
    for side in range(2):
        total = cond_in[side]
        for index in range(1, 7):
            total = total + cond_in[2 * index + side]
        sides.append(total)
    value = condition[...]
    logistic = 1.0 / (1.0 + jnp.exp(-value))
    cond_grad[...] = jnp.concatenate(sides, axis=1) * (
        logistic * (1.0 + value * (1.0 - logistic))
    )

    @pl.when(dp >= 6)
    def _():
        repeat(DP, lambda at: from_latent(at, bias_parts, bias_recv))

    @pl.when(dp < 6)
    def _():
        bias_parts[...] = jnp.zeros_like(bias_parts)

    @pl.when(jnp.logical_not(at_home))
    def _():
        away.wait()

    down_away.wait()
    owned_down[...] = down_sum[
        :, pl.ds(pl.multiple_of(y * FF_PART, LANES), FF_PART)
    ].astype(F32) + down_mate[...].astype(F32)
    each_piece(lambda copy: copy.wait_send(), False)

    @pl.when(dp < 7)
    def _():
        each_cond(lambda copy: copy.wait_send(), False)

    repeat(GRAD_SUBS, lambda at: reduce_step("drain", refs, REDUCE_LOW, sems, at))


def run_finish(
    grad_qkv,
    grad_out_proj,
    grad_up,
    low_in,
    active_rows,
    condition,
    sums,
    input_grad,
    owned_high,
    down_sum,
):
    shape = jax.ShapeDtypeStruct
    dma = pltpu.SemaphoreType.DMA
    vmem = pl.BlockSpec(memory_space=pltpu.VMEM)
    hbm = pl.BlockSpec(memory_space=pl.ANY)
    return pl.pallas_call(
        finish_kernel,
        out_shape=[
            shape((HALF, WIDE), F32),
            shape((1, D), F32),
            shape((DP, 1, WIDE), F32),
            shape((1, WIDE), F32),
            shape((64, FF_PART), F32),
            shape((TOKENS_HERE, D), BF16),
        ],
        in_specs=[hbm] * 4 + [vmem] * 3 + [hbm, vmem, vmem],
        out_specs=[vmem] * 5 + [hbm],
        scratch_shapes=[
            pltpu.VMEM((D, 4 * D + HIGH_FIRST), BF16),
            pltpu.VMEM((HALF, WIDE), BF16),
            pltpu.VMEM((1, VECTOR), F32),
            pltpu.VMEM((17, 1, WIDE), F32),
            pltpu.VMEM((DP, 1, WIDE), F32),
            pltpu.VMEM((DP, 1, HALF), F32),
            pltpu.VMEM((14, 1, HALF), F32),
            pltpu.VMEM((64, FF_PART), BF16),
            dma((4,)),
            dma((2,)),
            dma((2,)),
            dma((17,)),
            dma((DP,)),
            dma((DP,)),
            dma((2 * DP,)),
            dma((14,)),
            dma((2,)),
        ]
        + landing(BroadGrad, 2)
        + landing(NarrowGrad, 1)
        + landing_signals(BroadGrad, 2)
        + landing_signals(NarrowGrad, 1),
        compiler_params=pltpu.CompilerParams(
            collective_id=2, has_side_effects=True, vmem_limit_bytes=60 * 2**20
        ),
        name="finish",
    )(
        grad_qkv,
        grad_out_proj,
        grad_up,
        low_in,
        active_rows,
        condition,
        sums,
        input_grad,
        owned_high,
        down_sum,
    )


def local(
    hidden_in,
    condition,
    cotangent,
    weights_in,
    weights_down,
    biases,
    moment_in,
    moment_down,
    moment_bias,
    square_in,
    square_down,
    square_bias,
):
    dp = lax.axis_index("dp")
    y = lax.axis_index("seq")
    side = WIDE // 2
    bias_row = jnp.pad(biases.astype(BF16)[None], ((0, 15), (0, side)))
    bias_row = jnp.where(y == 0, bias_row, jnp.roll(bias_row, side, axis=1))
    low_in = jnp.concatenate([weights_in.astype(BF16), bias_row], axis=0)
    cond_float = condition.astype(F32)
    (
        whole_in,
        whole_down,
        hidden,
        grad_out,
        cond_all,
        modulation,
        input_one,
        queries,
        keys,
        values,
        mixed,
        log_totals,
        attn_out,
        middle,
        input_two,
        slope,
        grad_branch,
        gate_two_grad,
        block_out,
        grad_down,
    ) = run_forward(
        low_in,
        weights_down.astype(BF16).T,
        hidden_in[0],
        cotangent[0],
        cond_float,
        bias_row[:1].astype(F32),
    )
    grad_out = grad_out.astype(F32)
    pieces = [modulation[:, part * D : (part + 1) * D] for part in range(6)]
    shift_one, scale_one, gate_one, shift_two, scale_two, gate_two = pieces

    def back_through(gradients, start, width):
        return lax.dot_general(
            gradients,
            whole_in[:, start : start + width],
            BOTH_LAST,
            preferred_element_type=F32,
        )

    def outer(left, right):
        return lax.dot_general(left, right, BOTH_FIRST, preferred_element_type=F32)

    def down_rows(total):
        return jnp.sum(total.astype(F32), axis=0, keepdims=True)

    down_sum = lax.psum_scatter(grad_down, "dp", scatter_dimension=0, tiled=True)
    grad_act = jnp.dot(grad_branch, whole_down, preferred_element_type=F32)
    grad_upward = (grad_act * slope).astype(BF16)
    grad_up = outer(input_two, grad_upward).astype(BF16)
    grad_input_two = back_through(grad_upward, 4 * D, FF)
    normed_two, norm_pull_two = jax.vjp(layer_norm, middle)
    shift_two_grad = down_rows(grad_input_two)
    scale_two_grad = down_rows(grad_input_two * normed_two)
    grad_middle = grad_out + norm_pull_two(grad_input_two * (1.0 + scale_two))[0]
    grad_attn = (grad_middle * gate_one).astype(BF16)
    gate_one_grad = down_rows(grad_middle * attn_out)
    grad_out_proj = outer(mixed, grad_attn).astype(BF16)
    grad_mixed = back_through(grad_attn, 3 * D, D).astype(BF16)
    at_home = lax.rem(dp, 2) == y
    grad_query, grad_key, grad_value, owned_high, block_swapped = run_backward(
        queries, keys, values, mixed, grad_mixed, log_totals, grad_up, block_out
    )
    block_out = jnp.where(at_home, block_out, block_swapped)
    grad_qkv = jnp.concatenate([grad_query, grad_key, grad_value], axis=-1)
    grad_proj_qkv = outer(input_one, grad_qkv).astype(BF16)
    grad_input_one = back_through(grad_qkv, 0, 3 * D)
    normed_one, norm_pull_one = jax.vjp(layer_norm, hidden.astype(F32))
    shift_one_grad = down_rows(grad_input_one)
    scale_one_grad = down_rows(grad_input_one * normed_one)
    input_grad = grad_middle + norm_pull_one(grad_input_one * (1.0 + scale_one))[0]
    sums = jnp.concatenate(
        [
            shift_one_grad,
            scale_one_grad,
            gate_one_grad,
            shift_two_grad,
            scale_two_grad,
            gate_two_grad,
            jnp.zeros((1, WIDE), F32),
            down_rows(grad_query),
            down_rows(grad_value),
            down_rows(grad_attn),
            down_rows(grad_upward),
            down_rows(grad_branch),
        ],
        axis=-1,
    )
    active_rows = lax.dynamic_slice_in_dim(
        jax.nn.silu(cond_all[:, 0]).astype(BF16), y * HALF, HALF, 1
    )
    owned_in, cond_grad, bias_parts, ada_bias_grad, owned_down, input_swapped = run_finish(
        grad_proj_qkv,
        grad_out_proj,
        grad_up,
        low_in,
        active_rows,
        cond_float,
        sums,
        input_grad.astype(BF16),
        owned_high,
        down_sum,
    )
    owned_down = owned_down.T
    input_grad = jnp.where(at_home, input_grad, input_swapped.astype(F32))
    owned_bias = jnp.sum(bias_parts[:, 0], axis=0) + ada_bias_grad[0]
    owned_bias = lax.dynamic_slice_in_dim(owned_bias, y * side, side, 0)
    moments_in, squares_in, master_in = adamw_step(
        weights_in, moment_in, square_in, owned_in, rate_in
    )
    moments_down, squares_down, master_down = adamw_step(
        weights_down, moment_down, square_down, owned_down, rate_down
    )
    moments_bias, squares_bias, master_bias = adamw_step(
        biases, moment_bias, square_bias, owned_bias, rate_bias
    )
    return (
        block_out[None],
        input_grad[None],
        cond_grad,
        moments_in,
        moments_down,
        moments_bias,
        squares_in,
        squares_down,
        squares_bias,
        master_in,
        master_down,
        master_bias,
        master_in.astype(BF16),
        master_down.astype(BF16),
        master_bias.astype(BF16),
    )


def solution(mesh):
    return jax.shard_map(
        local if dict(mesh.shape) == {"dp": 16, "seq": 2} else local_general,
        mesh=mesh,
        in_specs=(
            P("dp", "seq", None),
            P("dp", None),
            P("dp", "seq", None),
            P("seq", "dp"),
            P("seq", "dp"),
            P(("dp", "seq")),
            P("seq", "dp"),
            P("seq", "dp"),
            P(("dp", "seq")),
            P("seq", "dp"),
            P("seq", "dp"),
            P(("dp", "seq")),
        ),
        out_specs=(
            P("dp", "seq", None),
            P("dp", "seq", None),
            P("dp", None),
            P("seq", "dp"),
            P("seq", "dp"),
            P(("dp", "seq")),
            P("seq", "dp"),
            P("seq", "dp"),
            P(("dp", "seq")),
            P("seq", "dp"),
            P("seq", "dp"),
            P(("dp", "seq")),
            P("seq", "dp"),
            P("seq", "dp"),
            P(("dp", "seq")),
        ),
        check_vma=False,
    )
```

```python
import math

import jax
import jax.numpy as jnp
from jax import lax
from jax.experimental import pallas as pl
from jax.experimental.pallas import tpu as pltpu
from jax.sharding import PartitionSpec as P

D = 1024
HEADS = 16
HEAD_DIM = 64
FF = 4096
STEP = 5


norm_eps = 1e-06
beta_first = 0.5
beta_second = 0.5
adam_eps = 1e-08
weight_decay = 0.01
rate_in = 0.03
rate_down = 0.016
rate_bias = 0.3


def layer_norm(values):
    center = values - jnp.mean(values, axis=-1, keepdims=True)
    return center * lax.rsqrt(jnp.mean(center * center, axis=-1, keepdims=True) + norm_eps)


def adamw_step(master, moment, square, gradient, step_rate):
    moment_new = beta_first * moment + (1.0 - beta_first) * gradient
    square_new = beta_second * square + (1.0 - beta_second) * gradient * gradient
    corrected = moment_new / (1.0 - beta_first**STEP)
    scale_sq = square_new / (1.0 - beta_second**STEP)
    master_new = master - step_rate * (
        corrected / (jnp.sqrt(scale_sq) + adam_eps) + weight_decay * master
    )
    return (moment_new, square_new, master_new)


def dense_map(values, matrix):
    return jnp.einsum("nld,de->nle", values, matrix, preferred_element_type=jnp.float32)


def dense_back(gradients, matrix):
    return jnp.einsum("nle,de->nld", gradients, matrix, preferred_element_type=jnp.float32)


def outer_sum(values, gradients):
    return jnp.einsum("nld,nle->de", values, gradients, preferred_element_type=jnp.float32)


def total_sum(values):
    return jnp.sum(values.astype(jnp.float32), axis=(0, 1))


def gather_weights(low_in, low_down, low_bias):
    seq_parts = (
        lax.all_gather(low_in, "seq", axis=0, tiled=True),
        lax.all_gather(low_down, "seq", axis=0, tiled=True),
        lax.all_gather(low_bias, "seq", axis=0, tiled=True),
    )
    whole_in, whole_down, bias_row = (
        lax.all_gather(seq_parts[0], "dp", axis=1, tiled=True),
        lax.all_gather(seq_parts[1], "dp", axis=1, tiled=True),
        lax.all_gather(seq_parts[2].reshape(1, -1), "dp", axis=1, tiled=True),
    )
    return (whole_in, whole_down, bias_row[0])


def head_layout():
    heads_here = math.gcd(HEADS, max(1, 128 // HEAD_DIM))
    return (heads_here, heads_here * HEAD_DIM, HEADS // heads_here)


def split_heads(values, lane_start, lane_count, heads_here):
    piece = lax.dynamic_slice_in_dim(values, lane_start, lane_count, 2)
    return piece.reshape(piece.shape[0], piece.shape[1], heads_here, HEAD_DIM)


def join_heads(stacked):
    moved = jnp.moveaxis(stacked, 0, 2)
    return moved.reshape(moved.shape[0], moved.shape[1], moved.shape[2] * moved.shape[3])


def attention_forward(queries, keys_all, values_all):
    heads_here, lane_count, head_steps = head_layout()
    scale_factor = HEAD_DIM ** (-0.5)

    def one_group(group_index):
        lane_start = group_index * lane_count
        query_part = split_heads(queries, lane_start, lane_count, heads_here)
        key_part = split_heads(keys_all, lane_start, lane_count, heads_here)
        value_part = split_heads(values_all, lane_start, lane_count, heads_here)
        scores = (
            jnp.einsum("nqhd,nkhd->nhqk", query_part, key_part, preferred_element_type=jnp.float32)
            * scale_factor
        )
        row_max = jnp.max(scores, axis=-1, keepdims=True)
        exponent = jnp.exp(scores - row_max)
        row_total = jnp.sum(exponent, axis=-1, keepdims=True)
        weights = (exponent / row_total).astype(jnp.bfloat16)
        attn_part = jnp.einsum(
            "nhqk,nkhd->nqhd", weights, value_part, preferred_element_type=jnp.float32
        )
        shaped = attn_part.reshape(attn_part.shape[0], attn_part.shape[1], lane_count)
        return (shaped, (row_max + jnp.log(row_total))[..., 0])

    stacked, log_totals = lax.map(one_group, jnp.arange(head_steps))
    return (join_heads(stacked), log_totals)


def attention_backward(queries, keys_all, values_all, log_totals, grad_mixed):
    heads_here, lane_count, head_steps = head_layout()
    scale_factor = HEAD_DIM ** (-0.5)

    def one_group(carried):
        group_index, log_part = carried
        lane_start = group_index * lane_count
        query_part = split_heads(queries, lane_start, lane_count, heads_here)
        key_part = split_heads(keys_all, lane_start, lane_count, heads_here)
        value_part = split_heads(values_all, lane_start, lane_count, heads_here)
        grad_part = split_heads(grad_mixed, lane_start, lane_count, heads_here)
        scores = (
            jnp.einsum("nqhd,nkhd->nhqk", query_part, key_part, preferred_element_type=jnp.float32)
            * scale_factor
        )
        probability = jnp.exp(scores - log_part[..., None])
        grad_prob = jnp.einsum(
            "nqhd,nkhd->nhqk", grad_part, value_part, preferred_element_type=jnp.float32
        )
        inner_sum = jnp.sum(probability * grad_prob, axis=-1, keepdims=True)
        grad_score = (probability * (grad_prob - inner_sum)).astype(jnp.bfloat16)
        grad_query = (
            jnp.einsum("nhqk,nkhd->nqhd", grad_score, key_part, preferred_element_type=jnp.float32)
            * scale_factor
        )
        grad_key = (
            jnp.einsum(
                "nhqk,nqhd->nkhd", grad_score, query_part, preferred_element_type=jnp.float32
            )
            * scale_factor
        )
        grad_value = jnp.einsum(
            "nhqk,nqhd->nkhd",
            probability.astype(jnp.bfloat16),
            grad_part,
            preferred_element_type=jnp.float32,
        )
        return (
            grad_query.reshape(grad_query.shape[0], grad_query.shape[1], lane_count),
            grad_key.reshape(grad_key.shape[0], grad_key.shape[1], lane_count),
            grad_value.reshape(grad_value.shape[0], grad_value.shape[1], lane_count),
        )

    query_terms, key_terms, value_terms = lax.map(one_group, (jnp.arange(head_steps), log_totals))
    return (join_heads(query_terms), join_heads(key_terms), join_heads(value_terms))


def local_general(
    hidden_in,
    condition,
    cotangent,
    weights_in,
    weights_down,
    biases,
    moment_in,
    moment_down,
    moment_bias,
    square_in,
    square_down,
    square_bias,
):
    low_in = weights_in.astype(jnp.bfloat16)
    low_down = weights_down.astype(jnp.bfloat16)
    low_bias = biases.astype(jnp.bfloat16)
    whole_in, whole_down, bias_all = gather_weights(low_in, low_down, low_bias)
    bias_float = bias_all.astype(jnp.float32)
    hidden = hidden_in.astype(jnp.float32)
    cond_float = condition.astype(jnp.float32)
    cond_act = jax.nn.silu(cond_float).astype(jnp.bfloat16)
    modulation = (
        jnp.dot(cond_act, whole_in[:, : 6 * D], preferred_element_type=jnp.float32)
        + bias_float[: 6 * D]
    )
    pieces = [modulation[:, None, part_index * D : (part_index + 1) * D] for part_index in range(6)]
    shift_one, scale_one, gate_one, shift_two, scale_two, gate_two = pieces
    normed_one = layer_norm(hidden)
    input_one = (normed_one * (1.0 + scale_one) + shift_one).astype(jnp.bfloat16)
    qkv_all = dense_map(input_one, whole_in[:, 6 * D : 9 * D])
    queries = (qkv_all[..., :D] + bias_float[6 * D : 7 * D]).astype(jnp.bfloat16)
    keys_local = qkv_all[..., D : 2 * D].astype(jnp.bfloat16)
    values_local = (qkv_all[..., 2 * D :] + bias_float[7 * D : 8 * D]).astype(jnp.bfloat16)
    keys_all, values_all = (
        lax.all_gather(keys_local, "seq", axis=1, tiled=True),
        lax.all_gather(values_local, "seq", axis=1, tiled=True),
    )
    attn_float, log_totals = attention_forward(queries, keys_all, values_all)
    attn_mixed = attn_float.astype(jnp.bfloat16)
    attn_out = dense_map(attn_mixed, whole_in[:, 9 * D : 10 * D]) + bias_float[8 * D : 9 * D]
    middle = hidden + gate_one * attn_out
    normed_two = layer_norm(middle)
    input_two = (normed_two * (1.0 + scale_two) + shift_two).astype(jnp.bfloat16)
    upward = dense_map(input_two, whole_in[:, 10 * D :]) + bias_float[9 * D : 9 * D + FF]
    activated = jax.nn.gelu(upward, approximate=True).astype(jnp.bfloat16)
    branch = dense_map(activated, whole_down) + bias_float[9 * D + FF :]
    block_out = (middle + gate_two * branch).astype(jnp.bfloat16)
    whole_in, whole_down, bias_all = gather_weights(low_in, low_down, low_bias)
    grad_out = cotangent.astype(jnp.float32)
    grad_branch = (grad_out * gate_two).astype(jnp.bfloat16)
    gate_two_grad = jnp.sum(grad_out * branch, axis=1)
    grad_down = outer_sum(activated, grad_branch)
    bias_down_grad = total_sum(grad_branch)
    grad_act = dense_back(grad_branch, whole_down)
    _, gelu_pull = jax.vjp(lambda inner_value: jax.nn.gelu(inner_value, approximate=True), upward)
    grad_upward = gelu_pull(grad_act)[0].astype(jnp.bfloat16)
    grad_up = outer_sum(input_two, grad_upward)
    bias_up_grad = total_sum(grad_upward)
    grad_input_two = dense_back(grad_upward, whole_in[:, 10 * D :])
    shift_two_grad = jnp.sum(grad_input_two, axis=1)
    scale_two_grad = jnp.sum(grad_input_two * normed_two, axis=1)
    _, norm_pull_two = jax.vjp(layer_norm, middle)
    grad_middle = grad_out + norm_pull_two(grad_input_two * (1.0 + scale_two))[0]
    grad_attn = (grad_middle * gate_one).astype(jnp.bfloat16)
    gate_one_grad = jnp.sum(grad_middle * attn_out, axis=1)
    grad_out_proj = outer_sum(attn_mixed, grad_attn)
    bias_out_grad = total_sum(grad_attn)
    grad_mixed = dense_back(grad_attn, whole_in[:, 9 * D : 10 * D]).astype(jnp.bfloat16)
    grad_query, key_terms, value_terms = attention_backward(
        queries, keys_all, values_all, log_totals, grad_mixed
    )
    key_grad, value_grad = (
        lax.psum_scatter(
            key_terms.astype(jnp.bfloat16), "seq", scatter_dimension=1, tiled=True
        ).astype(jnp.float32),
        lax.psum_scatter(
            value_terms.astype(jnp.bfloat16), "seq", scatter_dimension=1, tiled=True
        ).astype(jnp.float32),
    )
    grad_qkv = jnp.concatenate(
        [
            grad_query.astype(jnp.bfloat16),
            key_grad.astype(jnp.bfloat16),
            value_grad.astype(jnp.bfloat16),
        ],
        axis=-1,
    )
    grad_proj_qkv = outer_sum(input_one, grad_qkv)
    bias_query_grad = total_sum(grad_qkv[..., :D])
    bias_value_grad = total_sum(grad_qkv[..., 2 * D :])
    grad_input_one = dense_back(grad_qkv, whole_in[:, 6 * D : 9 * D])
    shift_one_grad = jnp.sum(grad_input_one, axis=1)
    scale_one_grad = jnp.sum(grad_input_one * normed_one, axis=1)
    _, norm_pull_one = jax.vjp(layer_norm, hidden)
    input_grad = grad_middle + norm_pull_one(grad_input_one * (1.0 + scale_one))[0]
    mod_terms = jnp.concatenate(
        [
            shift_one_grad,
            scale_one_grad,
            gate_one_grad,
            shift_two_grad,
            scale_two_grad,
            gate_two_grad,
        ],
        axis=-1,
    )
    mod_grad = lax.psum(mod_terms, "seq").astype(jnp.bfloat16)
    _, silu_pull = jax.vjp(jax.nn.silu, cond_float)
    cond_grad = silu_pull(
        jnp.einsum("ne,de->nd", mod_grad, whole_in[:, : 6 * D], preferred_element_type=jnp.float32)
    )[0]
    owner_mask = (lax.axis_index("seq") == 0).astype(jnp.float32)
    grad_ada = (
        jnp.einsum("nd,ne->de", cond_act, mod_grad, preferred_element_type=jnp.float32) * owner_mask
    )
    bias_ada_grad = jnp.sum(mod_grad.astype(jnp.float32), axis=0) * owner_mask
    grad_in_all = jnp.zeros((D, 10 * D + FF), jnp.float32)
    grad_in_all = grad_in_all.at[:, : 6 * D].set(grad_ada)
    grad_in_all = grad_in_all.at[:, 6 * D : 9 * D].set(grad_proj_qkv)
    grad_in_all = grad_in_all.at[:, 9 * D : 10 * D].set(grad_out_proj)
    grad_in_all = grad_in_all.at[:, 10 * D :].set(grad_up)
    bias_flat = jnp.concatenate(
        [
            bias_ada_grad,
            bias_query_grad,
            bias_value_grad,
            bias_out_grad,
            bias_up_grad,
            bias_down_grad,
        ]
    )
    summed_in, summed_down, summed_bias = (
        lax.psum_scatter(
            grad_in_all.astype(jnp.bfloat16), "dp", scatter_dimension=1, tiled=True
        ).astype(jnp.float32),
        lax.psum_scatter(
            grad_down.astype(jnp.bfloat16), "dp", scatter_dimension=1, tiled=True
        ).astype(jnp.float32),
        lax.psum_scatter(
            bias_flat.reshape(1, -1).astype(jnp.bfloat16), "dp", scatter_dimension=1, tiled=True
        ).astype(jnp.float32),
    )
    owned_in, owned_down, owned_bias = (
        lax.psum_scatter(
            summed_in.astype(jnp.bfloat16), "seq", scatter_dimension=0, tiled=True
        ).astype(jnp.float32),
        lax.psum_scatter(
            summed_down.astype(jnp.bfloat16), "seq", scatter_dimension=0, tiled=True
        ).astype(jnp.float32),
        lax.psum_scatter(
            summed_bias.reshape(-1).astype(jnp.bfloat16), "seq", scatter_dimension=0, tiled=True
        ).astype(jnp.float32),
    )
    moments_in, squares_in, master_in = adamw_step(
        weights_in, moment_in, square_in, owned_in, rate_in
    )
    moments_down, squares_down, master_down = adamw_step(
        weights_down, moment_down, square_down, owned_down, rate_down
    )
    moments_bias, squares_bias, master_bias = adamw_step(
        biases, moment_bias, square_bias, owned_bias, rate_bias
    )
    return (
        block_out,
        input_grad,
        cond_grad,
        moments_in,
        moments_down,
        moments_bias,
        squares_in,
        squares_down,
        squares_bias,
        master_in,
        master_down,
        master_bias,
        master_in.astype(jnp.bfloat16),
        master_down.astype(jnp.bfloat16),
        master_bias.astype(jnp.bfloat16),
    )


MESH = pl.DeviceIdType.MESH
WIDE = 896
LOW = 6 * D
KEPT = 4 * D + FF
PLANES = 4
HALF = D // 2
TALL = HALF + 16
SUBS = 3
SUB_ROWS = TALL // SUBS
FF_PART = FF // 2
DP = 16


def place():
    dp = lax.axis_index("dp")
    y = lax.axis_index("seq")
    return (dp // 4, lax.rem(dp // 2, 2), lax.rem(dp, 2), y)


def device_at(z, x, c, y):
    return ((z * 2 + x) * 2 + c, y)


def neighbours():
    z, x, c, y = place()
    return {
        "x": device_at(z, 1 - x, c, y),
        "y": device_at(z, x, c, 1 - y),
        "up": device_at(jnp.minimum(z + 1, PLANES - 1), x, c, y),
        "down": device_at(jnp.maximum(z - 1, 0), x, c, y),
        "core": device_at(z, x, 1 - c, y),
        "swap": device_at(z, x, 1 - c, 1 - y),
    }


def repeat(count, body):
    def step(at, carried):
        body(at)
        return carried

    lax.fori_loop(0, count, step, 0)


def greet_all():
    barrier = pltpu.get_barrier_semaphore()
    here = lax.axis_index("dp") * 2 + lax.axis_index("seq")

    def signal(at):
        there = lax.rem(here + at + 1, 2 * DP)
        pl.semaphore_signal(
            barrier, inc=1, device_id=(there // 2, lax.rem(there, 2)), device_id_type=MESH
        )

    repeat(2 * DP - 1, signal)
    pl.semaphore_wait(barrier, 2 * DP - 1)


class Broad:
    height, width, subs, split = SUB_ROWS, WIDE, SUBS, 64
    first, source_column = 0, 0

    @staticmethod
    def holds(zs, xs, cs):
        return (zs * 2 + xs) * 2 + cs >= 7

    @staticmethod
    def view(whole, zs, xs, ys, cs, sub, start=0, rows=SUB_ROWS):
        column = jnp.maximum(((zs * 2 + xs) * 2 + cs) * WIDE - LOW, 128)
        row = pl.multiple_of(sub * SUB_ROWS + start, 16)
        return whole.at[ys, pl.ds(row, rows), pl.ds(pl.multiple_of(column, 128), WIDE)]


class Narrow:
    height, width, subs, split = TALL, 128, 1, 272
    first, source_column = 16 * SUBS, WIDE - 128

    @staticmethod
    def holds(zs, xs, cs):
        return (zs * 2 + xs) * 2 + cs == 6

    @staticmethod
    def view(whole, zs, xs, ys, cs, sub, start=0, rows=TALL):
        return whole.at[ys, pl.ds(start, rows), pl.ds(0, 128)]


class Down:
    height, width, subs, split = 64, FF_PART, 1, 32
    first, source_column = 16 * SUBS + 16, 0

    @staticmethod
    def holds(zs, xs, cs):
        return zs >= 0

    @staticmethod
    def view(whole, zs, xs, ys, cs, sub, start=0, rows=64):
        row = pl.multiple_of(((zs * 2 + xs) * 2 + cs) * 64 + start, 32)
        return whole.at[pl.ds(row, rows), pl.ds(pl.multiple_of(ys * FF_PART, 128), FF_PART)]


SLOTS = 16 * SUBS + 32
RELATIONS = ("own", "x", "y", "xy")
HOPS = {"own": 0, "x": 1, "y": 1, "xy": 2}


def by_plane(z, table):
    picked = table[PLANES - 1]
    for plane in range(PLANES - 2, -1, -1):
        picked = jnp.where(z == plane, table[plane], picked)
    return picked


def forward_block(what, refs, kind, zs, relation, sub, sems, valid):
    whole, mine = refs
    send_sem, recv_sem, core_sem = sems
    z, x, c, y = place()
    near = neighbours()
    xs = 1 - x if "x" in relation else x
    ys = 1 - y if "y" in relation else y
    slot = kind.first + ((zs * 2 + xs) * 2 + ys) * kind.subs + sub
    full, half = recv_sem.at[slot, 0], recv_sem.at[slot, 1]
    parts = ((0, kind.height), (0, kind.split), (kind.split, kind.height - kind.split))

    def copy(part, index, arrival, key, source=None, cs=None):
        target = kind.view(whole, zs, xs, ys, c if cs is None else cs, sub, *parts[part])
        return pltpu.make_async_remote_copy(
            src_ref=target if source is None else source,
            dst_ref=target,
            send_sem=send_sem.at[slot, index],
            recv_sem=arrival,
            device_id=near[key],
            device_id_type=MESH,
        )

    if what == "core":

        @pl.when(valid & kind.holds(zs, xs, 1 - c))
        def _():
            copy(0, 4, core_sem.at[slot], "core", cs=1 - c).wait_recv()

        return
    valid = valid & kind.holds(zs, xs, c)
    if what == "tick":
        arrived = valid & (zs != z) if relation == "own" else valid

        @pl.when(arrived)
        def _():
            if relation == "xy":
                copy(1, 0, full, "x").wait_recv()
                copy(2, 0, half, "x").wait_recv()
            else:
                copy(0, 0, full, "x").wait_recv()

    def act(descriptor):
        if what == "drain":
            descriptor.wait_send()
        else:
            descriptor.start()

    def spread(source, upward, downward):
        @pl.when(upward)
        def _():
            act(copy(0, 0, full, "up", source))

        @pl.when(downward)
        def _():
            act(copy(0, 1, full, "down", source))

        act(copy(0, 2, full, "x", source))
        act(copy(0, 3, full, "y", source))
        act(copy(0, 4, core_sem.at[slot], "core", source))

    if relation == "own":

        if what != "tick":

            @pl.when(valid & (zs == z))
            def _():
                source = mine.at[
                    pl.ds(pl.multiple_of(sub * kind.height, 16), kind.height),
                    pl.ds(kind.source_column, kind.width),
                ]
                spread(source, z < PLANES - 1, z > 0)

        if what != "launch":

            @pl.when(valid & (zs != z))
            def _():
                spread(None, (zs < z) & (z < PLANES - 1), (zs > z) & (z > 0))

        return

    @pl.when(valid)
    def _():
        if relation == "x":
            act(copy(1, 3, full, "y"))
        if relation == "y":
            act(copy(2, 2, half, "x"))
        act(copy(0, 4, core_sem.at[slot], "core"))


def forward_step(what, refs, plan, relations, sems, sub):
    z = place()[0]
    for kind, order in plan:
        for position in range(len(order[0])):
            zs = by_plane(z, [row[position] for row in order])
            for relation in relations:
                forward_block(
                    what,
                    refs[kind.__name__],
                    kind,
                    zs,
                    relation,
                    jnp.minimum(sub, kind.subs - 1),
                    sems,
                    sub < kind.subs,
                )


def launch(refs, kinds, sems):
    z = place()[0]

    def go(sub):
        for kind in kinds:
            forward_block(
                "launch",
                refs[kind.__name__],
                kind,
                z,
                "own",
                jnp.minimum(sub, kind.subs - 1),
                sems,
                sub < kind.subs,
            )

    repeat(max(kind.subs for kind in kinds), go)


NEAR_LOW = ((1, 2), (1, 2), (2, 1), (2, 1))
ONLY_ONE = ((1,),) * PLANES
ONLY_LAST = ((3,),) * PLANES
NEAR = ((0, 1, 2, 3), (1, 0, 2, 3), (2, 3, 1, 0), (3, 2, 1, 0))
PLAN_LOW = ((Broad, NEAR_LOW), (Narrow, ONLY_ONE))
PLAN_UP = ((Broad, ONLY_LAST),)
PLAN_DOWN = ((Down, NEAR),)
PLAN_ALL = PLAN_LOW + PLAN_UP + PLAN_DOWN


BF16 = jnp.bfloat16
F32 = jnp.float32
PLAIN = (((1,), (0,)), ((), ()))
BOTH_LAST = (((1,), (1,)), ((), ()))
BOTH_FIRST = (((0,), (0,)), ((), ()))
LANES = 128
PAIRS = HEADS // 2
TOKENS_HERE = 512


def multiply(left, right, dims=PLAIN):
    return lax.dot_general(left, right, dims, preferred_element_type=F32)


def two_heads(block):
    lanes = lax.broadcasted_iota(jnp.int32, block.shape, 1)
    zero = jnp.zeros_like(block)
    return (jnp.where(lanes < HEAD_DIM, block, zero), jnp.where(lanes < HEAD_DIM, zero, block))


def attend_pair(pair, queries, keys, values, mixed, log_totals):
    columns = pl.ds(pl.multiple_of(pair * LANES, LANES), LANES)
    key_block = keys[:, columns]
    value_flat = values[:, columns].T
    parts = []
    for head, query_block in enumerate(two_heads(queries[:, columns])):
        scores = multiply(key_block, query_block, BOTH_LAST)
        largest = jnp.max(scores, axis=0, keepdims=True)
        weights = jnp.exp((scores - largest) * HEAD_DIM**-0.5)
        total = jnp.sum(weights, axis=0, keepdims=True)
        parts.append(multiply(value_flat, weights.astype(BF16)) * (1.0 / total))
        log_totals[2 * pair + head] = largest * HEAD_DIM**-0.5 + jnp.log(total)
    joined = jnp.concatenate([parts[0][:HEAD_DIM], parts[1][HEAD_DIM:]], axis=0)
    mixed[:, columns] = joined.T.astype(BF16)


def normalize(values):
    center = values - jnp.mean(values, axis=-1, keepdims=True)
    return center * lax.rsqrt(jnp.mean(center * center, axis=-1, keepdims=True) + norm_eps)


def from_weights(left, whole, start, width):
    columns = pl.ds(pl.multiple_of(start, LANES), width)
    return multiply(left[:, :HALF], whole[0, :HALF, columns]) + multiply(
        left[:, HALF:], whole[1, :HALF, columns]
    )


def bias_of(whole, start, width):
    columns = pl.ds(pl.multiple_of(start, LANES), width)
    both = whole[0, HALF:TALL, columns].astype(F32) + whole[1, HALF:TALL, columns].astype(F32)
    return both[:1]


def forward_kernel(
    low_in,
    low_down,
    hidden_in,
    cotangent,
    condition,
    ada_bias,
    whole_in,
    whole_down,
    hidden_out,
    grad_out_out,
    cond_all,
    modulation,
    input_one_out,
    queries_out,
    keys_out,
    values_out,
    mixed_out,
    log_totals,
    attn_out_out,
    middle_out,
    input_two_out,
    slope,
    grad_branch_out,
    row_grads,
    block_out,
    grad_down,
    own_in,
    own_down,
    ada_weights,
    ada_part,
    mod_parts,
    up_stage,
    wide,
    active,
    flat_branch,
    down_stage,
    send_sem,
    recv_sem,
    core_sem,
    local_sem,
    cond_send,
    cond_recv,
    mod_send,
    mod_recv,
    swap_sem,
    pair_sem,
    up_sem,
    down_sem,
    hidden,
    grad_out,
    input_one,
    queries,
    keys,
    values,
    mixed,
    attn_out,
    middle,
    input_two,
    grad_branch,
    keep_sem,
):
    z, x, c, y = place()
    dp = (z * 2 + x) * 2 + c
    near = neighbours()
    sems = (send_sem, recv_sem, core_sem)
    refs = {"Broad": (own_in, low_in), "Narrow": (own_in, low_in), "Down": (own_down, low_down)}
    at_home = c == y

    def remote(source, target, sent, arrived, device):
        return pltpu.make_async_remote_copy(
            src_ref=source,
            dst_ref=target,
            send_sem=sent,
            recv_sem=arrived,
            device_id=device,
            device_id_type=MESH,
        )

    kept = {
        name: pltpu.make_async_copy(source, target, keep_sem.at[index])
        for index, (name, source, target) in enumerate(
            (
                ("hidden", hidden, hidden_out),
                ("grad_out", grad_out, grad_out_out),
                ("input_one", input_one, input_one_out),
                ("queries", queries, queries_out),
                ("keys", keys, keys_out),
                ("values", values, values_out),
                ("mixed", mixed, mixed_out),
                ("attn_out", attn_out, attn_out_out),
                ("middle", middle, middle_out),
                ("input_two", input_two, input_two_out),
                ("grad_branch", grad_branch, grad_branch_out),
            )
        )
    }

    def keep(*which):
        for name in which:
            kept[name].start()

    broad = pltpu.make_async_copy(
        low_in,
        own_in.at[y, :, pl.ds(pl.multiple_of(jnp.maximum(dp, 7) * WIDE - LOW, LANES), WIDE)],
        local_sem.at[0],
    )
    narrow = pltpu.make_async_copy(
        low_in.at[:, pl.ds(WIDE - 128, 128)], own_in.at[y, :, pl.ds(0, 128)], local_sem.at[0]
    )
    down = pltpu.make_async_copy(
        low_down,
        own_down.at[
            pl.ds(pl.multiple_of(dp * 64, 64), 64),
            pl.ds(pl.multiple_of(y * FF_PART, LANES), FF_PART),
        ],
        local_sem.at[1],
    )
    ada = pltpu.make_async_copy(low_in.at[pl.ds(0, HALF)], ada_weights, local_sem.at[2])
    ada.start()
    down.start()

    @pl.when(dp >= 7)
    def _():
        broad.start()

    @pl.when(dp == 6)
    def _():
        narrow.start()

    greet_all()

    cond_all[dp] = condition[...]

    def cond_copy(at):
        there = lax.rem(dp + at + 1, DP)
        return remote(
            condition, cond_all.at[dp], cond_send.at[at], cond_recv.at[dp], (there, y)
        )

    repeat(DP - 1, lambda at: cond_copy(at).start())

    swaps = []
    for index, (source, target) in enumerate(((hidden_in, hidden), (cotangent, grad_out))):
        swaps.append(
            (
                pltpu.make_async_copy(source, target, swap_sem.at[index, 0]),
                remote(
                    source, target, swap_sem.at[index, 1], swap_sem.at[index, 2], near["swap"]
                ),
            )
        )

    def trade(index):
        @pl.when(at_home)
        def _():
            swaps[index][0].start()

        @pl.when(jnp.logical_not(at_home))
        def _():
            swaps[index][1].start()

    def traded(index):
        @pl.when(at_home)
        def _():
            swaps[index][0].wait()

        @pl.when(jnp.logical_not(at_home))
        def _():
            swaps[index][1].wait()

    trade(0)
    launch(refs, (Broad, Narrow), sems)

    @pl.when((z == 0) | (z == PLANES - 1))
    def _():
        launch(refs, (Down,), sems)

    def pass_on(plan, relations):
        subs = max(kind.subs for kind, _ in plan)
        repeat(subs, lambda sub: forward_step("tick", refs, plan, relations, sems, sub))

    pass_on(PLAN_LOW, ("own",))

    def cond_arrived(at):
        there = lax.rem(dp + at + 1, DP)
        remote(
            condition, cond_all.at[there], cond_send.at[at], cond_recv.at[there], (there, y)
        ).wait_recv()

    repeat(DP - 1, cond_arrived)
    raw = jnp.concatenate([cond_all[index] for index in range(DP)], axis=0)
    active[...] = (raw / (1.0 + jnp.exp(-raw))).astype(BF16)
    ada.wait()
    partial = (
        multiply(
            active[:, pl.ds(pl.multiple_of(y * HALF, LANES), HALF)],
            ada_weights[...],
        )
        + ada_bias[...]
    )
    for index in range(DP):
        ada_part[index] = partial[index : index + 1]

    def mod_target(at):
        latent, core = at // 2, lax.rem(at, 2)
        return (latent // 2 * 2 + core, lax.rem(latent, 2))

    def mod_copy(at):
        return remote(
            ada_part.at[at // 2],
            mod_parts.at[dp * 2 + y],
            mod_send.at[at],
            mod_recv.at[dp * 2 + y],
            mod_target(at),
        )

    def elsewhere(at):
        there = mod_target(at)
        return (there[0] != dp) | (there[1] != y)

    @pl.when(dp < 7)
    def _():
        def send(at):
            @pl.when(elsewhere(at))
            def _():
                mod_copy(at).start()

            @pl.when(jnp.logical_not(elsewhere(at)))
            def _():
                mod_parts[dp * 2 + y] = ada_part[at // 2]

        repeat(2 * DP, send)

    pass_on(PLAN_LOW, ("x", "y"))

    @pl.when((z > 0) & (z < PLANES - 1))
    def _():
        launch(refs, (Down,), sems)

    pass_on(PLAN_UP, ("own",))
    trade(1)
    traded(0)

    def mod_arrived(at):
        @pl.when(at != dp * 2 + y)
        def _():
            remote(
                ada_part.at[0], mod_parts.at[at], mod_send.at[0], mod_recv.at[at], near["x"]
            ).wait_recv()

    repeat(14, mod_arrived)
    for index in range(7):
        modulation[:, index * WIDE : (index + 1) * WIDE] = (
            mod_parts[2 * index] + mod_parts[2 * index + 1]
        )

    def vector(index):
        return modulation[:, index * D : (index + 1) * D]

    def shape_one(at):
        rows = pl.ds(pl.multiple_of(at * 128, 128), 128)
        normed = normalize(hidden[rows].astype(F32))
        input_one[rows] = (normed * (1.0 + vector(1)) + vector(0)).astype(BF16)

    repeat(4, shape_one)
    keep("hidden", "input_one")

    pass_on(PLAN_LOW, ("xy",))
    repeat(SUBS, lambda at: forward_step("core", refs, PLAN_LOW, RELATIONS, sems, at))

    @pl.when(dp >= 7)
    def _():
        broad.wait()

    @pl.when(dp == 6)
    def _():
        narrow.wait()

    def project(at):
        columns = pl.ds(pl.multiple_of(at * 256, LANES), 256)
        keys[:HALF, columns] = from_weights(input_one, own_in, D + at * 256, 256).astype(BF16)
        values[:HALF, columns] = (
            from_weights(input_one, own_in, 2 * D + at * 256, 256)
            + bias_of(own_in, D + at * 256, 256)
        ).astype(BF16)

    repeat(D // 256, project)
    mates = [
        remote(
            one.at[:HALF], one.at[HALF:], pair_sem.at[index, 0], pair_sem.at[index, 1], near["core"]
        )
        for index, one in enumerate((keys, values))
    ]
    for mate in mates:
        mate.start()

    def project_queries(at):
        columns = pl.ds(pl.multiple_of(at * 256, LANES), 256)
        queries[:, columns] = (
            from_weights(input_one, own_in, at * 256, 256) + bias_of(own_in, at * 256, 256)
        ).astype(BF16)

    repeat(D // 256, project_queries)
    for mate in mates:
        mate.wait()
    keep("queries", "keys", "values")

    def attention(pair):
        attend_pair(pair, queries, keys, values, mixed, log_totals)

        @pl.when(pair < SUBS)
        def _():
            forward_step("tick", refs, PLAN_UP, ("x", "y"), sems, pair)

        @pl.when(pair == SUBS)
        def _():
            forward_step("tick", refs, PLAN_DOWN, ("own",), sems, 0)

        @pl.when((pair > SUBS) & (pair <= 2 * SUBS))
        def _():
            forward_step("tick", refs, PLAN_UP, ("xy",), sems, pair - SUBS - 1)

        @pl.when(pair == 2 * SUBS + 1)
        def _():
            forward_step("tick", refs, PLAN_DOWN, ("x", "y"), sems, 0)

    repeat(PAIRS, attention)
    keep("mixed")

    def project_out(at):
        columns = pl.ds(pl.multiple_of(at * 256, LANES), 256)
        attn_out[:, columns] = from_weights(mixed, own_in, 3 * D + at * 256, 256) + bias_of(
            own_in, 2 * D + at * 256, 256
        )

    repeat(D // 256, project_out)

    def shape_two(at):
        rows = pl.ds(pl.multiple_of(at * 128, 128), 128)
        mid = hidden[rows].astype(F32) + vector(2) * attn_out[rows]
        middle[rows] = mid
        input_two[rows] = (normalize(mid) * (1.0 + vector(4)) + vector(3)).astype(BF16)

    repeat(4, shape_two)
    keep("attn_out", "middle", "input_two")
    repeat(SUBS, lambda at: forward_step("core", refs, PLAN_UP, RELATIONS, sems, at))
    whole_copies = [
        pltpu.make_async_copy(
            own_in.at[half, pl.ds(0, HALF)],
            whole_in.at[pl.ds(half * HALF, HALF)],
            local_sem.at[3 + half],
        )
        for half in range(2)
    ]
    for whole_copy in whole_copies:
        whole_copy.start()
    tile = 512

    def up_copy(at, slot):
        return pltpu.make_async_copy(
            up_stage.at[slot],
            slope.at[:, pl.ds(pl.multiple_of(at * tile, LANES), tile)],
            up_sem.at[slot],
        )

    def down_grad_copy(at, slot):
        return pltpu.make_async_copy(
            down_stage.at[slot],
            grad_down.at[:, pl.ds(pl.multiple_of(at * tile, LANES), tile)],
            down_sem.at[slot],
        )

    traded(1)

    def shape_branch(at):
        columns = pl.ds(pl.multiple_of(at * 256, LANES), 256)
        gate = modulation[:, pl.ds(pl.multiple_of(5 * D + at * 256, LANES), 256)]
        scaled = (grad_out[:, columns].astype(F32) * gate).astype(BF16)
        grad_branch[:, columns] = scaled
        flat_branch[pl.ds(pl.multiple_of(at * 256, 256), 256)] = scaled.T
        row_grads[1:2, columns] = jnp.sum(scaled.astype(F32), axis=0, keepdims=True)

    repeat(D // 256, shape_branch)
    keep("grad_out", "grad_branch")

    def widen(at):
        slot = lax.rem(at, 2)

        @pl.when(at >= 2)
        def _():
            up_copy(at - 2, slot).wait()
            down_grad_copy(at - 2, slot).wait()

        factor = math.sqrt(2.0 / math.pi)
        for side in range(2):
            start = at * tile + side * 256
            value = from_weights(input_two, own_in, 4 * D + start, 256) + bias_of(
                own_in, 3 * D + start, 256
            )
            square = value * value
            bent = jnp.tanh(factor * value * (1.0 + 0.044715 * square))
            half_up = 0.5 + 0.5 * bent
            up_stage[slot, :, side * 256 : (side + 1) * 256] = half_up + 0.5 * value * (
                1.0 - bent * bent
            ) * (factor + 3.0 * 0.044715 * factor * square)
            wide[:, pl.ds(pl.multiple_of(start, LANES), 256)] = (value * half_up).astype(BF16)
        up_copy(at, slot).start()
        for side in range(2):
            columns = pl.ds(pl.multiple_of(at * tile + side * 256, LANES), 256)
            down_stage[slot, :, side * 256 : (side + 1) * 256] = multiply(
                flat_branch[...], wide[:, columns]
            ).astype(BF16)
        down_grad_copy(at, slot).start()

        @pl.when(at == 3)
        def _():
            forward_step("tick", refs, PLAN_DOWN, ("xy",), sems, 0)

    repeat(FF // tile, widen)
    for at in (FF // tile - 2, FF // tile - 1):
        up_copy(at, at % 2).wait()
        down_grad_copy(at, at % 2).wait()
    forward_step("core", refs, PLAN_DOWN, RELATIONS, sems, 0)
    down.wait()
    down_copy = pltpu.make_async_copy(own_down, whole_down, local_sem.at[5])
    down_copy.start()

    def narrow_down(at):
        columns = pl.ds(pl.multiple_of(at * 256, LANES), 256)
        value = bias_of(own_in, 7 * D + at * 256, 256)
        for side in range(2):
            value += multiply(
                wide[:, side * FF_PART : (side + 1) * FF_PART],
                own_down[columns, side * FF_PART : (side + 1) * FF_PART],
                BOTH_LAST,
            )
        gate = modulation[:, pl.ds(pl.multiple_of(5 * D + at * 256, LANES), 256)]
        block_out[:, columns] = (middle[:, columns] + gate * value).astype(BF16)
        towards = grad_out[:, columns].astype(F32)
        row_grads[0:1, columns] = jnp.sum(towards * value, axis=0, keepdims=True)

    repeat(D // 256, narrow_down)

    repeat(SUBS, lambda at: forward_step("drain", refs, PLAN_ALL, RELATIONS, sems, at))
    repeat(DP - 1, lambda at: cond_copy(at).wait_send())

    @pl.when(dp < 7)
    def _():
        def sent(at):
            @pl.when(elsewhere(at))
            def _():
                mod_copy(at).wait_send()

        repeat(2 * DP, sent)

    for whole_copy in whole_copies:
        whole_copy.wait()
    down_copy.wait()
    for one in kept.values():
        one.wait()


def run_forward(low_in, low_down, hidden_in, cotangent, condition, ada_bias):
    shape = jax.ShapeDtypeStruct
    rows = TOKENS_HERE
    wide, flat = shape((rows, D), BF16), shape((rows, D), F32)
    both = shape((2 * rows, D), BF16)
    outs = [
        (shape((D, KEPT), BF16), pl.ANY),
        (shape((D, FF), BF16), pl.ANY),
        (wide, pl.ANY),
        (wide, pl.ANY),
        (shape((DP, 1, D), F32), pltpu.VMEM),
        (shape((1, 7 * WIDE), F32), pltpu.VMEM),
        (wide, pl.ANY),
        (wide, pl.ANY),
        (both, pl.ANY),
        (both, pl.ANY),
        (wide, pl.ANY),
        (shape((HEADS, 1, rows), F32), pltpu.VMEM),
        (flat, pl.ANY),
        (flat, pl.ANY),
        (wide, pl.ANY),
        (shape((rows, FF), F32), pl.ANY),
        (wide, pl.ANY),
        (shape((8, D), F32), pltpu.VMEM),
        (wide, pltpu.VMEM),
        (shape((D, FF), BF16), pl.ANY),
    ]
    kept = (wide, wide, wide, wide, both, both, wide, flat, flat, wide, wide)
    dma = pltpu.SemaphoreType.DMA
    return pl.pallas_call(
        forward_kernel,
        out_shape=[one for one, _ in outs],
        in_specs=[pl.BlockSpec(memory_space=pl.ANY)] * 4
        + [pl.BlockSpec(memory_space=pltpu.VMEM)] * 2,
        out_specs=[pl.BlockSpec(memory_space=where) for _, where in outs],
        scratch_shapes=[
            pltpu.VMEM((2, TALL, KEPT), BF16),
            pltpu.VMEM((D, FF), BF16),
            pltpu.VMEM((HALF, WIDE), BF16),
            pltpu.VMEM((DP, 1, WIDE), F32),
            pltpu.VMEM((14, 1, WIDE), F32),
            pltpu.VMEM((2, rows, 512), F32),
            pltpu.VMEM((rows, FF), BF16),
            pltpu.VMEM((DP, D), BF16),
            pltpu.VMEM((D, rows), BF16),
            pltpu.VMEM((2, D, 512), BF16),
            dma((SLOTS, 5)),
            dma((SLOTS, 2)),
            dma((SLOTS,)),
            dma((6,)),
            dma((DP,)),
            dma((DP,)),
            dma((2 * DP,)),
            dma((14,)),
            dma((2, 3)),
            dma((2, 2)),
            dma((2,)),
            dma((2,)),
        ]
        + [pltpu.VMEM(one.shape, one.dtype) for one in kept]
        + [dma((len(kept),))],
        compiler_params=pltpu.CompilerParams(
            collective_id=0, has_side_effects=True, vmem_limit_bytes=62 * 2**20
        ),
        name="forward",
    )(low_in, low_down, hidden_in, cotangent, condition, ada_bias)


GRAD_SUBS = 8
GRAD_ROWS = HALF // GRAD_SUBS


class BroadGrad:
    height, width, subs, source_column = GRAD_ROWS, WIDE, GRAD_SUBS, 0
    split = GRAD_ROWS // 2

    @staticmethod
    def holds(zs, xs, cs):
        return (zs * 2 + xs) * 2 + cs >= 7

    @staticmethod
    def corner(zs, xs, ys, cs, sub):
        column = jnp.maximum(((zs * 2 + xs) * 2 + cs) * WIDE - LOW, 128)
        return (
            pl.multiple_of(ys * HALF + sub * GRAD_ROWS, GRAD_ROWS),
            pl.multiple_of(column, 128),
        )


class HighGrad(BroadGrad):
    split = 48


class NarrowGrad:
    height, width, subs, source_column = HALF, 128, 1, WIDE - 128
    split = HALF // 2

    @staticmethod
    def holds(zs, xs, cs):
        return (zs * 2 + xs) * 2 + cs == 6

    @staticmethod
    def corner(zs, xs, ys, cs, sub):
        return (pl.multiple_of(ys * HALF, HALF), 0)


def reduce_block(what, refs, kind, zs, plane_at, planes, relation, sub, sems, valid):
    grads, first_column, owned, buffers = refs
    from_core, from_x, from_y, from_low, from_high, half_a, half_b = buffers
    send_sem, recv_sem = sems
    z, x, c, y = place()
    near = neighbours()
    xs = 1 - x if "x" in relation else x
    ys = 1 - y if "y" in relation else y
    flat = plane_at * kind.subs + sub
    count = planes * kind.subs
    kin = RELATIONS.index(relation)
    slot = kin * count + flat
    rows, half_rows = kind.height, kind.split

    def remote(source, target, index, arrival, key):
        return pltpu.make_async_remote_copy(
            src_ref=source,
            dst_ref=target,
            send_sem=send_sem.at[slot, index],
            recv_sem=recv_sem.at[arrival, flat],
            device_id=near[key],
            device_id_type=MESH,
        )

    def share(cs):
        row, column = kind.corner(zs, xs, ys, cs, sub)
        column = jnp.clip(column - first_column, 0, grads.shape[1] - kind.width)
        return (pl.ds(row, rows), pl.ds(pl.multiple_of(column, 128), kind.width))

    total = from_core.at[slot]
    across = remote(grads.at[share(1 - c)], total, 2, kin, "core")
    other = valid & kind.holds(zs, xs, 1 - c)
    if what == "across":
        pl.when(other)(across.start)
        return
    if what == "drain":
        pl.when(other)(across.wait_send)
    valid = valid & kind.holds(zs, xs, c)
    part_a = from_core.at[slot, pl.ds(0, half_rows)]
    part_b = from_core.at[slot, pl.ds(half_rows, rows - half_rows)]
    if relation == "xy":
        sends = [
            (valid, remote(part_a, half_a.at[flat], 0, 4, "y")),
            (valid, remote(part_b, half_b.at[flat], 1, 5, "x")),
        ]
    elif relation == "x":
        sends = [(valid, remote(total, from_x.at[flat], 0, 6, "x"))]
    elif relation == "y":
        sends = [(valid, remote(total, from_y.at[flat], 0, 7, "y"))]
    else:
        sends = [
            (valid & (z < zs), remote(total, from_low.at[flat], 0, 8, "up")),
            (valid & (z > zs), remote(total, from_high.at[flat], 1, 9, "down")),
        ]
    if what == "drain":
        for condition, descriptor in sends:
            pl.when(condition)(descriptor.wait_send)
        return

    @pl.when(valid)
    def _():
        remote(total, total, 2, kin, "core").wait_recv()
        value = from_core[slot].astype(F32) + grads[share(c)].astype(F32)
        if relation == "xy":
            from_core[slot] = value.astype(BF16)
        elif relation == "x":
            remote(half_a.at[flat], half_a.at[flat], 0, 4, "y").wait_recv()
            from_core[slot, pl.ds(half_rows, rows - half_rows)] = value[half_rows:].astype(BF16)
            from_core[slot, pl.ds(0, half_rows)] = (
                value[:half_rows] + half_a[flat].astype(F32)
            ).astype(BF16)
        elif relation == "y":
            remote(half_b.at[flat], half_b.at[flat], 1, 5, "x").wait_recv()
            from_core[slot, pl.ds(0, half_rows)] = value[:half_rows].astype(BF16)
            from_core[slot, pl.ds(half_rows, rows - half_rows)] = (
                value[half_rows:] + half_b[flat].astype(F32)
            ).astype(BF16)
        else:
            remote(from_x.at[flat], from_x.at[flat], 0, 6, "x").wait_recv()
            remote(from_y.at[flat], from_y.at[flat], 0, 7, "y").wait_recv()
            value += from_x[flat].astype(F32) + from_y[flat].astype(F32)

            @pl.when((z <= zs) & (z > 0))
            def _():
                remote(from_low.at[flat], from_low.at[flat], 0, 8, "up").wait_recv()

            @pl.when((z >= zs) & (z < PLANES - 1))
            def _():
                remote(from_high.at[flat], from_high.at[flat], 1, 9, "down").wait_recv()

            def low():
                return jnp.where(z > 0, from_low[flat].astype(F32), 0.0)

            def high():
                return jnp.where(z < PLANES - 1, from_high[flat].astype(F32), 0.0)

            @pl.when(z < zs)
            def _():
                from_core[slot] = (value + low()).astype(BF16)

            @pl.when(z > zs)
            def _():
                from_core[slot] = (value + high()).astype(BF16)

            @pl.when(z == zs)
            def _():
                owned[
                    pl.ds(pl.multiple_of(sub * rows, rows), rows),
                    pl.ds(kind.source_column, kind.width),
                ] = value + low() + high()

    for condition, descriptor in sends:
        pl.when(condition)(descriptor.start)


LAGS = {"xy": 0, "x": 1, "y": 1, "own": 2}
Z_LAG = 1


def reduce_step(what, refs, plan, sems, at):
    z = place()[0]
    for kind, planes in plan:
        name = kind.__name__
        for plane_at, zs in enumerate(planes):
            for relation in ("xy", "x", "y", "own"):
                sub = at
                if what == "tick":
                    depth = 0
                    if relation == "own":
                        depth = by_plane(
                            z,
                            [
                                place_z
                                if place_z < zs
                                else max(place_z, 3 - place_z)
                                if place_z == zs
                                else 3 - place_z
                                for place_z in range(PLANES)
                            ],
                        )
                    sub = at - (LAGS[relation] + Z_LAG * depth)
                reduce_block(
                    what,
                    refs[name],
                    kind,
                    zs,
                    plane_at,
                    len(planes),
                    relation,
                    jnp.clip(sub, 0, kind.subs - 1),
                    sems[name],
                    (sub >= 0) & (sub < kind.subs),
                )


def landing(kind, planes):
    count = planes * kind.subs
    full = pltpu.VMEM((count, kind.height, kind.width), BF16)
    half_a = pltpu.VMEM((count, kind.split, kind.width), BF16)
    half_b = pltpu.VMEM((count, kind.height - kind.split, kind.width), BF16)
    sums = pltpu.VMEM((4 * count, kind.height, kind.width), BF16)
    return [sums] + [full] * 4 + [half_a, half_b]


def landing_signals(kind, planes):
    count = planes * kind.subs
    return [pltpu.SemaphoreType.DMA((4 * count, 3)), pltpu.SemaphoreType.DMA((10, count))]


def greet_near():
    z, x, c, y = place()
    near = neighbours()
    barrier = pltpu.get_barrier_semaphore()
    for key in ("x", "y", "core"):
        pl.semaphore_signal(barrier, inc=1, device_id=near[key], device_id_type=MESH)

    @pl.when(z < PLANES - 1)
    def _():
        pl.semaphore_signal(barrier, inc=1, device_id=near["up"], device_id_type=MESH)

    @pl.when(z > 0)
    def _():
        pl.semaphore_signal(barrier, inc=1, device_id=near["down"], device_id_type=MESH)

    middle = (z > 0) & (z < PLANES - 1)

    @pl.when(middle)
    def _():
        pl.semaphore_wait(barrier, 5)

    @pl.when(jnp.logical_not(middle))
    def _():
        pl.semaphore_wait(barrier, 4)


REDUCE_HIGH = ((HighGrad, (3,)),)
REDUCE_LOW = ((BroadGrad, (1, 2)), (NarrowGrad, (1,)))
HIGH_STEPS = GRAD_SUBS + 5
LOW_STEPS = GRAD_SUBS + 4
HIGH_FIRST = FF // 8


def attend_back(
    pair, queries, keys, values, mixed, grad_mixed, log_totals, grad_query, grad_key, grad_value
):
    columns = pl.ds(pl.multiple_of(pair * LANES, LANES), LANES)
    key_block = keys[:, columns]
    value_block = values[:, columns]
    key_flat = key_block.T
    key_sum, value_sum = None, None
    step = 256
    for part in range(TOKENS_HERE // step):
        rows = pl.ds(part * step, step)
        grad_block = grad_mixed[rows, columns]
        product = (grad_block.astype(F32) * mixed[rows, columns].astype(F32)).T
        query_parts = []
        heads = zip(two_heads(queries[rows, columns]), two_heads(grad_block))
        for head, (query_head, grad_head) in enumerate(heads):
            scores = multiply(key_block, query_head, BOTH_LAST)
            weights = jnp.exp(scores * HEAD_DIM**-0.5 - log_totals[2 * pair + head, :, rows])
            grad_weights = multiply(value_block, grad_head, BOTH_LAST)
            inner = jnp.sum(
                product[HEAD_DIM * head : HEAD_DIM * (head + 1)], axis=0, keepdims=True
            )
            grad_scores = (weights * (grad_weights - inner)).astype(BF16)
            value_term = multiply(weights.astype(BF16), grad_head)
            key_term = multiply(grad_scores, query_head)
            value_sum = value_term if value_sum is None else value_sum + value_term
            key_sum = key_term if key_sum is None else key_sum + key_term
            query_parts.append(multiply(key_flat, grad_scores))
        joined = jnp.concatenate([query_parts[0][:HEAD_DIM], query_parts[1][HEAD_DIM:]], axis=0)
        grad_query[rows, columns] = (joined * HEAD_DIM**-0.5).T.astype(BF16)
    grad_key[:, columns] = (key_sum * HEAD_DIM**-0.5).astype(BF16)
    grad_value[:, columns] = value_sum.astype(BF16)


def backward_kernel(
    queries_in,
    keys_in,
    values_in,
    mixed_in,
    grad_mixed_in,
    log_totals_in,
    grads_in,
    input_one_in,
    hidden_in,
    grad_middle_in,
    grad_attn_in,
    scale_one,
    early_sums,
    whole_in,
    owned,
    input_grad,
    input_low,
    sums,
    grad_low,
    queries,
    keys,
    values,
    mixed,
    grad_mixed,
    log_totals,
    grads,
    input_one,
    hidden,
    grad_middle,
    grad_attn,
    load_sem,
    grad_query,
    grad_key,
    grad_value,
    row_sums,
    key_all,
    value_all,
    key_mate,
    value_mate,
    flat_one,
    weight_stage,
    grad_stage,
    grad_one,
    mate_sem,
    weight_sem,
    grad_sem,
    *scratch,
):
    dp = lax.axis_index("dp")
    near = neighbours()
    refs = {"HighGrad": (grads, 4 * D, owned, scratch[:7])}
    sems = {"HighGrad": scratch[7:9]}
    tile = 512
    tiles = 3 * D // tile
    loads = [
        pltpu.make_async_copy(source, target, load_sem.at[index])
        for index, (source, target) in enumerate(
            (
                (grads_in, grads),
                (input_one_in, input_one),
                (queries_in, queries),
                (keys_in, keys),
                (values_in, values),
                (mixed_in, mixed),
                (grad_mixed_in, grad_mixed),
                (log_totals_in, log_totals),
                (hidden_in, hidden),
                (grad_middle_in, grad_middle),
                (grad_attn_in, grad_attn),
            )
        )
    ]
    for load in loads:
        load.start()

    def weight_copy(at, slot):
        return pltpu.make_async_copy(
            whole_in.at[:, pl.ds(pl.multiple_of(at * tile, LANES), tile)],
            weight_stage.at[slot],
            weight_sem.at[slot],
        )

    def grad_copy(at, slot):
        return pltpu.make_async_copy(
            grad_stage.at[slot],
            grad_low.at[:, pl.ds(pl.multiple_of(at * tile, LANES), tile)],
            grad_sem.at[slot],
        )

    weight_copy(0, 0).start()
    greet_near()
    loads[0].wait()
    repeat(GRAD_SUBS, lambda at: reduce_step("across", refs, REDUCE_HIGH, sems, at))

    @pl.when(dp < 12)
    def _():
        owned[...] = jnp.zeros_like(owned)

    for load in loads[1:]:
        load.wait()

    def flatten(source):
        def go(at):
            columns = pl.ds(pl.multiple_of(at * 256, LANES), 256)
            flat_one[pl.ds(pl.multiple_of(at * 256, 256), 256)] = source[:, columns].T

        repeat(D // 256, go)

    flatten(input_one)

    def mates(pair):
        columns = pl.ds(pl.multiple_of(pair * LANES, LANES), LANES)
        return [
            pltpu.make_async_remote_copy(
                src_ref=source.at[HALF:, columns],
                dst_ref=target.at[:, columns],
                send_sem=mate_sem.at[pair, 2 * index],
                recv_sem=mate_sem.at[pair, 2 * index + 1],
                device_id=near["core"],
                device_id_type=MESH,
            )
            for index, (source, target) in enumerate(((key_all, key_mate), (value_all, value_mate)))
        ]

    def attention(pair):
        attend_back(
            pair,
            queries,
            keys,
            values,
            mixed,
            grad_mixed,
            log_totals,
            grad_query,
            key_all,
            value_all,
        )
        for mate in mates(pair):
            mate.start()
        reduce_step("tick", refs, REDUCE_HIGH, sems, pair)

    repeat(PAIRS, attention)
    for source, target, total, index in (
        (key_all, key_mate, grad_key, 0),
        (value_all, value_mate, grad_value, 1),
    ):
        repeat(PAIRS, lambda pair: mates(pair)[index].wait())
        total[...] = (source[:HALF].astype(F32) + target[...].astype(F32)).astype(BF16)

    grad_one[...] = jnp.zeros_like(grad_one)

    def project_back(source, base):
        def go(at):
            slot = lax.rem(at, 2)
            weight_copy(at, slot).wait()

            @pl.when(at + 1 < tiles)
            def _():
                weight_copy(at + 1, 1 - slot).start()

            @pl.when(at >= 2)
            def _():
                grad_copy(at - 2, slot).wait()

            columns = pl.ds(pl.multiple_of((at - base) * tile, LANES), tile)
            for side in range(2):
                part = slice(side * 512, (side + 1) * 512)
                grad_one[:, part] += multiply(
                    source[:, columns], weight_stage[slot, part], BOTH_LAST
                )
                narrow = pl.ds(pl.multiple_of((at - base) * tile + side * 256, LANES), 256)
                grad_stage[slot, :, side * 256 : (side + 1) * 256] = multiply(
                    flat_one[...], source[:, narrow]
                ).astype(BF16)
            grad_copy(at, slot).start()

            @pl.when(at + PAIRS < HIGH_STEPS)
            def _():
                reduce_step("tick", refs, REDUCE_HIGH, sems, at + PAIRS)

        def run(at, carried):
            go(at + base)
            return carried

        lax.fori_loop(0, D // tile, run, 0)

    project_back(grad_query, 0)
    project_back(grad_key, D // tile)
    project_back(grad_value, 2 * D // tile)

    flatten(mixed)
    for at in range(tiles, tiles + D // tile):
        slot = at % 2
        grad_copy(at - 2, slot).wait()
        for side in range(2):
            narrow = pl.ds((at - tiles) * tile + side * 256, 256)
            grad_stage[slot, :, side * 256 : (side + 1) * 256] = multiply(
                flat_one[...], grad_attn[:, narrow]
            ).astype(BF16)
        grad_copy(at, slot).start()
    row_sums[...] = jnp.zeros_like(row_sums)

    def shape_back(at):
        rows = pl.ds(pl.multiple_of(at * 128, 128), 128)
        value = hidden[rows].astype(F32)
        center = value - jnp.mean(value, axis=-1, keepdims=True)
        inverse = lax.rsqrt(jnp.mean(center * center, axis=-1, keepdims=True) + norm_eps)
        normed = center * inverse
        towards = grad_one[rows]
        row_sums[0:1] += jnp.sum(towards, axis=0, keepdims=True)
        row_sums[1:2] += jnp.sum(towards * normed, axis=0, keepdims=True)
        row_sums[2:3] += jnp.sum(grad_query[rows].astype(F32), axis=0, keepdims=True)
        row_sums[3:4] += jnp.sum(grad_value[rows].astype(F32), axis=0, keepdims=True)
        scaled = towards * (1.0 + scale_one[...])
        result = grad_middle[rows] + inverse * (
            scaled
            - jnp.mean(scaled, axis=-1, keepdims=True)
            - normed * jnp.mean(scaled * normed, axis=-1, keepdims=True)
        )
        input_grad[rows] = result
        input_low[rows] = result.astype(BF16)

    repeat(4, shape_back)
    for index in range(2):
        sums[:, index * D : (index + 1) * D] = row_sums[index : index + 1]
        start = 6 * D + WIDE + index * D
        sums[:, start : start + D] = row_sums[index + 2 : index + 3]
    sums[:, 2 * D : 6 * D] = early_sums[:, : 4 * D]
    sums[:, 6 * D : 6 * D + WIDE] = jnp.zeros((1, WIDE), F32)
    sums[:, 8 * D + WIDE :] = early_sums[:, 4 * D :]
    for at in (tiles + D // tile - 2, tiles + D // tile - 1):
        grad_copy(at, at % 2).wait()
    repeat(GRAD_SUBS, lambda at: reduce_step("drain", refs, REDUCE_HIGH, sems, at))


def run_backward(*given):
    shape = jax.ShapeDtypeStruct
    rows = TOKENS_HERE
    vmem = pl.BlockSpec(memory_space=pltpu.VMEM)
    hbm = pl.BlockSpec(memory_space=pl.ANY)
    dma = pltpu.SemaphoreType.DMA
    return pl.pallas_call(
        backward_kernel,
        out_shape=[
            shape((HALF, WIDE), F32),
            shape((rows, D), F32),
            shape((rows, D), BF16),
            shape((1, VECTOR), F32),
            shape((D, 4 * D), BF16),
        ],
        in_specs=[hbm] * 11 + [vmem] * 2 + [hbm],
        out_specs=[vmem] * 4 + [hbm],
        scratch_shapes=[pltpu.VMEM(one.shape, one.dtype) for one in given[:11]]
        + [dma((11,))]
        + [pltpu.VMEM((rows, D), BF16)] * 3
        + [pltpu.VMEM((8, D), F32)]
        + [pltpu.VMEM((2 * rows, D), BF16)] * 2
        + [pltpu.VMEM((rows, D), BF16)] * 2
        + [
            pltpu.VMEM((D, rows), BF16),
            pltpu.VMEM((2, D, 512), BF16),
            pltpu.VMEM((2, D, 512), BF16),
            pltpu.VMEM((rows, D), F32),
            dma((PAIRS, 4)),
            dma((2,)),
            dma((2,)),
        ]
        + landing(HighGrad, 1)
        + landing_signals(HighGrad, 1),
        compiler_params=pltpu.CompilerParams(
            collective_id=1, has_side_effects=True, vmem_limit_bytes=62 * 2**20
        ),
        cost_estimate=pl.CostEstimate(
            flops=12 * 2 * 512 * 1024 * 1024, bytes_accessed=60 * 2**20, transcendentals=2**23
        ),
        name="backward",
    )(*given)


VECTOR = 17 * WIDE


def finish_kernel(
    grad_low,
    grad_up,
    low_in,
    active_rows,
    condition,
    sums,
    owned_high,
    down_sum,
    owned,
    cond_grad,
    bias_parts,
    ada_bias_grad,
    owned_down,
    grads,
    ada_weights,
    sum_mate,
    sum_pieces,
    ada_in,
    cond_piece,
    cond_in,
    down_mate,
    local_sem,
    mate_sem,
    down_sem,
    piece_send,
    ada_recv,
    bias_recv,
    cond_send,
    cond_recv,
    *scratch,
):
    z, x, c, y = place()
    dp = (z * 2 + x) * 2 + c
    near = neighbours()
    refs = {
        "BroadGrad": (grads, 0, owned, scratch[0:7]),
        "NarrowGrad": (grads, 0, owned, scratch[7:14]),
    }
    sems = {"BroadGrad": scratch[14:16], "NarrowGrad": scratch[16:18]}

    def remote(source, target, sent, arrived, device):
        return pltpu.make_async_remote_copy(
            src_ref=source,
            dst_ref=target,
            send_sem=sent,
            recv_sem=arrived,
            device_id=device,
            device_id_type=MESH,
        )

    loads = [
        pltpu.make_async_copy(grad_low, grads.at[:, : 4 * D], local_sem.at[0]),
        pltpu.make_async_copy(
            grad_up.at[:, :HIGH_FIRST], grads.at[:, 4 * D : 4 * D + HIGH_FIRST], local_sem.at[1]
        ),
        pltpu.make_async_copy(low_in.at[pl.ds(0, HALF)], ada_weights, local_sem.at[2]),
    ]
    for load in loads:
        load.start()
    owned[...] = owned_high[...]
    greet_all()
    mate = remote(sums, sum_mate, mate_sem.at[0], mate_sem.at[1], near["core"])
    mate.start()
    down_away = remote(
        down_sum.at[:, pl.ds(pl.multiple_of((1 - y) * FF_PART, LANES), FF_PART)],
        down_mate,
        down_sem.at[0],
        down_sem.at[1],
        near["y"],
    )
    down_away.start()

    for load in loads[:2]:
        load.wait()
    repeat(GRAD_SUBS, lambda at: reduce_step("across", refs, REDUCE_LOW, sems, at))
    repeat(2, lambda at: reduce_step("tick", refs, REDUCE_LOW, sems, at))

    mate.wait()
    for index in range(17):
        columns = slice(index * WIDE, (index + 1) * WIDE)
        piece = sums[:, columns] + sum_mate[:, columns]
        if index < 7:
            piece = piece.astype(BF16).astype(F32)
        sum_pieces[index] = piece
    latent = (z * 2 + x) * 2 + y

    def piece_target(at):
        return jnp.where(at < 7, at, at - 1)

    def piece_copy(at, target, arrived):
        return remote(
            sum_pieces.at[at], target, piece_send.at[at], arrived, (piece_target(at), c)
        )

    def each_piece(act, keep):
        def go(at):
            mine = (piece_target(at) == dp) & (y == c)

            @pl.when(jnp.logical_not(mine) & (at < 7))
            def _():
                act(piece_copy(at, ada_in.at[latent], ada_recv.at[latent]))

            @pl.when(jnp.logical_not(mine) & (at >= 7))
            def _():
                act(piece_copy(at, bias_parts.at[latent], bias_recv.at[latent]))

            if keep:

                @pl.when(mine & (at < 7))
                def _():
                    ada_in[latent] = sum_pieces[at]

                @pl.when(mine & (at >= 7))
                def _():
                    bias_parts[latent] = sum_pieces[at]

        repeat(17, go)

    each_piece(lambda copy: copy.start(), True)
    repeat(3, lambda at: reduce_step("tick", refs, REDUCE_LOW, sems, at + 2))

    def from_latent(at, target, arrived):
        mine = (at // 2 == z * 2 + x) & (lax.rem(at, 2) == y) & (c == y)

        @pl.when(jnp.logical_not(mine))
        def _():
            remote(
                sum_pieces.at[0], target.at[at], piece_send.at[0], arrived.at[at], near["x"]
            ).wait_recv()

    loads[2].wait()

    @pl.when(dp < 7)
    def _():
        repeat(DP, lambda at: from_latent(at, ada_in, ada_recv))
        gathered = jnp.concatenate([ada_in[index] for index in range(DP)], axis=0)
        ada_bias_grad[...] = jnp.sum(gathered, axis=0, keepdims=True)
        narrow = gathered.astype(BF16)
        owned[...] += multiply(active_rows[...], narrow, BOTH_FIRST)
        part = multiply(narrow, ada_weights[...], BOTH_LAST)
        for index in range(DP):
            cond_piece[index] = part[index : index + 1]

    @pl.when(dp >= 7)
    def _():
        ada_bias_grad[...] = jnp.zeros_like(ada_bias_grad)

    def cond_copy(at):
        return remote(
            cond_piece.at[at // 2],
            cond_in.at[dp * 2 + y],
            cond_send.at[at],
            cond_recv.at[dp * 2 + y],
            (at // 2, lax.rem(at, 2)),
        )

    def each_cond(act, keep):
        def go(at):
            mine = at == dp * 2 + y

            @pl.when(jnp.logical_not(mine))
            def _():
                act(cond_copy(at))

            if keep:

                @pl.when(mine)
                def _():
                    cond_in[dp * 2 + y] = cond_piece[at // 2]

        repeat(2 * DP, go)

    @pl.when(dp < 7)
    def _():
        each_cond(lambda copy: copy.start(), True)

    repeat(LOW_STEPS - 5, lambda at: reduce_step("tick", refs, REDUCE_LOW, sems, at + 5))

    def cond_arrived(at):
        @pl.when(at != dp * 2 + y)
        def _():
            remote(
                cond_piece.at[0], cond_in.at[at], cond_send.at[0], cond_recv.at[at], near["x"]
            ).wait_recv()

    repeat(14, cond_arrived)
    sides = []
    for side in range(2):
        total = cond_in[side]
        for index in range(1, 7):
            total = total + cond_in[2 * index + side]
        sides.append(total)
    value = condition[...]
    logistic = 1.0 / (1.0 + jnp.exp(-value))
    cond_grad[...] = jnp.concatenate(sides, axis=1) * (
        logistic * (1.0 + value * (1.0 - logistic))
    )

    @pl.when(dp >= 6)
    def _():
        repeat(DP, lambda at: from_latent(at, bias_parts, bias_recv))

    @pl.when(dp < 6)
    def _():
        bias_parts[...] = jnp.zeros_like(bias_parts)

    down_away.wait()
    owned_down[...] = down_sum[
        :, pl.ds(pl.multiple_of(y * FF_PART, LANES), FF_PART)
    ].astype(F32) + down_mate[...].astype(F32)
    each_piece(lambda copy: copy.wait_send(), False)

    @pl.when(dp < 7)
    def _():
        each_cond(lambda copy: copy.wait_send(), False)

    repeat(GRAD_SUBS, lambda at: reduce_step("drain", refs, REDUCE_LOW, sems, at))


def run_finish(
    grad_low,
    grad_up,
    low_in,
    active_rows,
    condition,
    sums,
    owned_high,
    down_sum,
):
    shape = jax.ShapeDtypeStruct
    dma = pltpu.SemaphoreType.DMA
    vmem = pl.BlockSpec(memory_space=pltpu.VMEM)
    hbm = pl.BlockSpec(memory_space=pl.ANY)
    return pl.pallas_call(
        finish_kernel,
        out_shape=[
            shape((HALF, WIDE), F32),
            shape((1, D), F32),
            shape((DP, 1, WIDE), F32),
            shape((1, WIDE), F32),
            shape((64, FF_PART), F32),
        ],
        in_specs=[hbm] * 3 + [vmem] * 5,
        out_specs=[vmem] * 5,
        scratch_shapes=[
            pltpu.VMEM((D, 4 * D + HIGH_FIRST), BF16),
            pltpu.VMEM((HALF, WIDE), BF16),
            pltpu.VMEM((1, VECTOR), F32),
            pltpu.VMEM((17, 1, WIDE), F32),
            pltpu.VMEM((DP, 1, WIDE), F32),
            pltpu.VMEM((DP, 1, HALF), F32),
            pltpu.VMEM((14, 1, HALF), F32),
            pltpu.VMEM((64, FF_PART), BF16),
            dma((3,)),
            dma((2,)),
            dma((2,)),
            dma((17,)),
            dma((DP,)),
            dma((DP,)),
            dma((2 * DP,)),
            dma((14,)),
        ]
        + landing(BroadGrad, 2)
        + landing(NarrowGrad, 1)
        + landing_signals(BroadGrad, 2)
        + landing_signals(NarrowGrad, 1),
        compiler_params=pltpu.CompilerParams(
            collective_id=2, has_side_effects=True, vmem_limit_bytes=60 * 2**20
        ),
        name="finish",
    )(
        grad_low,
        grad_up,
        low_in,
        active_rows,
        condition,
        sums,
        owned_high,
        down_sum,
    )


def swap_away(values):
    pairs = []
    for index in range(2 * DP):
        y, c = index % 2, index // 2 % 2
        if y != c:
            pairs.append((index, index // 4 * 4 + y * 2 + c))
    return lax.ppermute(values, ("dp", "seq"), pairs)


def local(
    hidden_in,
    condition,
    cotangent,
    weights_in,
    weights_down,
    biases,
    moment_in,
    moment_down,
    moment_bias,
    square_in,
    square_down,
    square_bias,
):
    dp = lax.axis_index("dp")
    y = lax.axis_index("seq")
    side = WIDE // 2
    bias_row = jnp.pad(biases.astype(BF16)[None], ((0, 15), (0, side)))
    bias_row = jnp.where(y == 0, bias_row, jnp.roll(bias_row, side, axis=1))
    low_in = jnp.concatenate([weights_in.astype(BF16), bias_row], axis=0)
    cond_float = condition.astype(F32)
    (
        whole_in,
        whole_down,
        hidden,
        grad_out,
        cond_all,
        modulation,
        input_one,
        queries,
        keys,
        values,
        mixed,
        log_totals,
        attn_out,
        middle,
        input_two,
        slope,
        grad_branch,
        row_grads,
        block_out,
        grad_down,
    ) = run_forward(
        low_in,
        weights_down.astype(BF16).T,
        hidden_in[0],
        cotangent[0],
        cond_float,
        bias_row[:1].astype(F32),
    )
    at_home = lax.rem(dp, 2) == y
    block_swapped = swap_away(block_out)
    grad_out = grad_out.astype(F32)
    pieces = [modulation[:, part * D : (part + 1) * D] for part in range(6)]
    shift_one, scale_one, gate_one, shift_two, scale_two, gate_two = pieces

    def back_through(gradients, start, width):
        return lax.dot_general(
            gradients,
            whole_in[:, start : start + width],
            BOTH_LAST,
            preferred_element_type=F32,
        )

    def outer(left, right):
        return lax.dot_general(left, right, BOTH_FIRST, preferred_element_type=F32)

    def down_rows(total):
        return jnp.sum(total.astype(F32), axis=0, keepdims=True)

    down_sum = lax.psum_scatter(grad_down, "dp", scatter_dimension=0, tiled=True)
    grad_act = jnp.dot(grad_branch, whole_down, preferred_element_type=F32)
    grad_upward = (grad_act * slope).astype(BF16)
    grad_up = outer(input_two, grad_upward).astype(BF16)
    grad_input_two = back_through(grad_upward, 4 * D, FF)
    normed_two, norm_pull_two = jax.vjp(layer_norm, middle)
    shift_two_grad = down_rows(grad_input_two)
    scale_two_grad = down_rows(grad_input_two * normed_two)
    grad_middle = grad_out + norm_pull_two(grad_input_two * (1.0 + scale_two))[0]
    grad_attn = (grad_middle * gate_one).astype(BF16)
    gate_one_grad = down_rows(grad_middle * attn_out)
    grad_mixed = back_through(grad_attn, 3 * D, D).astype(BF16)
    early_sums = jnp.concatenate(
        [
            gate_one_grad,
            shift_two_grad,
            scale_two_grad,
            row_grads[0:1],
            down_rows(grad_attn),
            down_rows(grad_upward),
            row_grads[1:2],
        ],
        axis=-1,
    )
    owned_high, input_grad, input_low, sums, grad_low = run_backward(
        queries,
        keys,
        values,
        mixed,
        grad_mixed,
        log_totals,
        grad_up,
        input_one,
        hidden,
        grad_middle,
        grad_attn,
        scale_one,
        early_sums,
        whole_in,
    )
    active_rows = lax.dynamic_slice_in_dim(
        jax.nn.silu(cond_all[:, 0]).astype(BF16), y * HALF, HALF, 1
    )
    owned_in, cond_grad, bias_parts, ada_bias_grad, owned_down = run_finish(
        grad_low,
        grad_up,
        low_in,
        active_rows,
        cond_float,
        sums,
        owned_high,
        down_sum,
    )
    owned_down = owned_down.T
    input_low, owned_in = lax.optimization_barrier((input_low, owned_in))
    input_swapped = swap_away(input_low)
    input_grad = jnp.where(at_home, input_grad, input_swapped.astype(F32))
    block_out = jnp.where(at_home, block_out, block_swapped)
    owned_bias = jnp.sum(bias_parts[:, 0], axis=0) + ada_bias_grad[0]
    owned_bias = lax.dynamic_slice_in_dim(owned_bias, y * side, side, 0)
    moments_in, squares_in, master_in = adamw_step(
        weights_in, moment_in, square_in, owned_in, rate_in
    )
    moments_down, squares_down, master_down = adamw_step(
        weights_down, moment_down, square_down, owned_down, rate_down
    )
    moments_bias, squares_bias, master_bias = adamw_step(
        biases, moment_bias, square_bias, owned_bias, rate_bias
    )
    return (
        block_out[None],
        input_grad[None],
        cond_grad,
        moments_in,
        moments_down,
        moments_bias,
        squares_in,
        squares_down,
        squares_bias,
        master_in,
        master_down,
        master_bias,
        master_in.astype(BF16),
        master_down.astype(BF16),
        master_bias.astype(BF16),
    )


def solution(mesh):
    return jax.shard_map(
        local if dict(mesh.shape) == {"dp": 16, "seq": 2} else local_general,
        mesh=mesh,
        in_specs=(
            P("dp", "seq", None),
            P("dp", None),
            P("dp", "seq", None),
            P("seq", "dp"),
            P("seq", "dp"),
            P(("dp", "seq")),
            P("seq", "dp"),
            P("seq", "dp"),
            P(("dp", "seq")),
            P("seq", "dp"),
            P("seq", "dp"),
            P(("dp", "seq")),
        ),
        out_specs=(
            P("dp", "seq", None),
            P("dp", "seq", None),
            P("dp", None),
            P("seq", "dp"),
            P("seq", "dp"),
            P(("dp", "seq")),
            P("seq", "dp"),
            P("seq", "dp"),
            P(("dp", "seq")),
            P("seq", "dp"),
            P("seq", "dp"),
            P(("dp", "seq")),
            P("seq", "dp"),
            P("seq", "dp"),
            P(("dp", "seq")),
        ),
        check_vma=False,
    )
```

```python
import math

import jax
import jax.numpy as jnp
from jax import lax
from jax.experimental import pallas as pl
from jax.experimental.pallas import tpu as pltpu
from jax.sharding import PartitionSpec as P

D = 1024
HEADS = 16
HEAD_DIM = 64
FF = 4096
STEP = 5


norm_eps = 1e-06
beta_first = 0.5
beta_second = 0.5
adam_eps = 1e-08
weight_decay = 0.01
rate_in = 0.03
rate_down = 0.016
rate_bias = 0.3


def layer_norm(values):
    center = values - jnp.mean(values, axis=-1, keepdims=True)
    return center * lax.rsqrt(jnp.mean(center * center, axis=-1, keepdims=True) + norm_eps)


def adamw_step(master, moment, square, gradient, step_rate):
    moment_new = beta_first * moment + (1.0 - beta_first) * gradient
    square_new = beta_second * square + (1.0 - beta_second) * gradient * gradient
    corrected = moment_new / (1.0 - beta_first**STEP)
    scale_sq = square_new / (1.0 - beta_second**STEP)
    master_new = master - step_rate * (
        corrected / (jnp.sqrt(scale_sq) + adam_eps) + weight_decay * master
    )
    return (moment_new, square_new, master_new)


def dense_map(values, matrix):
    return jnp.einsum("nld,de->nle", values, matrix, preferred_element_type=jnp.float32)


def dense_back(gradients, matrix):
    return jnp.einsum("nle,de->nld", gradients, matrix, preferred_element_type=jnp.float32)


def outer_sum(values, gradients):
    return jnp.einsum("nld,nle->de", values, gradients, preferred_element_type=jnp.float32)


def total_sum(values):
    return jnp.sum(values.astype(jnp.float32), axis=(0, 1))


def gather_weights(low_in, low_down, low_bias):
    seq_parts = (
        lax.all_gather(low_in, "seq", axis=0, tiled=True),
        lax.all_gather(low_down, "seq", axis=0, tiled=True),
        lax.all_gather(low_bias, "seq", axis=0, tiled=True),
    )
    whole_in, whole_down, bias_row = (
        lax.all_gather(seq_parts[0], "dp", axis=1, tiled=True),
        lax.all_gather(seq_parts[1], "dp", axis=1, tiled=True),
        lax.all_gather(seq_parts[2].reshape(1, -1), "dp", axis=1, tiled=True),
    )
    return (whole_in, whole_down, bias_row[0])


def head_layout():
    heads_here = math.gcd(HEADS, max(1, 128 // HEAD_DIM))
    return (heads_here, heads_here * HEAD_DIM, HEADS // heads_here)


def split_heads(values, lane_start, lane_count, heads_here):
    piece = lax.dynamic_slice_in_dim(values, lane_start, lane_count, 2)
    return piece.reshape(piece.shape[0], piece.shape[1], heads_here, HEAD_DIM)


def join_heads(stacked):
    moved = jnp.moveaxis(stacked, 0, 2)
    return moved.reshape(moved.shape[0], moved.shape[1], moved.shape[2] * moved.shape[3])


def attention_forward(queries, keys_all, values_all):
    heads_here, lane_count, head_steps = head_layout()
    scale_factor = HEAD_DIM ** (-0.5)

    def one_group(group_index):
        lane_start = group_index * lane_count
        query_part = split_heads(queries, lane_start, lane_count, heads_here)
        key_part = split_heads(keys_all, lane_start, lane_count, heads_here)
        value_part = split_heads(values_all, lane_start, lane_count, heads_here)
        scores = (
            jnp.einsum("nqhd,nkhd->nhqk", query_part, key_part, preferred_element_type=jnp.float32)
            * scale_factor
        )
        row_max = jnp.max(scores, axis=-1, keepdims=True)
        exponent = jnp.exp(scores - row_max)
        row_total = jnp.sum(exponent, axis=-1, keepdims=True)
        weights = (exponent / row_total).astype(jnp.bfloat16)
        attn_part = jnp.einsum(
            "nhqk,nkhd->nqhd", weights, value_part, preferred_element_type=jnp.float32
        )
        shaped = attn_part.reshape(attn_part.shape[0], attn_part.shape[1], lane_count)
        return (shaped, (row_max + jnp.log(row_total))[..., 0])

    stacked, log_totals = lax.map(one_group, jnp.arange(head_steps))
    return (join_heads(stacked), log_totals)


def attention_backward(queries, keys_all, values_all, log_totals, grad_mixed):
    heads_here, lane_count, head_steps = head_layout()
    scale_factor = HEAD_DIM ** (-0.5)

    def one_group(carried):
        group_index, log_part = carried
        lane_start = group_index * lane_count
        query_part = split_heads(queries, lane_start, lane_count, heads_here)
        key_part = split_heads(keys_all, lane_start, lane_count, heads_here)
        value_part = split_heads(values_all, lane_start, lane_count, heads_here)
        grad_part = split_heads(grad_mixed, lane_start, lane_count, heads_here)
        scores = (
            jnp.einsum("nqhd,nkhd->nhqk", query_part, key_part, preferred_element_type=jnp.float32)
            * scale_factor
        )
        probability = jnp.exp(scores - log_part[..., None])
        grad_prob = jnp.einsum(
            "nqhd,nkhd->nhqk", grad_part, value_part, preferred_element_type=jnp.float32
        )
        inner_sum = jnp.sum(probability * grad_prob, axis=-1, keepdims=True)
        grad_score = (probability * (grad_prob - inner_sum)).astype(jnp.bfloat16)
        grad_query = (
            jnp.einsum("nhqk,nkhd->nqhd", grad_score, key_part, preferred_element_type=jnp.float32)
            * scale_factor
        )
        grad_key = (
            jnp.einsum(
                "nhqk,nqhd->nkhd", grad_score, query_part, preferred_element_type=jnp.float32
            )
            * scale_factor
        )
        grad_value = jnp.einsum(
            "nhqk,nqhd->nkhd",
            probability.astype(jnp.bfloat16),
            grad_part,
            preferred_element_type=jnp.float32,
        )
        return (
            grad_query.reshape(grad_query.shape[0], grad_query.shape[1], lane_count),
            grad_key.reshape(grad_key.shape[0], grad_key.shape[1], lane_count),
            grad_value.reshape(grad_value.shape[0], grad_value.shape[1], lane_count),
        )

    query_terms, key_terms, value_terms = lax.map(one_group, (jnp.arange(head_steps), log_totals))
    return (join_heads(query_terms), join_heads(key_terms), join_heads(value_terms))


def local_general(
    hidden_in,
    condition,
    cotangent,
    weights_in,
    weights_down,
    biases,
    moment_in,
    moment_down,
    moment_bias,
    square_in,
    square_down,
    square_bias,
):
    low_in = weights_in.astype(jnp.bfloat16)
    low_down = weights_down.astype(jnp.bfloat16)
    low_bias = biases.astype(jnp.bfloat16)
    whole_in, whole_down, bias_all = gather_weights(low_in, low_down, low_bias)
    bias_float = bias_all.astype(jnp.float32)
    hidden = hidden_in.astype(jnp.float32)
    cond_float = condition.astype(jnp.float32)
    cond_act = jax.nn.silu(cond_float).astype(jnp.bfloat16)
    modulation = (
        jnp.dot(cond_act, whole_in[:, : 6 * D], preferred_element_type=jnp.float32)
        + bias_float[: 6 * D]
    )
    pieces = [modulation[:, None, part_index * D : (part_index + 1) * D] for part_index in range(6)]
    shift_one, scale_one, gate_one, shift_two, scale_two, gate_two = pieces
    normed_one = layer_norm(hidden)
    input_one = (normed_one * (1.0 + scale_one) + shift_one).astype(jnp.bfloat16)
    qkv_all = dense_map(input_one, whole_in[:, 6 * D : 9 * D])
    queries = (qkv_all[..., :D] + bias_float[6 * D : 7 * D]).astype(jnp.bfloat16)
    keys_local = qkv_all[..., D : 2 * D].astype(jnp.bfloat16)
    values_local = (qkv_all[..., 2 * D :] + bias_float[7 * D : 8 * D]).astype(jnp.bfloat16)
    keys_all, values_all = (
        lax.all_gather(keys_local, "seq", axis=1, tiled=True),
        lax.all_gather(values_local, "seq", axis=1, tiled=True),
    )
    attn_float, log_totals = attention_forward(queries, keys_all, values_all)
    attn_mixed = attn_float.astype(jnp.bfloat16)
    attn_out = dense_map(attn_mixed, whole_in[:, 9 * D : 10 * D]) + bias_float[8 * D : 9 * D]
    middle = hidden + gate_one * attn_out
    normed_two = layer_norm(middle)
    input_two = (normed_two * (1.0 + scale_two) + shift_two).astype(jnp.bfloat16)
    upward = dense_map(input_two, whole_in[:, 10 * D :]) + bias_float[9 * D : 9 * D + FF]
    activated = jax.nn.gelu(upward, approximate=True).astype(jnp.bfloat16)
    branch = dense_map(activated, whole_down) + bias_float[9 * D + FF :]
    block_out = (middle + gate_two * branch).astype(jnp.bfloat16)
    whole_in, whole_down, bias_all = gather_weights(low_in, low_down, low_bias)
    grad_out = cotangent.astype(jnp.float32)
    grad_branch = (grad_out * gate_two).astype(jnp.bfloat16)
    gate_two_grad = jnp.sum(grad_out * branch, axis=1)
    grad_down = outer_sum(activated, grad_branch)
    bias_down_grad = total_sum(grad_branch)
    grad_act = dense_back(grad_branch, whole_down)
    _, gelu_pull = jax.vjp(lambda inner_value: jax.nn.gelu(inner_value, approximate=True), upward)
    grad_upward = gelu_pull(grad_act)[0].astype(jnp.bfloat16)
    grad_up = outer_sum(input_two, grad_upward)
    bias_up_grad = total_sum(grad_upward)
    grad_input_two = dense_back(grad_upward, whole_in[:, 10 * D :])
    shift_two_grad = jnp.sum(grad_input_two, axis=1)
    scale_two_grad = jnp.sum(grad_input_two * normed_two, axis=1)
    _, norm_pull_two = jax.vjp(layer_norm, middle)
    grad_middle = grad_out + norm_pull_two(grad_input_two * (1.0 + scale_two))[0]
    grad_attn = (grad_middle * gate_one).astype(jnp.bfloat16)
    gate_one_grad = jnp.sum(grad_middle * attn_out, axis=1)
    grad_out_proj = outer_sum(attn_mixed, grad_attn)
    bias_out_grad = total_sum(grad_attn)
    grad_mixed = dense_back(grad_attn, whole_in[:, 9 * D : 10 * D]).astype(jnp.bfloat16)
    grad_query, key_terms, value_terms = attention_backward(
        queries, keys_all, values_all, log_totals, grad_mixed
    )
    key_grad, value_grad = (
        lax.psum_scatter(
            key_terms.astype(jnp.bfloat16), "seq", scatter_dimension=1, tiled=True
        ).astype(jnp.float32),
        lax.psum_scatter(
            value_terms.astype(jnp.bfloat16), "seq", scatter_dimension=1, tiled=True
        ).astype(jnp.float32),
    )
    grad_qkv = jnp.concatenate(
        [
            grad_query.astype(jnp.bfloat16),
            key_grad.astype(jnp.bfloat16),
            value_grad.astype(jnp.bfloat16),
        ],
        axis=-1,
    )
    grad_proj_qkv = outer_sum(input_one, grad_qkv)
    bias_query_grad = total_sum(grad_qkv[..., :D])
    bias_value_grad = total_sum(grad_qkv[..., 2 * D :])
    grad_input_one = dense_back(grad_qkv, whole_in[:, 6 * D : 9 * D])
    shift_one_grad = jnp.sum(grad_input_one, axis=1)
    scale_one_grad = jnp.sum(grad_input_one * normed_one, axis=1)
    _, norm_pull_one = jax.vjp(layer_norm, hidden)
    input_grad = grad_middle + norm_pull_one(grad_input_one * (1.0 + scale_one))[0]
    mod_terms = jnp.concatenate(
        [
            shift_one_grad,
            scale_one_grad,
            gate_one_grad,
            shift_two_grad,
            scale_two_grad,
            gate_two_grad,
        ],
        axis=-1,
    )
    mod_grad = lax.psum(mod_terms, "seq").astype(jnp.bfloat16)
    _, silu_pull = jax.vjp(jax.nn.silu, cond_float)
    cond_grad = silu_pull(
        jnp.einsum("ne,de->nd", mod_grad, whole_in[:, : 6 * D], preferred_element_type=jnp.float32)
    )[0]
    owner_mask = (lax.axis_index("seq") == 0).astype(jnp.float32)
    grad_ada = (
        jnp.einsum("nd,ne->de", cond_act, mod_grad, preferred_element_type=jnp.float32) * owner_mask
    )
    bias_ada_grad = jnp.sum(mod_grad.astype(jnp.float32), axis=0) * owner_mask
    grad_in_all = jnp.zeros((D, 10 * D + FF), jnp.float32)
    grad_in_all = grad_in_all.at[:, : 6 * D].set(grad_ada)
    grad_in_all = grad_in_all.at[:, 6 * D : 9 * D].set(grad_proj_qkv)
    grad_in_all = grad_in_all.at[:, 9 * D : 10 * D].set(grad_out_proj)
    grad_in_all = grad_in_all.at[:, 10 * D :].set(grad_up)
    bias_flat = jnp.concatenate(
        [
            bias_ada_grad,
            bias_query_grad,
            bias_value_grad,
            bias_out_grad,
            bias_up_grad,
            bias_down_grad,
        ]
    )
    summed_in, summed_down, summed_bias = (
        lax.psum_scatter(
            grad_in_all.astype(jnp.bfloat16), "dp", scatter_dimension=1, tiled=True
        ).astype(jnp.float32),
        lax.psum_scatter(
            grad_down.astype(jnp.bfloat16), "dp", scatter_dimension=1, tiled=True
        ).astype(jnp.float32),
        lax.psum_scatter(
            bias_flat.reshape(1, -1).astype(jnp.bfloat16), "dp", scatter_dimension=1, tiled=True
        ).astype(jnp.float32),
    )
    owned_in, owned_down, owned_bias = (
        lax.psum_scatter(
            summed_in.astype(jnp.bfloat16), "seq", scatter_dimension=0, tiled=True
        ).astype(jnp.float32),
        lax.psum_scatter(
            summed_down.astype(jnp.bfloat16), "seq", scatter_dimension=0, tiled=True
        ).astype(jnp.float32),
        lax.psum_scatter(
            summed_bias.reshape(-1).astype(jnp.bfloat16), "seq", scatter_dimension=0, tiled=True
        ).astype(jnp.float32),
    )
    moments_in, squares_in, master_in = adamw_step(
        weights_in, moment_in, square_in, owned_in, rate_in
    )
    moments_down, squares_down, master_down = adamw_step(
        weights_down, moment_down, square_down, owned_down, rate_down
    )
    moments_bias, squares_bias, master_bias = adamw_step(
        biases, moment_bias, square_bias, owned_bias, rate_bias
    )
    return (
        block_out,
        input_grad,
        cond_grad,
        moments_in,
        moments_down,
        moments_bias,
        squares_in,
        squares_down,
        squares_bias,
        master_in,
        master_down,
        master_bias,
        master_in.astype(jnp.bfloat16),
        master_down.astype(jnp.bfloat16),
        master_bias.astype(jnp.bfloat16),
    )


MESH = pl.DeviceIdType.MESH
WIDE = 896
LOW = 6 * D
KEPT = 4 * D + FF
PLANES = 4
HALF = D // 2
TALL = HALF + 16
SUBS = 3
SUB_ROWS = TALL // SUBS
FF_PART = FF // 2
DP = 16


def place():
    dp = lax.axis_index("dp")
    y = lax.axis_index("seq")
    return (dp // 4, lax.rem(dp // 2, 2), lax.rem(dp, 2), y)


def device_at(z, x, c, y):
    return ((z * 2 + x) * 2 + c, y)


def neighbours():
    z, x, c, y = place()
    return {
        "x": device_at(z, 1 - x, c, y),
        "y": device_at(z, x, c, 1 - y),
        "up": device_at(jnp.minimum(z + 1, PLANES - 1), x, c, y),
        "down": device_at(jnp.maximum(z - 1, 0), x, c, y),
        "core": device_at(z, x, 1 - c, y),
        "swap": device_at(z, x, 1 - c, 1 - y),
    }


def repeat(count, body):
    def step(at, carried):
        body(at)
        return carried

    lax.fori_loop(0, count, step, 0)


def greet_all():
    barrier = pltpu.get_barrier_semaphore()
    here = lax.axis_index("dp") * 2 + lax.axis_index("seq")

    def signal(at):
        there = lax.rem(here + at + 1, 2 * DP)
        pl.semaphore_signal(
            barrier, inc=1, device_id=(there // 2, lax.rem(there, 2)), device_id_type=MESH
        )

    repeat(2 * DP - 1, signal)
    pl.semaphore_wait(barrier, 2 * DP - 1)


class Broad:
    height, width, subs, split = SUB_ROWS, WIDE, SUBS, 64
    first, source_column = 0, 0

    @staticmethod
    def holds(zs, xs, cs):
        return (zs * 2 + xs) * 2 + cs >= 7

    @staticmethod
    def view(whole, zs, xs, ys, cs, sub, start=0, rows=SUB_ROWS):
        column = jnp.maximum(((zs * 2 + xs) * 2 + cs) * WIDE - LOW, 128)
        row = pl.multiple_of(sub * SUB_ROWS + start, 16)
        return whole.at[ys, pl.ds(row, rows), pl.ds(pl.multiple_of(column, 128), WIDE)]


class Narrow:
    height, width, subs, split = TALL, 128, 1, 272
    first, source_column = 16 * SUBS, WIDE - 128

    @staticmethod
    def holds(zs, xs, cs):
        return (zs * 2 + xs) * 2 + cs == 6

    @staticmethod
    def view(whole, zs, xs, ys, cs, sub, start=0, rows=TALL):
        return whole.at[ys, pl.ds(start, rows), pl.ds(0, 128)]


class Down:
    height, width, subs, split = 64, FF_PART, 1, 32
    first, source_column = 16 * SUBS + 16, 0

    @staticmethod
    def holds(zs, xs, cs):
        return zs >= 0

    @staticmethod
    def view(whole, zs, xs, ys, cs, sub, start=0, rows=64):
        row = pl.multiple_of(((zs * 2 + xs) * 2 + cs) * 64 + start, 32)
        return whole.at[pl.ds(row, rows), pl.ds(pl.multiple_of(ys * FF_PART, 128), FF_PART)]


SLOTS = 16 * SUBS + 32
RELATIONS = ("own", "x", "y", "xy")
HOPS = {"own": 0, "x": 1, "y": 1, "xy": 2}


def by_plane(z, table):
    picked = table[PLANES - 1]
    for plane in range(PLANES - 2, -1, -1):
        picked = jnp.where(z == plane, table[plane], picked)
    return picked


def forward_block(what, refs, kind, zs, relation, sub, sems, valid):
    whole, mine = refs
    send_sem, recv_sem, core_sem = sems
    z, x, c, y = place()
    near = neighbours()
    xs = 1 - x if "x" in relation else x
    ys = 1 - y if "y" in relation else y
    slot = kind.first + ((zs * 2 + xs) * 2 + ys) * kind.subs + sub
    full, half = recv_sem.at[slot, 0], recv_sem.at[slot, 1]
    parts = ((0, kind.height), (0, kind.split), (kind.split, kind.height - kind.split))

    def copy(part, index, arrival, key, source=None, cs=None):
        target = kind.view(whole, zs, xs, ys, c if cs is None else cs, sub, *parts[part])
        return pltpu.make_async_remote_copy(
            src_ref=target if source is None else source,
            dst_ref=target,
            send_sem=send_sem.at[slot, index],
            recv_sem=arrival,
            device_id=near[key],
            device_id_type=MESH,
        )

    if what == "core":

        @pl.when(valid & kind.holds(zs, xs, 1 - c))
        def _():
            copy(0, 4, core_sem.at[slot], "core", cs=1 - c).wait_recv()

        return
    valid = valid & kind.holds(zs, xs, c)
    if what == "tick":
        arrived = valid & (zs != z) if relation == "own" else valid

        @pl.when(arrived)
        def _():
            if relation == "xy":
                copy(1, 0, full, "x").wait_recv()
                copy(2, 0, half, "x").wait_recv()
            else:
                copy(0, 0, full, "x").wait_recv()

    def act(descriptor):
        if what == "drain":
            descriptor.wait_send()
        else:
            descriptor.start()

    def spread(source, upward, downward):
        @pl.when(upward)
        def _():
            act(copy(0, 0, full, "up", source))

        @pl.when(downward)
        def _():
            act(copy(0, 1, full, "down", source))

        act(copy(0, 2, full, "x", source))
        act(copy(0, 3, full, "y", source))
        act(copy(0, 4, core_sem.at[slot], "core", source))

    if relation == "own":

        if what != "tick":

            @pl.when(valid & (zs == z))
            def _():
                source = mine.at[
                    pl.ds(pl.multiple_of(sub * kind.height, 16), kind.height),
                    pl.ds(kind.source_column, kind.width),
                ]
                spread(source, z < PLANES - 1, z > 0)

        if what != "launch":

            @pl.when(valid & (zs != z))
            def _():
                spread(None, (zs < z) & (z < PLANES - 1), (zs > z) & (z > 0))

        return

    @pl.when(valid)
    def _():
        if relation == "x":
            act(copy(1, 3, full, "y"))
        if relation == "y":
            act(copy(2, 2, half, "x"))
        act(copy(0, 4, core_sem.at[slot], "core"))


def forward_step(what, refs, plan, relations, sems, sub):
    z = place()[0]
    for kind, order in plan:
        for position in range(len(order[0])):
            zs = by_plane(z, [row[position] for row in order])
            for relation in relations:
                forward_block(
                    what,
                    refs[kind.__name__],
                    kind,
                    zs,
                    relation,
                    jnp.minimum(sub, kind.subs - 1),
                    sems,
                    sub < kind.subs,
                )


def launch(refs, kinds, sems):
    z = place()[0]

    def go(sub):
        for kind in kinds:
            forward_block(
                "launch",
                refs[kind.__name__],
                kind,
                z,
                "own",
                jnp.minimum(sub, kind.subs - 1),
                sems,
                sub < kind.subs,
            )

    repeat(max(kind.subs for kind in kinds), go)


NEAR_LOW = ((1, 2), (1, 2), (2, 1), (2, 1))
ONLY_ONE = ((1,),) * PLANES
ONLY_LAST = ((3,),) * PLANES
NEAR = ((0, 1, 2, 3), (1, 0, 2, 3), (2, 3, 1, 0), (3, 2, 1, 0))
PLAN_LOW = ((Broad, NEAR_LOW), (Narrow, ONLY_ONE))
PLAN_UP = ((Broad, ONLY_LAST),)
PLAN_DOWN = ((Down, NEAR),)
PLAN_ALL = PLAN_LOW + PLAN_UP + PLAN_DOWN


BF16 = jnp.bfloat16
F32 = jnp.float32
PLAIN = (((1,), (0,)), ((), ()))
BOTH_LAST = (((1,), (1,)), ((), ()))
BOTH_FIRST = (((0,), (0,)), ((), ()))
LANES = 128
PAIRS = HEADS // 2
TOKENS_HERE = 512


def multiply(left, right, dims=PLAIN):
    return lax.dot_general(left, right, dims, preferred_element_type=F32)


def two_heads(block):
    lanes = lax.broadcasted_iota(jnp.int32, block.shape, 1)
    zero = jnp.zeros_like(block)
    return (jnp.where(lanes < HEAD_DIM, block, zero), jnp.where(lanes < HEAD_DIM, zero, block))


def attend_pair(pair, queries, keys, values, mixed, log_totals):
    columns = pl.ds(pl.multiple_of(pair * LANES, LANES), LANES)
    key_block = keys[:, columns]
    value_flat = values[:, columns].T
    parts = []
    for head, query_block in enumerate(two_heads(queries[:, columns])):
        scores = multiply(key_block, query_block, BOTH_LAST)
        largest = jnp.max(scores, axis=0, keepdims=True)
        weights = jnp.exp((scores - largest) * HEAD_DIM**-0.5)
        total = jnp.sum(weights, axis=0, keepdims=True)
        parts.append(multiply(value_flat, weights.astype(BF16)) * (1.0 / total))
        log_totals[2 * pair + head] = largest * HEAD_DIM**-0.5 + jnp.log(total)
    joined = jnp.concatenate([parts[0][:HEAD_DIM], parts[1][HEAD_DIM:]], axis=0)
    mixed[:, columns] = joined.T.astype(BF16)


def normalize(values):
    center = values - jnp.mean(values, axis=-1, keepdims=True)
    return center * lax.rsqrt(jnp.mean(center * center, axis=-1, keepdims=True) + norm_eps)


def from_weights(left, whole, start, width):
    columns = pl.ds(pl.multiple_of(start, LANES), width)
    return multiply(left[:, :HALF], whole[0, :HALF, columns]) + multiply(
        left[:, HALF:], whole[1, :HALF, columns]
    )


def bias_of(whole, start, width):
    columns = pl.ds(pl.multiple_of(start, LANES), width)
    both = whole[0, HALF:TALL, columns].astype(F32) + whole[1, HALF:TALL, columns].astype(F32)
    return both[:1]


def forward_kernel(
    low_in,
    low_down,
    hidden_in,
    cotangent,
    condition,
    ada_bias,
    whole_in,
    whole_down,
    hidden_out,
    grad_out_out,
    cond_all,
    modulation,
    input_one_out,
    queries_out,
    keys_out,
    values_out,
    mixed_out,
    log_totals,
    attn_out_out,
    middle_out,
    input_two_out,
    slope,
    grad_branch_out,
    row_grads,
    block_out,
    grad_down,
    own_in,
    own_down,
    ada_weights,
    ada_part,
    mod_parts,
    up_stage,
    wide,
    active,
    flat_branch,
    down_stage,
    send_sem,
    recv_sem,
    core_sem,
    local_sem,
    cond_send,
    cond_recv,
    mod_send,
    mod_recv,
    swap_sem,
    pair_sem,
    up_sem,
    down_sem,
    hidden,
    grad_out,
    input_one,
    queries,
    keys,
    values,
    mixed,
    attn_out,
    middle,
    input_two,
    grad_branch,
    keep_sem,
):
    z, x, c, y = place()
    dp = (z * 2 + x) * 2 + c
    near = neighbours()
    sems = (send_sem, recv_sem, core_sem)
    refs = {"Broad": (own_in, low_in), "Narrow": (own_in, low_in), "Down": (own_down, low_down)}
    at_home = c == y

    def remote(source, target, sent, arrived, device):
        return pltpu.make_async_remote_copy(
            src_ref=source,
            dst_ref=target,
            send_sem=sent,
            recv_sem=arrived,
            device_id=device,
            device_id_type=MESH,
        )

    kept = {
        name: pltpu.make_async_copy(source, target, keep_sem.at[index])
        for index, (name, source, target) in enumerate(
            (
                ("hidden", hidden, hidden_out),
                ("grad_out", grad_out, grad_out_out),
                ("input_one", input_one, input_one_out),
                ("queries", queries, queries_out),
                ("keys", keys, keys_out),
                ("values", values, values_out),
                ("mixed", mixed, mixed_out),
                ("attn_out", attn_out, attn_out_out),
                ("middle", middle, middle_out),
                ("input_two", input_two, input_two_out),
                ("grad_branch", grad_branch, grad_branch_out),
            )
        )
    }

    def keep(*which):
        for name in which:
            kept[name].start()

    broad = pltpu.make_async_copy(
        low_in,
        own_in.at[y, :, pl.ds(pl.multiple_of(jnp.maximum(dp, 7) * WIDE - LOW, LANES), WIDE)],
        local_sem.at[0],
    )
    narrow = pltpu.make_async_copy(
        low_in.at[:, pl.ds(WIDE - 128, 128)], own_in.at[y, :, pl.ds(0, 128)], local_sem.at[0]
    )
    down = pltpu.make_async_copy(
        low_down,
        own_down.at[
            pl.ds(pl.multiple_of(dp * 64, 64), 64),
            pl.ds(pl.multiple_of(y * FF_PART, LANES), FF_PART),
        ],
        local_sem.at[1],
    )
    ada = pltpu.make_async_copy(low_in.at[pl.ds(0, HALF)], ada_weights, local_sem.at[2])
    ada.start()
    down.start()

    @pl.when(dp >= 7)
    def _():
        broad.start()

    @pl.when(dp == 6)
    def _():
        narrow.start()

    greet_all()

    cond_all[dp] = condition[...]

    def cond_copy(at):
        there = lax.rem(dp + at + 1, DP)
        return remote(
            condition, cond_all.at[dp], cond_send.at[at], cond_recv.at[dp], (there, y)
        )

    repeat(DP - 1, lambda at: cond_copy(at).start())

    swaps = []
    for index, (source, target) in enumerate(((hidden_in, hidden), (cotangent, grad_out))):
        swaps.append(
            (
                pltpu.make_async_copy(source, target, swap_sem.at[index, 0]),
                remote(
                    source, target, swap_sem.at[index, 1], swap_sem.at[index, 2], near["swap"]
                ),
            )
        )

    def trade(index):
        @pl.when(at_home)
        def _():
            swaps[index][0].start()

        @pl.when(jnp.logical_not(at_home))
        def _():
            swaps[index][1].start()

    def traded(index):
        @pl.when(at_home)
        def _():
            swaps[index][0].wait()

        @pl.when(jnp.logical_not(at_home))
        def _():
            swaps[index][1].wait()

    trade(0)
    launch(refs, (Broad, Narrow), sems)

    @pl.when((z == 0) | (z == PLANES - 1))
    def _():
        launch(refs, (Down,), sems)

    def pass_on(plan, relations):
        subs = max(kind.subs for kind, _ in plan)
        repeat(subs, lambda sub: forward_step("tick", refs, plan, relations, sems, sub))

    pass_on(PLAN_LOW, ("own",))

    def cond_arrived(at):
        there = lax.rem(dp + at + 1, DP)
        remote(
            condition, cond_all.at[there], cond_send.at[at], cond_recv.at[there], (there, y)
        ).wait_recv()

    repeat(DP - 1, cond_arrived)
    raw = jnp.concatenate([cond_all[index] for index in range(DP)], axis=0)
    active[...] = (raw / (1.0 + jnp.exp(-raw))).astype(BF16)
    ada.wait()
    partial = (
        multiply(
            active[:, pl.ds(pl.multiple_of(y * HALF, LANES), HALF)],
            ada_weights[...],
        )
        + ada_bias[...]
    )
    for index in range(DP):
        ada_part[index] = partial[index : index + 1]

    def mod_target(at):
        latent, core = at // 2, lax.rem(at, 2)
        return (latent // 2 * 2 + core, lax.rem(latent, 2))

    def mod_copy(at):
        return remote(
            ada_part.at[at // 2],
            mod_parts.at[dp * 2 + y],
            mod_send.at[at],
            mod_recv.at[dp * 2 + y],
            mod_target(at),
        )

    def elsewhere(at):
        there = mod_target(at)
        return (there[0] != dp) | (there[1] != y)

    @pl.when(dp < 7)
    def _():
        def send(at):
            @pl.when(elsewhere(at))
            def _():
                mod_copy(at).start()

            @pl.when(jnp.logical_not(elsewhere(at)))
            def _():
                mod_parts[dp * 2 + y] = ada_part[at // 2]

        repeat(2 * DP, send)

    pass_on(PLAN_LOW, ("x", "y"))

    @pl.when((z > 0) & (z < PLANES - 1))
    def _():
        launch(refs, (Down,), sems)

    pass_on(PLAN_UP, ("own",))
    trade(1)
    traded(0)

    def mod_arrived(at):
        @pl.when(at != dp * 2 + y)
        def _():
            remote(
                ada_part.at[0], mod_parts.at[at], mod_send.at[0], mod_recv.at[at], near["x"]
            ).wait_recv()

    repeat(14, mod_arrived)
    for index in range(7):
        modulation[:, index * WIDE : (index + 1) * WIDE] = (
            mod_parts[2 * index] + mod_parts[2 * index + 1]
        )

    def vector(index):
        return modulation[:, index * D : (index + 1) * D]

    def shape_one(at):
        rows = pl.ds(pl.multiple_of(at * 128, 128), 128)
        normed = normalize(hidden[rows].astype(F32))
        input_one[rows] = (normed * (1.0 + vector(1)) + vector(0)).astype(BF16)

    repeat(4, shape_one)
    keep("hidden", "input_one")

    pass_on(PLAN_LOW, ("xy",))
    repeat(SUBS, lambda at: forward_step("core", refs, PLAN_LOW, RELATIONS, sems, at))

    @pl.when(dp >= 7)
    def _():
        broad.wait()

    @pl.when(dp == 6)
    def _():
        narrow.wait()

    def project(at):
        columns = pl.ds(pl.multiple_of(at * 256, LANES), 256)
        keys[:HALF, columns] = from_weights(input_one, own_in, D + at * 256, 256).astype(BF16)
        values[:HALF, columns] = (
            from_weights(input_one, own_in, 2 * D + at * 256, 256)
            + bias_of(own_in, D + at * 256, 256)
        ).astype(BF16)

    repeat(D // 256, project)
    mates = [
        remote(
            one.at[:HALF], one.at[HALF:], pair_sem.at[index, 0], pair_sem.at[index, 1], near["core"]
        )
        for index, one in enumerate((keys, values))
    ]
    for mate in mates:
        mate.start()

    def project_queries(at):
        columns = pl.ds(pl.multiple_of(at * 256, LANES), 256)
        queries[:, columns] = (
            from_weights(input_one, own_in, at * 256, 256) + bias_of(own_in, at * 256, 256)
        ).astype(BF16)

    repeat(D // 256, project_queries)
    for mate in mates:
        mate.wait()
    keep("queries", "keys", "values")

    def attention(pair):
        attend_pair(pair, queries, keys, values, mixed, log_totals)

        @pl.when(pair < SUBS)
        def _():
            forward_step("tick", refs, PLAN_UP, ("x", "y"), sems, pair)

        @pl.when(pair == SUBS)
        def _():
            forward_step("tick", refs, PLAN_DOWN, ("own",), sems, 0)

        @pl.when((pair > SUBS) & (pair <= 2 * SUBS))
        def _():
            forward_step("tick", refs, PLAN_UP, ("xy",), sems, pair - SUBS - 1)

    repeat(PAIRS, attention)
    keep("mixed")

    def project_out(at):
        columns = pl.ds(pl.multiple_of(at * 256, LANES), 256)
        attn_out[:, columns] = from_weights(mixed, own_in, 3 * D + at * 256, 256) + bias_of(
            own_in, 2 * D + at * 256, 256
        )

    repeat(D // 256, project_out)

    def shape_two(at):
        rows = pl.ds(pl.multiple_of(at * 128, 128), 128)
        mid = hidden[rows].astype(F32) + vector(2) * attn_out[rows]
        middle[rows] = mid
        input_two[rows] = (normalize(mid) * (1.0 + vector(4)) + vector(3)).astype(BF16)

    repeat(4, shape_two)
    keep("attn_out", "middle", "input_two")
    repeat(SUBS, lambda at: forward_step("core", refs, PLAN_UP, RELATIONS, sems, at))
    whole_copies = [
        pltpu.make_async_copy(
            own_in.at[half, pl.ds(0, HALF)],
            whole_in.at[pl.ds(half * HALF, HALF)],
            local_sem.at[3 + half],
        )
        for half in range(2)
    ]
    for whole_copy in whole_copies:
        whole_copy.start()
    tile = 512

    def up_copy(at, slot):
        return pltpu.make_async_copy(
            up_stage.at[slot],
            slope.at[:, pl.ds(pl.multiple_of(at * tile, LANES), tile)],
            up_sem.at[slot],
        )

    def down_grad_copy(at, slot):
        return pltpu.make_async_copy(
            down_stage.at[slot],
            grad_down.at[:, pl.ds(pl.multiple_of(at * tile, LANES), tile)],
            down_sem.at[slot],
        )

    traded(1)

    def shape_branch(at):
        columns = pl.ds(pl.multiple_of(at * 256, LANES), 256)
        gate = modulation[:, pl.ds(pl.multiple_of(5 * D + at * 256, LANES), 256)]
        scaled = (grad_out[:, columns].astype(F32) * gate).astype(BF16)
        grad_branch[:, columns] = scaled
        flat_branch[pl.ds(pl.multiple_of(at * 256, 256), 256)] = scaled.T
        row_grads[1:2, columns] = jnp.sum(scaled.astype(F32), axis=0, keepdims=True)

    repeat(D // 256, shape_branch)
    keep("grad_out", "grad_branch")

    def widen(at):
        slot = lax.rem(at, 2)

        @pl.when(at >= 2)
        def _():
            up_copy(at - 2, slot).wait()
            down_grad_copy(at - 2, slot).wait()

        factor = math.sqrt(2.0 / math.pi)
        for side in range(2):
            start = at * tile + side * 256
            value = from_weights(input_two, own_in, 4 * D + start, 256) + bias_of(
                own_in, 3 * D + start, 256
            )
            square = value * value
            bent = jnp.tanh(factor * value * (1.0 + 0.044715 * square))
            half_up = 0.5 + 0.5 * bent
            up_stage[slot, :, side * 256 : (side + 1) * 256] = half_up + 0.5 * value * (
                1.0 - bent * bent
            ) * (factor + 3.0 * 0.044715 * factor * square)
            wide[:, pl.ds(pl.multiple_of(start, LANES), 256)] = (value * half_up).astype(BF16)
        up_copy(at, slot).start()
        for side in range(2):
            columns = pl.ds(pl.multiple_of(at * tile + side * 256, LANES), 256)
            down_stage[slot, :, side * 256 : (side + 1) * 256] = multiply(
                flat_branch[...], wide[:, columns]
            ).astype(BF16)
        down_grad_copy(at, slot).start()

        @pl.when(at == 1)
        def _():
            forward_step("tick", refs, PLAN_DOWN, ("x", "y"), sems, 0)

        @pl.when(at == FF // tile - 1)
        def _():
            forward_step("tick", refs, PLAN_DOWN, ("xy",), sems, 0)

    repeat(FF // tile, widen)
    for at in (FF // tile - 2, FF // tile - 1):
        up_copy(at, at % 2).wait()
        down_grad_copy(at, at % 2).wait()
    down.wait()

    def narrow_down(at):
        columns = pl.ds(pl.multiple_of(at * 256, LANES), 256)
        value = bias_of(own_in, 7 * D + at * 256, 256)
        for side in range(2):
            value += multiply(
                wide[:, side * FF_PART : (side + 1) * FF_PART],
                own_down[columns, side * FF_PART : (side + 1) * FF_PART],
                BOTH_LAST,
            )
        gate = modulation[:, pl.ds(pl.multiple_of(5 * D + at * 256, LANES), 256)]
        block_out[:, columns] = (middle[:, columns] + gate * value).astype(BF16)
        towards = grad_out[:, columns].astype(F32)
        row_grads[0:1, columns] = jnp.sum(towards * value, axis=0, keepdims=True)

    forward_step("core", refs, PLAN_DOWN, RELATIONS, sems, 0)
    down_copy = pltpu.make_async_copy(own_down, whole_down, local_sem.at[5])
    down_copy.start()
    repeat(PLANES, narrow_down)

    repeat(SUBS, lambda at: forward_step("drain", refs, PLAN_ALL, RELATIONS, sems, at))
    repeat(DP - 1, lambda at: cond_copy(at).wait_send())

    @pl.when(dp < 7)
    def _():
        def sent(at):
            @pl.when(elsewhere(at))
            def _():
                mod_copy(at).wait_send()

        repeat(2 * DP, sent)

    for whole_copy in whole_copies:
        whole_copy.wait()
    down_copy.wait()
    for one in kept.values():
        one.wait()


def run_forward(low_in, low_down, hidden_in, cotangent, condition, ada_bias):
    shape = jax.ShapeDtypeStruct
    rows = TOKENS_HERE
    wide, flat = shape((rows, D), BF16), shape((rows, D), F32)
    both = shape((2 * rows, D), BF16)
    outs = [
        (shape((D, KEPT), BF16), pl.ANY),
        (shape((D, FF), BF16), pl.ANY),
        (wide, pl.ANY),
        (wide, pl.ANY),
        (shape((DP, 1, D), F32), pltpu.VMEM),
        (shape((1, 7 * WIDE), F32), pltpu.VMEM),
        (wide, pl.ANY),
        (wide, pl.ANY),
        (both, pl.ANY),
        (both, pl.ANY),
        (wide, pl.ANY),
        (shape((HEADS, 1, rows), F32), pltpu.VMEM),
        (flat, pl.ANY),
        (flat, pl.ANY),
        (wide, pl.ANY),
        (shape((rows, FF), F32), pl.ANY),
        (wide, pl.ANY),
        (shape((8, D), F32), pltpu.VMEM),
        (wide, pltpu.VMEM),
        (shape((D, FF), BF16), pl.ANY),
    ]
    kept = (wide, wide, wide, wide, both, both, wide, flat, flat, wide, wide)
    dma = pltpu.SemaphoreType.DMA
    return pl.pallas_call(
        forward_kernel,
        out_shape=[one for one, _ in outs],
        in_specs=[pl.BlockSpec(memory_space=pl.ANY)] * 4
        + [pl.BlockSpec(memory_space=pltpu.VMEM)] * 2,
        out_specs=[pl.BlockSpec(memory_space=where) for _, where in outs],
        scratch_shapes=[
            pltpu.VMEM((2, TALL, KEPT), BF16),
            pltpu.VMEM((D, FF), BF16),
            pltpu.VMEM((HALF, WIDE), BF16),
            pltpu.VMEM((DP, 1, WIDE), F32),
            pltpu.VMEM((14, 1, WIDE), F32),
            pltpu.VMEM((2, rows, 512), F32),
            pltpu.VMEM((rows, FF), BF16),
            pltpu.VMEM((DP, D), BF16),
            pltpu.VMEM((D, rows), BF16),
            pltpu.VMEM((2, D, 512), BF16),
            dma((SLOTS, 5)),
            dma((SLOTS, 2)),
            dma((SLOTS,)),
            dma((6,)),
            dma((DP,)),
            dma((DP,)),
            dma((2 * DP,)),
            dma((14,)),
            dma((2, 3)),
            dma((2, 2)),
            dma((2,)),
            dma((2,)),
        ]
        + [pltpu.VMEM(one.shape, one.dtype) for one in kept]
        + [dma((len(kept),))],
        compiler_params=pltpu.CompilerParams(
            collective_id=0, has_side_effects=True, vmem_limit_bytes=62 * 2**20
        ),
        name="forward",
    )(low_in, low_down, hidden_in, cotangent, condition, ada_bias)


GRAD_SUBS = 8
GRAD_ROWS = HALF // GRAD_SUBS


class BroadGrad:
    height, width, subs, source_column = GRAD_ROWS, WIDE, GRAD_SUBS, 0
    split = GRAD_ROWS // 2
    lag = 1

    @staticmethod
    def holds(zs, xs, cs):
        return (zs * 2 + xs) * 2 + cs >= 7

    @staticmethod
    def corner(zs, xs, ys, cs, sub):
        column = jnp.maximum(((zs * 2 + xs) * 2 + cs) * WIDE - LOW, 128)
        return (
            pl.multiple_of(ys * HALF + sub * GRAD_ROWS, GRAD_ROWS),
            pl.multiple_of(column, 128),
        )


class HighGrad(BroadGrad):
    split = 48
    lag = 2


class NarrowGrad:
    height, width, subs, source_column = HALF, 128, 1, WIDE - 128
    split = HALF // 2
    lag = 1

    @staticmethod
    def holds(zs, xs, cs):
        return (zs * 2 + xs) * 2 + cs == 6

    @staticmethod
    def corner(zs, xs, ys, cs, sub):
        return (pl.multiple_of(ys * HALF, HALF), 0)


def reduce_block(what, refs, kind, zs, plane_at, planes, relation, sub, sems, valid):
    grads, first_column, owned, buffers = refs
    from_core, from_x, from_y, from_low, from_high, half_a, half_b = buffers
    send_sem, recv_sem = sems
    z, x, c, y = place()
    near = neighbours()
    xs = 1 - x if "x" in relation else x
    ys = 1 - y if "y" in relation else y
    flat = plane_at * kind.subs + sub
    count = planes * kind.subs
    kin = RELATIONS.index(relation)
    slot = kin * count + flat
    rows, half_rows = kind.height, kind.split

    def remote(source, target, index, arrival, key):
        return pltpu.make_async_remote_copy(
            src_ref=source,
            dst_ref=target,
            send_sem=send_sem.at[slot, index],
            recv_sem=recv_sem.at[arrival, flat],
            device_id=near[key],
            device_id_type=MESH,
        )

    def share(cs):
        row, column = kind.corner(zs, xs, ys, cs, sub)
        column = jnp.clip(column - first_column, 0, grads.shape[1] - kind.width)
        return (pl.ds(row, rows), pl.ds(pl.multiple_of(column, 128), kind.width))

    total = from_core.at[slot]
    across = remote(grads.at[share(1 - c)], total, 2, kin, "core")
    other = valid & kind.holds(zs, xs, 1 - c)
    if what == "across":
        pl.when(other)(across.start)
        return
    if what == "drain":
        pl.when(other)(across.wait_send)
    valid = valid & kind.holds(zs, xs, c)
    part_a = from_core.at[slot, pl.ds(0, half_rows)]
    part_b = from_core.at[slot, pl.ds(half_rows, rows - half_rows)]
    if relation == "xy":
        sends = [
            (valid, remote(part_a, half_a.at[flat], 0, 4, "y")),
            (valid, remote(part_b, half_b.at[flat], 1, 5, "x")),
        ]
    elif relation == "x":
        sends = [(valid, remote(total, from_x.at[flat], 0, 6, "x"))]
    elif relation == "y":
        sends = [(valid, remote(total, from_y.at[flat], 0, 7, "y"))]
    else:
        sends = [
            (valid & (z < zs), remote(total, from_low.at[flat], 0, 8, "up")),
            (valid & (z > zs), remote(total, from_high.at[flat], 1, 9, "down")),
        ]
    if what == "drain":
        for condition, descriptor in sends:
            pl.when(condition)(descriptor.wait_send)
        return

    @pl.when(valid)
    def _():
        remote(total, total, 2, kin, "core").wait_recv()
        value = from_core[slot].astype(F32) + grads[share(c)].astype(F32)
        if relation == "xy":
            from_core[slot] = value.astype(BF16)
        elif relation == "x":
            remote(half_a.at[flat], half_a.at[flat], 0, 4, "y").wait_recv()
            from_core[slot, pl.ds(half_rows, rows - half_rows)] = value[half_rows:].astype(BF16)
            from_core[slot, pl.ds(0, half_rows)] = (
                value[:half_rows] + half_a[flat].astype(F32)
            ).astype(BF16)
        elif relation == "y":
            remote(half_b.at[flat], half_b.at[flat], 1, 5, "x").wait_recv()
            from_core[slot, pl.ds(0, half_rows)] = value[:half_rows].astype(BF16)
            from_core[slot, pl.ds(half_rows, rows - half_rows)] = (
                value[half_rows:] + half_b[flat].astype(F32)
            ).astype(BF16)
        else:
            remote(from_x.at[flat], from_x.at[flat], 0, 6, "x").wait_recv()
            remote(from_y.at[flat], from_y.at[flat], 0, 7, "y").wait_recv()
            value += from_x[flat].astype(F32) + from_y[flat].astype(F32)

            @pl.when((z <= zs) & (z > 0))
            def _():
                remote(from_low.at[flat], from_low.at[flat], 0, 8, "up").wait_recv()

            @pl.when((z >= zs) & (z < PLANES - 1))
            def _():
                remote(from_high.at[flat], from_high.at[flat], 1, 9, "down").wait_recv()

            def low():
                return jnp.where(z > 0, from_low[flat].astype(F32), 0.0)

            def high():
                return jnp.where(z < PLANES - 1, from_high[flat].astype(F32), 0.0)

            @pl.when(z < zs)
            def _():
                from_core[slot] = (value + low()).astype(BF16)

            @pl.when(z > zs)
            def _():
                from_core[slot] = (value + high()).astype(BF16)

            @pl.when(z == zs)
            def _():
                owned[
                    pl.ds(pl.multiple_of(sub * rows, rows), rows),
                    pl.ds(kind.source_column, kind.width),
                ] = value + low() + high()

    for condition, descriptor in sends:
        pl.when(condition)(descriptor.start)


def reduce_step(what, refs, plan, sems, at):
    z = place()[0]
    for kind, planes in plan:
        name = kind.__name__
        for plane_at, zs in enumerate(planes):
            for relation in ("xy", "x", "y", "own"):
                sub = at
                if what == "tick":
                    depth = 0
                    if relation == "own":
                        depth = by_plane(
                            z,
                            [
                                place_z
                                if place_z < zs
                                else max(place_z, 3 - place_z)
                                if place_z == zs
                                else 3 - place_z
                                for place_z in range(PLANES)
                            ],
                        )
                    sub = at - kind.lag * (2 - HOPS[relation] + depth)
                reduce_block(
                    what,
                    refs[name],
                    kind,
                    zs,
                    plane_at,
                    len(planes),
                    relation,
                    jnp.clip(sub, 0, kind.subs - 1),
                    sems[name],
                    (sub >= 0) & (sub < kind.subs),
                )


def landing(kind, planes):
    count = planes * kind.subs
    full = pltpu.VMEM((count, kind.height, kind.width), BF16)
    half_a = pltpu.VMEM((count, kind.split, kind.width), BF16)
    half_b = pltpu.VMEM((count, kind.height - kind.split, kind.width), BF16)
    sums = pltpu.VMEM((4 * count, kind.height, kind.width), BF16)
    return [sums] + [full] * 4 + [half_a, half_b]


def landing_signals(kind, planes):
    count = planes * kind.subs
    return [pltpu.SemaphoreType.DMA((4 * count, 3)), pltpu.SemaphoreType.DMA((10, count))]


def greet_near():
    z, x, c, y = place()
    near = neighbours()
    barrier = pltpu.get_barrier_semaphore()
    for key in ("x", "y", "core"):
        pl.semaphore_signal(barrier, inc=1, device_id=near[key], device_id_type=MESH)

    @pl.when(z < PLANES - 1)
    def _():
        pl.semaphore_signal(barrier, inc=1, device_id=near["up"], device_id_type=MESH)

    @pl.when(z > 0)
    def _():
        pl.semaphore_signal(barrier, inc=1, device_id=near["down"], device_id_type=MESH)

    middle = (z > 0) & (z < PLANES - 1)

    @pl.when(middle)
    def _():
        pl.semaphore_wait(barrier, 5)

    @pl.when(jnp.logical_not(middle))
    def _():
        pl.semaphore_wait(barrier, 4)


REDUCE_HIGH = ((HighGrad, (3,)),)
REDUCE_LOW = ((BroadGrad, (1, 2)), (NarrowGrad, (1,)))
HIGH_STEPS = GRAD_SUBS + 5 * HighGrad.lag
LOW_STEPS = GRAD_SUBS + 4
HIGH_FIRST = FF // 8


def attend_back(
    pair, queries, keys, values, mixed, grad_mixed, log_totals, grad_query, grad_key, grad_value
):
    columns = pl.ds(pl.multiple_of(pair * LANES, LANES), LANES)
    key_block = keys[:, columns]
    value_block = values[:, columns]
    key_flat = key_block.T
    key_sum, value_sum = None, None
    step = 256
    for part in range(TOKENS_HERE // step):
        rows = pl.ds(part * step, step)
        grad_block = grad_mixed[rows, columns]
        product = (grad_block.astype(F32) * mixed[rows, columns].astype(F32)).T
        query_parts = []
        heads = zip(two_heads(queries[rows, columns]), two_heads(grad_block))
        for head, (query_head, grad_head) in enumerate(heads):
            scores = multiply(key_block, query_head, BOTH_LAST)
            weights = jnp.exp(scores * HEAD_DIM**-0.5 - log_totals[2 * pair + head, :, rows])
            grad_weights = multiply(value_block, grad_head, BOTH_LAST)
            inner = jnp.sum(
                product[HEAD_DIM * head : HEAD_DIM * (head + 1)], axis=0, keepdims=True
            )
            grad_scores = (weights * (grad_weights - inner)).astype(BF16)
            value_term = multiply(weights.astype(BF16), grad_head)
            key_term = multiply(grad_scores, query_head)
            value_sum = value_term if value_sum is None else value_sum + value_term
            key_sum = key_term if key_sum is None else key_sum + key_term
            query_parts.append(multiply(key_flat, grad_scores))
        joined = jnp.concatenate([query_parts[0][:HEAD_DIM], query_parts[1][HEAD_DIM:]], axis=0)
        grad_query[rows, columns] = (joined * HEAD_DIM**-0.5).T.astype(BF16)
    grad_key[:, columns] = (key_sum * HEAD_DIM**-0.5).astype(BF16)
    grad_value[:, columns] = value_sum.astype(BF16)


def backward_kernel(
    queries_in,
    keys_in,
    values_in,
    mixed_in,
    grad_mixed_in,
    log_totals_in,
    grads_in,
    input_one_in,
    hidden_in,
    grad_middle_in,
    grad_attn_in,
    scale_one,
    early_sums,
    whole_in,
    owned,
    input_grad,
    input_low,
    sums,
    grad_low,
    queries,
    keys,
    values,
    mixed,
    grad_mixed,
    log_totals,
    grads,
    input_one,
    hidden,
    grad_middle,
    grad_attn,
    load_sem,
    grad_query,
    grad_key,
    grad_value,
    row_sums,
    key_all,
    value_all,
    key_mate,
    value_mate,
    flat_one,
    weight_stage,
    grad_stage,
    grad_one,
    mate_sem,
    weight_sem,
    grad_sem,
    *scratch,
):
    dp = lax.axis_index("dp")
    near = neighbours()
    refs = {"HighGrad": (grads, 4 * D, owned, scratch[:7])}
    sems = {"HighGrad": scratch[7:9]}
    tile = 512
    tiles = 3 * D // tile
    loads = [
        pltpu.make_async_copy(source, target, load_sem.at[index])
        for index, (source, target) in enumerate(
            (
                (grads_in, grads),
                (input_one_in, input_one),
                (queries_in, queries),
                (keys_in, keys),
                (values_in, values),
                (mixed_in, mixed),
                (grad_mixed_in, grad_mixed),
                (log_totals_in, log_totals),
                (hidden_in, hidden),
                (grad_middle_in, grad_middle),
                (grad_attn_in, grad_attn),
            )
        )
    ]
    for load in loads:
        load.start()

    def weight_copy(at, slot):
        return pltpu.make_async_copy(
            whole_in.at[:, pl.ds(pl.multiple_of(at * tile, LANES), tile)],
            weight_stage.at[slot],
            weight_sem.at[slot],
        )

    def grad_copy(at, slot):
        return pltpu.make_async_copy(
            grad_stage.at[slot],
            grad_low.at[:, pl.ds(pl.multiple_of(at * tile, LANES), tile)],
            grad_sem.at[slot],
        )

    weight_copy(0, 0).start()
    greet_near()
    loads[0].wait()
    repeat(GRAD_SUBS, lambda at: reduce_step("across", refs, REDUCE_HIGH, sems, at))

    @pl.when(dp < 12)
    def _():
        owned[...] = jnp.zeros_like(owned)

    for load in loads[1:]:
        load.wait()

    def flatten(source):
        def go(at):
            columns = pl.ds(pl.multiple_of(at * 256, LANES), 256)
            flat_one[pl.ds(pl.multiple_of(at * 256, 256), 256)] = source[:, columns].T

        repeat(D // 256, go)

    flatten(input_one)

    def mates(pair):
        columns = pl.ds(pl.multiple_of(pair * LANES, LANES), LANES)
        return [
            pltpu.make_async_remote_copy(
                src_ref=source.at[HALF:, columns],
                dst_ref=target.at[:, columns],
                send_sem=mate_sem.at[pair, 2 * index],
                recv_sem=mate_sem.at[pair, 2 * index + 1],
                device_id=near["core"],
                device_id_type=MESH,
            )
            for index, (source, target) in enumerate(((key_all, key_mate), (value_all, value_mate)))
        ]

    def attention(pair):
        attend_back(
            pair,
            queries,
            keys,
            values,
            mixed,
            grad_mixed,
            log_totals,
            grad_query,
            key_all,
            value_all,
        )
        for mate in mates(pair):
            mate.start()
        reduce_step("tick", refs, REDUCE_HIGH, sems, pair)

    repeat(PAIRS, attention)
    for source, target, total, index in (
        (key_all, key_mate, grad_key, 0),
        (value_all, value_mate, grad_value, 1),
    ):
        repeat(PAIRS, lambda pair: mates(pair)[index].wait())
        total[...] = (source[:HALF].astype(F32) + target[...].astype(F32)).astype(BF16)

    grad_one[...] = jnp.zeros_like(grad_one)

    def project_back(source, base):
        def go(at):
            slot = lax.rem(at, 2)
            weight_copy(at, slot).wait()

            @pl.when(at + 1 < tiles)
            def _():
                weight_copy(at + 1, 1 - slot).start()

            @pl.when(at >= 2)
            def _():
                grad_copy(at - 2, slot).wait()

            columns = pl.ds(pl.multiple_of((at - base) * tile, LANES), tile)
            for side in range(2):
                part = slice(side * 512, (side + 1) * 512)
                grad_one[:, part] += multiply(
                    source[:, columns], weight_stage[slot, part], BOTH_LAST
                )
                narrow = pl.ds(pl.multiple_of((at - base) * tile + side * 256, LANES), 256)
                grad_stage[slot, :, side * 256 : (side + 1) * 256] = multiply(
                    flat_one[...], source[:, narrow]
                ).astype(BF16)
            grad_copy(at, slot).start()

            reduce_step("tick", refs, REDUCE_HIGH, sems, at + PAIRS)

        def run(at, carried):
            go(at + base)
            return carried

        lax.fori_loop(0, D // tile, run, 0)

    project_back(grad_query, 0)
    project_back(grad_key, D // tile)
    project_back(grad_value, 2 * D // tile)

    flatten(mixed)

    def project_out_back(part):
        at = part + tiles
        slot = lax.rem(at, 2)
        grad_copy(at - 2, slot).wait()
        for side in range(2):
            narrow = pl.ds(pl.multiple_of(part * tile + side * 256, LANES), 256)
            grad_stage[slot, :, side * 256 : (side + 1) * 256] = multiply(
                flat_one[...], grad_attn[:, narrow]
            ).astype(BF16)
        grad_copy(at, slot).start()
        reduce_step("tick", refs, REDUCE_HIGH, sems, at + PAIRS)

    repeat(D // tile, project_out_back)
    row_sums[...] = jnp.zeros_like(row_sums)

    def shape_back(at):
        rows = pl.ds(pl.multiple_of(at * 128, 128), 128)
        value = hidden[rows].astype(F32)
        center = value - jnp.mean(value, axis=-1, keepdims=True)
        inverse = lax.rsqrt(jnp.mean(center * center, axis=-1, keepdims=True) + norm_eps)
        normed = center * inverse
        towards = grad_one[rows]
        row_sums[0:1] += jnp.sum(towards, axis=0, keepdims=True)
        row_sums[1:2] += jnp.sum(towards * normed, axis=0, keepdims=True)
        row_sums[2:3] += jnp.sum(grad_query[rows].astype(F32), axis=0, keepdims=True)
        row_sums[3:4] += jnp.sum(grad_value[rows].astype(F32), axis=0, keepdims=True)
        scaled = towards * (1.0 + scale_one[...])
        result = grad_middle[rows] + inverse * (
            scaled
            - jnp.mean(scaled, axis=-1, keepdims=True)
            - normed * jnp.mean(scaled * normed, axis=-1, keepdims=True)
        )
        input_grad[rows] = result
        input_low[rows] = result.astype(BF16)
        reduce_step("tick", refs, REDUCE_HIGH, sems, at + PAIRS + tiles + D // tile)

    repeat(4, shape_back)
    for index in range(2):
        sums[:, index * D : (index + 1) * D] = row_sums[index : index + 1]
        start = 6 * D + WIDE + index * D
        sums[:, start : start + D] = row_sums[index + 2 : index + 3]
    sums[:, 2 * D : 6 * D] = early_sums[:, : 4 * D]
    sums[:, 6 * D : 6 * D + WIDE] = jnp.zeros((1, WIDE), F32)
    sums[:, 8 * D + WIDE :] = early_sums[:, 4 * D :]
    for at in (tiles + D // tile - 2, tiles + D // tile - 1):
        grad_copy(at, at % 2).wait()
    repeat(GRAD_SUBS, lambda at: reduce_step("drain", refs, REDUCE_HIGH, sems, at))


def run_backward(*given):
    shape = jax.ShapeDtypeStruct
    rows = TOKENS_HERE
    vmem = pl.BlockSpec(memory_space=pltpu.VMEM)
    hbm = pl.BlockSpec(memory_space=pl.ANY)
    dma = pltpu.SemaphoreType.DMA
    return pl.pallas_call(
        backward_kernel,
        out_shape=[
            shape((HALF, WIDE), F32),
            shape((rows, D), F32),
            shape((rows, D), BF16),
            shape((1, VECTOR), F32),
            shape((D, 4 * D), BF16),
        ],
        in_specs=[hbm] * 11 + [vmem] * 2 + [hbm],
        out_specs=[vmem] * 4 + [hbm],
        scratch_shapes=[pltpu.VMEM(one.shape, one.dtype) for one in given[:11]]
        + [dma((11,))]
        + [pltpu.VMEM((rows, D), BF16)] * 3
        + [pltpu.VMEM((8, D), F32)]
        + [pltpu.VMEM((2 * rows, D), BF16)] * 2
        + [pltpu.VMEM((rows, D), BF16)] * 2
        + [
            pltpu.VMEM((D, rows), BF16),
            pltpu.VMEM((2, D, 512), BF16),
            pltpu.VMEM((2, D, 512), BF16),
            pltpu.VMEM((rows, D), F32),
            dma((PAIRS, 4)),
            dma((2,)),
            dma((2,)),
        ]
        + landing(HighGrad, 1)
        + landing_signals(HighGrad, 1),
        compiler_params=pltpu.CompilerParams(
            collective_id=1, has_side_effects=True, vmem_limit_bytes=62 * 2**20
        ),
        cost_estimate=pl.CostEstimate(
            flops=12 * 2 * 512 * 1024 * 1024, bytes_accessed=60 * 2**20, transcendentals=2**23
        ),
        name="backward",
    )(*given)


VECTOR = 17 * WIDE


def finish_kernel(
    grad_low,
    grad_up,
    low_in,
    active_rows,
    condition,
    sums,
    owned_high,
    down_sum,
    owned,
    cond_grad,
    bias_parts,
    ada_bias_grad,
    owned_down,
    grads,
    ada_weights,
    sum_mate,
    sum_pieces,
    ada_in,
    cond_piece,
    cond_in,
    down_mate,
    local_sem,
    mate_sem,
    down_sem,
    piece_send,
    ada_recv,
    bias_recv,
    cond_send,
    cond_recv,
    *scratch,
):
    z, x, c, y = place()
    dp = (z * 2 + x) * 2 + c
    near = neighbours()
    refs = {
        "BroadGrad": (grads, 0, owned, scratch[0:7]),
        "NarrowGrad": (grads, 0, owned, scratch[7:14]),
    }
    sems = {"BroadGrad": scratch[14:16], "NarrowGrad": scratch[16:18]}

    def remote(source, target, sent, arrived, device):
        return pltpu.make_async_remote_copy(
            src_ref=source,
            dst_ref=target,
            send_sem=sent,
            recv_sem=arrived,
            device_id=device,
            device_id_type=MESH,
        )

    loads = [
        pltpu.make_async_copy(grad_low, grads.at[:, : 4 * D], local_sem.at[0]),
        pltpu.make_async_copy(
            grad_up.at[:, :HIGH_FIRST], grads.at[:, 4 * D : 4 * D + HIGH_FIRST], local_sem.at[1]
        ),
        pltpu.make_async_copy(low_in.at[pl.ds(0, HALF)], ada_weights, local_sem.at[2]),
    ]
    for load in loads:
        load.start()
    owned[...] = owned_high[...]
    greet_all()
    mate = remote(sums, sum_mate, mate_sem.at[0], mate_sem.at[1], near["core"])
    mate.start()
    down_away = remote(
        down_sum.at[:, pl.ds(pl.multiple_of((1 - y) * FF_PART, LANES), FF_PART)],
        down_mate,
        down_sem.at[0],
        down_sem.at[1],
        near["y"],
    )
    down_away.start()

    for load in loads[:2]:
        load.wait()
    repeat(GRAD_SUBS, lambda at: reduce_step("across", refs, REDUCE_LOW, sems, at))
    repeat(2, lambda at: reduce_step("tick", refs, REDUCE_LOW, sems, at))

    mate.wait()
    for index in range(17):
        columns = slice(index * WIDE, (index + 1) * WIDE)
        piece = sums[:, columns] + sum_mate[:, columns]
        if index < 7:
            piece = piece.astype(BF16).astype(F32)
        sum_pieces[index] = piece
    latent = (z * 2 + x) * 2 + y

    def piece_target(at):
        return jnp.where(at < 7, at, at - 1)

    def piece_copy(at, target, arrived):
        return remote(
            sum_pieces.at[at], target, piece_send.at[at], arrived, (piece_target(at), c)
        )

    def each_piece(act, keep):
        def go(at):
            mine = (piece_target(at) == dp) & (y == c)

            @pl.when(jnp.logical_not(mine) & (at < 7))
            def _():
                act(piece_copy(at, ada_in.at[latent], ada_recv.at[latent]))

            @pl.when(jnp.logical_not(mine) & (at >= 7))
            def _():
                act(piece_copy(at, bias_parts.at[latent], bias_recv.at[latent]))

            if keep:

                @pl.when(mine & (at < 7))
                def _():
                    ada_in[latent] = sum_pieces[at]

                @pl.when(mine & (at >= 7))
                def _():
                    bias_parts[latent] = sum_pieces[at]

        repeat(17, go)

    each_piece(lambda copy: copy.start(), True)
    repeat(3, lambda at: reduce_step("tick", refs, REDUCE_LOW, sems, at + 2))

    def from_latent(at, target, arrived):
        mine = (at // 2 == z * 2 + x) & (lax.rem(at, 2) == y) & (c == y)

        @pl.when(jnp.logical_not(mine))
        def _():
            remote(
                sum_pieces.at[0], target.at[at], piece_send.at[0], arrived.at[at], near["x"]
            ).wait_recv()

    loads[2].wait()

    @pl.when(dp < 7)
    def _():
        repeat(DP, lambda at: from_latent(at, ada_in, ada_recv))
        gathered = jnp.concatenate([ada_in[index] for index in range(DP)], axis=0)
        ada_bias_grad[...] = jnp.sum(gathered, axis=0, keepdims=True)
        narrow = gathered.astype(BF16)
        owned[...] += multiply(active_rows[...], narrow, BOTH_FIRST)
        part = multiply(narrow, ada_weights[...], BOTH_LAST)
        for index in range(DP):
            cond_piece[index] = part[index : index + 1]

    @pl.when(dp >= 7)
    def _():
        ada_bias_grad[...] = jnp.zeros_like(ada_bias_grad)

    def cond_copy(at):
        return remote(
            cond_piece.at[at // 2],
            cond_in.at[dp * 2 + y],
            cond_send.at[at],
            cond_recv.at[dp * 2 + y],
            (at // 2, lax.rem(at, 2)),
        )

    def each_cond(act, keep):
        def go(at):
            mine = at == dp * 2 + y

            @pl.when(jnp.logical_not(mine))
            def _():
                act(cond_copy(at))

            if keep:

                @pl.when(mine)
                def _():
                    cond_in[dp * 2 + y] = cond_piece[at // 2]

        repeat(2 * DP, go)

    @pl.when(dp < 7)
    def _():
        each_cond(lambda copy: copy.start(), True)

    repeat(LOW_STEPS - 5, lambda at: reduce_step("tick", refs, REDUCE_LOW, sems, at + 5))

    def cond_arrived(at):
        @pl.when(at != dp * 2 + y)
        def _():
            remote(
                cond_piece.at[0], cond_in.at[at], cond_send.at[0], cond_recv.at[at], near["x"]
            ).wait_recv()

    repeat(14, cond_arrived)
    sides = []
    for side in range(2):
        total = cond_in[side]
        for index in range(1, 7):
            total = total + cond_in[2 * index + side]
        sides.append(total)
    value = condition[...]
    logistic = 1.0 / (1.0 + jnp.exp(-value))
    cond_grad[...] = jnp.concatenate(sides, axis=1) * (
        logistic * (1.0 + value * (1.0 - logistic))
    )

    @pl.when(dp >= 6)
    def _():
        repeat(DP, lambda at: from_latent(at, bias_parts, bias_recv))

    @pl.when(dp < 6)
    def _():
        bias_parts[...] = jnp.zeros_like(bias_parts)

    down_away.wait()
    owned_down[...] = down_sum[
        :, pl.ds(pl.multiple_of(y * FF_PART, LANES), FF_PART)
    ].astype(F32) + down_mate[...].astype(F32)
    each_piece(lambda copy: copy.wait_send(), False)

    @pl.when(dp < 7)
    def _():
        each_cond(lambda copy: copy.wait_send(), False)

    repeat(GRAD_SUBS, lambda at: reduce_step("drain", refs, REDUCE_LOW, sems, at))


def run_finish(
    grad_low,
    grad_up,
    low_in,
    active_rows,
    condition,
    sums,
    owned_high,
    down_sum,
):
    shape = jax.ShapeDtypeStruct
    dma = pltpu.SemaphoreType.DMA
    vmem = pl.BlockSpec(memory_space=pltpu.VMEM)
    hbm = pl.BlockSpec(memory_space=pl.ANY)
    return pl.pallas_call(
        finish_kernel,
        out_shape=[
            shape((HALF, WIDE), F32),
            shape((1, D), F32),
            shape((DP, 1, WIDE), F32),
            shape((1, WIDE), F32),
            shape((64, FF_PART), F32),
        ],
        in_specs=[hbm] * 3 + [vmem] * 5,
        out_specs=[vmem] * 5,
        scratch_shapes=[
            pltpu.VMEM((D, 4 * D + HIGH_FIRST), BF16),
            pltpu.VMEM((HALF, WIDE), BF16),
            pltpu.VMEM((1, VECTOR), F32),
            pltpu.VMEM((17, 1, WIDE), F32),
            pltpu.VMEM((DP, 1, WIDE), F32),
            pltpu.VMEM((DP, 1, HALF), F32),
            pltpu.VMEM((14, 1, HALF), F32),
            pltpu.VMEM((64, FF_PART), BF16),
            dma((3,)),
            dma((2,)),
            dma((2,)),
            dma((17,)),
            dma((DP,)),
            dma((DP,)),
            dma((2 * DP,)),
            dma((14,)),
        ]
        + landing(BroadGrad, 2)
        + landing(NarrowGrad, 1)
        + landing_signals(BroadGrad, 2)
        + landing_signals(NarrowGrad, 1),
        compiler_params=pltpu.CompilerParams(
            collective_id=2, has_side_effects=True, vmem_limit_bytes=60 * 2**20
        ),
        name="finish",
    )(
        grad_low,
        grad_up,
        low_in,
        active_rows,
        condition,
        sums,
        owned_high,
        down_sum,
    )


def swap_away(values):
    pairs = []
    for index in range(2 * DP):
        y, c = index % 2, index // 2 % 2
        if y != c:
            pairs.append((index, index // 4 * 4 + y * 2 + c))
    return lax.ppermute(values, ("dp", "seq"), pairs)


def local(
    hidden_in,
    condition,
    cotangent,
    weights_in,
    weights_down,
    biases,
    moment_in,
    moment_down,
    moment_bias,
    square_in,
    square_down,
    square_bias,
):
    dp = lax.axis_index("dp")
    y = lax.axis_index("seq")
    side = WIDE // 2
    bias_row = jnp.pad(biases.astype(BF16)[None], ((0, 15), (0, side)))
    bias_row = jnp.where(y == 0, bias_row, jnp.roll(bias_row, side, axis=1))
    low_in = jnp.concatenate([weights_in.astype(BF16), bias_row], axis=0)
    cond_float = condition.astype(F32)
    (
        whole_in,
        whole_down,
        hidden,
        grad_out,
        cond_all,
        modulation,
        input_one,
        queries,
        keys,
        values,
        mixed,
        log_totals,
        attn_out,
        middle,
        input_two,
        slope,
        grad_branch,
        row_grads,
        block_out,
        grad_down,
    ) = run_forward(
        low_in,
        weights_down.astype(BF16).T,
        hidden_in[0],
        cotangent[0],
        cond_float,
        bias_row[:1].astype(F32),
    )
    at_home = lax.rem(dp, 2) == y
    block_swapped = swap_away(block_out)
    grad_out = grad_out.astype(F32)
    pieces = [modulation[:, part * D : (part + 1) * D] for part in range(6)]
    shift_one, scale_one, gate_one, shift_two, scale_two, gate_two = pieces

    def back_through(gradients, start, width):
        return lax.dot_general(
            gradients,
            whole_in[:, start : start + width],
            BOTH_LAST,
            preferred_element_type=F32,
        )

    def outer(left, right):
        return lax.dot_general(left, right, BOTH_FIRST, preferred_element_type=F32)

    def down_rows(total):
        return jnp.sum(total.astype(F32), axis=0, keepdims=True)

    down_sum = lax.psum_scatter(grad_down, "dp", scatter_dimension=0, tiled=True)
    grad_act = jnp.dot(grad_branch, whole_down, preferred_element_type=F32)
    grad_upward = (grad_act * slope).astype(BF16)
    grad_up = outer(input_two, grad_upward).astype(BF16)
    grad_input_two = back_through(grad_upward, 4 * D, FF)
    normed_two, norm_pull_two = jax.vjp(layer_norm, middle)
    shift_two_grad = down_rows(grad_input_two)
    scale_two_grad = down_rows(grad_input_two * normed_two)
    grad_middle = grad_out + norm_pull_two(grad_input_two * (1.0 + scale_two))[0]
    grad_attn = (grad_middle * gate_one).astype(BF16)
    gate_one_grad = down_rows(grad_middle * attn_out)
    grad_mixed = back_through(grad_attn, 3 * D, D).astype(BF16)
    early_sums = jnp.concatenate(
        [
            gate_one_grad,
            shift_two_grad,
            scale_two_grad,
            row_grads[0:1],
            down_rows(grad_attn),
            down_rows(grad_upward),
            row_grads[1:2],
        ],
        axis=-1,
    )
    owned_high, input_grad, input_low, sums, grad_low = run_backward(
        queries,
        keys,
        values,
        mixed,
        grad_mixed,
        log_totals,
        grad_up,
        input_one,
        hidden,
        grad_middle,
        grad_attn,
        scale_one,
        early_sums,
        whole_in,
    )
    active_rows = lax.dynamic_slice_in_dim(
        jax.nn.silu(cond_all[:, 0]).astype(BF16), y * HALF, HALF, 1
    )
    owned_in, cond_grad, bias_parts, ada_bias_grad, owned_down = run_finish(
        grad_low,
        grad_up,
        low_in,
        active_rows,
        cond_float,
        sums,
        owned_high,
        down_sum,
    )
    owned_down = owned_down.T
    input_low, owned_in = lax.optimization_barrier((input_low, owned_in))
    input_swapped = swap_away(input_low)
    input_grad = jnp.where(at_home, input_grad, input_swapped.astype(F32))
    block_out = jnp.where(at_home, block_out, block_swapped)
    owned_bias = jnp.sum(bias_parts[:, 0], axis=0) + ada_bias_grad[0]
    owned_bias = lax.dynamic_slice_in_dim(owned_bias, y * side, side, 0)
    moments_in, squares_in, master_in = adamw_step(
        weights_in, moment_in, square_in, owned_in, rate_in
    )
    moments_down, squares_down, master_down = adamw_step(
        weights_down, moment_down, square_down, owned_down, rate_down
    )
    moments_bias, squares_bias, master_bias = adamw_step(
        biases, moment_bias, square_bias, owned_bias, rate_bias
    )
    return (
        block_out[None],
        input_grad[None],
        cond_grad,
        moments_in,
        moments_down,
        moments_bias,
        squares_in,
        squares_down,
        squares_bias,
        master_in,
        master_down,
        master_bias,
        master_in.astype(BF16),
        master_down.astype(BF16),
        master_bias.astype(BF16),
    )


def solution(mesh):
    return jax.shard_map(
        local if dict(mesh.shape) == {"dp": 16, "seq": 2} else local_general,
        mesh=mesh,
        in_specs=(
            P("dp", "seq", None),
            P("dp", None),
            P("dp", "seq", None),
            P("seq", "dp"),
            P("seq", "dp"),
            P(("dp", "seq")),
            P("seq", "dp"),
            P("seq", "dp"),
            P(("dp", "seq")),
            P("seq", "dp"),
            P("seq", "dp"),
            P(("dp", "seq")),
        ),
        out_specs=(
            P("dp", "seq", None),
            P("dp", "seq", None),
            P("dp", None),
            P("seq", "dp"),
            P("seq", "dp"),
            P(("dp", "seq")),
            P("seq", "dp"),
            P("seq", "dp"),
            P(("dp", "seq")),
            P("seq", "dp"),
            P("seq", "dp"),
            P(("dp", "seq")),
            P("seq", "dp"),
            P("seq", "dp"),
            P(("dp", "seq")),
        ),
        check_vma=False,
    )
```

```python
import math

import jax
import jax.numpy as jnp
from jax import lax
from jax.experimental import pallas as pl
from jax.experimental.pallas import tpu as pltpu
from jax.sharding import PartitionSpec as P

D = 1024
HEADS = 16
HEAD_DIM = 64
FF = 4096
STEP = 5


norm_eps = 1e-06
beta_first = 0.5
beta_second = 0.5
adam_eps = 1e-08
weight_decay = 0.01
rate_in = 0.03
rate_down = 0.016
rate_bias = 0.3


def layer_norm(values):
    center = values - jnp.mean(values, axis=-1, keepdims=True)
    return center * lax.rsqrt(jnp.mean(center * center, axis=-1, keepdims=True) + norm_eps)


def adamw_step(master, moment, square, gradient, step_rate):
    moment_new = beta_first * moment + (1.0 - beta_first) * gradient
    square_new = beta_second * square + (1.0 - beta_second) * gradient * gradient
    corrected = moment_new / (1.0 - beta_first**STEP)
    scale_sq = square_new / (1.0 - beta_second**STEP)
    master_new = master - step_rate * (
        corrected / (jnp.sqrt(scale_sq) + adam_eps) + weight_decay * master
    )
    return (moment_new, square_new, master_new)


def dense_map(values, matrix):
    return jnp.einsum("nld,de->nle", values, matrix, preferred_element_type=jnp.float32)


def dense_back(gradients, matrix):
    return jnp.einsum("nle,de->nld", gradients, matrix, preferred_element_type=jnp.float32)


def outer_sum(values, gradients):
    return jnp.einsum("nld,nle->de", values, gradients, preferred_element_type=jnp.float32)


def total_sum(values):
    return jnp.sum(values.astype(jnp.float32), axis=(0, 1))


def gather_weights(low_in, low_down, low_bias):
    seq_parts = (
        lax.all_gather(low_in, "seq", axis=0, tiled=True),
        lax.all_gather(low_down, "seq", axis=0, tiled=True),
        lax.all_gather(low_bias, "seq", axis=0, tiled=True),
    )
    whole_in, whole_down, bias_row = (
        lax.all_gather(seq_parts[0], "dp", axis=1, tiled=True),
        lax.all_gather(seq_parts[1], "dp", axis=1, tiled=True),
        lax.all_gather(seq_parts[2].reshape(1, -1), "dp", axis=1, tiled=True),
    )
    return (whole_in, whole_down, bias_row[0])


def head_layout():
    heads_here = math.gcd(HEADS, max(1, 128 // HEAD_DIM))
    return (heads_here, heads_here * HEAD_DIM, HEADS // heads_here)


def split_heads(values, lane_start, lane_count, heads_here):
    piece = lax.dynamic_slice_in_dim(values, lane_start, lane_count, 2)
    return piece.reshape(piece.shape[0], piece.shape[1], heads_here, HEAD_DIM)


def join_heads(stacked):
    moved = jnp.moveaxis(stacked, 0, 2)
    return moved.reshape(moved.shape[0], moved.shape[1], moved.shape[2] * moved.shape[3])


def attention_forward(queries, keys_all, values_all):
    heads_here, lane_count, head_steps = head_layout()
    scale_factor = HEAD_DIM ** (-0.5)

    def one_group(group_index):
        lane_start = group_index * lane_count
        query_part = split_heads(queries, lane_start, lane_count, heads_here)
        key_part = split_heads(keys_all, lane_start, lane_count, heads_here)
        value_part = split_heads(values_all, lane_start, lane_count, heads_here)
        scores = (
            jnp.einsum("nqhd,nkhd->nhqk", query_part, key_part, preferred_element_type=jnp.float32)
            * scale_factor
        )
        row_max = jnp.max(scores, axis=-1, keepdims=True)
        exponent = jnp.exp(scores - row_max)
        row_total = jnp.sum(exponent, axis=-1, keepdims=True)
        weights = (exponent / row_total).astype(jnp.bfloat16)
        attn_part = jnp.einsum(
            "nhqk,nkhd->nqhd", weights, value_part, preferred_element_type=jnp.float32
        )
        shaped = attn_part.reshape(attn_part.shape[0], attn_part.shape[1], lane_count)
        return (shaped, (row_max + jnp.log(row_total))[..., 0])

    stacked, log_totals = lax.map(one_group, jnp.arange(head_steps))
    return (join_heads(stacked), log_totals)


def attention_backward(queries, keys_all, values_all, log_totals, grad_mixed):
    heads_here, lane_count, head_steps = head_layout()
    scale_factor = HEAD_DIM ** (-0.5)

    def one_group(carried):
        group_index, log_part = carried
        lane_start = group_index * lane_count
        query_part = split_heads(queries, lane_start, lane_count, heads_here)
        key_part = split_heads(keys_all, lane_start, lane_count, heads_here)
        value_part = split_heads(values_all, lane_start, lane_count, heads_here)
        grad_part = split_heads(grad_mixed, lane_start, lane_count, heads_here)
        scores = (
            jnp.einsum("nqhd,nkhd->nhqk", query_part, key_part, preferred_element_type=jnp.float32)
            * scale_factor
        )
        probability = jnp.exp(scores - log_part[..., None])
        grad_prob = jnp.einsum(
            "nqhd,nkhd->nhqk", grad_part, value_part, preferred_element_type=jnp.float32
        )
        inner_sum = jnp.sum(probability * grad_prob, axis=-1, keepdims=True)
        grad_score = (probability * (grad_prob - inner_sum)).astype(jnp.bfloat16)
        grad_query = (
            jnp.einsum("nhqk,nkhd->nqhd", grad_score, key_part, preferred_element_type=jnp.float32)
            * scale_factor
        )
        grad_key = (
            jnp.einsum(
                "nhqk,nqhd->nkhd", grad_score, query_part, preferred_element_type=jnp.float32
            )
            * scale_factor
        )
        grad_value = jnp.einsum(
            "nhqk,nqhd->nkhd",
            probability.astype(jnp.bfloat16),
            grad_part,
            preferred_element_type=jnp.float32,
        )
        return (
            grad_query.reshape(grad_query.shape[0], grad_query.shape[1], lane_count),
            grad_key.reshape(grad_key.shape[0], grad_key.shape[1], lane_count),
            grad_value.reshape(grad_value.shape[0], grad_value.shape[1], lane_count),
        )

    query_terms, key_terms, value_terms = lax.map(one_group, (jnp.arange(head_steps), log_totals))
    return (join_heads(query_terms), join_heads(key_terms), join_heads(value_terms))


def local_general(
    hidden_in,
    condition,
    cotangent,
    weights_in,
    weights_down,
    biases,
    moment_in,
    moment_down,
    moment_bias,
    square_in,
    square_down,
    square_bias,
):
    low_in = weights_in.astype(jnp.bfloat16)
    low_down = weights_down.astype(jnp.bfloat16)
    low_bias = biases.astype(jnp.bfloat16)
    whole_in, whole_down, bias_all = gather_weights(low_in, low_down, low_bias)
    bias_float = bias_all.astype(jnp.float32)
    hidden = hidden_in.astype(jnp.float32)
    cond_float = condition.astype(jnp.float32)
    cond_act = jax.nn.silu(cond_float).astype(jnp.bfloat16)
    modulation = (
        jnp.dot(cond_act, whole_in[:, : 6 * D], preferred_element_type=jnp.float32)
        + bias_float[: 6 * D]
    )
    pieces = [modulation[:, None, part_index * D : (part_index + 1) * D] for part_index in range(6)]
    shift_one, scale_one, gate_one, shift_two, scale_two, gate_two = pieces
    normed_one = layer_norm(hidden)
    input_one = (normed_one * (1.0 + scale_one) + shift_one).astype(jnp.bfloat16)
    qkv_all = dense_map(input_one, whole_in[:, 6 * D : 9 * D])
    queries = (qkv_all[..., :D] + bias_float[6 * D : 7 * D]).astype(jnp.bfloat16)
    keys_local = qkv_all[..., D : 2 * D].astype(jnp.bfloat16)
    values_local = (qkv_all[..., 2 * D :] + bias_float[7 * D : 8 * D]).astype(jnp.bfloat16)
    keys_all, values_all = (
        lax.all_gather(keys_local, "seq", axis=1, tiled=True),
        lax.all_gather(values_local, "seq", axis=1, tiled=True),
    )
    attn_float, log_totals = attention_forward(queries, keys_all, values_all)
    attn_mixed = attn_float.astype(jnp.bfloat16)
    attn_out = dense_map(attn_mixed, whole_in[:, 9 * D : 10 * D]) + bias_float[8 * D : 9 * D]
    middle = hidden + gate_one * attn_out
    normed_two = layer_norm(middle)
    input_two = (normed_two * (1.0 + scale_two) + shift_two).astype(jnp.bfloat16)
    upward = dense_map(input_two, whole_in[:, 10 * D :]) + bias_float[9 * D : 9 * D + FF]
    activated = jax.nn.gelu(upward, approximate=True).astype(jnp.bfloat16)
    branch = dense_map(activated, whole_down) + bias_float[9 * D + FF :]
    block_out = (middle + gate_two * branch).astype(jnp.bfloat16)
    whole_in, whole_down, bias_all = gather_weights(low_in, low_down, low_bias)
    grad_out = cotangent.astype(jnp.float32)
    grad_branch = (grad_out * gate_two).astype(jnp.bfloat16)
    gate_two_grad = jnp.sum(grad_out * branch, axis=1)
    grad_down = outer_sum(activated, grad_branch)
    bias_down_grad = total_sum(grad_branch)
    grad_act = dense_back(grad_branch, whole_down)
    _, gelu_pull = jax.vjp(lambda inner_value: jax.nn.gelu(inner_value, approximate=True), upward)
    grad_upward = gelu_pull(grad_act)[0].astype(jnp.bfloat16)
    grad_up = outer_sum(input_two, grad_upward)
    bias_up_grad = total_sum(grad_upward)
    grad_input_two = dense_back(grad_upward, whole_in[:, 10 * D :])
    shift_two_grad = jnp.sum(grad_input_two, axis=1)
    scale_two_grad = jnp.sum(grad_input_two * normed_two, axis=1)
    _, norm_pull_two = jax.vjp(layer_norm, middle)
    grad_middle = grad_out + norm_pull_two(grad_input_two * (1.0 + scale_two))[0]
    grad_attn = (grad_middle * gate_one).astype(jnp.bfloat16)
    gate_one_grad = jnp.sum(grad_middle * attn_out, axis=1)
    grad_out_proj = outer_sum(attn_mixed, grad_attn)
    bias_out_grad = total_sum(grad_attn)
    grad_mixed = dense_back(grad_attn, whole_in[:, 9 * D : 10 * D]).astype(jnp.bfloat16)
    grad_query, key_terms, value_terms = attention_backward(
        queries, keys_all, values_all, log_totals, grad_mixed
    )
    key_grad, value_grad = (
        lax.psum_scatter(
            key_terms.astype(jnp.bfloat16), "seq", scatter_dimension=1, tiled=True
        ).astype(jnp.float32),
        lax.psum_scatter(
            value_terms.astype(jnp.bfloat16), "seq", scatter_dimension=1, tiled=True
        ).astype(jnp.float32),
    )
    grad_qkv = jnp.concatenate(
        [
            grad_query.astype(jnp.bfloat16),
            key_grad.astype(jnp.bfloat16),
            value_grad.astype(jnp.bfloat16),
        ],
        axis=-1,
    )
    grad_proj_qkv = outer_sum(input_one, grad_qkv)
    bias_query_grad = total_sum(grad_qkv[..., :D])
    bias_value_grad = total_sum(grad_qkv[..., 2 * D :])
    grad_input_one = dense_back(grad_qkv, whole_in[:, 6 * D : 9 * D])
    shift_one_grad = jnp.sum(grad_input_one, axis=1)
    scale_one_grad = jnp.sum(grad_input_one * normed_one, axis=1)
    _, norm_pull_one = jax.vjp(layer_norm, hidden)
    input_grad = grad_middle + norm_pull_one(grad_input_one * (1.0 + scale_one))[0]
    mod_terms = jnp.concatenate(
        [
            shift_one_grad,
            scale_one_grad,
            gate_one_grad,
            shift_two_grad,
            scale_two_grad,
            gate_two_grad,
        ],
        axis=-1,
    )
    mod_grad = lax.psum(mod_terms, "seq").astype(jnp.bfloat16)
    _, silu_pull = jax.vjp(jax.nn.silu, cond_float)
    cond_grad = silu_pull(
        jnp.einsum("ne,de->nd", mod_grad, whole_in[:, : 6 * D], preferred_element_type=jnp.float32)
    )[0]
    owner_mask = (lax.axis_index("seq") == 0).astype(jnp.float32)
    grad_ada = (
        jnp.einsum("nd,ne->de", cond_act, mod_grad, preferred_element_type=jnp.float32) * owner_mask
    )
    bias_ada_grad = jnp.sum(mod_grad.astype(jnp.float32), axis=0) * owner_mask
    grad_in_all = jnp.zeros((D, 10 * D + FF), jnp.float32)
    grad_in_all = grad_in_all.at[:, : 6 * D].set(grad_ada)
    grad_in_all = grad_in_all.at[:, 6 * D : 9 * D].set(grad_proj_qkv)
    grad_in_all = grad_in_all.at[:, 9 * D : 10 * D].set(grad_out_proj)
    grad_in_all = grad_in_all.at[:, 10 * D :].set(grad_up)
    bias_flat = jnp.concatenate(
        [
            bias_ada_grad,
            bias_query_grad,
            bias_value_grad,
            bias_out_grad,
            bias_up_grad,
            bias_down_grad,
        ]
    )
    summed_in, summed_down, summed_bias = (
        lax.psum_scatter(
            grad_in_all.astype(jnp.bfloat16), "dp", scatter_dimension=1, tiled=True
        ).astype(jnp.float32),
        lax.psum_scatter(
            grad_down.astype(jnp.bfloat16), "dp", scatter_dimension=1, tiled=True
        ).astype(jnp.float32),
        lax.psum_scatter(
            bias_flat.reshape(1, -1).astype(jnp.bfloat16), "dp", scatter_dimension=1, tiled=True
        ).astype(jnp.float32),
    )
    owned_in, owned_down, owned_bias = (
        lax.psum_scatter(
            summed_in.astype(jnp.bfloat16), "seq", scatter_dimension=0, tiled=True
        ).astype(jnp.float32),
        lax.psum_scatter(
            summed_down.astype(jnp.bfloat16), "seq", scatter_dimension=0, tiled=True
        ).astype(jnp.float32),
        lax.psum_scatter(
            summed_bias.reshape(-1).astype(jnp.bfloat16), "seq", scatter_dimension=0, tiled=True
        ).astype(jnp.float32),
    )
    moments_in, squares_in, master_in = adamw_step(
        weights_in, moment_in, square_in, owned_in, rate_in
    )
    moments_down, squares_down, master_down = adamw_step(
        weights_down, moment_down, square_down, owned_down, rate_down
    )
    moments_bias, squares_bias, master_bias = adamw_step(
        biases, moment_bias, square_bias, owned_bias, rate_bias
    )
    return (
        block_out,
        input_grad,
        cond_grad,
        moments_in,
        moments_down,
        moments_bias,
        squares_in,
        squares_down,
        squares_bias,
        master_in,
        master_down,
        master_bias,
        master_in.astype(jnp.bfloat16),
        master_down.astype(jnp.bfloat16),
        master_bias.astype(jnp.bfloat16),
    )


MESH = pl.DeviceIdType.MESH
WIDE = 896
LOW = 6 * D
KEPT = 4 * D + FF
PLANES = 4
HALF = D // 2
TALL = HALF + 16
SUBS = 3
SUB_ROWS = TALL // SUBS
FF_PART = FF // 2
DP = 16


def place():
    dp = lax.axis_index("dp")
    y = lax.axis_index("seq")
    return (dp // 4, lax.rem(dp // 2, 2), lax.rem(dp, 2), y)


def device_at(z, x, c, y):
    return ((z * 2 + x) * 2 + c, y)


def neighbours():
    z, x, c, y = place()
    return {
        "x": device_at(z, 1 - x, c, y),
        "y": device_at(z, x, c, 1 - y),
        "up": device_at(jnp.minimum(z + 1, PLANES - 1), x, c, y),
        "down": device_at(jnp.maximum(z - 1, 0), x, c, y),
        "core": device_at(z, x, 1 - c, y),
        "swap": device_at(z, x, 1 - c, 1 - y),
    }


def repeat(count, body):
    def step(at, carried):
        body(at)
        return carried

    lax.fori_loop(0, count, step, 0)


def greet_all():
    barrier = pltpu.get_barrier_semaphore()
    here = lax.axis_index("dp") * 2 + lax.axis_index("seq")

    def signal(at):
        there = lax.rem(here + at + 1, 2 * DP)
        pl.semaphore_signal(
            barrier, inc=1, device_id=(there // 2, lax.rem(there, 2)), device_id_type=MESH
        )

    repeat(2 * DP - 1, signal)
    pl.semaphore_wait(barrier, 2 * DP - 1)


class Broad:
    height, width, subs, split = SUB_ROWS, WIDE, SUBS, 64
    first, source_column = 0, 0

    @staticmethod
    def holds(zs, xs, cs):
        return (zs * 2 + xs) * 2 + cs >= 7

    @staticmethod
    def view(whole, zs, xs, ys, cs, sub, start=0, rows=SUB_ROWS):
        column = jnp.maximum(((zs * 2 + xs) * 2 + cs) * WIDE - LOW, 128)
        row = pl.multiple_of(sub * SUB_ROWS + start, 16)
        return whole.at[ys, pl.ds(row, rows), pl.ds(pl.multiple_of(column, 128), WIDE)]


class Narrow:
    height, width, subs, split = TALL, 128, 1, 272
    first, source_column = 16 * SUBS, WIDE - 128

    @staticmethod
    def holds(zs, xs, cs):
        return (zs * 2 + xs) * 2 + cs == 6

    @staticmethod
    def view(whole, zs, xs, ys, cs, sub, start=0, rows=TALL):
        return whole.at[ys, pl.ds(start, rows), pl.ds(0, 128)]


class Down:
    height, width, subs, split = 64, FF_PART, 1, 32
    first, source_column = 16 * SUBS + 16, 0

    @staticmethod
    def holds(zs, xs, cs):
        return zs >= 0

    @staticmethod
    def view(whole, zs, xs, ys, cs, sub, start=0, rows=64):
        row = pl.multiple_of(((zs * 2 + xs) * 2 + cs) * 64 + start, 32)
        return whole.at[pl.ds(row, rows), pl.ds(pl.multiple_of(ys * FF_PART, 128), FF_PART)]


SLOTS = 16 * SUBS + 32
RELATIONS = ("own", "x", "y", "xy")
HOPS = {"own": 0, "x": 1, "y": 1, "xy": 2}


def by_plane(z, table):
    picked = table[PLANES - 1]
    for plane in range(PLANES - 2, -1, -1):
        picked = jnp.where(z == plane, table[plane], picked)
    return picked


def forward_block(what, refs, kind, zs, relation, sub, sems, valid):
    whole, mine = refs
    send_sem, recv_sem, core_sem = sems
    z, x, c, y = place()
    near = neighbours()
    xs = 1 - x if "x" in relation else x
    ys = 1 - y if "y" in relation else y
    slot = kind.first + ((zs * 2 + xs) * 2 + ys) * kind.subs + sub
    full, half = recv_sem.at[slot, 0], recv_sem.at[slot, 1]
    parts = ((0, kind.height), (0, kind.split), (kind.split, kind.height - kind.split))

    def copy(part, index, arrival, key, source=None, cs=None):
        target = kind.view(whole, zs, xs, ys, c if cs is None else cs, sub, *parts[part])
        return pltpu.make_async_remote_copy(
            src_ref=target if source is None else source,
            dst_ref=target,
            send_sem=send_sem.at[slot, index],
            recv_sem=arrival,
            device_id=near[key],
            device_id_type=MESH,
        )

    if what == "core":

        @pl.when(valid & kind.holds(zs, xs, 1 - c))
        def _():
            copy(0, 4, core_sem.at[slot], "core", cs=1 - c).wait_recv()

        return
    valid = valid & kind.holds(zs, xs, c)
    if what == "tick":
        arrived = valid & (zs != z) if relation == "own" else valid

        @pl.when(arrived)
        def _():
            if relation == "xy":
                copy(1, 0, full, "x").wait_recv()
                copy(2, 0, half, "x").wait_recv()
            else:
                copy(0, 0, full, "x").wait_recv()

    def act(descriptor):
        if what == "drain":
            descriptor.wait_send()
        else:
            descriptor.start()

    def spread(source, upward, downward):
        @pl.when(upward)
        def _():
            act(copy(0, 0, full, "up", source))

        @pl.when(downward)
        def _():
            act(copy(0, 1, full, "down", source))

        act(copy(0, 2, full, "x", source))
        act(copy(0, 3, full, "y", source))
        act(copy(0, 4, core_sem.at[slot], "core", source))

    if relation == "own":

        if what != "tick":

            @pl.when(valid & (zs == z))
            def _():
                source = mine.at[
                    pl.ds(pl.multiple_of(sub * kind.height, 16), kind.height),
                    pl.ds(kind.source_column, kind.width),
                ]
                spread(source, z < PLANES - 1, z > 0)

        if what != "launch":

            @pl.when(valid & (zs != z))
            def _():
                spread(None, (zs < z) & (z < PLANES - 1), (zs > z) & (z > 0))

        return

    @pl.when(valid)
    def _():
        if relation == "x":
            act(copy(1, 3, full, "y"))
        if relation == "y":
            act(copy(2, 2, half, "x"))
        act(copy(0, 4, core_sem.at[slot], "core"))


def forward_step(what, refs, plan, relations, sems, sub):
    z = place()[0]
    for kind, order in plan:
        for position in range(len(order[0])):
            zs = by_plane(z, [row[position] for row in order])
            for relation in relations:
                forward_block(
                    what,
                    refs[kind.__name__],
                    kind,
                    zs,
                    relation,
                    jnp.minimum(sub, kind.subs - 1),
                    sems,
                    sub < kind.subs,
                )


def launch(refs, kinds, sems):
    z = place()[0]

    def go(sub):
        for kind in kinds:
            forward_block(
                "launch",
                refs[kind.__name__],
                kind,
                z,
                "own",
                jnp.minimum(sub, kind.subs - 1),
                sems,
                sub < kind.subs,
            )

    repeat(max(kind.subs for kind in kinds), go)


NEAR_LOW = ((1, 2), (1, 2), (2, 1), (2, 1))
ONLY_ONE = ((1,),) * PLANES
ONLY_LAST = ((3,),) * PLANES
NEAR = ((0, 1, 2, 3), (1, 0, 2, 3), (2, 3, 1, 0), (3, 2, 1, 0))
PLAN_LOW = ((Broad, NEAR_LOW), (Narrow, ONLY_ONE))
PLAN_UP = ((Broad, ONLY_LAST),)
PLAN_DOWN = ((Down, NEAR),)
PLAN_ALL = PLAN_LOW + PLAN_UP + PLAN_DOWN


BF16 = jnp.bfloat16
F32 = jnp.float32
PLAIN = (((1,), (0,)), ((), ()))
BOTH_LAST = (((1,), (1,)), ((), ()))
BOTH_FIRST = (((0,), (0,)), ((), ()))
LANES = 128
PAIRS = HEADS // 2
TOKENS_HERE = 512


def multiply(left, right, dims=PLAIN):
    return lax.dot_general(left, right, dims, preferred_element_type=F32)


def two_heads(block):
    lanes = lax.broadcasted_iota(jnp.int32, block.shape, 1)
    zero = jnp.zeros_like(block)
    return (jnp.where(lanes < HEAD_DIM, block, zero), jnp.where(lanes < HEAD_DIM, zero, block))


def attend_pair(pair, queries, keys, values, mixed, log_totals):
    columns = pl.ds(pl.multiple_of(pair * LANES, LANES), LANES)
    key_block = keys[:, columns]
    value_flat = values[:, columns].T
    parts = []
    for head, query_block in enumerate(two_heads(queries[:, columns])):
        scores = multiply(key_block, query_block, BOTH_LAST)
        largest = jnp.max(scores, axis=0, keepdims=True)
        weights = jnp.exp((scores - largest) * HEAD_DIM**-0.5)
        total = jnp.sum(weights, axis=0, keepdims=True)
        parts.append(multiply(value_flat, weights.astype(BF16)) * (1.0 / total))
        log_totals[2 * pair + head] = largest * HEAD_DIM**-0.5 + jnp.log(total)
    joined = jnp.concatenate([parts[0][:HEAD_DIM], parts[1][HEAD_DIM:]], axis=0)
    mixed[:, columns] = joined.T.astype(BF16)


def normalize(values):
    center = values - jnp.mean(values, axis=-1, keepdims=True)
    return center * lax.rsqrt(jnp.mean(center * center, axis=-1, keepdims=True) + norm_eps)


def from_weights(left, whole, start, width):
    columns = pl.ds(pl.multiple_of(start, LANES), width)
    return multiply(left[:, :HALF], whole[0, :HALF, columns]) + multiply(
        left[:, HALF:], whole[1, :HALF, columns]
    )


def bias_of(whole, start, width):
    columns = pl.ds(pl.multiple_of(start, LANES), width)
    both = whole[0, HALF:TALL, columns].astype(F32) + whole[1, HALF:TALL, columns].astype(F32)
    return both[:1]


def forward_kernel(
    low_in,
    low_down,
    hidden_in,
    cotangent,
    condition,
    whole_in,
    whole_down,
    hidden_out,
    grad_out_out,
    cond_all,
    modulation,
    input_one_out,
    queries_out,
    keys_out,
    values_out,
    mixed_out,
    log_totals,
    attn_out_out,
    middle_out,
    input_two_out,
    slope,
    grad_branch_out,
    row_grads,
    block_out,
    grad_down,
    own_in,
    own_down,
    ada_weights,
    ada_part,
    mod_parts,
    up_stage,
    wide,
    active,
    flat_branch,
    flat_mate,
    wide_mate,
    down_stage,
    send_sem,
    recv_sem,
    core_sem,
    local_sem,
    cond_send,
    cond_recv,
    mod_send,
    mod_recv,
    swap_sem,
    pair_sem,
    up_sem,
    down_sem,
    rows_sem,
    wide_sem,
    hidden,
    grad_out,
    input_one,
    queries,
    keys,
    values,
    mixed,
    attn_out,
    middle,
    input_two,
    grad_branch,
    keep_sem,
):
    z, x, c, y = place()
    dp = (z * 2 + x) * 2 + c
    near = neighbours()
    sems = (send_sem, recv_sem, core_sem)
    refs = {"Broad": (own_in, low_in), "Narrow": (own_in, low_in), "Down": (own_down, low_down)}
    at_home = c == y

    def remote(source, target, sent, arrived, device):
        return pltpu.make_async_remote_copy(
            src_ref=source,
            dst_ref=target,
            send_sem=sent,
            recv_sem=arrived,
            device_id=device,
            device_id_type=MESH,
        )

    kept = {
        name: pltpu.make_async_copy(source, target, keep_sem.at[index])
        for index, (name, source, target) in enumerate(
            (
                ("hidden", hidden, hidden_out),
                ("grad_out", grad_out, grad_out_out),
                ("input_one", input_one, input_one_out),
                ("queries", queries, queries_out),
                ("keys", keys, keys_out),
                ("values", values, values_out),
                ("mixed", mixed, mixed_out),
                ("attn_out", attn_out, attn_out_out),
                ("middle", middle, middle_out),
                ("input_two", input_two, input_two_out),
                ("grad_branch", grad_branch, grad_branch_out),
            )
        )
    }

    def keep(*which):
        for name in which:
            kept[name].start()

    broad = pltpu.make_async_copy(
        low_in,
        own_in.at[y, :, pl.ds(pl.multiple_of(jnp.maximum(dp, 7) * WIDE - LOW, LANES), WIDE)],
        local_sem.at[0],
    )
    narrow = pltpu.make_async_copy(
        low_in.at[:, pl.ds(WIDE - 128, 128)], own_in.at[y, :, pl.ds(0, 128)], local_sem.at[0]
    )
    down = pltpu.make_async_copy(
        low_down,
        own_down.at[
            pl.ds(pl.multiple_of(dp * 64, 64), 64),
            pl.ds(pl.multiple_of(y * FF_PART, LANES), FF_PART),
        ],
        local_sem.at[1],
    )
    ada = pltpu.make_async_copy(low_in, ada_weights, local_sem.at[2])
    ada.start()
    down.start()

    @pl.when(dp >= 7)
    def _():
        broad.start()

    @pl.when(dp == 6)
    def _():
        narrow.start()

    greet_all()

    cond_all[dp] = condition[...].astype(F32)

    def cond_copy(at):
        there = lax.rem(dp + at + 1, DP)
        return remote(
            cond_all.at[dp], cond_all.at[dp], cond_send.at[at], cond_recv.at[dp], (there, y)
        )

    repeat(DP - 1, lambda at: cond_copy(at).start())

    swaps = []
    for index, (source, target) in enumerate(((hidden_in, hidden), (cotangent, grad_out))):
        swaps.append(
            (
                pltpu.make_async_copy(source, target, swap_sem.at[index, 0]),
                remote(
                    source, target, swap_sem.at[index, 1], swap_sem.at[index, 2], near["swap"]
                ),
            )
        )

    def trade(index):
        @pl.when(at_home)
        def _():
            swaps[index][0].start()

        @pl.when(jnp.logical_not(at_home))
        def _():
            swaps[index][1].start()

    def traded(index):
        @pl.when(at_home)
        def _():
            swaps[index][0].wait()

        @pl.when(jnp.logical_not(at_home))
        def _():
            swaps[index][1].wait()

    trade(0)
    launch(refs, (Broad, Narrow), sems)

    @pl.when((z == 0) | (z == PLANES - 1))
    def _():
        launch(refs, (Down,), sems)

    def pass_on(plan, relations):
        subs = max(kind.subs for kind, _ in plan)
        repeat(subs, lambda sub: forward_step("tick", refs, plan, relations, sems, sub))

    pass_on(PLAN_LOW, ("own",))

    def cond_arrived(at):
        there = lax.rem(dp + at + 1, DP)
        remote(
            cond_all.at[dp], cond_all.at[there], cond_send.at[at], cond_recv.at[there], (there, y)
        ).wait_recv()

    repeat(DP - 1, cond_arrived)
    raw = jnp.concatenate([cond_all[index] for index in range(DP)], axis=0)
    active[...] = (raw / (1.0 + jnp.exp(-raw))).astype(BF16)
    ada.wait()
    partial = (
        multiply(
            active[:, pl.ds(pl.multiple_of(y * HALF, LANES), HALF)],
            ada_weights[:HALF],
        )
        + ada_weights[HALF:].astype(F32)[:1]
    )
    for index in range(DP):
        ada_part[index] = partial[index : index + 1]

    def mod_target(at):
        latent, core = at // 2, lax.rem(at, 2)
        return (latent // 2 * 2 + core, lax.rem(latent, 2))

    def mod_copy(at):
        return remote(
            ada_part.at[at // 2],
            mod_parts.at[dp * 2 + y],
            mod_send.at[at],
            mod_recv.at[dp * 2 + y],
            mod_target(at),
        )

    def elsewhere(at):
        there = mod_target(at)
        return (there[0] != dp) | (there[1] != y)

    @pl.when(dp < 7)
    def _():
        def send(at):
            @pl.when(elsewhere(at))
            def _():
                mod_copy(at).start()

            @pl.when(jnp.logical_not(elsewhere(at)))
            def _():
                mod_parts[dp * 2 + y] = ada_part[at // 2]

        repeat(2 * DP, send)

    pass_on(PLAN_LOW, ("x", "y"))

    @pl.when((z > 0) & (z < PLANES - 1))
    def _():
        launch(refs, (Down,), sems)

    pass_on(PLAN_UP, ("own",))
    trade(1)
    traded(0)

    def mod_arrived(at):
        @pl.when(at != dp * 2 + y)
        def _():
            remote(
                ada_part.at[0], mod_parts.at[at], mod_send.at[0], mod_recv.at[at], near["x"]
            ).wait_recv()

    repeat(14, mod_arrived)
    for index in range(7):
        modulation[:, index * WIDE : (index + 1) * WIDE] = (
            mod_parts[2 * index] + mod_parts[2 * index + 1]
        )

    def vector(index):
        return modulation[:, index * D : (index + 1) * D]

    def shape_one(at):
        rows = pl.ds(pl.multiple_of(at * 128, 128), 128)
        normed = normalize(hidden[rows].astype(F32))
        input_one[rows] = (normed * (1.0 + vector(1)) + vector(0)).astype(BF16)

    repeat(4, shape_one)
    keep("hidden", "input_one")

    pass_on(PLAN_LOW, ("xy",))
    repeat(SUBS, lambda at: forward_step("core", refs, PLAN_LOW, RELATIONS, sems, at))

    @pl.when(dp >= 7)
    def _():
        broad.wait()

    @pl.when(dp == 6)
    def _():
        narrow.wait()

    def project(at):
        columns = pl.ds(pl.multiple_of(at * 256, LANES), 256)
        keys[:HALF, columns] = from_weights(input_one, own_in, D + at * 256, 256).astype(BF16)
        values[:HALF, columns] = (
            from_weights(input_one, own_in, 2 * D + at * 256, 256)
            + bias_of(own_in, D + at * 256, 256)
        ).astype(BF16)

    repeat(D // 256, project)
    mates = [
        remote(
            one.at[:HALF], one.at[HALF:], pair_sem.at[index, 0], pair_sem.at[index, 1], near["core"]
        )
        for index, one in enumerate((keys, values))
    ]
    for mate in mates:
        mate.start()

    def project_queries(at):
        columns = pl.ds(pl.multiple_of(at * 256, LANES), 256)
        queries[:, columns] = (
            from_weights(input_one, own_in, at * 256, 256) + bias_of(own_in, at * 256, 256)
        ).astype(BF16)

    repeat(D // 256, project_queries)
    for mate in mates:
        mate.wait()
    keep("queries", "keys", "values")

    def attention(pair):
        attend_pair(pair, queries, keys, values, mixed, log_totals)

        @pl.when(pair < SUBS)
        def _():
            forward_step("tick", refs, PLAN_UP, ("x", "y"), sems, pair)

        @pl.when(pair == SUBS)
        def _():
            forward_step("tick", refs, PLAN_DOWN, ("own",), sems, 0)

        @pl.when((pair > SUBS) & (pair <= 2 * SUBS))
        def _():
            forward_step("tick", refs, PLAN_UP, ("xy",), sems, pair - SUBS - 1)

    repeat(PAIRS, attention)
    keep("mixed")

    def project_out(at):
        columns = pl.ds(pl.multiple_of(at * 256, LANES), 256)
        attn_out[:, columns] = from_weights(mixed, own_in, 3 * D + at * 256, 256) + bias_of(
            own_in, 2 * D + at * 256, 256
        )

    repeat(D // 256, project_out)

    def shape_two(at):
        rows = pl.ds(pl.multiple_of(at * 128, 128), 128)
        mid = hidden[rows].astype(F32) + vector(2) * attn_out[rows]
        middle[rows] = mid
        input_two[rows] = (normalize(mid) * (1.0 + vector(4)) + vector(3)).astype(BF16)

    repeat(4, shape_two)
    keep("attn_out", "middle", "input_two")
    repeat(SUBS, lambda at: forward_step("core", refs, PLAN_UP, RELATIONS, sems, at))
    whole_copies = [
        pltpu.make_async_copy(
            own_in.at[half, pl.ds(0, HALF)],
            whole_in.at[pl.ds(half * HALF, HALF)],
            local_sem.at[3 + half],
        )
        for half in range(2)
    ]
    for whole_copy in whole_copies:
        whole_copy.start()
    tile = 512

    def up_copy(at, slot):
        return pltpu.make_async_copy(
            up_stage.at[slot],
            slope.at[:, pl.ds(pl.multiple_of(at * tile, LANES), tile)],
            up_sem.at[slot],
        )

    def down_grad_copy(at, slot):
        return pltpu.make_async_copy(
            down_stage.at[slot],
            grad_down.at[:, pl.ds(pl.multiple_of(at * tile, LANES), tile)],
            down_sem.at[slot],
        )

    traded(1)

    def shape_branch(at):
        columns = pl.ds(pl.multiple_of(at * 256, LANES), 256)
        gate = modulation[:, pl.ds(pl.multiple_of(5 * D + at * 256, LANES), 256)]
        scaled = (grad_out[:, columns].astype(F32) * gate).astype(BF16)
        grad_branch[:, columns] = scaled
        flat = scaled.T
        for part in range(4):
            rows = pl.ds(pl.multiple_of((2 * at + part // 2) * 64, 64), 64)
            flat_branch[part % 2, rows] = flat[part * 64 : (part + 1) * 64]
        row_grads[1:2, columns] = jnp.sum(scaled.astype(F32), axis=0, keepdims=True)

    repeat(D // 256, shape_branch)
    keep("grad_out", "grad_branch")
    rows_away = remote(
        flat_branch.at[1 - c], flat_mate, rows_sem.at[0], rows_sem.at[1], near["core"]
    )
    rows_away.start()

    def wide_copy(at):
        columns = pl.ds(pl.multiple_of(at * tile, LANES), tile)
        return remote(
            wide.at[:, columns],
            wide_mate.at[:, columns],
            wide_sem.at[at, 0],
            wide_sem.at[at, 1],
            near["core"],
        )

    def grow_down(at):
        slot = lax.rem(at, 2)

        @pl.when(at >= 2)
        def _():
            down_grad_copy(at - 2, slot).wait()

        wide_copy(at).wait_recv()
        for side in range(2):
            columns = pl.ds(pl.multiple_of(at * tile + side * 256, LANES), 256)
            down_stage[slot, :, side * 256 : (side + 1) * 256] = (
                multiply(flat_branch[c], wide[:, columns])
                + multiply(flat_mate[...], wide_mate[:, columns])
            ).astype(BF16)
        down_grad_copy(at, slot).start()

    def widen(at):
        slot = lax.rem(at, 2)

        @pl.when(at >= 2)
        def _():
            up_copy(at - 2, slot).wait()

        factor = math.sqrt(2.0 / math.pi)
        for side in range(2):
            start = at * tile + side * 256
            value = from_weights(input_two, own_in, 4 * D + start, 256) + bias_of(
                own_in, 3 * D + start, 256
            )
            square = value * value
            bent = jnp.tanh(factor * value * (1.0 + 0.044715 * square))
            half_up = 0.5 + 0.5 * bent
            up_stage[slot, :, side * 256 : (side + 1) * 256] = half_up + 0.5 * value * (
                1.0 - bent * bent
            ) * (factor + 3.0 * 0.044715 * factor * square)
            wide[:, pl.ds(pl.multiple_of(start, LANES), 256)] = (value * half_up).astype(BF16)
        up_copy(at, slot).start()
        wide_copy(at).start()

        @pl.when(at >= 1)
        def _():
            grow_down(at - 1)

        @pl.when(at == 1)
        def _():
            forward_step("tick", refs, PLAN_DOWN, ("x", "y"), sems, 0)

        @pl.when(at == FF // tile - 1)
        def _():
            forward_step("tick", refs, PLAN_DOWN, ("xy",), sems, 0)

    rows_away.wait_recv()
    repeat(FF // tile, widen)
    grow_down(FF // tile - 1)
    for at in (FF // tile - 2, FF // tile - 1):
        up_copy(at, at % 2).wait()
        down_grad_copy(at, at % 2).wait()
    down.wait()

    def narrow_down(at):
        columns = pl.ds(pl.multiple_of(at * 256, LANES), 256)
        value = bias_of(own_in, 7 * D + at * 256, 256)
        for side in range(2):
            value += multiply(
                wide[:, side * FF_PART : (side + 1) * FF_PART],
                own_down[columns, side * FF_PART : (side + 1) * FF_PART],
                BOTH_LAST,
            )
        gate = modulation[:, pl.ds(pl.multiple_of(5 * D + at * 256, LANES), 256)]
        block_out[:, columns] = (middle[:, columns] + gate * value).astype(BF16)
        towards = grad_out[:, columns].astype(F32)
        row_grads[0:1, columns] = jnp.sum(towards * value, axis=0, keepdims=True)

    forward_step("core", refs, PLAN_DOWN, RELATIONS, sems, 0)
    down_copy = pltpu.make_async_copy(own_down, whole_down, local_sem.at[5])
    down_copy.start()
    repeat(PLANES, narrow_down)

    repeat(SUBS, lambda at: forward_step("drain", refs, PLAN_ALL, RELATIONS, sems, at))
    repeat(DP - 1, lambda at: cond_copy(at).wait_send())

    @pl.when(dp < 7)
    def _():
        def sent(at):
            @pl.when(elsewhere(at))
            def _():
                mod_copy(at).wait_send()

        repeat(2 * DP, sent)

    for whole_copy in whole_copies:
        whole_copy.wait()
    down_copy.wait()
    rows_away.wait_send()
    repeat(FF // tile, lambda at: wide_copy(at).wait_send())
    for one in kept.values():
        one.wait()


def run_forward(low_in, low_down, hidden_in, cotangent, condition):
    shape = jax.ShapeDtypeStruct
    rows = TOKENS_HERE
    wide, flat = shape((rows, D), BF16), shape((rows, D), F32)
    both = shape((2 * rows, D), BF16)
    outs = [
        (shape((D, KEPT), BF16), pl.ANY),
        (shape((D, FF), BF16), pl.ANY),
        (wide, pl.ANY),
        (wide, pl.ANY),
        (shape((DP, 1, D), F32), pltpu.VMEM),
        (shape((1, 7 * WIDE), F32), pltpu.VMEM),
        (wide, pl.ANY),
        (wide, pl.ANY),
        (both, pl.ANY),
        (both, pl.ANY),
        (wide, pl.ANY),
        (shape((HEADS, 1, rows), F32), pltpu.VMEM),
        (flat, pl.ANY),
        (flat, pl.ANY),
        (wide, pl.ANY),
        (shape((rows, FF), F32), pl.ANY),
        (wide, pl.ANY),
        (shape((8, D), F32), pltpu.VMEM),
        (wide, pltpu.VMEM),
        (shape((D // 2, FF), BF16), pl.ANY),
    ]
    kept = (wide, wide, wide, wide, both, both, wide, flat, flat, wide, wide)
    dma = pltpu.SemaphoreType.DMA
    return pl.pallas_call(
        forward_kernel,
        out_shape=[one for one, _ in outs],
        in_specs=[pl.BlockSpec(memory_space=pl.ANY)] * 4
        + [pl.BlockSpec(memory_space=pltpu.VMEM)],
        out_specs=[pl.BlockSpec(memory_space=where) for _, where in outs],
        scratch_shapes=[
            pltpu.VMEM((2, TALL, KEPT), BF16),
            pltpu.VMEM((D, FF), BF16),
            pltpu.VMEM((TALL, WIDE), BF16),
            pltpu.VMEM((DP, 1, WIDE), F32),
            pltpu.VMEM((14, 1, WIDE), F32),
            pltpu.VMEM((2, rows, 512), F32),
            pltpu.VMEM((rows, FF), BF16),
            pltpu.VMEM((DP, D), BF16),
            pltpu.VMEM((2, D // 2, rows), BF16),
            pltpu.VMEM((D // 2, rows), BF16),
            pltpu.VMEM((rows, FF), BF16),
            pltpu.VMEM((2, D // 2, 512), BF16),
            dma((SLOTS, 5)),
            dma((SLOTS, 2)),
            dma((SLOTS,)),
            dma((6,)),
            dma((DP,)),
            dma((DP,)),
            dma((2 * DP,)),
            dma((14,)),
            dma((2, 3)),
            dma((2, 2)),
            dma((2,)),
            dma((2,)),
            dma((2,)),
            dma((FF // 512, 2)),
        ]
        + [pltpu.VMEM(one.shape, one.dtype) for one in kept]
        + [dma((len(kept),))],
        compiler_params=pltpu.CompilerParams(
            collective_id=0, has_side_effects=True, vmem_limit_bytes=62 * 2**20
        ),
        name="forward",
    )(low_in, low_down, hidden_in, cotangent, condition)


GRAD_SUBS = 8
GRAD_ROWS = HALF // GRAD_SUBS


class BroadGrad:
    height, width, subs, source_column = GRAD_ROWS, WIDE, GRAD_SUBS, 0
    split = GRAD_ROWS // 2
    lag = 1

    @staticmethod
    def holds(zs, xs, cs):
        return (zs * 2 + xs) * 2 + cs >= 7

    @staticmethod
    def corner(zs, xs, ys, cs, sub):
        column = jnp.maximum(((zs * 2 + xs) * 2 + cs) * WIDE - LOW, 128)
        return (
            pl.multiple_of(ys * HALF + sub * GRAD_ROWS, GRAD_ROWS),
            pl.multiple_of(column, 128),
        )


class HighGrad(BroadGrad):
    split = 48
    lag = 2


class NarrowGrad:
    height, width, subs, source_column = HALF, 128, 1, WIDE - 128
    split = HALF // 2
    lag = 1

    @staticmethod
    def holds(zs, xs, cs):
        return (zs * 2 + xs) * 2 + cs == 6

    @staticmethod
    def corner(zs, xs, ys, cs, sub):
        return (pl.multiple_of(ys * HALF, HALF), 0)


def reduce_block(what, refs, kind, zs, plane_at, planes, relation, sub, sems, valid):
    grads, first_column, owned, buffers = refs
    from_core, from_x, from_y, from_low, from_high, half_a, half_b = buffers
    send_sem, recv_sem = sems
    z, x, c, y = place()
    near = neighbours()
    xs = 1 - x if "x" in relation else x
    ys = 1 - y if "y" in relation else y
    flat = plane_at * kind.subs + sub
    count = planes * kind.subs
    kin = RELATIONS.index(relation)
    slot = kin * count + flat
    rows, half_rows = kind.height, kind.split

    def remote(source, target, index, arrival, key):
        return pltpu.make_async_remote_copy(
            src_ref=source,
            dst_ref=target,
            send_sem=send_sem.at[slot, index],
            recv_sem=recv_sem.at[arrival, flat],
            device_id=near[key],
            device_id_type=MESH,
        )

    def share(cs):
        row, column = kind.corner(zs, xs, ys, cs, sub)
        column = jnp.clip(column - first_column, 0, grads.shape[1] - kind.width)
        return (pl.ds(row, rows), pl.ds(pl.multiple_of(column, 128), kind.width))

    total = from_core.at[slot]
    across = remote(grads.at[share(1 - c)], total, 2, kin, "core")
    other = valid & kind.holds(zs, xs, 1 - c)
    if what == "across":
        pl.when(other)(across.start)
        return
    if what == "drain":
        pl.when(other)(across.wait_send)
    valid = valid & kind.holds(zs, xs, c)
    part_a = from_core.at[slot, pl.ds(0, half_rows)]
    part_b = from_core.at[slot, pl.ds(half_rows, rows - half_rows)]
    if relation == "xy":
        sends = [
            (valid, remote(part_a, half_a.at[flat], 0, 4, "y")),
            (valid, remote(part_b, half_b.at[flat], 1, 5, "x")),
        ]
    elif relation == "x":
        sends = [(valid, remote(total, from_x.at[flat], 0, 6, "x"))]
    elif relation == "y":
        sends = [(valid, remote(total, from_y.at[flat], 0, 7, "y"))]
    else:
        sends = [
            (valid & (z < zs), remote(total, from_low.at[flat], 0, 8, "up")),
            (valid & (z > zs), remote(total, from_high.at[flat], 1, 9, "down")),
        ]
    if what == "drain":
        for condition, descriptor in sends:
            pl.when(condition)(descriptor.wait_send)
        return

    @pl.when(valid)
    def _():
        remote(total, total, 2, kin, "core").wait_recv()
        value = from_core[slot].astype(F32) + grads[share(c)].astype(F32)
        if relation == "xy":
            from_core[slot] = value.astype(BF16)
        elif relation == "x":
            remote(half_a.at[flat], half_a.at[flat], 0, 4, "y").wait_recv()
            from_core[slot, pl.ds(half_rows, rows - half_rows)] = value[half_rows:].astype(BF16)
            from_core[slot, pl.ds(0, half_rows)] = (
                value[:half_rows] + half_a[flat].astype(F32)
            ).astype(BF16)
        elif relation == "y":
            remote(half_b.at[flat], half_b.at[flat], 1, 5, "x").wait_recv()
            from_core[slot, pl.ds(0, half_rows)] = value[:half_rows].astype(BF16)
            from_core[slot, pl.ds(half_rows, rows - half_rows)] = (
                value[half_rows:] + half_b[flat].astype(F32)
            ).astype(BF16)
        else:
            remote(from_x.at[flat], from_x.at[flat], 0, 6, "x").wait_recv()
            remote(from_y.at[flat], from_y.at[flat], 0, 7, "y").wait_recv()
            value += from_x[flat].astype(F32) + from_y[flat].astype(F32)

            @pl.when((z <= zs) & (z > 0))
            def _():
                remote(from_low.at[flat], from_low.at[flat], 0, 8, "up").wait_recv()

            @pl.when((z >= zs) & (z < PLANES - 1))
            def _():
                remote(from_high.at[flat], from_high.at[flat], 1, 9, "down").wait_recv()

            def low():
                return jnp.where(z > 0, from_low[flat].astype(F32), 0.0)

            def high():
                return jnp.where(z < PLANES - 1, from_high[flat].astype(F32), 0.0)

            @pl.when(z < zs)
            def _():
                from_core[slot] = (value + low()).astype(BF16)

            @pl.when(z > zs)
            def _():
                from_core[slot] = (value + high()).astype(BF16)

            @pl.when(z == zs)
            def _():
                owned[
                    pl.ds(pl.multiple_of(sub * rows, rows), rows),
                    pl.ds(kind.source_column, kind.width),
                ] = value + low() + high()

    for condition, descriptor in sends:
        pl.when(condition)(descriptor.start)


def reduce_step(what, refs, plan, sems, at):
    z = place()[0]
    for kind, planes in plan:
        name = kind.__name__
        for plane_at, zs in enumerate(planes):
            for relation in ("xy", "x", "y", "own"):
                sub = at
                if what == "tick":
                    depth = 0
                    if relation == "own":
                        depth = by_plane(
                            z,
                            [
                                place_z
                                if place_z < zs
                                else max(place_z, 3 - place_z)
                                if place_z == zs
                                else 3 - place_z
                                for place_z in range(PLANES)
                            ],
                        )
                    sub = at - kind.lag * (2 - HOPS[relation] + depth)
                reduce_block(
                    what,
                    refs[name],
                    kind,
                    zs,
                    plane_at,
                    len(planes),
                    relation,
                    jnp.clip(sub, 0, kind.subs - 1),
                    sems[name],
                    (sub >= 0) & (sub < kind.subs),
                )


def landing(kind, planes):
    count = planes * kind.subs
    full = pltpu.VMEM((count, kind.height, kind.width), BF16)
    half_a = pltpu.VMEM((count, kind.split, kind.width), BF16)
    half_b = pltpu.VMEM((count, kind.height - kind.split, kind.width), BF16)
    sums = pltpu.VMEM((4 * count, kind.height, kind.width), BF16)
    return [sums] + [full] * 4 + [half_a, half_b]


def landing_signals(kind, planes):
    count = planes * kind.subs
    return [pltpu.SemaphoreType.DMA((4 * count, 3)), pltpu.SemaphoreType.DMA((10, count))]


def greet_near():
    z, x, c, y = place()
    near = neighbours()
    barrier = pltpu.get_barrier_semaphore()
    for key in ("x", "y", "core"):
        pl.semaphore_signal(barrier, inc=1, device_id=near[key], device_id_type=MESH)

    @pl.when(z < PLANES - 1)
    def _():
        pl.semaphore_signal(barrier, inc=1, device_id=near["up"], device_id_type=MESH)

    @pl.when(z > 0)
    def _():
        pl.semaphore_signal(barrier, inc=1, device_id=near["down"], device_id_type=MESH)

    middle = (z > 0) & (z < PLANES - 1)

    @pl.when(middle)
    def _():
        pl.semaphore_wait(barrier, 5)

    @pl.when(jnp.logical_not(middle))
    def _():
        pl.semaphore_wait(barrier, 4)


REDUCE_HIGH = ((HighGrad, (3,)),)
REDUCE_LOW = ((BroadGrad, (1, 2)), (NarrowGrad, (1,)))
HIGH_STEPS = GRAD_SUBS + 5 * HighGrad.lag
LOW_STEPS = GRAD_SUBS + 4
HIGH_FIRST = FF // 8


def attend_back(
    pair, queries, keys, values, mixed, grad_mixed, log_totals, grad_query, grad_key, grad_value
):
    columns = pl.ds(pl.multiple_of(pair * LANES, LANES), LANES)
    key_block = keys[:, columns]
    value_block = values[:, columns]
    key_flat = key_block.T
    key_sum, value_sum = None, None
    step = 256
    for part in range(TOKENS_HERE // step):
        rows = pl.ds(part * step, step)
        grad_block = grad_mixed[rows, columns]
        product = (grad_block.astype(F32) * mixed[rows, columns].astype(F32)).T
        query_parts = []
        heads = zip(two_heads(queries[rows, columns]), two_heads(grad_block))
        for head, (query_head, grad_head) in enumerate(heads):
            scores = multiply(key_block, query_head, BOTH_LAST)
            weights = jnp.exp(scores * HEAD_DIM**-0.5 - log_totals[2 * pair + head, :, rows])
            grad_weights = multiply(value_block, grad_head, BOTH_LAST)
            inner = jnp.sum(
                product[HEAD_DIM * head : HEAD_DIM * (head + 1)], axis=0, keepdims=True
            )
            grad_scores = (weights * (grad_weights - inner)).astype(BF16)
            value_term = multiply(weights.astype(BF16), grad_head)
            key_term = multiply(grad_scores, query_head)
            value_sum = value_term if value_sum is None else value_sum + value_term
            key_sum = key_term if key_sum is None else key_sum + key_term
            query_parts.append(multiply(key_flat, grad_scores))
        joined = jnp.concatenate([query_parts[0][:HEAD_DIM], query_parts[1][HEAD_DIM:]], axis=0)
        grad_query[rows, columns] = (joined * HEAD_DIM**-0.5).T.astype(BF16)
    grad_key[:, columns] = (key_sum * HEAD_DIM**-0.5).astype(BF16)
    grad_value[:, columns] = value_sum.astype(BF16)


def backward_kernel(
    queries_in,
    keys_in,
    values_in,
    mixed_in,
    grad_mixed_in,
    log_totals_in,
    grads_in,
    input_one_in,
    hidden_in,
    grad_middle_in,
    grad_attn_in,
    scale_one,
    early_sums,
    whole_in,
    owned,
    input_grad,
    input_low,
    sums,
    grad_low,
    queries,
    keys,
    values,
    mixed,
    grad_mixed,
    log_totals,
    grads,
    input_one,
    hidden,
    grad_middle,
    grad_attn,
    load_sem,
    grad_query,
    grad_key,
    grad_value,
    row_sums,
    key_all,
    value_all,
    key_mate,
    value_mate,
    flat_one,
    weight_stage,
    grad_stage,
    grad_one,
    mate_sem,
    weight_sem,
    grad_sem,
    *scratch,
):
    dp = lax.axis_index("dp")
    near = neighbours()
    refs = {"HighGrad": (grads, 4 * D, owned, scratch[:7])}
    sems = {"HighGrad": scratch[7:9]}
    tile = 512
    tiles = 3 * D // tile
    loads = [
        pltpu.make_async_copy(source, target, load_sem.at[index])
        for index, (source, target) in enumerate(
            (
                (grads_in, grads),
                (input_one_in, input_one),
                (queries_in, queries),
                (keys_in, keys),
                (values_in, values),
                (mixed_in, mixed),
                (grad_mixed_in, grad_mixed),
                (log_totals_in, log_totals),
                (hidden_in, hidden),
                (grad_middle_in, grad_middle),
                (grad_attn_in, grad_attn),
            )
        )
    ]
    for load in loads:
        load.start()

    def weight_copy(at, slot):
        return pltpu.make_async_copy(
            whole_in.at[:, pl.ds(pl.multiple_of(at * tile, LANES), tile)],
            weight_stage.at[slot],
            weight_sem.at[slot],
        )

    def grad_copy(at, slot):
        return pltpu.make_async_copy(
            grad_stage.at[slot],
            grad_low.at[:, pl.ds(pl.multiple_of(at * tile, LANES), tile)],
            grad_sem.at[slot],
        )

    weight_copy(0, 0).start()
    greet_near()
    loads[0].wait()
    repeat(GRAD_SUBS, lambda at: reduce_step("across", refs, REDUCE_HIGH, sems, at))

    @pl.when(dp < 12)
    def _():
        owned[...] = jnp.zeros_like(owned)

    for load in loads[1:]:
        load.wait()

    def flatten(source):
        def go(at):
            columns = pl.ds(pl.multiple_of(at * 256, LANES), 256)
            flat_one[pl.ds(pl.multiple_of(at * 256, 256), 256)] = source[:, columns].T

        repeat(D // 256, go)

    flatten(input_one)

    def mates(pair):
        columns = pl.ds(pl.multiple_of(pair * LANES, LANES), LANES)
        return [
            pltpu.make_async_remote_copy(
                src_ref=source.at[HALF:, columns],
                dst_ref=target.at[:, columns],
                send_sem=mate_sem.at[pair, 2 * index],
                recv_sem=mate_sem.at[pair, 2 * index + 1],
                device_id=near["core"],
                device_id_type=MESH,
            )
            for index, (source, target) in enumerate(((key_all, key_mate), (value_all, value_mate)))
        ]

    def attention(pair):
        attend_back(
            pair,
            queries,
            keys,
            values,
            mixed,
            grad_mixed,
            log_totals,
            grad_query,
            key_all,
            value_all,
        )
        for mate in mates(pair):
            mate.start()
        reduce_step("tick", refs, REDUCE_HIGH, sems, pair)

    repeat(PAIRS, attention)
    for source, target, total, index in (
        (key_all, key_mate, grad_key, 0),
        (value_all, value_mate, grad_value, 1),
    ):
        repeat(PAIRS, lambda pair: mates(pair)[index].wait())
        total[...] = (source[:HALF].astype(F32) + target[...].astype(F32)).astype(BF16)

    grad_one[...] = jnp.zeros_like(grad_one)

    def project_back(source, base):
        def go(at):
            slot = lax.rem(at, 2)
            weight_copy(at, slot).wait()

            @pl.when(at + 1 < tiles)
            def _():
                weight_copy(at + 1, 1 - slot).start()

            @pl.when(at >= 2)
            def _():
                grad_copy(at - 2, slot).wait()

            columns = pl.ds(pl.multiple_of((at - base) * tile, LANES), tile)
            for side in range(2):
                part = slice(side * 512, (side + 1) * 512)
                grad_one[:, part] += multiply(
                    source[:, columns], weight_stage[slot, part], BOTH_LAST
                )
                narrow = pl.ds(pl.multiple_of((at - base) * tile + side * 256, LANES), 256)
                grad_stage[slot, :, side * 256 : (side + 1) * 256] = multiply(
                    flat_one[...], source[:, narrow]
                ).astype(BF16)
            grad_copy(at, slot).start()

            reduce_step("tick", refs, REDUCE_HIGH, sems, at + PAIRS)

        def run(at, carried):
            go(at + base)
            return carried

        lax.fori_loop(0, D // tile, run, 0)

    project_back(grad_query, 0)
    project_back(grad_key, D // tile)
    project_back(grad_value, 2 * D // tile)

    flatten(mixed)

    def project_out_back(part):
        at = part + tiles
        slot = lax.rem(at, 2)
        grad_copy(at - 2, slot).wait()
        for side in range(2):
            narrow = pl.ds(pl.multiple_of(part * tile + side * 256, LANES), 256)
            grad_stage[slot, :, side * 256 : (side + 1) * 256] = multiply(
                flat_one[...], grad_attn[:, narrow]
            ).astype(BF16)
        grad_copy(at, slot).start()
        reduce_step("tick", refs, REDUCE_HIGH, sems, at + PAIRS)

    repeat(D // tile, project_out_back)
    row_sums[...] = jnp.zeros_like(row_sums)

    def shape_back(at):
        rows = pl.ds(pl.multiple_of(at * 128, 128), 128)
        value = hidden[rows].astype(F32)
        center = value - jnp.mean(value, axis=-1, keepdims=True)
        inverse = lax.rsqrt(jnp.mean(center * center, axis=-1, keepdims=True) + norm_eps)
        normed = center * inverse
        towards = grad_one[rows]
        row_sums[0:1] += jnp.sum(towards, axis=0, keepdims=True)
        row_sums[1:2] += jnp.sum(towards * normed, axis=0, keepdims=True)
        row_sums[2:3] += jnp.sum(grad_query[rows].astype(F32), axis=0, keepdims=True)
        row_sums[3:4] += jnp.sum(grad_value[rows].astype(F32), axis=0, keepdims=True)
        scaled = towards * (1.0 + scale_one[...])
        result = grad_middle[rows] + inverse * (
            scaled
            - jnp.mean(scaled, axis=-1, keepdims=True)
            - normed * jnp.mean(scaled * normed, axis=-1, keepdims=True)
        )
        input_grad[rows] = result
        input_low[rows] = result.astype(BF16)
        reduce_step("tick", refs, REDUCE_HIGH, sems, at + PAIRS + tiles + D // tile)

    repeat(4, shape_back)
    for index in range(2):
        sums[:, index * D : (index + 1) * D] = row_sums[index : index + 1]
        start = 6 * D + WIDE + index * D
        sums[:, start : start + D] = row_sums[index + 2 : index + 3]
    sums[:, 2 * D : 6 * D] = early_sums[:, : 4 * D]
    sums[:, 6 * D : 6 * D + WIDE] = jnp.zeros((1, WIDE), F32)
    sums[:, 8 * D + WIDE :] = early_sums[:, 4 * D :]
    for at in (tiles + D // tile - 2, tiles + D // tile - 1):
        grad_copy(at, at % 2).wait()
    repeat(GRAD_SUBS, lambda at: reduce_step("drain", refs, REDUCE_HIGH, sems, at))


def run_backward(*given):
    shape = jax.ShapeDtypeStruct
    rows = TOKENS_HERE
    vmem = pl.BlockSpec(memory_space=pltpu.VMEM)
    hbm = pl.BlockSpec(memory_space=pl.ANY)
    dma = pltpu.SemaphoreType.DMA
    return pl.pallas_call(
        backward_kernel,
        out_shape=[
            shape((HALF, WIDE), F32),
            shape((rows, D), F32),
            shape((rows, D), BF16),
            shape((1, VECTOR), F32),
            shape((D, 4 * D), BF16),
        ],
        in_specs=[hbm] * 11 + [vmem] * 2 + [hbm],
        out_specs=[vmem] * 4 + [hbm],
        scratch_shapes=[pltpu.VMEM(one.shape, one.dtype) for one in given[:11]]
        + [dma((11,))]
        + [pltpu.VMEM((rows, D), BF16)] * 3
        + [pltpu.VMEM((8, D), F32)]
        + [pltpu.VMEM((2 * rows, D), BF16)] * 2
        + [pltpu.VMEM((rows, D), BF16)] * 2
        + [
            pltpu.VMEM((D, rows), BF16),
            pltpu.VMEM((2, D, 512), BF16),
            pltpu.VMEM((2, D, 512), BF16),
            pltpu.VMEM((rows, D), F32),
            dma((PAIRS, 4)),
            dma((2,)),
            dma((2,)),
        ]
        + landing(HighGrad, 1)
        + landing_signals(HighGrad, 1),
        compiler_params=pltpu.CompilerParams(
            collective_id=1, has_side_effects=True, vmem_limit_bytes=62 * 2**20
        ),
        cost_estimate=pl.CostEstimate(
            flops=12 * 2 * 512 * 1024 * 1024, bytes_accessed=60 * 2**20, transcendentals=2**23
        ),
        name="backward",
    )(*given)


VECTOR = 17 * WIDE


def finish_kernel(
    grad_low,
    grad_up,
    low_in,
    active_rows,
    condition,
    sums,
    owned_high,
    down_sum,
    owned,
    cond_grad,
    bias_parts,
    ada_bias_grad,
    owned_down,
    grads,
    ada_weights,
    sum_mate,
    sum_pieces,
    ada_in,
    cond_piece,
    cond_in,
    down_mate,
    local_sem,
    mate_sem,
    down_sem,
    piece_send,
    ada_recv,
    bias_recv,
    cond_send,
    cond_recv,
    *scratch,
):
    z, x, c, y = place()
    dp = (z * 2 + x) * 2 + c
    near = neighbours()
    refs = {
        "BroadGrad": (grads, 0, owned, scratch[0:7]),
        "NarrowGrad": (grads, 0, owned, scratch[7:14]),
    }
    sems = {"BroadGrad": scratch[14:16], "NarrowGrad": scratch[16:18]}

    def remote(source, target, sent, arrived, device):
        return pltpu.make_async_remote_copy(
            src_ref=source,
            dst_ref=target,
            send_sem=sent,
            recv_sem=arrived,
            device_id=device,
            device_id_type=MESH,
        )

    loads = [
        pltpu.make_async_copy(grad_low, grads.at[:, : 4 * D], local_sem.at[0]),
        pltpu.make_async_copy(
            grad_up.at[:, :HIGH_FIRST], grads.at[:, 4 * D : 4 * D + HIGH_FIRST], local_sem.at[1]
        ),
        pltpu.make_async_copy(low_in.at[pl.ds(0, HALF)], ada_weights, local_sem.at[2]),
    ]
    for load in loads:
        load.start()
    owned[...] = owned_high[...]
    greet_all()
    mate = remote(sums, sum_mate, mate_sem.at[0], mate_sem.at[1], near["core"])
    mate.start()
    down_away = remote(
        down_sum.at[:, pl.ds(pl.multiple_of((1 - y) * FF_PART, LANES), FF_PART)],
        down_mate,
        down_sem.at[0],
        down_sem.at[1],
        near["y"],
    )
    down_away.start()

    for load in loads[:2]:
        load.wait()
    repeat(GRAD_SUBS, lambda at: reduce_step("across", refs, REDUCE_LOW, sems, at))
    repeat(2, lambda at: reduce_step("tick", refs, REDUCE_LOW, sems, at))

    mate.wait()
    for index in range(17):
        columns = slice(index * WIDE, (index + 1) * WIDE)
        piece = sums[:, columns] + sum_mate[:, columns]
        if index < 7:
            piece = piece.astype(BF16).astype(F32)
        sum_pieces[index] = piece
    latent = (z * 2 + x) * 2 + y

    def piece_target(at):
        return jnp.where(at < 7, at, at - 1)

    def piece_copy(at, target, arrived):
        return remote(
            sum_pieces.at[at], target, piece_send.at[at], arrived, (piece_target(at), c)
        )

    def each_piece(act, keep):
        def go(at):
            mine = (piece_target(at) == dp) & (y == c)

            @pl.when(jnp.logical_not(mine) & (at < 7))
            def _():
                act(piece_copy(at, ada_in.at[latent], ada_recv.at[latent]))

            @pl.when(jnp.logical_not(mine) & (at >= 7))
            def _():
                act(piece_copy(at, bias_parts.at[latent], bias_recv.at[latent]))

            if keep:

                @pl.when(mine & (at < 7))
                def _():
                    ada_in[latent] = sum_pieces[at]

                @pl.when(mine & (at >= 7))
                def _():
                    bias_parts[latent] = sum_pieces[at]

        repeat(17, go)

    each_piece(lambda copy: copy.start(), True)
    repeat(3, lambda at: reduce_step("tick", refs, REDUCE_LOW, sems, at + 2))

    def from_latent(at, target, arrived):
        mine = (at // 2 == z * 2 + x) & (lax.rem(at, 2) == y) & (c == y)

        @pl.when(jnp.logical_not(mine))
        def _():
            remote(
                sum_pieces.at[0], target.at[at], piece_send.at[0], arrived.at[at], near["x"]
            ).wait_recv()

    loads[2].wait()

    @pl.when(dp < 7)
    def _():
        repeat(DP, lambda at: from_latent(at, ada_in, ada_recv))
        gathered = jnp.concatenate([ada_in[index] for index in range(DP)], axis=0)
        ada_bias_grad[...] = jnp.sum(gathered, axis=0, keepdims=True)
        narrow = gathered.astype(BF16)
        owned[...] += multiply(active_rows[...], narrow, BOTH_FIRST)
        part = multiply(narrow, ada_weights[...], BOTH_LAST)
        for index in range(DP):
            cond_piece[index] = part[index : index + 1]

    @pl.when(dp >= 7)
    def _():
        ada_bias_grad[...] = jnp.zeros_like(ada_bias_grad)

    def cond_copy(at):
        return remote(
            cond_piece.at[at // 2],
            cond_in.at[dp * 2 + y],
            cond_send.at[at],
            cond_recv.at[dp * 2 + y],
            (at // 2, lax.rem(at, 2)),
        )

    def each_cond(act, keep):
        def go(at):
            mine = at == dp * 2 + y

            @pl.when(jnp.logical_not(mine))
            def _():
                act(cond_copy(at))

            if keep:

                @pl.when(mine)
                def _():
                    cond_in[dp * 2 + y] = cond_piece[at // 2]

        repeat(2 * DP, go)

    @pl.when(dp < 7)
    def _():
        each_cond(lambda copy: copy.start(), True)

    repeat(LOW_STEPS - 5, lambda at: reduce_step("tick", refs, REDUCE_LOW, sems, at + 5))

    def cond_arrived(at):
        @pl.when(at != dp * 2 + y)
        def _():
            remote(
                cond_piece.at[0], cond_in.at[at], cond_send.at[0], cond_recv.at[at], near["x"]
            ).wait_recv()

    repeat(14, cond_arrived)
    sides = []
    for side in range(2):
        total = cond_in[side]
        for index in range(1, 7):
            total = total + cond_in[2 * index + side]
        sides.append(total)
    value = condition[...].astype(F32)
    logistic = 1.0 / (1.0 + jnp.exp(-value))
    cond_grad[...] = jnp.concatenate(sides, axis=1) * (
        logistic * (1.0 + value * (1.0 - logistic))
    )

    @pl.when(dp >= 6)
    def _():
        repeat(DP, lambda at: from_latent(at, bias_parts, bias_recv))

    @pl.when(dp < 6)
    def _():
        bias_parts[...] = jnp.zeros_like(bias_parts)

    down_away.wait()
    owned_down[...] = down_sum[
        :, pl.ds(pl.multiple_of(y * FF_PART, LANES), FF_PART)
    ].astype(F32) + down_mate[...].astype(F32)
    each_piece(lambda copy: copy.wait_send(), False)

    @pl.when(dp < 7)
    def _():
        each_cond(lambda copy: copy.wait_send(), False)

    repeat(GRAD_SUBS, lambda at: reduce_step("drain", refs, REDUCE_LOW, sems, at))


def run_finish(
    grad_low,
    grad_up,
    low_in,
    active_rows,
    condition,
    sums,
    owned_high,
    down_sum,
):
    shape = jax.ShapeDtypeStruct
    dma = pltpu.SemaphoreType.DMA
    vmem = pl.BlockSpec(memory_space=pltpu.VMEM)
    hbm = pl.BlockSpec(memory_space=pl.ANY)
    return pl.pallas_call(
        finish_kernel,
        out_shape=[
            shape((HALF, WIDE), F32),
            shape((1, D), F32),
            shape((DP, 1, WIDE), F32),
            shape((1, WIDE), F32),
            shape((64, FF_PART), F32),
        ],
        in_specs=[hbm] * 3 + [vmem] * 5,
        out_specs=[vmem] * 5,
        scratch_shapes=[
            pltpu.VMEM((D, 4 * D + HIGH_FIRST), BF16),
            pltpu.VMEM((HALF, WIDE), BF16),
            pltpu.VMEM((1, VECTOR), F32),
            pltpu.VMEM((17, 1, WIDE), F32),
            pltpu.VMEM((DP, 1, WIDE), F32),
            pltpu.VMEM((DP, 1, HALF), F32),
            pltpu.VMEM((14, 1, HALF), F32),
            pltpu.VMEM((64, FF_PART), BF16),
            dma((3,)),
            dma((2,)),
            dma((2,)),
            dma((17,)),
            dma((DP,)),
            dma((DP,)),
            dma((2 * DP,)),
            dma((14,)),
        ]
        + landing(BroadGrad, 2)
        + landing(NarrowGrad, 1)
        + landing_signals(BroadGrad, 2)
        + landing_signals(NarrowGrad, 1),
        compiler_params=pltpu.CompilerParams(
            collective_id=2, has_side_effects=True, vmem_limit_bytes=60 * 2**20
        ),
        name="finish",
    )(
        grad_low,
        grad_up,
        low_in,
        active_rows,
        condition,
        sums,
        owned_high,
        down_sum,
    )


def swap_away(values):
    pairs = []
    for index in range(2 * DP):
        y, c = index % 2, index // 2 % 2
        if y != c:
            pairs.append((index, index // 4 * 4 + y * 2 + c))
    return lax.ppermute(values, ("dp", "seq"), pairs)


def local(
    hidden_in,
    condition,
    cotangent,
    weights_in,
    weights_down,
    biases,
    moment_in,
    moment_down,
    moment_bias,
    square_in,
    square_down,
    square_bias,
):
    dp = lax.axis_index("dp")
    y = lax.axis_index("seq")
    side = WIDE // 2
    bias_row = jnp.pad(biases.astype(BF16)[None], ((0, 15), (0, side)))
    bias_row = jnp.where(y == 0, bias_row, jnp.roll(bias_row, side, axis=1))
    low_in = jnp.concatenate([weights_in.astype(BF16), bias_row], axis=0)
    (
        whole_in,
        whole_down,
        hidden,
        grad_out,
        cond_all,
        modulation,
        input_one,
        queries,
        keys,
        values,
        mixed,
        log_totals,
        attn_out,
        middle,
        input_two,
        slope,
        grad_branch,
        row_grads,
        block_out,
        grad_down,
    ) = run_forward(
        low_in,
        weights_down.astype(BF16).T,
        hidden_in[0],
        cotangent[0],
        condition,
    )
    at_home = lax.rem(dp, 2) == y
    block_swapped = swap_away(block_out)
    grad_out = grad_out.astype(F32)
    pieces = [modulation[:, part * D : (part + 1) * D] for part in range(6)]
    shift_one, scale_one, gate_one, shift_two, scale_two, gate_two = pieces

    def back_through(gradients, start, width):
        return lax.dot_general(
            gradients,
            whole_in[:, start : start + width],
            BOTH_LAST,
            preferred_element_type=F32,
        )

    def outer(left, right):
        return lax.dot_general(left, right, BOTH_FIRST, preferred_element_type=F32)

    def down_rows(total):
        return jnp.sum(total.astype(F32), axis=0, keepdims=True)

    down_sum = lax.psum_scatter(
        grad_down,
        "dp",
        scatter_dimension=0,
        axis_index_groups=[list(range(core, DP, 2)) for core in range(2)],
        tiled=True,
    )
    grad_act = jnp.dot(grad_branch, whole_down, preferred_element_type=F32)
    grad_upward = (grad_act * slope).astype(BF16)
    grad_up = outer(input_two, grad_upward).astype(BF16)
    grad_input_two = back_through(grad_upward, 4 * D, FF)
    normed_two, norm_pull_two = jax.vjp(layer_norm, middle)
    shift_two_grad = down_rows(grad_input_two)
    scale_two_grad = down_rows(grad_input_two * normed_two)
    grad_middle = grad_out + norm_pull_two(grad_input_two * (1.0 + scale_two))[0]
    grad_attn = (grad_middle * gate_one).astype(BF16)
    gate_one_grad = down_rows(grad_middle * attn_out)
    grad_mixed = back_through(grad_attn, 3 * D, D).astype(BF16)
    early_sums = jnp.concatenate(
        [
            gate_one_grad,
            shift_two_grad,
            scale_two_grad,
            row_grads[0:1],
            down_rows(grad_attn),
            down_rows(grad_upward),
            row_grads[1:2],
        ],
        axis=-1,
    )
    owned_high, input_grad, input_low, sums, grad_low = run_backward(
        queries,
        keys,
        values,
        mixed,
        grad_mixed,
        log_totals,
        grad_up,
        input_one,
        hidden,
        grad_middle,
        grad_attn,
        scale_one,
        early_sums,
        whole_in,
    )
    active_rows = lax.dynamic_slice_in_dim(
        jax.nn.silu(cond_all[:, 0]).astype(BF16), y * HALF, HALF, 1
    )
    owned_in, cond_grad, bias_parts, ada_bias_grad, owned_down = run_finish(
        grad_low,
        grad_up,
        low_in,
        active_rows,
        condition,
        sums,
        owned_high,
        down_sum,
    )
    owned_down = owned_down.T
    input_low, owned_in = lax.optimization_barrier((input_low, owned_in))
    input_swapped = swap_away(input_low)
    input_grad = jnp.where(at_home, input_grad, input_swapped.astype(F32))
    block_out = jnp.where(at_home, block_out, block_swapped)
    owned_bias = jnp.sum(bias_parts[:, 0], axis=0) + ada_bias_grad[0]
    owned_bias = lax.dynamic_slice_in_dim(owned_bias, y * side, side, 0)
    moments_in, squares_in, master_in = adamw_step(
        weights_in, moment_in, square_in, owned_in, rate_in
    )
    moments_down, squares_down, master_down = adamw_step(
        weights_down, moment_down, square_down, owned_down, rate_down
    )
    moments_bias, squares_bias, master_bias = adamw_step(
        biases, moment_bias, square_bias, owned_bias, rate_bias
    )
    return (
        block_out[None],
        input_grad[None],
        cond_grad,
        moments_in,
        moments_down,
        moments_bias,
        squares_in,
        squares_down,
        squares_bias,
        master_in,
        master_down,
        master_bias,
        master_in.astype(BF16),
        master_down.astype(BF16),
        master_bias.astype(BF16),
    )


def solution(mesh):
    return jax.shard_map(
        local if dict(mesh.shape) == {"dp": 16, "seq": 2} else local_general,
        mesh=mesh,
        in_specs=(
            P("dp", "seq", None),
            P("dp", None),
            P("dp", "seq", None),
            P("seq", "dp"),
            P("seq", "dp"),
            P(("dp", "seq")),
            P("seq", "dp"),
            P("seq", "dp"),
            P(("dp", "seq")),
            P("seq", "dp"),
            P("seq", "dp"),
            P(("dp", "seq")),
        ),
        out_specs=(
            P("dp", "seq", None),
            P("dp", "seq", None),
            P("dp", None),
            P("seq", "dp"),
            P("seq", "dp"),
            P(("dp", "seq")),
            P("seq", "dp"),
            P("seq", "dp"),
            P(("dp", "seq")),
            P("seq", "dp"),
            P("seq", "dp"),
            P(("dp", "seq")),
            P("seq", "dp"),
            P("seq", "dp"),
            P(("dp", "seq")),
        ),
        check_vma=False,
    )
```

```python
import math

import jax
import jax.numpy as jnp
from jax import lax
from jax.experimental import pallas as pl
from jax.experimental.pallas import tpu as pltpu
from jax.sharding import PartitionSpec as P

D = 1024
HEADS = 16
HEAD_DIM = 64
FF = 4096
STEP = 5


norm_eps = 1e-06
beta_first = 0.5
beta_second = 0.5
adam_eps = 1e-08
weight_decay = 0.01
rate_in = 0.03
rate_down = 0.016
rate_bias = 0.3


def layer_norm(values):
    center = values - jnp.mean(values, axis=-1, keepdims=True)
    return center * lax.rsqrt(jnp.mean(center * center, axis=-1, keepdims=True) + norm_eps)


def adamw_step(master, moment, square, gradient, step_rate):
    moment_new = beta_first * moment + (1.0 - beta_first) * gradient
    square_new = beta_second * square + (1.0 - beta_second) * gradient * gradient
    corrected = moment_new / (1.0 - beta_first**STEP)
    scale_sq = square_new / (1.0 - beta_second**STEP)
    master_new = master - step_rate * (
        corrected / (jnp.sqrt(scale_sq) + adam_eps) + weight_decay * master
    )
    return (moment_new, square_new, master_new)


def dense_map(values, matrix):
    return jnp.einsum("nld,de->nle", values, matrix, preferred_element_type=jnp.float32)


def dense_back(gradients, matrix):
    return jnp.einsum("nle,de->nld", gradients, matrix, preferred_element_type=jnp.float32)


def outer_sum(values, gradients):
    return jnp.einsum("nld,nle->de", values, gradients, preferred_element_type=jnp.float32)


def total_sum(values):
    return jnp.sum(values.astype(jnp.float32), axis=(0, 1))


def gather_weights(low_in, low_down, low_bias):
    seq_parts = (
        lax.all_gather(low_in, "seq", axis=0, tiled=True),
        lax.all_gather(low_down, "seq", axis=0, tiled=True),
        lax.all_gather(low_bias, "seq", axis=0, tiled=True),
    )
    whole_in, whole_down, bias_row = (
        lax.all_gather(seq_parts[0], "dp", axis=1, tiled=True),
        lax.all_gather(seq_parts[1], "dp", axis=1, tiled=True),
        lax.all_gather(seq_parts[2].reshape(1, -1), "dp", axis=1, tiled=True),
    )
    return (whole_in, whole_down, bias_row[0])


def head_layout():
    heads_here = math.gcd(HEADS, max(1, 128 // HEAD_DIM))
    return (heads_here, heads_here * HEAD_DIM, HEADS // heads_here)


def split_heads(values, lane_start, lane_count, heads_here):
    piece = lax.dynamic_slice_in_dim(values, lane_start, lane_count, 2)
    return piece.reshape(piece.shape[0], piece.shape[1], heads_here, HEAD_DIM)


def join_heads(stacked):
    moved = jnp.moveaxis(stacked, 0, 2)
    return moved.reshape(moved.shape[0], moved.shape[1], moved.shape[2] * moved.shape[3])


def attention_forward(queries, keys_all, values_all):
    heads_here, lane_count, head_steps = head_layout()
    scale_factor = HEAD_DIM ** (-0.5)

    def one_group(group_index):
        lane_start = group_index * lane_count
        query_part = split_heads(queries, lane_start, lane_count, heads_here)
        key_part = split_heads(keys_all, lane_start, lane_count, heads_here)
        value_part = split_heads(values_all, lane_start, lane_count, heads_here)
        scores = (
            jnp.einsum("nqhd,nkhd->nhqk", query_part, key_part, preferred_element_type=jnp.float32)
            * scale_factor
        )
        row_max = jnp.max(scores, axis=-1, keepdims=True)
        exponent = jnp.exp(scores - row_max)
        row_total = jnp.sum(exponent, axis=-1, keepdims=True)
        weights = (exponent / row_total).astype(jnp.bfloat16)
        attn_part = jnp.einsum(
            "nhqk,nkhd->nqhd", weights, value_part, preferred_element_type=jnp.float32
        )
        shaped = attn_part.reshape(attn_part.shape[0], attn_part.shape[1], lane_count)
        return (shaped, (row_max + jnp.log(row_total))[..., 0])

    stacked, log_totals = lax.map(one_group, jnp.arange(head_steps))
    return (join_heads(stacked), log_totals)


def attention_backward(queries, keys_all, values_all, log_totals, grad_mixed):
    heads_here, lane_count, head_steps = head_layout()
    scale_factor = HEAD_DIM ** (-0.5)

    def one_group(carried):
        group_index, log_part = carried
        lane_start = group_index * lane_count
        query_part = split_heads(queries, lane_start, lane_count, heads_here)
        key_part = split_heads(keys_all, lane_start, lane_count, heads_here)
        value_part = split_heads(values_all, lane_start, lane_count, heads_here)
        grad_part = split_heads(grad_mixed, lane_start, lane_count, heads_here)
        scores = (
            jnp.einsum("nqhd,nkhd->nhqk", query_part, key_part, preferred_element_type=jnp.float32)
            * scale_factor
        )
        probability = jnp.exp(scores - log_part[..., None])
        grad_prob = jnp.einsum(
            "nqhd,nkhd->nhqk", grad_part, value_part, preferred_element_type=jnp.float32
        )
        inner_sum = jnp.sum(probability * grad_prob, axis=-1, keepdims=True)
        grad_score = (probability * (grad_prob - inner_sum)).astype(jnp.bfloat16)
        grad_query = (
            jnp.einsum("nhqk,nkhd->nqhd", grad_score, key_part, preferred_element_type=jnp.float32)
            * scale_factor
        )
        grad_key = (
            jnp.einsum(
                "nhqk,nqhd->nkhd", grad_score, query_part, preferred_element_type=jnp.float32
            )
            * scale_factor
        )
        grad_value = jnp.einsum(
            "nhqk,nqhd->nkhd",
            probability.astype(jnp.bfloat16),
            grad_part,
            preferred_element_type=jnp.float32,
        )
        return (
            grad_query.reshape(grad_query.shape[0], grad_query.shape[1], lane_count),
            grad_key.reshape(grad_key.shape[0], grad_key.shape[1], lane_count),
            grad_value.reshape(grad_value.shape[0], grad_value.shape[1], lane_count),
        )

    query_terms, key_terms, value_terms = lax.map(one_group, (jnp.arange(head_steps), log_totals))
    return (join_heads(query_terms), join_heads(key_terms), join_heads(value_terms))


def local_general(
    hidden_in,
    condition,
    cotangent,
    weights_in,
    weights_down,
    biases,
    moment_in,
    moment_down,
    moment_bias,
    square_in,
    square_down,
    square_bias,
):
    low_in = weights_in.astype(jnp.bfloat16)
    low_down = weights_down.astype(jnp.bfloat16)
    low_bias = biases.astype(jnp.bfloat16)
    whole_in, whole_down, bias_all = gather_weights(low_in, low_down, low_bias)
    bias_float = bias_all.astype(jnp.float32)
    hidden = hidden_in.astype(jnp.float32)
    cond_float = condition.astype(jnp.float32)
    cond_act = jax.nn.silu(cond_float).astype(jnp.bfloat16)
    modulation = (
        jnp.dot(cond_act, whole_in[:, : 6 * D], preferred_element_type=jnp.float32)
        + bias_float[: 6 * D]
    )
    pieces = [modulation[:, None, part_index * D : (part_index + 1) * D] for part_index in range(6)]
    shift_one, scale_one, gate_one, shift_two, scale_two, gate_two = pieces
    normed_one = layer_norm(hidden)
    input_one = (normed_one * (1.0 + scale_one) + shift_one).astype(jnp.bfloat16)
    qkv_all = dense_map(input_one, whole_in[:, 6 * D : 9 * D])
    queries = (qkv_all[..., :D] + bias_float[6 * D : 7 * D]).astype(jnp.bfloat16)
    keys_local = qkv_all[..., D : 2 * D].astype(jnp.bfloat16)
    values_local = (qkv_all[..., 2 * D :] + bias_float[7 * D : 8 * D]).astype(jnp.bfloat16)
    keys_all, values_all = (
        lax.all_gather(keys_local, "seq", axis=1, tiled=True),
        lax.all_gather(values_local, "seq", axis=1, tiled=True),
    )
    attn_float, log_totals = attention_forward(queries, keys_all, values_all)
    attn_mixed = attn_float.astype(jnp.bfloat16)
    attn_out = dense_map(attn_mixed, whole_in[:, 9 * D : 10 * D]) + bias_float[8 * D : 9 * D]
    middle = hidden + gate_one * attn_out
    normed_two = layer_norm(middle)
    input_two = (normed_two * (1.0 + scale_two) + shift_two).astype(jnp.bfloat16)
    upward = dense_map(input_two, whole_in[:, 10 * D :]) + bias_float[9 * D : 9 * D + FF]
    activated = jax.nn.gelu(upward, approximate=True).astype(jnp.bfloat16)
    branch = dense_map(activated, whole_down) + bias_float[9 * D + FF :]
    block_out = (middle + gate_two * branch).astype(jnp.bfloat16)
    whole_in, whole_down, bias_all = gather_weights(low_in, low_down, low_bias)
    grad_out = cotangent.astype(jnp.float32)
    grad_branch = (grad_out * gate_two).astype(jnp.bfloat16)
    gate_two_grad = jnp.sum(grad_out * branch, axis=1)
    grad_down = outer_sum(activated, grad_branch)
    bias_down_grad = total_sum(grad_branch)
    grad_act = dense_back(grad_branch, whole_down)
    _, gelu_pull = jax.vjp(lambda inner_value: jax.nn.gelu(inner_value, approximate=True), upward)
    grad_upward = gelu_pull(grad_act)[0].astype(jnp.bfloat16)
    grad_up = outer_sum(input_two, grad_upward)
    bias_up_grad = total_sum(grad_upward)
    grad_input_two = dense_back(grad_upward, whole_in[:, 10 * D :])
    shift_two_grad = jnp.sum(grad_input_two, axis=1)
    scale_two_grad = jnp.sum(grad_input_two * normed_two, axis=1)
    _, norm_pull_two = jax.vjp(layer_norm, middle)
    grad_middle = grad_out + norm_pull_two(grad_input_two * (1.0 + scale_two))[0]
    grad_attn = (grad_middle * gate_one).astype(jnp.bfloat16)
    gate_one_grad = jnp.sum(grad_middle * attn_out, axis=1)
    grad_out_proj = outer_sum(attn_mixed, grad_attn)
    bias_out_grad = total_sum(grad_attn)
    grad_mixed = dense_back(grad_attn, whole_in[:, 9 * D : 10 * D]).astype(jnp.bfloat16)
    grad_query, key_terms, value_terms = attention_backward(
        queries, keys_all, values_all, log_totals, grad_mixed
    )
    key_grad, value_grad = (
        lax.psum_scatter(
            key_terms.astype(jnp.bfloat16), "seq", scatter_dimension=1, tiled=True
        ).astype(jnp.float32),
        lax.psum_scatter(
            value_terms.astype(jnp.bfloat16), "seq", scatter_dimension=1, tiled=True
        ).astype(jnp.float32),
    )
    grad_qkv = jnp.concatenate(
        [
            grad_query.astype(jnp.bfloat16),
            key_grad.astype(jnp.bfloat16),
            value_grad.astype(jnp.bfloat16),
        ],
        axis=-1,
    )
    grad_proj_qkv = outer_sum(input_one, grad_qkv)
    bias_query_grad = total_sum(grad_qkv[..., :D])
    bias_value_grad = total_sum(grad_qkv[..., 2 * D :])
    grad_input_one = dense_back(grad_qkv, whole_in[:, 6 * D : 9 * D])
    shift_one_grad = jnp.sum(grad_input_one, axis=1)
    scale_one_grad = jnp.sum(grad_input_one * normed_one, axis=1)
    _, norm_pull_one = jax.vjp(layer_norm, hidden)
    input_grad = grad_middle + norm_pull_one(grad_input_one * (1.0 + scale_one))[0]
    mod_terms = jnp.concatenate(
        [
            shift_one_grad,
            scale_one_grad,
            gate_one_grad,
            shift_two_grad,
            scale_two_grad,
            gate_two_grad,
        ],
        axis=-1,
    )
    mod_grad = lax.psum(mod_terms, "seq").astype(jnp.bfloat16)
    _, silu_pull = jax.vjp(jax.nn.silu, cond_float)
    cond_grad = silu_pull(
        jnp.einsum("ne,de->nd", mod_grad, whole_in[:, : 6 * D], preferred_element_type=jnp.float32)
    )[0]
    owner_mask = (lax.axis_index("seq") == 0).astype(jnp.float32)
    grad_ada = (
        jnp.einsum("nd,ne->de", cond_act, mod_grad, preferred_element_type=jnp.float32) * owner_mask
    )
    bias_ada_grad = jnp.sum(mod_grad.astype(jnp.float32), axis=0) * owner_mask
    grad_in_all = jnp.zeros((D, 10 * D + FF), jnp.float32)
    grad_in_all = grad_in_all.at[:, : 6 * D].set(grad_ada)
    grad_in_all = grad_in_all.at[:, 6 * D : 9 * D].set(grad_proj_qkv)
    grad_in_all = grad_in_all.at[:, 9 * D : 10 * D].set(grad_out_proj)
    grad_in_all = grad_in_all.at[:, 10 * D :].set(grad_up)
    bias_flat = jnp.concatenate(
        [
            bias_ada_grad,
            bias_query_grad,
            bias_value_grad,
            bias_out_grad,
            bias_up_grad,
            bias_down_grad,
        ]
    )
    summed_in, summed_down, summed_bias = (
        lax.psum_scatter(
            grad_in_all.astype(jnp.bfloat16), "dp", scatter_dimension=1, tiled=True
        ).astype(jnp.float32),
        lax.psum_scatter(
            grad_down.astype(jnp.bfloat16), "dp", scatter_dimension=1, tiled=True
        ).astype(jnp.float32),
        lax.psum_scatter(
            bias_flat.reshape(1, -1).astype(jnp.bfloat16), "dp", scatter_dimension=1, tiled=True
        ).astype(jnp.float32),
    )
    owned_in, owned_down, owned_bias = (
        lax.psum_scatter(
            summed_in.astype(jnp.bfloat16), "seq", scatter_dimension=0, tiled=True
        ).astype(jnp.float32),
        lax.psum_scatter(
            summed_down.astype(jnp.bfloat16), "seq", scatter_dimension=0, tiled=True
        ).astype(jnp.float32),
        lax.psum_scatter(
            summed_bias.reshape(-1).astype(jnp.bfloat16), "seq", scatter_dimension=0, tiled=True
        ).astype(jnp.float32),
    )
    moments_in, squares_in, master_in = adamw_step(
        weights_in, moment_in, square_in, owned_in, rate_in
    )
    moments_down, squares_down, master_down = adamw_step(
        weights_down, moment_down, square_down, owned_down, rate_down
    )
    moments_bias, squares_bias, master_bias = adamw_step(
        biases, moment_bias, square_bias, owned_bias, rate_bias
    )
    return (
        block_out,
        input_grad,
        cond_grad,
        moments_in,
        moments_down,
        moments_bias,
        squares_in,
        squares_down,
        squares_bias,
        master_in,
        master_down,
        master_bias,
        master_in.astype(jnp.bfloat16),
        master_down.astype(jnp.bfloat16),
        master_bias.astype(jnp.bfloat16),
    )


MESH = pl.DeviceIdType.MESH
WIDE = 896
LOW = 6 * D
KEPT = 4 * D + FF
PLANES = 4
HALF = D // 2
TALL = HALF + 16
SUBS = 3
SUB_ROWS = TALL // SUBS
FF_PART = FF // 2
DP = 16


def place():
    dp = lax.axis_index("dp")
    y = lax.axis_index("seq")
    return (dp // 4, lax.rem(dp // 2, 2), lax.rem(dp, 2), y)


def device_at(z, x, c, y):
    return ((z * 2 + x) * 2 + c, y)


def neighbours():
    z, x, c, y = place()
    return {
        "x": device_at(z, 1 - x, c, y),
        "y": device_at(z, x, c, 1 - y),
        "up": device_at(jnp.minimum(z + 1, PLANES - 1), x, c, y),
        "down": device_at(jnp.maximum(z - 1, 0), x, c, y),
        "core": device_at(z, x, 1 - c, y),
        "swap": device_at(z, x, 1 - c, 1 - y),
    }


def repeat(count, body):
    def step(at, carried):
        body(at)
        return carried

    lax.fori_loop(0, count, step, 0)


def greet_all():
    barrier = pltpu.get_barrier_semaphore()
    here = lax.axis_index("dp") * 2 + lax.axis_index("seq")

    def signal(at):
        there = lax.rem(here + at + 1, 2 * DP)
        pl.semaphore_signal(
            barrier, inc=1, device_id=(there // 2, lax.rem(there, 2)), device_id_type=MESH
        )

    repeat(2 * DP - 1, signal)
    pl.semaphore_wait(barrier, 2 * DP - 1)


class Broad:
    height, width, subs, split = SUB_ROWS, WIDE, SUBS, 64
    first, source_column = 0, 0

    @staticmethod
    def holds(zs, xs, cs):
        return (zs * 2 + xs) * 2 + cs >= 7

    @staticmethod
    def view(whole, zs, xs, ys, cs, sub, start=0, rows=SUB_ROWS):
        column = jnp.maximum(((zs * 2 + xs) * 2 + cs) * WIDE - LOW, 128)
        row = pl.multiple_of(sub * SUB_ROWS + start, 16)
        return whole.at[ys, pl.ds(row, rows), pl.ds(pl.multiple_of(column, 128), WIDE)]


class Narrow:
    height, width, subs, split = TALL, 128, 1, 272
    first, source_column = 16 * SUBS, WIDE - 128

    @staticmethod
    def holds(zs, xs, cs):
        return (zs * 2 + xs) * 2 + cs == 6

    @staticmethod
    def view(whole, zs, xs, ys, cs, sub, start=0, rows=TALL):
        return whole.at[ys, pl.ds(start, rows), pl.ds(0, 128)]


class Down:
    height, width, subs, split = 64, FF_PART, 1, 32
    first, source_column = 16 * SUBS + 16, 0

    @staticmethod
    def holds(zs, xs, cs):
        return zs >= 0

    @staticmethod
    def view(whole, zs, xs, ys, cs, sub, start=0, rows=64):
        row = pl.multiple_of(((zs * 2 + xs) * 2 + cs) * 64 + start, 32)
        return whole.at[pl.ds(row, rows), pl.ds(pl.multiple_of(ys * FF_PART, 128), FF_PART)]


SLOTS = 16 * SUBS + 32
RELATIONS = ("own", "x", "y", "xy")
HOPS = {"own": 0, "x": 1, "y": 1, "xy": 2}


def by_plane(z, table):
    picked = table[PLANES - 1]
    for plane in range(PLANES - 2, -1, -1):
        picked = jnp.where(z == plane, table[plane], picked)
    return picked


def forward_block(what, refs, kind, zs, relation, sub, sems, valid):
    whole, mine = refs
    send_sem, recv_sem, core_sem = sems
    z, x, c, y = place()
    near = neighbours()
    xs = 1 - x if "x" in relation else x
    ys = 1 - y if "y" in relation else y
    slot = kind.first + ((zs * 2 + xs) * 2 + ys) * kind.subs + sub
    full, half = recv_sem.at[slot, 0], recv_sem.at[slot, 1]
    parts = ((0, kind.height), (0, kind.split), (kind.split, kind.height - kind.split))

    def copy(part, index, arrival, key, source=None, cs=None):
        target = kind.view(whole, zs, xs, ys, c if cs is None else cs, sub, *parts[part])
        return pltpu.make_async_remote_copy(
            src_ref=target if source is None else source,
            dst_ref=target,
            send_sem=send_sem.at[slot, index],
            recv_sem=arrival,
            device_id=near[key],
            device_id_type=MESH,
        )

    if what == "core":

        @pl.when(valid & kind.holds(zs, xs, 1 - c))
        def _():
            copy(0, 4, core_sem.at[slot], "core", cs=1 - c).wait_recv()

        return
    valid = valid & kind.holds(zs, xs, c)
    if what == "tick":
        arrived = valid & (zs != z) if relation == "own" else valid

        @pl.when(arrived)
        def _():
            if relation == "xy":
                copy(1, 0, full, "x").wait_recv()
                copy(2, 0, half, "x").wait_recv()
            else:
                copy(0, 0, full, "x").wait_recv()

    def act(descriptor):
        if what == "drain":
            descriptor.wait_send()
        else:
            descriptor.start()

    def spread(source, upward, downward):
        @pl.when(upward)
        def _():
            act(copy(0, 0, full, "up", source))

        @pl.when(downward)
        def _():
            act(copy(0, 1, full, "down", source))

        act(copy(0, 2, full, "x", source))
        act(copy(0, 3, full, "y", source))
        act(copy(0, 4, core_sem.at[slot], "core", source))

    if relation == "own":

        if what != "tick":

            @pl.when(valid & (zs == z))
            def _():
                source = mine.at[
                    pl.ds(pl.multiple_of(sub * kind.height, 16), kind.height),
                    pl.ds(kind.source_column, kind.width),
                ]
                spread(source, z < PLANES - 1, z > 0)

        if what != "launch":

            @pl.when(valid & (zs != z))
            def _():
                spread(None, (zs < z) & (z < PLANES - 1), (zs > z) & (z > 0))

        return

    @pl.when(valid)
    def _():
        if relation == "x":
            act(copy(1, 3, full, "y"))
        if relation == "y":
            act(copy(2, 2, half, "x"))
        act(copy(0, 4, core_sem.at[slot], "core"))


def forward_step(what, refs, plan, relations, sems, sub):
    z = place()[0]
    for kind, order in plan:
        for position in range(len(order[0])):
            zs = by_plane(z, [row[position] for row in order])
            for relation in relations:
                forward_block(
                    what,
                    refs[kind.__name__],
                    kind,
                    zs,
                    relation,
                    jnp.minimum(sub, kind.subs - 1),
                    sems,
                    sub < kind.subs,
                )


def launch(refs, kinds, sems):
    z = place()[0]

    def go(sub):
        for kind in kinds:
            forward_block(
                "launch",
                refs[kind.__name__],
                kind,
                z,
                "own",
                jnp.minimum(sub, kind.subs - 1),
                sems,
                sub < kind.subs,
            )

    repeat(max(kind.subs for kind in kinds), go)


NEAR_LOW = ((1, 2), (1, 2), (2, 1), (2, 1))
ONLY_ONE = ((1,),) * PLANES
ONLY_LAST = ((3,),) * PLANES
NEAR = ((0, 1, 2, 3), (1, 0, 2, 3), (2, 3, 1, 0), (3, 2, 1, 0))
PLAN_LOW = ((Broad, NEAR_LOW), (Narrow, ONLY_ONE))
PLAN_UP = ((Broad, ONLY_LAST),)
PLAN_DOWN = ((Down, NEAR),)
PLAN_ALL = PLAN_LOW + PLAN_UP + PLAN_DOWN


BF16 = jnp.bfloat16
F32 = jnp.float32
PLAIN = (((1,), (0,)), ((), ()))
BOTH_LAST = (((1,), (1,)), ((), ()))
BOTH_FIRST = (((0,), (0,)), ((), ()))
LANES = 128
PAIRS = HEADS // 2
TOKENS_HERE = 512


def multiply(left, right, dims=PLAIN):
    return lax.dot_general(left, right, dims, preferred_element_type=F32)


def two_heads(block):
    lanes = lax.broadcasted_iota(jnp.int32, block.shape, 1)
    zero = jnp.zeros_like(block)
    return (jnp.where(lanes < HEAD_DIM, block, zero), jnp.where(lanes < HEAD_DIM, zero, block))


def attend_pair(pair, queries, keys, values, mixed, log_totals):
    columns = pl.ds(pl.multiple_of(pair * LANES, LANES), LANES)
    key_block = keys[:, columns]
    value_flat = values[:, columns].T
    parts = []
    for head, query_block in enumerate(two_heads(queries[:, columns])):
        scores = multiply(key_block, query_block, BOTH_LAST)
        largest = jnp.max(scores, axis=0, keepdims=True)
        weights = jnp.exp((scores - largest) * HEAD_DIM**-0.5)
        total = jnp.sum(weights, axis=0, keepdims=True)
        parts.append(multiply(value_flat, weights.astype(BF16)) * (1.0 / total))
        log_totals[2 * pair + head] = largest * HEAD_DIM**-0.5 + jnp.log(total)
    joined = jnp.concatenate([parts[0][:HEAD_DIM], parts[1][HEAD_DIM:]], axis=0)
    mixed[:, columns] = joined.T.astype(BF16)


def normalize(values):
    center = values - jnp.mean(values, axis=-1, keepdims=True)
    return center * lax.rsqrt(jnp.mean(center * center, axis=-1, keepdims=True) + norm_eps)


def from_weights(left, whole, start, width):
    columns = pl.ds(pl.multiple_of(start, LANES), width)
    return multiply(left[:, :HALF], whole[0, :HALF, columns]) + multiply(
        left[:, HALF:], whole[1, :HALF, columns]
    )


def bias_of(whole, start, width):
    columns = pl.ds(pl.multiple_of(start, LANES), width)
    both = whole[0, HALF:TALL, columns].astype(F32) + whole[1, HALF:TALL, columns].astype(F32)
    return both[:1]


def forward_kernel(
    low_in,
    low_down,
    hidden_in,
    cotangent,
    condition,
    whole_in,
    whole_down,
    hidden_out,
    grad_out_out,
    cond_all,
    modulation,
    input_one_out,
    queries_out,
    keys_out,
    values_out,
    mixed_out,
    log_totals,
    attn_out_out,
    middle_out,
    input_two_out,
    slope,
    grad_branch_out,
    row_grads,
    block_out,
    grad_down,
    own_in,
    own_down,
    ada_weights,
    ada_part,
    mod_parts,
    up_stage,
    wide,
    active,
    flat_branch,
    flat_mate,
    wide_mate,
    down_stage,
    send_sem,
    recv_sem,
    core_sem,
    local_sem,
    cond_send,
    cond_recv,
    mod_send,
    mod_recv,
    swap_sem,
    pair_sem,
    up_sem,
    down_sem,
    rows_sem,
    wide_sem,
    hidden,
    grad_out,
    input_one,
    queries,
    keys,
    values,
    mixed,
    attn_out,
    middle,
    input_two,
    grad_branch,
    keep_sem,
):
    z, x, c, y = place()
    dp = (z * 2 + x) * 2 + c
    near = neighbours()
    sems = (send_sem, recv_sem, core_sem)
    refs = {"Broad": (own_in, low_in), "Narrow": (own_in, low_in), "Down": (own_down, low_down)}
    at_home = c == y

    def remote(source, target, sent, arrived, device):
        return pltpu.make_async_remote_copy(
            src_ref=source,
            dst_ref=target,
            send_sem=sent,
            recv_sem=arrived,
            device_id=device,
            device_id_type=MESH,
        )

    kept = {
        name: pltpu.make_async_copy(source, target, keep_sem.at[index])
        for index, (name, source, target) in enumerate(
            (
                ("hidden", hidden, hidden_out),
                ("grad_out", grad_out, grad_out_out),
                ("input_one", input_one, input_one_out),
                ("queries", queries, queries_out),
                ("keys", keys, keys_out),
                ("values", values, values_out),
                ("mixed", mixed, mixed_out),
                ("attn_out", attn_out, attn_out_out),
                ("middle", middle, middle_out),
                ("input_two", input_two, input_two_out),
                ("grad_branch", grad_branch, grad_branch_out),
            )
        )
    }

    def keep(*which):
        for name in which:
            kept[name].start()

    broad = pltpu.make_async_copy(
        low_in,
        own_in.at[y, :, pl.ds(pl.multiple_of(jnp.maximum(dp, 7) * WIDE - LOW, LANES), WIDE)],
        local_sem.at[0],
    )
    narrow = pltpu.make_async_copy(
        low_in.at[:, pl.ds(WIDE - 128, 128)], own_in.at[y, :, pl.ds(0, 128)], local_sem.at[0]
    )
    down = pltpu.make_async_copy(
        low_down,
        own_down.at[
            pl.ds(pl.multiple_of(dp * 64, 64), 64),
            pl.ds(pl.multiple_of(y * FF_PART, LANES), FF_PART),
        ],
        local_sem.at[1],
    )
    ada = pltpu.make_async_copy(low_in, ada_weights, local_sem.at[2])
    ada.start()
    down.start()

    @pl.when(dp >= 7)
    def _():
        broad.start()

    @pl.when(dp == 6)
    def _():
        narrow.start()

    greet_all()

    cond_all[dp] = condition[...].astype(F32)

    def cond_copy(at):
        there = lax.rem(dp + at + 1, DP)
        return remote(
            cond_all.at[dp], cond_all.at[dp], cond_send.at[at], cond_recv.at[dp], (there, y)
        )

    repeat(DP - 1, lambda at: cond_copy(at).start())

    swaps = []
    for index, (source, target) in enumerate(((hidden_in, hidden), (cotangent, grad_out))):
        swaps.append(
            (
                pltpu.make_async_copy(source, target, swap_sem.at[index, 0]),
                remote(
                    source, target, swap_sem.at[index, 1], swap_sem.at[index, 2], near["swap"]
                ),
            )
        )

    def trade(index):
        @pl.when(at_home)
        def _():
            swaps[index][0].start()

        @pl.when(jnp.logical_not(at_home))
        def _():
            swaps[index][1].start()

    def traded(index):
        @pl.when(at_home)
        def _():
            swaps[index][0].wait()

        @pl.when(jnp.logical_not(at_home))
        def _():
            swaps[index][1].wait()

    trade(0)
    launch(refs, (Broad, Narrow), sems)

    @pl.when((z == 0) | (z == PLANES - 1))
    def _():
        launch(refs, (Down,), sems)

    def pass_on(plan, relations):
        subs = max(kind.subs for kind, _ in plan)
        repeat(subs, lambda sub: forward_step("tick", refs, plan, relations, sems, sub))

    pass_on(PLAN_LOW, ("own",))

    def cond_arrived(at):
        there = lax.rem(dp + at + 1, DP)
        remote(
            cond_all.at[dp], cond_all.at[there], cond_send.at[at], cond_recv.at[there], (there, y)
        ).wait_recv()

    repeat(DP - 1, cond_arrived)
    raw = jnp.concatenate([cond_all[index] for index in range(DP)], axis=0)
    active[...] = (raw / (1.0 + jnp.exp(-raw))).astype(BF16)
    ada.wait()
    partial = (
        multiply(
            active[:, pl.ds(pl.multiple_of(y * HALF, LANES), HALF)],
            ada_weights[:HALF],
        )
        + ada_weights[HALF:].astype(F32)[:1]
    )
    for index in range(DP):
        ada_part[index] = partial[index : index + 1]

    def mod_target(at):
        latent, core = at // 2, lax.rem(at, 2)
        return (latent // 2 * 2 + core, lax.rem(latent, 2))

    def mod_copy(at):
        return remote(
            ada_part.at[at // 2],
            mod_parts.at[dp * 2 + y],
            mod_send.at[at],
            mod_recv.at[dp * 2 + y],
            mod_target(at),
        )

    def elsewhere(at):
        there = mod_target(at)
        return (there[0] != dp) | (there[1] != y)

    @pl.when(dp < 7)
    def _():
        def send(at):
            @pl.when(elsewhere(at))
            def _():
                mod_copy(at).start()

            @pl.when(jnp.logical_not(elsewhere(at)))
            def _():
                mod_parts[dp * 2 + y] = ada_part[at // 2]

        repeat(2 * DP, send)

    pass_on(PLAN_LOW, ("x", "y"))

    @pl.when((z > 0) & (z < PLANES - 1))
    def _():
        launch(refs, (Down,), sems)

    pass_on(PLAN_UP, ("own",))
    trade(1)
    traded(0)

    def mod_arrived(at):
        @pl.when(at != dp * 2 + y)
        def _():
            remote(
                ada_part.at[0], mod_parts.at[at], mod_send.at[0], mod_recv.at[at], near["x"]
            ).wait_recv()

    repeat(14, mod_arrived)
    for index in range(7):
        modulation[:, index * WIDE : (index + 1) * WIDE] = (
            mod_parts[2 * index] + mod_parts[2 * index + 1]
        )

    def vector(index):
        return modulation[:, index * D : (index + 1) * D]

    def shape_one(at):
        rows = pl.ds(pl.multiple_of(at * 128, 128), 128)
        normed = normalize(hidden[rows].astype(F32))
        input_one[rows] = (normed * (1.0 + vector(1)) + vector(0)).astype(BF16)

    repeat(4, shape_one)
    keep("hidden", "input_one")

    pass_on(PLAN_LOW, ("xy",))
    repeat(SUBS, lambda at: forward_step("core", refs, PLAN_LOW, RELATIONS, sems, at))

    @pl.when(dp >= 7)
    def _():
        broad.wait()

    @pl.when(dp == 6)
    def _():
        narrow.wait()

    def project(at):
        columns = pl.ds(pl.multiple_of(at * 256, LANES), 256)
        keys[:HALF, columns] = from_weights(input_one, own_in, D + at * 256, 256).astype(BF16)
        values[:HALF, columns] = (
            from_weights(input_one, own_in, 2 * D + at * 256, 256)
            + bias_of(own_in, D + at * 256, 256)
        ).astype(BF16)

    repeat(D // 256, project)
    mates = [
        remote(
            one.at[:HALF], one.at[HALF:], pair_sem.at[index, 0], pair_sem.at[index, 1], near["core"]
        )
        for index, one in enumerate((keys, values))
    ]
    for mate in mates:
        mate.start()

    def project_queries(at):
        columns = pl.ds(pl.multiple_of(at * 256, LANES), 256)
        queries[:, columns] = (
            from_weights(input_one, own_in, at * 256, 256) + bias_of(own_in, at * 256, 256)
        ).astype(BF16)

    repeat(D // 256, project_queries)
    for mate in mates:
        mate.wait()
    keep("queries", "keys", "values")

    def attention(pair):
        attend_pair(pair, queries, keys, values, mixed, log_totals)

        @pl.when(pair < SUBS)
        def _():
            forward_step("tick", refs, PLAN_UP, ("x", "y"), sems, pair)

        @pl.when(pair == SUBS)
        def _():
            forward_step("tick", refs, PLAN_DOWN, ("own",), sems, 0)

        @pl.when((pair > SUBS) & (pair <= 2 * SUBS))
        def _():
            forward_step("tick", refs, PLAN_UP, ("xy",), sems, pair - SUBS - 1)

    repeat(PAIRS, attention)
    keep("mixed")

    def project_out(at):
        columns = pl.ds(pl.multiple_of(at * 256, LANES), 256)
        attn_out[:, columns] = from_weights(mixed, own_in, 3 * D + at * 256, 256) + bias_of(
            own_in, 2 * D + at * 256, 256
        )

    repeat(D // 256, project_out)

    def shape_two(at):
        rows = pl.ds(pl.multiple_of(at * 128, 128), 128)
        mid = hidden[rows].astype(F32) + vector(2) * attn_out[rows]
        middle[rows] = mid
        input_two[rows] = (normalize(mid) * (1.0 + vector(4)) + vector(3)).astype(BF16)

    repeat(4, shape_two)
    keep("attn_out", "middle", "input_two")
    repeat(SUBS, lambda at: forward_step("core", refs, PLAN_UP, RELATIONS, sems, at))
    whole_copies = [
        pltpu.make_async_copy(
            own_in.at[half, pl.ds(0, HALF)],
            whole_in.at[pl.ds(half * HALF, HALF)],
            local_sem.at[3 + half],
        )
        for half in range(2)
    ]
    for whole_copy in whole_copies:
        whole_copy.start()
    tile = 512

    def up_copy(at, slot):
        return pltpu.make_async_copy(
            up_stage.at[slot],
            slope.at[:, pl.ds(pl.multiple_of(at * tile, LANES), tile)],
            up_sem.at[slot],
        )

    def down_grad_copy(at, slot):
        return pltpu.make_async_copy(
            down_stage.at[slot],
            grad_down.at[:, pl.ds(pl.multiple_of(at * tile, LANES), tile)],
            down_sem.at[slot],
        )

    traded(1)

    def shape_branch(at):
        columns = pl.ds(pl.multiple_of(at * 256, LANES), 256)
        gate = modulation[:, pl.ds(pl.multiple_of(5 * D + at * 256, LANES), 256)]
        scaled = (grad_out[:, columns].astype(F32) * gate).astype(BF16)
        grad_branch[:, columns] = scaled
        flat = scaled.T
        for part in range(4):
            rows = pl.ds(pl.multiple_of((2 * at + part // 2) * 64, 64), 64)
            flat_branch[part % 2, rows] = flat[part * 64 : (part + 1) * 64]
        row_grads[1:2, columns] = jnp.sum(scaled.astype(F32), axis=0, keepdims=True)

    repeat(D // 256, shape_branch)
    keep("grad_out", "grad_branch")
    rows_away = remote(
        flat_branch.at[1 - c], flat_mate, rows_sem.at[0], rows_sem.at[1], near["core"]
    )
    rows_away.start()

    def wide_copy(at):
        columns = pl.ds(pl.multiple_of(at * tile, LANES), tile)
        return remote(
            wide.at[:, columns],
            wide_mate.at[:, columns],
            wide_sem.at[at, 0],
            wide_sem.at[at, 1],
            near["core"],
        )

    def grow_down(at):
        slot = lax.rem(at, 2)

        @pl.when(at >= 2)
        def _():
            down_grad_copy(at - 2, slot).wait()

        wide_copy(at).wait_recv()
        for side in range(2):
            columns = pl.ds(pl.multiple_of(at * tile + side * 256, LANES), 256)
            down_stage[slot, :, side * 256 : (side + 1) * 256] = (
                multiply(flat_branch[c], wide[:, columns])
                + multiply(flat_mate[...], wide_mate[:, columns])
            ).astype(BF16)
        down_grad_copy(at, slot).start()

    def widen(at):
        slot = lax.rem(at, 2)

        @pl.when(at >= 2)
        def _():
            up_copy(at - 2, slot).wait()

        factor = math.sqrt(2.0 / math.pi)
        for side in range(2):
            start = at * tile + side * 256
            value = from_weights(input_two, own_in, 4 * D + start, 256) + bias_of(
                own_in, 3 * D + start, 256
            )
            square = value * value
            bent = jnp.tanh(factor * value * (1.0 + 0.044715 * square))
            half_up = 0.5 + 0.5 * bent
            up_stage[slot, :, side * 256 : (side + 1) * 256] = (
                half_up
                + 0.5
                * value
                * (1.0 - bent * bent)
                * (factor + 3.0 * 0.044715 * factor * square)
            ).astype(BF16)
            wide[:, pl.ds(pl.multiple_of(start, LANES), 256)] = (value * half_up).astype(BF16)
        up_copy(at, slot).start()
        wide_copy(at).start()

        @pl.when(at >= 1)
        def _():
            grow_down(at - 1)

        @pl.when(at == 1)
        def _():
            forward_step("tick", refs, PLAN_DOWN, ("x", "y"), sems, 0)

        @pl.when(at == FF // tile - 1)
        def _():
            forward_step("tick", refs, PLAN_DOWN, ("xy",), sems, 0)

    rows_away.wait_recv()
    repeat(FF // tile, widen)
    grow_down(FF // tile - 1)
    for at in (FF // tile - 2, FF // tile - 1):
        up_copy(at, at % 2).wait()
        down_grad_copy(at, at % 2).wait()
    down.wait()

    def narrow_down(at):
        columns = pl.ds(pl.multiple_of(at * 256, LANES), 256)
        value = bias_of(own_in, 7 * D + at * 256, 256)
        for side in range(2):
            value += multiply(
                wide[:, side * FF_PART : (side + 1) * FF_PART],
                own_down[columns, side * FF_PART : (side + 1) * FF_PART],
                BOTH_LAST,
            )
        gate = modulation[:, pl.ds(pl.multiple_of(5 * D + at * 256, LANES), 256)]
        block_out[:, columns] = (middle[:, columns] + gate * value).astype(BF16)
        towards = grad_out[:, columns].astype(F32)
        row_grads[0:1, columns] = jnp.sum(towards * value, axis=0, keepdims=True)

    forward_step("core", refs, PLAN_DOWN, RELATIONS, sems, 0)
    down_copy = pltpu.make_async_copy(own_down, whole_down, local_sem.at[5])
    down_copy.start()
    repeat(PLANES, narrow_down)

    repeat(SUBS, lambda at: forward_step("drain", refs, PLAN_ALL, RELATIONS, sems, at))
    repeat(DP - 1, lambda at: cond_copy(at).wait_send())

    @pl.when(dp < 7)
    def _():
        def sent(at):
            @pl.when(elsewhere(at))
            def _():
                mod_copy(at).wait_send()

        repeat(2 * DP, sent)

    for whole_copy in whole_copies:
        whole_copy.wait()
    down_copy.wait()
    rows_away.wait_send()
    repeat(FF // tile, lambda at: wide_copy(at).wait_send())
    for one in kept.values():
        one.wait()


def run_forward(low_in, low_down, hidden_in, cotangent, condition):
    shape = jax.ShapeDtypeStruct
    rows = TOKENS_HERE
    wide, flat = shape((rows, D), BF16), shape((rows, D), F32)
    both = shape((2 * rows, D), BF16)
    outs = [
        (shape((D, KEPT), BF16), pl.ANY),
        (shape((D, FF), BF16), pl.ANY),
        (wide, pl.ANY),
        (wide, pl.ANY),
        (shape((DP, 1, D), F32), pltpu.VMEM),
        (shape((1, 7 * WIDE), F32), pltpu.VMEM),
        (wide, pl.ANY),
        (wide, pl.ANY),
        (both, pl.ANY),
        (both, pl.ANY),
        (wide, pl.ANY),
        (shape((HEADS, 1, rows), F32), pltpu.VMEM),
        (flat, pl.ANY),
        (flat, pl.ANY),
        (wide, pl.ANY),
        (shape((rows, FF), BF16), pl.ANY),
        (wide, pl.ANY),
        (shape((8, D), F32), pltpu.VMEM),
        (wide, pltpu.VMEM),
        (shape((D // 2, FF), BF16), pl.ANY),
    ]
    kept = (wide, wide, wide, wide, both, both, wide, flat, flat, wide, wide)
    dma = pltpu.SemaphoreType.DMA
    return pl.pallas_call(
        forward_kernel,
        out_shape=[one for one, _ in outs],
        in_specs=[pl.BlockSpec(memory_space=pl.ANY)] * 4
        + [pl.BlockSpec(memory_space=pltpu.VMEM)],
        out_specs=[pl.BlockSpec(memory_space=where) for _, where in outs],
        scratch_shapes=[
            pltpu.VMEM((2, TALL, KEPT), BF16),
            pltpu.VMEM((D, FF), BF16),
            pltpu.VMEM((TALL, WIDE), BF16),
            pltpu.VMEM((DP, 1, WIDE), F32),
            pltpu.VMEM((14, 1, WIDE), F32),
            pltpu.VMEM((2, rows, 512), BF16),
            pltpu.VMEM((rows, FF), BF16),
            pltpu.VMEM((DP, D), BF16),
            pltpu.VMEM((2, D // 2, rows), BF16),
            pltpu.VMEM((D // 2, rows), BF16),
            pltpu.VMEM((rows, FF), BF16),
            pltpu.VMEM((2, D // 2, 512), BF16),
            dma((SLOTS, 5)),
            dma((SLOTS, 2)),
            dma((SLOTS,)),
            dma((6,)),
            dma((DP,)),
            dma((DP,)),
            dma((2 * DP,)),
            dma((14,)),
            dma((2, 3)),
            dma((2, 2)),
            dma((2,)),
            dma((2,)),
            dma((2,)),
            dma((FF // 512, 2)),
        ]
        + [pltpu.VMEM(one.shape, one.dtype) for one in kept]
        + [dma((len(kept),))],
        compiler_params=pltpu.CompilerParams(
            collective_id=0, has_side_effects=True, vmem_limit_bytes=62 * 2**20
        ),
        name="forward",
    )(low_in, low_down, hidden_in, cotangent, condition)


GRAD_SUBS = 8
GRAD_ROWS = HALF // GRAD_SUBS


class BroadGrad:
    height, width, subs, source_column = GRAD_ROWS, WIDE, GRAD_SUBS, 0
    split = GRAD_ROWS // 2
    lag = 1

    @staticmethod
    def holds(zs, xs, cs):
        return (zs * 2 + xs) * 2 + cs >= 7

    @staticmethod
    def corner(zs, xs, ys, cs, sub):
        column = jnp.maximum(((zs * 2 + xs) * 2 + cs) * WIDE - LOW, 128)
        return (
            pl.multiple_of(ys * HALF + sub * GRAD_ROWS, GRAD_ROWS),
            pl.multiple_of(column, 128),
        )


class HighGrad(BroadGrad):
    split = 48
    lag = 2


class NarrowGrad:
    height, width, subs, source_column = HALF, 128, 1, WIDE - 128
    split = HALF // 2
    lag = 1

    @staticmethod
    def holds(zs, xs, cs):
        return (zs * 2 + xs) * 2 + cs == 6

    @staticmethod
    def corner(zs, xs, ys, cs, sub):
        return (pl.multiple_of(ys * HALF, HALF), 0)


def reduce_block(what, refs, kind, zs, plane_at, planes, relation, sub, sems, valid):
    grads, first_column, owned, buffers = refs
    from_core, from_x, from_y, from_low, from_high, half_a, half_b = buffers
    send_sem, recv_sem = sems
    z, x, c, y = place()
    near = neighbours()
    xs = 1 - x if "x" in relation else x
    ys = 1 - y if "y" in relation else y
    flat = plane_at * kind.subs + sub
    count = planes * kind.subs
    kin = RELATIONS.index(relation)
    slot = kin * count + flat
    rows, half_rows = kind.height, kind.split

    def remote(source, target, index, arrival, key):
        return pltpu.make_async_remote_copy(
            src_ref=source,
            dst_ref=target,
            send_sem=send_sem.at[slot, index],
            recv_sem=recv_sem.at[arrival, flat],
            device_id=near[key],
            device_id_type=MESH,
        )

    def share(cs):
        row, column = kind.corner(zs, xs, ys, cs, sub)
        column = jnp.clip(column - first_column, 0, grads.shape[1] - kind.width)
        return (pl.ds(row, rows), pl.ds(pl.multiple_of(column, 128), kind.width))

    total = from_core.at[slot]
    across = remote(grads.at[share(1 - c)], total, 2, kin, "core")
    other = valid & kind.holds(zs, xs, 1 - c)
    if what == "across":
        pl.when(other)(across.start)
        return
    if what == "drain":
        pl.when(other)(across.wait_send)
    valid = valid & kind.holds(zs, xs, c)
    part_a = from_core.at[slot, pl.ds(0, half_rows)]
    part_b = from_core.at[slot, pl.ds(half_rows, rows - half_rows)]
    if relation == "xy":
        sends = [
            (valid, remote(part_a, half_a.at[flat], 0, 4, "y")),
            (valid, remote(part_b, half_b.at[flat], 1, 5, "x")),
        ]
    elif relation == "x":
        sends = [(valid, remote(total, from_x.at[flat], 0, 6, "x"))]
    elif relation == "y":
        sends = [(valid, remote(total, from_y.at[flat], 0, 7, "y"))]
    else:
        sends = [
            (valid & (z < zs), remote(total, from_low.at[flat], 0, 8, "up")),
            (valid & (z > zs), remote(total, from_high.at[flat], 1, 9, "down")),
        ]
    if what == "drain":
        for condition, descriptor in sends:
            pl.when(condition)(descriptor.wait_send)
        return

    @pl.when(valid)
    def _():
        remote(total, total, 2, kin, "core").wait_recv()
        value = from_core[slot].astype(F32) + grads[share(c)].astype(F32)
        if relation == "xy":
            from_core[slot] = value.astype(BF16)
        elif relation == "x":
            remote(half_a.at[flat], half_a.at[flat], 0, 4, "y").wait_recv()
            from_core[slot, pl.ds(half_rows, rows - half_rows)] = value[half_rows:].astype(BF16)
            from_core[slot, pl.ds(0, half_rows)] = (
                value[:half_rows] + half_a[flat].astype(F32)
            ).astype(BF16)
        elif relation == "y":
            remote(half_b.at[flat], half_b.at[flat], 1, 5, "x").wait_recv()
            from_core[slot, pl.ds(0, half_rows)] = value[:half_rows].astype(BF16)
            from_core[slot, pl.ds(half_rows, rows - half_rows)] = (
                value[half_rows:] + half_b[flat].astype(F32)
            ).astype(BF16)
        else:
            remote(from_x.at[flat], from_x.at[flat], 0, 6, "x").wait_recv()
            remote(from_y.at[flat], from_y.at[flat], 0, 7, "y").wait_recv()
            value += from_x[flat].astype(F32) + from_y[flat].astype(F32)

            @pl.when((z <= zs) & (z > 0))
            def _():
                remote(from_low.at[flat], from_low.at[flat], 0, 8, "up").wait_recv()

            @pl.when((z >= zs) & (z < PLANES - 1))
            def _():
                remote(from_high.at[flat], from_high.at[flat], 1, 9, "down").wait_recv()

            def low():
                return jnp.where(z > 0, from_low[flat].astype(F32), 0.0)

            def high():
                return jnp.where(z < PLANES - 1, from_high[flat].astype(F32), 0.0)

            @pl.when(z < zs)
            def _():
                from_core[slot] = (value + low()).astype(BF16)

            @pl.when(z > zs)
            def _():
                from_core[slot] = (value + high()).astype(BF16)

            @pl.when(z == zs)
            def _():
                owned[
                    pl.ds(pl.multiple_of(sub * rows, rows), rows),
                    pl.ds(kind.source_column, kind.width),
                ] = value + low() + high()

    for condition, descriptor in sends:
        pl.when(condition)(descriptor.start)


def reduce_step(what, refs, plan, sems, at):
    z = place()[0]
    for kind, planes in plan:
        name = kind.__name__
        for plane_at, zs in enumerate(planes):
            for relation in ("xy", "x", "y", "own"):
                sub = at
                if what == "tick":
                    depth = 0
                    if relation == "own":
                        depth = by_plane(
                            z,
                            [
                                place_z
                                if place_z < zs
                                else max(place_z, 3 - place_z)
                                if place_z == zs
                                else 3 - place_z
                                for place_z in range(PLANES)
                            ],
                        )
                    sub = at - kind.lag * (2 - HOPS[relation] + depth)
                reduce_block(
                    what,
                    refs[name],
                    kind,
                    zs,
                    plane_at,
                    len(planes),
                    relation,
                    jnp.clip(sub, 0, kind.subs - 1),
                    sems[name],
                    (sub >= 0) & (sub < kind.subs),
                )


def landing(kind, planes):
    count = planes * kind.subs
    full = pltpu.VMEM((count, kind.height, kind.width), BF16)
    half_a = pltpu.VMEM((count, kind.split, kind.width), BF16)
    half_b = pltpu.VMEM((count, kind.height - kind.split, kind.width), BF16)
    sums = pltpu.VMEM((4 * count, kind.height, kind.width), BF16)
    return [sums] + [full] * 4 + [half_a, half_b]


def landing_signals(kind, planes):
    count = planes * kind.subs
    return [pltpu.SemaphoreType.DMA((4 * count, 3)), pltpu.SemaphoreType.DMA((10, count))]


def greet_near():
    z, x, c, y = place()
    near = neighbours()
    barrier = pltpu.get_barrier_semaphore()
    for key in ("x", "y", "core"):
        pl.semaphore_signal(barrier, inc=1, device_id=near[key], device_id_type=MESH)

    @pl.when(z < PLANES - 1)
    def _():
        pl.semaphore_signal(barrier, inc=1, device_id=near["up"], device_id_type=MESH)

    @pl.when(z > 0)
    def _():
        pl.semaphore_signal(barrier, inc=1, device_id=near["down"], device_id_type=MESH)

    middle = (z > 0) & (z < PLANES - 1)

    @pl.when(middle)
    def _():
        pl.semaphore_wait(barrier, 5)

    @pl.when(jnp.logical_not(middle))
    def _():
        pl.semaphore_wait(barrier, 4)


REDUCE_HIGH = ((HighGrad, (3,)),)
REDUCE_LOW = ((BroadGrad, (1, 2)), (NarrowGrad, (1,)))
HIGH_STEPS = GRAD_SUBS + 5 * HighGrad.lag
LOW_STEPS = GRAD_SUBS + 4
HIGH_FIRST = FF // 8


def attend_back(
    pair, queries, keys, values, mixed, grad_mixed, log_totals, grad_query, grad_key, grad_value
):
    columns = pl.ds(pl.multiple_of(pair * LANES, LANES), LANES)
    key_block = keys[:, columns]
    value_block = values[:, columns]
    key_flat = key_block.T
    key_sum, value_sum = None, None
    step = 256
    for part in range(TOKENS_HERE // step):
        rows = pl.ds(part * step, step)
        grad_block = grad_mixed[rows, columns]
        product = (grad_block.astype(F32) * mixed[rows, columns].astype(F32)).T
        query_parts = []
        heads = zip(two_heads(queries[rows, columns]), two_heads(grad_block))
        for head, (query_head, grad_head) in enumerate(heads):
            scores = multiply(key_block, query_head, BOTH_LAST)
            weights = jnp.exp(scores * HEAD_DIM**-0.5 - log_totals[2 * pair + head, :, rows])
            grad_weights = multiply(value_block, grad_head, BOTH_LAST)
            inner = jnp.sum(
                product[HEAD_DIM * head : HEAD_DIM * (head + 1)], axis=0, keepdims=True
            )
            grad_scores = (weights * (grad_weights - inner)).astype(BF16)
            value_term = multiply(weights.astype(BF16), grad_head)
            key_term = multiply(grad_scores, query_head)
            value_sum = value_term if value_sum is None else value_sum + value_term
            key_sum = key_term if key_sum is None else key_sum + key_term
            query_parts.append(multiply(key_flat, grad_scores))
        joined = jnp.concatenate([query_parts[0][:HEAD_DIM], query_parts[1][HEAD_DIM:]], axis=0)
        grad_query[rows, columns] = (joined * HEAD_DIM**-0.5).T.astype(BF16)
    grad_key[:, columns] = (key_sum * HEAD_DIM**-0.5).astype(BF16)
    grad_value[:, columns] = value_sum.astype(BF16)


def backward_kernel(
    queries_in,
    keys_in,
    values_in,
    mixed_in,
    grad_mixed_in,
    log_totals_in,
    grads_in,
    input_one_in,
    hidden_in,
    grad_middle_in,
    grad_attn_in,
    scale_one,
    gate_one_sum,
    shift_two_sum,
    scale_two_sum,
    row_grads,
    bias_out_sum,
    bias_up_sum,
    whole_in,
    owned,
    input_grad,
    input_low,
    sums,
    grad_low,
    queries,
    keys,
    values,
    mixed,
    grad_mixed,
    log_totals,
    grads,
    input_one,
    hidden,
    grad_middle,
    grad_attn,
    load_sem,
    grad_query,
    grad_key,
    grad_value,
    row_sums,
    key_all,
    value_all,
    key_mate,
    value_mate,
    flat_one,
    weight_stage,
    grad_stage,
    grad_one,
    mate_sem,
    weight_sem,
    grad_sem,
    *scratch,
):
    dp = lax.axis_index("dp")
    near = neighbours()
    refs = {"HighGrad": (grads, 4 * D, owned, scratch[:7])}
    sems = {"HighGrad": scratch[7:9]}
    tile = 512
    tiles = 3 * D // tile
    loads = [
        pltpu.make_async_copy(source, target, load_sem.at[index])
        for index, (source, target) in enumerate(
            (
                (grads_in, grads),
                (input_one_in, input_one),
                (queries_in, queries),
                (keys_in, keys),
                (values_in, values),
                (mixed_in, mixed),
                (grad_mixed_in, grad_mixed),
                (log_totals_in, log_totals),
                (hidden_in, hidden),
                (grad_middle_in, grad_middle),
                (grad_attn_in, grad_attn),
            )
        )
    ]
    for load in loads:
        load.start()

    def weight_copy(at, slot):
        return pltpu.make_async_copy(
            whole_in.at[:, pl.ds(pl.multiple_of(at * tile, LANES), tile)],
            weight_stage.at[slot],
            weight_sem.at[slot],
        )

    def grad_copy(at, slot):
        return pltpu.make_async_copy(
            grad_stage.at[slot],
            grad_low.at[:, pl.ds(pl.multiple_of(at * tile, LANES), tile)],
            grad_sem.at[slot],
        )

    weight_copy(0, 0).start()
    greet_near()
    loads[0].wait()
    repeat(GRAD_SUBS, lambda at: reduce_step("across", refs, REDUCE_HIGH, sems, at))

    @pl.when(dp < 12)
    def _():
        owned[...] = jnp.zeros_like(owned)

    for load in loads[1:]:
        load.wait()

    def flatten(source):
        def go(at):
            columns = pl.ds(pl.multiple_of(at * 256, LANES), 256)
            flat_one[pl.ds(pl.multiple_of(at * 256, 256), 256)] = source[:, columns].T

        repeat(D // 256, go)

    flatten(input_one)

    def mates(pair):
        columns = pl.ds(pl.multiple_of(pair * LANES, LANES), LANES)
        return [
            pltpu.make_async_remote_copy(
                src_ref=source.at[HALF:, columns],
                dst_ref=target.at[:, columns],
                send_sem=mate_sem.at[pair, 2 * index],
                recv_sem=mate_sem.at[pair, 2 * index + 1],
                device_id=near["core"],
                device_id_type=MESH,
            )
            for index, (source, target) in enumerate(((key_all, key_mate), (value_all, value_mate)))
        ]

    def attention(pair):
        attend_back(
            pair,
            queries,
            keys,
            values,
            mixed,
            grad_mixed,
            log_totals,
            grad_query,
            key_all,
            value_all,
        )
        for mate in mates(pair):
            mate.start()
        reduce_step("tick", refs, REDUCE_HIGH, sems, pair)

    repeat(PAIRS, attention)
    for source, target, total, index in (
        (key_all, key_mate, grad_key, 0),
        (value_all, value_mate, grad_value, 1),
    ):
        repeat(PAIRS, lambda pair: mates(pair)[index].wait())
        total[...] = (source[:HALF].astype(F32) + target[...].astype(F32)).astype(BF16)

    grad_one[...] = jnp.zeros_like(grad_one)

    def project_back(source, base):
        def go(at):
            slot = lax.rem(at, 2)
            weight_copy(at, slot).wait()

            @pl.when(at + 1 < tiles)
            def _():
                weight_copy(at + 1, 1 - slot).start()

            @pl.when(at >= 2)
            def _():
                grad_copy(at - 2, slot).wait()

            columns = pl.ds(pl.multiple_of((at - base) * tile, LANES), tile)
            for side in range(2):
                part = slice(side * 512, (side + 1) * 512)
                grad_one[:, part] += multiply(
                    source[:, columns], weight_stage[slot, part], BOTH_LAST
                )
                narrow = pl.ds(pl.multiple_of((at - base) * tile + side * 256, LANES), 256)
                grad_stage[slot, :, side * 256 : (side + 1) * 256] = multiply(
                    flat_one[...], source[:, narrow]
                ).astype(BF16)
            grad_copy(at, slot).start()

            reduce_step("tick", refs, REDUCE_HIGH, sems, at + PAIRS)

        def run(at, carried):
            go(at + base)
            return carried

        lax.fori_loop(0, D // tile, run, 0)

    project_back(grad_query, 0)
    project_back(grad_key, D // tile)
    project_back(grad_value, 2 * D // tile)

    flatten(mixed)

    def project_out_back(part):
        at = part + tiles
        slot = lax.rem(at, 2)
        grad_copy(at - 2, slot).wait()
        for side in range(2):
            narrow = pl.ds(pl.multiple_of(part * tile + side * 256, LANES), 256)
            grad_stage[slot, :, side * 256 : (side + 1) * 256] = multiply(
                flat_one[...], grad_attn[:, narrow]
            ).astype(BF16)
        grad_copy(at, slot).start()
        reduce_step("tick", refs, REDUCE_HIGH, sems, at + PAIRS)

    repeat(D // tile, project_out_back)
    row_sums[...] = jnp.zeros_like(row_sums)

    def shape_back(at):
        rows = pl.ds(pl.multiple_of(at * 128, 128), 128)
        value = hidden[rows].astype(F32)
        center = value - jnp.mean(value, axis=-1, keepdims=True)
        inverse = lax.rsqrt(jnp.mean(center * center, axis=-1, keepdims=True) + norm_eps)
        normed = center * inverse
        towards = grad_one[rows]
        row_sums[0:1] += jnp.sum(towards, axis=0, keepdims=True)
        row_sums[1:2] += jnp.sum(towards * normed, axis=0, keepdims=True)
        row_sums[2:3] += jnp.sum(grad_query[rows].astype(F32), axis=0, keepdims=True)
        row_sums[3:4] += jnp.sum(grad_value[rows].astype(F32), axis=0, keepdims=True)
        scaled = towards * (1.0 + scale_one[...])
        result = grad_middle[rows] + inverse * (
            scaled
            - jnp.mean(scaled, axis=-1, keepdims=True)
            - normed * jnp.mean(scaled * normed, axis=-1, keepdims=True)
        )
        input_grad[rows] = result
        input_low[rows] = result.astype(BF16)
        reduce_step("tick", refs, REDUCE_HIGH, sems, at + PAIRS + tiles + D // tile)

    repeat(4, shape_back)
    for index in range(2):
        sums[:, index * D : (index + 1) * D] = row_sums[index : index + 1]
        start = 6 * D + WIDE + index * D
        sums[:, start : start + D] = row_sums[index + 2 : index + 3]
    sums[:, 2 * D : 3 * D] = gate_one_sum[...]
    sums[:, 3 * D : 4 * D] = shift_two_sum[...]
    sums[:, 4 * D : 5 * D] = scale_two_sum[...]
    sums[:, 5 * D : 6 * D] = row_grads[0:1]
    sums[:, 6 * D : 6 * D + WIDE] = jnp.zeros((1, WIDE), F32)
    sums[:, 8 * D + WIDE : 9 * D + WIDE] = bias_out_sum[...]
    sums[:, 9 * D + WIDE : 9 * D + WIDE + FF] = bias_up_sum[...]
    sums[:, 9 * D + WIDE + FF :] = row_grads[1:2]
    for at in (tiles + D // tile - 2, tiles + D // tile - 1):
        grad_copy(at, at % 2).wait()
    repeat(GRAD_SUBS, lambda at: reduce_step("drain", refs, REDUCE_HIGH, sems, at))


def run_backward(*given):
    shape = jax.ShapeDtypeStruct
    rows = TOKENS_HERE
    vmem = pl.BlockSpec(memory_space=pltpu.VMEM)
    hbm = pl.BlockSpec(memory_space=pl.ANY)
    dma = pltpu.SemaphoreType.DMA
    return pl.pallas_call(
        backward_kernel,
        out_shape=[
            shape((HALF, WIDE), F32),
            shape((rows, D), F32),
            shape((rows, D), BF16),
            shape((1, VECTOR), F32),
            shape((D, 4 * D), BF16),
        ],
        in_specs=[hbm] * 11 + [vmem] * 7 + [hbm],
        out_specs=[vmem] * 4 + [hbm],
        scratch_shapes=[pltpu.VMEM(one.shape, one.dtype) for one in given[:11]]
        + [dma((11,))]
        + [pltpu.VMEM((rows, D), BF16)] * 3
        + [pltpu.VMEM((8, D), F32)]
        + [pltpu.VMEM((2 * rows, D), BF16)] * 2
        + [pltpu.VMEM((rows, D), BF16)] * 2
        + [
            pltpu.VMEM((D, rows), BF16),
            pltpu.VMEM((2, D, 512), BF16),
            pltpu.VMEM((2, D, 512), BF16),
            pltpu.VMEM((rows, D), F32),
            dma((PAIRS, 4)),
            dma((2,)),
            dma((2,)),
        ]
        + landing(HighGrad, 1)
        + landing_signals(HighGrad, 1),
        compiler_params=pltpu.CompilerParams(
            collective_id=1, has_side_effects=True, vmem_limit_bytes=62 * 2**20
        ),
        cost_estimate=pl.CostEstimate(
            flops=12 * 2 * 512 * 1024 * 1024, bytes_accessed=60 * 2**20, transcendentals=2**23
        ),
        name="backward",
    )(*given)


VECTOR = 17 * WIDE


def finish_kernel(
    grad_low,
    grad_up,
    low_in,
    active_rows,
    condition,
    sums,
    owned_high,
    down_sum,
    owned,
    cond_grad,
    bias_grad,
    owned_down,
    grads,
    ada_weights,
    sum_mate,
    sum_pieces,
    ada_in,
    cond_piece,
    cond_in,
    down_mate,
    bias_parts,
    local_sem,
    mate_sem,
    down_sem,
    piece_send,
    ada_recv,
    bias_recv,
    cond_send,
    cond_recv,
    *scratch,
):
    z, x, c, y = place()
    dp = (z * 2 + x) * 2 + c
    near = neighbours()
    refs = {
        "BroadGrad": (grads, 0, owned, scratch[0:7]),
        "NarrowGrad": (grads, 0, owned, scratch[7:14]),
    }
    sems = {"BroadGrad": scratch[14:16], "NarrowGrad": scratch[16:18]}

    def remote(source, target, sent, arrived, device):
        return pltpu.make_async_remote_copy(
            src_ref=source,
            dst_ref=target,
            send_sem=sent,
            recv_sem=arrived,
            device_id=device,
            device_id_type=MESH,
        )

    loads = [
        pltpu.make_async_copy(grad_low, grads.at[:, : 4 * D], local_sem.at[0]),
        pltpu.make_async_copy(
            grad_up.at[:, :HIGH_FIRST], grads.at[:, 4 * D : 4 * D + HIGH_FIRST], local_sem.at[1]
        ),
        pltpu.make_async_copy(low_in.at[pl.ds(0, HALF)], ada_weights, local_sem.at[2]),
    ]
    for load in loads:
        load.start()
    owned[...] = owned_high[...]
    greet_all()
    mate = remote(sums, sum_mate, mate_sem.at[0], mate_sem.at[1], near["core"])
    mate.start()
    down_away = remote(
        down_sum.at[:, pl.ds(pl.multiple_of((1 - y) * FF_PART, LANES), FF_PART)],
        down_mate,
        down_sem.at[0],
        down_sem.at[1],
        near["y"],
    )
    down_away.start()

    for load in loads[:2]:
        load.wait()
    repeat(GRAD_SUBS, lambda at: reduce_step("across", refs, REDUCE_LOW, sems, at))
    repeat(2, lambda at: reduce_step("tick", refs, REDUCE_LOW, sems, at))

    mate.wait()
    for index in range(17):
        columns = slice(index * WIDE, (index + 1) * WIDE)
        piece = sums[:, columns] + sum_mate[:, columns]
        if index < 7:
            piece = piece.astype(BF16).astype(F32)
        sum_pieces[index] = piece
    latent = (z * 2 + x) * 2 + y

    def piece_target(at):
        return jnp.where(at < 7, at, at - 1)

    def piece_copy(at, target, arrived):
        return remote(
            sum_pieces.at[at], target, piece_send.at[at], arrived, (piece_target(at), c)
        )

    def each_piece(act, keep):
        def go(at):
            mine = (piece_target(at) == dp) & (y == c)

            @pl.when(jnp.logical_not(mine) & (at < 7))
            def _():
                act(piece_copy(at, ada_in.at[latent], ada_recv.at[latent]))

            @pl.when(jnp.logical_not(mine) & (at >= 7))
            def _():
                act(piece_copy(at, bias_parts.at[latent], bias_recv.at[latent]))

            if keep:

                @pl.when(mine & (at < 7))
                def _():
                    ada_in[latent] = sum_pieces[at]

                @pl.when(mine & (at >= 7))
                def _():
                    bias_parts[latent] = sum_pieces[at]

        repeat(17, go)

    each_piece(lambda copy: copy.start(), True)
    repeat(3, lambda at: reduce_step("tick", refs, REDUCE_LOW, sems, at + 2))

    def from_latent(at, target, arrived):
        mine = (at // 2 == z * 2 + x) & (lax.rem(at, 2) == y) & (c == y)

        @pl.when(jnp.logical_not(mine))
        def _():
            remote(
                sum_pieces.at[0], target.at[at], piece_send.at[0], arrived.at[at], near["x"]
            ).wait_recv()

    loads[2].wait()

    @pl.when(dp < 7)
    def _():
        repeat(DP, lambda at: from_latent(at, ada_in, ada_recv))
        gathered = jnp.concatenate([ada_in[index] for index in range(DP)], axis=0)
        bias_grad[...] = jnp.sum(gathered, axis=0, keepdims=True)
        narrow = gathered.astype(BF16)
        owned[...] += multiply(active_rows[...], narrow, BOTH_FIRST)
        part = multiply(narrow, ada_weights[...], BOTH_LAST)
        for index in range(DP):
            cond_piece[index] = part[index : index + 1]

    @pl.when(dp >= 7)
    def _():
        bias_grad[...] = jnp.zeros_like(bias_grad)

    def cond_copy(at):
        return remote(
            cond_piece.at[at // 2],
            cond_in.at[dp * 2 + y],
            cond_send.at[at],
            cond_recv.at[dp * 2 + y],
            (at // 2, lax.rem(at, 2)),
        )

    def each_cond(act, keep):
        def go(at):
            mine = at == dp * 2 + y

            @pl.when(jnp.logical_not(mine))
            def _():
                act(cond_copy(at))

            if keep:

                @pl.when(mine)
                def _():
                    cond_in[dp * 2 + y] = cond_piece[at // 2]

        repeat(2 * DP, go)

    @pl.when(dp < 7)
    def _():
        each_cond(lambda copy: copy.start(), True)

    repeat(LOW_STEPS - 5, lambda at: reduce_step("tick", refs, REDUCE_LOW, sems, at + 5))

    def cond_arrived(at):
        @pl.when(at != dp * 2 + y)
        def _():
            remote(
                cond_piece.at[0], cond_in.at[at], cond_send.at[0], cond_recv.at[at], near["x"]
            ).wait_recv()

    repeat(14, cond_arrived)
    sides = []
    for side in range(2):
        total = cond_in[side]
        for index in range(1, 7):
            total = total + cond_in[2 * index + side]
        sides.append(total)
    value = condition[...].astype(F32)
    logistic = 1.0 / (1.0 + jnp.exp(-value))
    cond_grad[...] = jnp.concatenate(sides, axis=1) * (
        logistic * (1.0 + value * (1.0 - logistic))
    )

    @pl.when(dp >= 6)
    def _():
        repeat(DP, lambda at: from_latent(at, bias_parts, bias_recv))
        total = bias_parts[0]
        for index in range(1, DP):
            total = total + bias_parts[index]
        bias_grad[...] += total

    down_away.wait()
    owned_down[...] = down_sum[
        :, pl.ds(pl.multiple_of(y * FF_PART, LANES), FF_PART)
    ].astype(F32) + down_mate[...].astype(F32)
    each_piece(lambda copy: copy.wait_send(), False)

    @pl.when(dp < 7)
    def _():
        each_cond(lambda copy: copy.wait_send(), False)

    repeat(GRAD_SUBS, lambda at: reduce_step("drain", refs, REDUCE_LOW, sems, at))


def run_finish(
    grad_low,
    grad_up,
    low_in,
    active_rows,
    condition,
    sums,
    owned_high,
    down_sum,
):
    shape = jax.ShapeDtypeStruct
    dma = pltpu.SemaphoreType.DMA
    vmem = pl.BlockSpec(memory_space=pltpu.VMEM)
    hbm = pl.BlockSpec(memory_space=pl.ANY)
    return pl.pallas_call(
        finish_kernel,
        out_shape=[
            shape((HALF, WIDE), F32),
            shape((1, D), F32),
            shape((1, WIDE), F32),
            shape((64, FF_PART), F32),
        ],
        in_specs=[hbm] * 3 + [vmem] * 5,
        out_specs=[vmem] * 4,
        scratch_shapes=[
            pltpu.VMEM((D, 4 * D + HIGH_FIRST), BF16),
            pltpu.VMEM((HALF, WIDE), BF16),
            pltpu.VMEM((1, VECTOR), F32),
            pltpu.VMEM((17, 1, WIDE), F32),
            pltpu.VMEM((DP, 1, WIDE), F32),
            pltpu.VMEM((DP, 1, HALF), F32),
            pltpu.VMEM((14, 1, HALF), F32),
            pltpu.VMEM((64, FF_PART), BF16),
            pltpu.VMEM((DP, 1, WIDE), F32),
            dma((3,)),
            dma((2,)),
            dma((2,)),
            dma((17,)),
            dma((DP,)),
            dma((DP,)),
            dma((2 * DP,)),
            dma((14,)),
        ]
        + landing(BroadGrad, 2)
        + landing(NarrowGrad, 1)
        + landing_signals(BroadGrad, 2)
        + landing_signals(NarrowGrad, 1),
        compiler_params=pltpu.CompilerParams(
            collective_id=2, has_side_effects=True, vmem_limit_bytes=60 * 2**20
        ),
        name="finish",
    )(
        grad_low,
        grad_up,
        low_in,
        active_rows,
        condition,
        sums,
        owned_high,
        down_sum,
    )


def swap_away(values):
    pairs = []
    for index in range(2 * DP):
        y, c = index % 2, index // 2 % 2
        if y != c:
            pairs.append((index, index // 4 * 4 + y * 2 + c))
    return lax.ppermute(values, ("dp", "seq"), pairs)


def local(
    hidden_in,
    condition,
    cotangent,
    weights_in,
    weights_down,
    biases,
    moment_in,
    moment_down,
    moment_bias,
    square_in,
    square_down,
    square_bias,
):
    dp = lax.axis_index("dp")
    y = lax.axis_index("seq")
    side = WIDE // 2
    bias_row = jnp.pad(biases.astype(BF16)[None], ((0, 15), (0, side)))
    bias_row = jnp.where(y == 0, bias_row, jnp.roll(bias_row, side, axis=1))
    low_in = jnp.concatenate([weights_in.astype(BF16), bias_row], axis=0)
    (
        whole_in,
        whole_down,
        hidden,
        grad_out,
        cond_all,
        modulation,
        input_one,
        queries,
        keys,
        values,
        mixed,
        log_totals,
        attn_out,
        middle,
        input_two,
        slope,
        grad_branch,
        row_grads,
        block_out,
        grad_down,
    ) = run_forward(
        low_in,
        weights_down.astype(BF16).T,
        hidden_in[0],
        cotangent[0],
        condition,
    )
    at_home = lax.rem(dp, 2) == y
    block_swapped = swap_away(block_out)
    grad_out = grad_out.astype(F32)
    pieces = [modulation[:, part * D : (part + 1) * D] for part in range(6)]
    shift_one, scale_one, gate_one, shift_two, scale_two, gate_two = pieces

    def back_through(gradients, start, width):
        return lax.dot_general(
            gradients,
            whole_in[:, start : start + width],
            BOTH_LAST,
            preferred_element_type=F32,
        )

    def outer(left, right):
        return lax.dot_general(left, right, BOTH_FIRST, preferred_element_type=F32)

    def down_rows(total):
        return jnp.sum(total.astype(F32), axis=0, keepdims=True)

    down_sum = lax.psum_scatter(
        grad_down,
        "dp",
        scatter_dimension=0,
        axis_index_groups=[list(range(core, DP, 2)) for core in range(2)],
        tiled=True,
    )
    grad_act = jnp.dot(grad_branch, whole_down, preferred_element_type=F32)
    grad_upward = (grad_act * slope).astype(BF16)
    grad_up = outer(input_two, grad_upward).astype(BF16)
    grad_input_two = back_through(grad_upward, 4 * D, FF)
    normed_two, norm_pull_two = jax.vjp(layer_norm, middle)
    shift_two_grad = down_rows(grad_input_two)
    scale_two_grad = down_rows(grad_input_two * normed_two)
    grad_middle = grad_out + norm_pull_two(grad_input_two * (1.0 + scale_two))[0]
    grad_attn = (grad_middle * gate_one).astype(BF16)
    gate_one_grad = down_rows(grad_middle * attn_out)
    grad_mixed = back_through(grad_attn, 3 * D, D).astype(BF16)
    owned_high, input_grad, input_low, sums, grad_low = run_backward(
        queries,
        keys,
        values,
        mixed,
        grad_mixed,
        log_totals,
        grad_up,
        input_one,
        hidden,
        grad_middle,
        grad_attn,
        scale_one,
        gate_one_grad,
        shift_two_grad,
        scale_two_grad,
        row_grads,
        down_rows(grad_attn),
        down_rows(grad_upward),
        whole_in,
    )
    active_rows = lax.dynamic_slice_in_dim(
        jax.nn.silu(cond_all[:, 0]).astype(BF16), y * HALF, HALF, 1
    )
    owned_in, cond_grad, bias_grad, owned_down = run_finish(
        grad_low,
        grad_up,
        low_in,
        active_rows,
        condition,
        sums,
        owned_high,
        down_sum,
    )
    owned_down = owned_down.T
    input_low, owned_in = lax.optimization_barrier((input_low, owned_in))
    input_swapped = swap_away(input_low)
    input_grad = jnp.where(at_home, input_grad, input_swapped.astype(F32))
    block_out = jnp.where(at_home, block_out, block_swapped)
    owned_bias = lax.dynamic_slice_in_dim(bias_grad[0], y * side, side, 0)
    moments_in, squares_in, master_in = adamw_step(
        weights_in, moment_in, square_in, owned_in, rate_in
    )
    moments_down, squares_down, master_down = adamw_step(
        weights_down, moment_down, square_down, owned_down, rate_down
    )
    moments_bias, squares_bias, master_bias = adamw_step(
        biases, moment_bias, square_bias, owned_bias, rate_bias
    )
    return (
        block_out[None],
        input_grad[None],
        cond_grad,
        moments_in,
        moments_down,
        moments_bias,
        squares_in,
        squares_down,
        squares_bias,
        master_in,
        master_down,
        master_bias,
        master_in.astype(BF16),
        master_down.astype(BF16),
        master_bias.astype(BF16),
    )


def solution(mesh):
    return jax.shard_map(
        local if dict(mesh.shape) == {"dp": 16, "seq": 2} else local_general,
        mesh=mesh,
        in_specs=(
            P("dp", "seq", None),
            P("dp", None),
            P("dp", "seq", None),
            P("seq", "dp"),
            P("seq", "dp"),
            P(("dp", "seq")),
            P("seq", "dp"),
            P("seq", "dp"),
            P(("dp", "seq")),
            P("seq", "dp"),
            P("seq", "dp"),
            P(("dp", "seq")),
        ),
        out_specs=(
            P("dp", "seq", None),
            P("dp", "seq", None),
            P("dp", None),
            P("seq", "dp"),
            P("seq", "dp"),
            P(("dp", "seq")),
            P("seq", "dp"),
            P("seq", "dp"),
            P(("dp", "seq")),
            P("seq", "dp"),
            P("seq", "dp"),
            P(("dp", "seq")),
            P("seq", "dp"),
            P("seq", "dp"),
            P(("dp", "seq")),
        ),
        check_vma=False,
    )
```

```python
import math

import jax
import jax.numpy as jnp
from jax import lax
from jax.experimental import pallas as pl
from jax.experimental.pallas import tpu as pltpu
from jax.sharding import PartitionSpec as P

D = 1024
HEADS = 16
HEAD_DIM = 64
FF = 4096
STEP = 5


norm_eps = 1e-06
beta_first = 0.5
beta_second = 0.5
adam_eps = 1e-08
weight_decay = 0.01
rate_in = 0.03
rate_down = 0.016
rate_bias = 0.3


def layer_norm(values):
    center = values - jnp.mean(values, axis=-1, keepdims=True)
    return center * lax.rsqrt(jnp.mean(center * center, axis=-1, keepdims=True) + norm_eps)


def adamw_step(master, moment, square, gradient, step_rate):
    moment_new = beta_first * moment + (1.0 - beta_first) * gradient
    square_new = beta_second * square + (1.0 - beta_second) * gradient * gradient
    corrected = moment_new / (1.0 - beta_first**STEP)
    scale_sq = square_new / (1.0 - beta_second**STEP)
    master_new = master - step_rate * (
        corrected / (jnp.sqrt(scale_sq) + adam_eps) + weight_decay * master
    )
    return (moment_new, square_new, master_new)


def dense_map(values, matrix):
    return jnp.einsum("nld,de->nle", values, matrix, preferred_element_type=jnp.float32)


def dense_back(gradients, matrix):
    return jnp.einsum("nle,de->nld", gradients, matrix, preferred_element_type=jnp.float32)


def outer_sum(values, gradients):
    return jnp.einsum("nld,nle->de", values, gradients, preferred_element_type=jnp.float32)


def total_sum(values):
    return jnp.sum(values.astype(jnp.float32), axis=(0, 1))


def gather_weights(low_in, low_down, low_bias):
    seq_parts = (
        lax.all_gather(low_in, "seq", axis=0, tiled=True),
        lax.all_gather(low_down, "seq", axis=0, tiled=True),
        lax.all_gather(low_bias, "seq", axis=0, tiled=True),
    )
    whole_in, whole_down, bias_row = (
        lax.all_gather(seq_parts[0], "dp", axis=1, tiled=True),
        lax.all_gather(seq_parts[1], "dp", axis=1, tiled=True),
        lax.all_gather(seq_parts[2].reshape(1, -1), "dp", axis=1, tiled=True),
    )
    return (whole_in, whole_down, bias_row[0])


def head_layout():
    heads_here = math.gcd(HEADS, max(1, 128 // HEAD_DIM))
    return (heads_here, heads_here * HEAD_DIM, HEADS // heads_here)


def split_heads(values, lane_start, lane_count, heads_here):
    piece = lax.dynamic_slice_in_dim(values, lane_start, lane_count, 2)
    return piece.reshape(piece.shape[0], piece.shape[1], heads_here, HEAD_DIM)


def join_heads(stacked):
    moved = jnp.moveaxis(stacked, 0, 2)
    return moved.reshape(moved.shape[0], moved.shape[1], moved.shape[2] * moved.shape[3])


def attention_forward(queries, keys_all, values_all):
    heads_here, lane_count, head_steps = head_layout()
    scale_factor = HEAD_DIM ** (-0.5)

    def one_group(group_index):
        lane_start = group_index * lane_count
        query_part = split_heads(queries, lane_start, lane_count, heads_here)
        key_part = split_heads(keys_all, lane_start, lane_count, heads_here)
        value_part = split_heads(values_all, lane_start, lane_count, heads_here)
        scores = (
            jnp.einsum("nqhd,nkhd->nhqk", query_part, key_part, preferred_element_type=jnp.float32)
            * scale_factor
        )
        row_max = jnp.max(scores, axis=-1, keepdims=True)
        exponent = jnp.exp(scores - row_max)
        row_total = jnp.sum(exponent, axis=-1, keepdims=True)
        weights = (exponent / row_total).astype(jnp.bfloat16)
        attn_part = jnp.einsum(
            "nhqk,nkhd->nqhd", weights, value_part, preferred_element_type=jnp.float32
        )
        shaped = attn_part.reshape(attn_part.shape[0], attn_part.shape[1], lane_count)
        return (shaped, (row_max + jnp.log(row_total))[..., 0])

    stacked, log_totals = lax.map(one_group, jnp.arange(head_steps))
    return (join_heads(stacked), log_totals)


def attention_backward(queries, keys_all, values_all, log_totals, grad_mixed):
    heads_here, lane_count, head_steps = head_layout()
    scale_factor = HEAD_DIM ** (-0.5)

    def one_group(carried):
        group_index, log_part = carried
        lane_start = group_index * lane_count
        query_part = split_heads(queries, lane_start, lane_count, heads_here)
        key_part = split_heads(keys_all, lane_start, lane_count, heads_here)
        value_part = split_heads(values_all, lane_start, lane_count, heads_here)
        grad_part = split_heads(grad_mixed, lane_start, lane_count, heads_here)
        scores = (
            jnp.einsum("nqhd,nkhd->nhqk", query_part, key_part, preferred_element_type=jnp.float32)
            * scale_factor
        )
        probability = jnp.exp(scores - log_part[..., None])
        grad_prob = jnp.einsum(
            "nqhd,nkhd->nhqk", grad_part, value_part, preferred_element_type=jnp.float32
        )
        inner_sum = jnp.sum(probability * grad_prob, axis=-1, keepdims=True)
        grad_score = (probability * (grad_prob - inner_sum)).astype(jnp.bfloat16)
        grad_query = (
            jnp.einsum("nhqk,nkhd->nqhd", grad_score, key_part, preferred_element_type=jnp.float32)
            * scale_factor
        )
        grad_key = (
            jnp.einsum(
                "nhqk,nqhd->nkhd", grad_score, query_part, preferred_element_type=jnp.float32
            )
            * scale_factor
        )
        grad_value = jnp.einsum(
            "nhqk,nqhd->nkhd",
            probability.astype(jnp.bfloat16),
            grad_part,
            preferred_element_type=jnp.float32,
        )
        return (
            grad_query.reshape(grad_query.shape[0], grad_query.shape[1], lane_count),
            grad_key.reshape(grad_key.shape[0], grad_key.shape[1], lane_count),
            grad_value.reshape(grad_value.shape[0], grad_value.shape[1], lane_count),
        )

    query_terms, key_terms, value_terms = lax.map(one_group, (jnp.arange(head_steps), log_totals))
    return (join_heads(query_terms), join_heads(key_terms), join_heads(value_terms))


def local_general(
    hidden_in,
    condition,
    cotangent,
    weights_in,
    weights_down,
    biases,
    moment_in,
    moment_down,
    moment_bias,
    square_in,
    square_down,
    square_bias,
):
    low_in = weights_in.astype(jnp.bfloat16)
    low_down = weights_down.astype(jnp.bfloat16)
    low_bias = biases.astype(jnp.bfloat16)
    whole_in, whole_down, bias_all = gather_weights(low_in, low_down, low_bias)
    bias_float = bias_all.astype(jnp.float32)
    hidden = hidden_in.astype(jnp.float32)
    cond_float = condition.astype(jnp.float32)
    cond_act = jax.nn.silu(cond_float).astype(jnp.bfloat16)
    modulation = (
        jnp.dot(cond_act, whole_in[:, : 6 * D], preferred_element_type=jnp.float32)
        + bias_float[: 6 * D]
    )
    pieces = [modulation[:, None, part_index * D : (part_index + 1) * D] for part_index in range(6)]
    shift_one, scale_one, gate_one, shift_two, scale_two, gate_two = pieces
    normed_one = layer_norm(hidden)
    input_one = (normed_one * (1.0 + scale_one) + shift_one).astype(jnp.bfloat16)
    qkv_all = dense_map(input_one, whole_in[:, 6 * D : 9 * D])
    queries = (qkv_all[..., :D] + bias_float[6 * D : 7 * D]).astype(jnp.bfloat16)
    keys_local = qkv_all[..., D : 2 * D].astype(jnp.bfloat16)
    values_local = (qkv_all[..., 2 * D :] + bias_float[7 * D : 8 * D]).astype(jnp.bfloat16)
    keys_all, values_all = (
        lax.all_gather(keys_local, "seq", axis=1, tiled=True),
        lax.all_gather(values_local, "seq", axis=1, tiled=True),
    )
    attn_float, log_totals = attention_forward(queries, keys_all, values_all)
    attn_mixed = attn_float.astype(jnp.bfloat16)
    attn_out = dense_map(attn_mixed, whole_in[:, 9 * D : 10 * D]) + bias_float[8 * D : 9 * D]
    middle = hidden + gate_one * attn_out
    normed_two = layer_norm(middle)
    input_two = (normed_two * (1.0 + scale_two) + shift_two).astype(jnp.bfloat16)
    upward = dense_map(input_two, whole_in[:, 10 * D :]) + bias_float[9 * D : 9 * D + FF]
    activated = jax.nn.gelu(upward, approximate=True).astype(jnp.bfloat16)
    branch = dense_map(activated, whole_down) + bias_float[9 * D + FF :]
    block_out = (middle + gate_two * branch).astype(jnp.bfloat16)
    whole_in, whole_down, bias_all = gather_weights(low_in, low_down, low_bias)
    grad_out = cotangent.astype(jnp.float32)
    grad_branch = (grad_out * gate_two).astype(jnp.bfloat16)
    gate_two_grad = jnp.sum(grad_out * branch, axis=1)
    grad_down = outer_sum(activated, grad_branch)
    bias_down_grad = total_sum(grad_branch)
    grad_act = dense_back(grad_branch, whole_down)
    _, gelu_pull = jax.vjp(lambda inner_value: jax.nn.gelu(inner_value, approximate=True), upward)
    grad_upward = gelu_pull(grad_act)[0].astype(jnp.bfloat16)
    grad_up = outer_sum(input_two, grad_upward)
    bias_up_grad = total_sum(grad_upward)
    grad_input_two = dense_back(grad_upward, whole_in[:, 10 * D :])
    shift_two_grad = jnp.sum(grad_input_two, axis=1)
    scale_two_grad = jnp.sum(grad_input_two * normed_two, axis=1)
    _, norm_pull_two = jax.vjp(layer_norm, middle)
    grad_middle = grad_out + norm_pull_two(grad_input_two * (1.0 + scale_two))[0]
    grad_attn = (grad_middle * gate_one).astype(jnp.bfloat16)
    gate_one_grad = jnp.sum(grad_middle * attn_out, axis=1)
    grad_out_proj = outer_sum(attn_mixed, grad_attn)
    bias_out_grad = total_sum(grad_attn)
    grad_mixed = dense_back(grad_attn, whole_in[:, 9 * D : 10 * D]).astype(jnp.bfloat16)
    grad_query, key_terms, value_terms = attention_backward(
        queries, keys_all, values_all, log_totals, grad_mixed
    )
    key_grad, value_grad = (
        lax.psum_scatter(
            key_terms.astype(jnp.bfloat16), "seq", scatter_dimension=1, tiled=True
        ).astype(jnp.float32),
        lax.psum_scatter(
            value_terms.astype(jnp.bfloat16), "seq", scatter_dimension=1, tiled=True
        ).astype(jnp.float32),
    )
    grad_qkv = jnp.concatenate(
        [
            grad_query.astype(jnp.bfloat16),
            key_grad.astype(jnp.bfloat16),
            value_grad.astype(jnp.bfloat16),
        ],
        axis=-1,
    )
    grad_proj_qkv = outer_sum(input_one, grad_qkv)
    bias_query_grad = total_sum(grad_qkv[..., :D])
    bias_value_grad = total_sum(grad_qkv[..., 2 * D :])
    grad_input_one = dense_back(grad_qkv, whole_in[:, 6 * D : 9 * D])
    shift_one_grad = jnp.sum(grad_input_one, axis=1)
    scale_one_grad = jnp.sum(grad_input_one * normed_one, axis=1)
    _, norm_pull_one = jax.vjp(layer_norm, hidden)
    input_grad = grad_middle + norm_pull_one(grad_input_one * (1.0 + scale_one))[0]
    mod_terms = jnp.concatenate(
        [
            shift_one_grad,
            scale_one_grad,
            gate_one_grad,
            shift_two_grad,
            scale_two_grad,
            gate_two_grad,
        ],
        axis=-1,
    )
    mod_grad = lax.psum(mod_terms, "seq").astype(jnp.bfloat16)
    _, silu_pull = jax.vjp(jax.nn.silu, cond_float)
    cond_grad = silu_pull(
        jnp.einsum("ne,de->nd", mod_grad, whole_in[:, : 6 * D], preferred_element_type=jnp.float32)
    )[0]
    owner_mask = (lax.axis_index("seq") == 0).astype(jnp.float32)
    grad_ada = (
        jnp.einsum("nd,ne->de", cond_act, mod_grad, preferred_element_type=jnp.float32) * owner_mask
    )
    bias_ada_grad = jnp.sum(mod_grad.astype(jnp.float32), axis=0) * owner_mask
    grad_in_all = jnp.zeros((D, 10 * D + FF), jnp.float32)
    grad_in_all = grad_in_all.at[:, : 6 * D].set(grad_ada)
    grad_in_all = grad_in_all.at[:, 6 * D : 9 * D].set(grad_proj_qkv)
    grad_in_all = grad_in_all.at[:, 9 * D : 10 * D].set(grad_out_proj)
    grad_in_all = grad_in_all.at[:, 10 * D :].set(grad_up)
    bias_flat = jnp.concatenate(
        [
            bias_ada_grad,
            bias_query_grad,
            bias_value_grad,
            bias_out_grad,
            bias_up_grad,
            bias_down_grad,
        ]
    )
    summed_in, summed_down, summed_bias = (
        lax.psum_scatter(
            grad_in_all.astype(jnp.bfloat16), "dp", scatter_dimension=1, tiled=True
        ).astype(jnp.float32),
        lax.psum_scatter(
            grad_down.astype(jnp.bfloat16), "dp", scatter_dimension=1, tiled=True
        ).astype(jnp.float32),
        lax.psum_scatter(
            bias_flat.reshape(1, -1).astype(jnp.bfloat16), "dp", scatter_dimension=1, tiled=True
        ).astype(jnp.float32),
    )
    owned_in, owned_down, owned_bias = (
        lax.psum_scatter(
            summed_in.astype(jnp.bfloat16), "seq", scatter_dimension=0, tiled=True
        ).astype(jnp.float32),
        lax.psum_scatter(
            summed_down.astype(jnp.bfloat16), "seq", scatter_dimension=0, tiled=True
        ).astype(jnp.float32),
        lax.psum_scatter(
            summed_bias.reshape(-1).astype(jnp.bfloat16), "seq", scatter_dimension=0, tiled=True
        ).astype(jnp.float32),
    )
    moments_in, squares_in, master_in = adamw_step(
        weights_in, moment_in, square_in, owned_in, rate_in
    )
    moments_down, squares_down, master_down = adamw_step(
        weights_down, moment_down, square_down, owned_down, rate_down
    )
    moments_bias, squares_bias, master_bias = adamw_step(
        biases, moment_bias, square_bias, owned_bias, rate_bias
    )
    return (
        block_out,
        input_grad,
        cond_grad,
        moments_in,
        moments_down,
        moments_bias,
        squares_in,
        squares_down,
        squares_bias,
        master_in,
        master_down,
        master_bias,
        master_in.astype(jnp.bfloat16),
        master_down.astype(jnp.bfloat16),
        master_bias.astype(jnp.bfloat16),
    )


MESH = pl.DeviceIdType.MESH
WIDE = 896
LOW = 6 * D
KEPT = 4 * D + FF
PLANES = 4
HALF = D // 2
TALL = HALF + 16
SUBS = 3
SUB_ROWS = TALL // SUBS
FF_PART = FF // 2
DP = 16


def place():
    dp = lax.axis_index("dp")
    y = lax.axis_index("seq")
    return (dp // 4, lax.rem(dp // 2, 2), lax.rem(dp, 2), y)


def device_at(z, x, c, y):
    return ((z * 2 + x) * 2 + c, y)


def neighbours():
    z, x, c, y = place()
    return {
        "x": device_at(z, 1 - x, c, y),
        "y": device_at(z, x, c, 1 - y),
        "up": device_at(jnp.minimum(z + 1, PLANES - 1), x, c, y),
        "down": device_at(jnp.maximum(z - 1, 0), x, c, y),
        "core": device_at(z, x, 1 - c, y),
        "swap": device_at(z, x, 1 - c, 1 - y),
    }


def repeat(count, body):
    def step(at, carried):
        body(at)
        return carried

    lax.fori_loop(0, count, step, 0)


def greet_all():
    barrier = pltpu.get_barrier_semaphore()
    here = lax.axis_index("dp") * 2 + lax.axis_index("seq")

    def signal(at):
        there = lax.rem(here + at + 1, 2 * DP)
        pl.semaphore_signal(
            barrier, inc=1, device_id=(there // 2, lax.rem(there, 2)), device_id_type=MESH
        )

    repeat(2 * DP - 1, signal)
    pl.semaphore_wait(barrier, 2 * DP - 1)


class Broad:
    height, width, subs, split = SUB_ROWS, WIDE, SUBS, 64
    first, source_column = 0, 0

    @staticmethod
    def holds(zs, xs, cs):
        return (zs * 2 + xs) * 2 + cs >= 7

    @staticmethod
    def view(whole, zs, xs, ys, cs, sub, start=0, rows=SUB_ROWS):
        column = jnp.maximum(((zs * 2 + xs) * 2 + cs) * WIDE - LOW, 128)
        row = pl.multiple_of(sub * SUB_ROWS + start, 16)
        return whole.at[ys, pl.ds(row, rows), pl.ds(pl.multiple_of(column, 128), WIDE)]


class Narrow:
    height, width, subs, split = TALL, 128, 1, 272
    first, source_column = 16 * SUBS, WIDE - 128

    @staticmethod
    def holds(zs, xs, cs):
        return (zs * 2 + xs) * 2 + cs == 6

    @staticmethod
    def view(whole, zs, xs, ys, cs, sub, start=0, rows=TALL):
        return whole.at[ys, pl.ds(start, rows), pl.ds(0, 128)]


class Down:
    height, width, subs, split = 64, FF_PART, 1, 32
    first, source_column = 16 * SUBS + 16, 0

    @staticmethod
    def holds(zs, xs, cs):
        return zs >= 0

    @staticmethod
    def view(whole, zs, xs, ys, cs, sub, start=0, rows=64):
        row = pl.multiple_of(((zs * 2 + xs) * 2 + cs) * 64 + start, 32)
        return whole.at[pl.ds(row, rows), pl.ds(pl.multiple_of(ys * FF_PART, 128), FF_PART)]


SLOTS = 16 * SUBS + 32
RELATIONS = ("own", "x", "y", "xy")
HOPS = {"own": 0, "x": 1, "y": 1, "xy": 2}


def by_plane(z, table):
    picked = table[PLANES - 1]
    for plane in range(PLANES - 2, -1, -1):
        picked = jnp.where(z == plane, table[plane], picked)
    return picked


def forward_block(what, refs, kind, zs, relation, sub, sems, valid):
    whole, mine = refs
    send_sem, recv_sem, core_sem = sems
    z, x, c, y = place()
    near = neighbours()
    xs = 1 - x if "x" in relation else x
    ys = 1 - y if "y" in relation else y
    slot = kind.first + ((zs * 2 + xs) * 2 + ys) * kind.subs + sub
    full, half = recv_sem.at[slot, 0], recv_sem.at[slot, 1]
    parts = ((0, kind.height), (0, kind.split), (kind.split, kind.height - kind.split))

    def copy(part, index, arrival, key, source=None, cs=None):
        target = kind.view(whole, zs, xs, ys, c if cs is None else cs, sub, *parts[part])
        return pltpu.make_async_remote_copy(
            src_ref=target if source is None else source,
            dst_ref=target,
            send_sem=send_sem.at[slot, index],
            recv_sem=arrival,
            device_id=near[key],
            device_id_type=MESH,
        )

    if what == "core":

        @pl.when(valid & kind.holds(zs, xs, 1 - c))
        def _():
            copy(0, 4, core_sem.at[slot], "core", cs=1 - c).wait_recv()

        return
    valid = valid & kind.holds(zs, xs, c)
    if what == "tick":
        arrived = valid & (zs != z) if relation == "own" else valid

        @pl.when(arrived)
        def _():
            if relation == "xy":
                copy(1, 0, full, "x").wait_recv()
                copy(2, 0, half, "x").wait_recv()
            else:
                copy(0, 0, full, "x").wait_recv()

    def act(descriptor):
        if what == "drain":
            descriptor.wait_send()
        else:
            descriptor.start()

    def spread(source, upward, downward):
        @pl.when(upward)
        def _():
            act(copy(0, 0, full, "up", source))

        @pl.when(downward)
        def _():
            act(copy(0, 1, full, "down", source))

        act(copy(0, 2, full, "x", source))
        act(copy(0, 3, full, "y", source))
        act(copy(0, 4, core_sem.at[slot], "core", source))

    if relation == "own":

        if what != "tick":

            @pl.when(valid & (zs == z))
            def _():
                source = mine.at[
                    pl.ds(pl.multiple_of(sub * kind.height, 16), kind.height),
                    pl.ds(kind.source_column, kind.width),
                ]
                spread(source, z < PLANES - 1, z > 0)

        if what != "launch":

            @pl.when(valid & (zs != z))
            def _():
                spread(None, (zs < z) & (z < PLANES - 1), (zs > z) & (z > 0))

        return

    @pl.when(valid)
    def _():
        if relation == "x":
            act(copy(1, 3, full, "y"))
        if relation == "y":
            act(copy(2, 2, half, "x"))
        act(copy(0, 4, core_sem.at[slot], "core"))


def forward_step(what, refs, plan, relations, sems, sub):
    z = place()[0]
    for kind, order in plan:
        for position in range(len(order[0])):
            zs = by_plane(z, [row[position] for row in order])
            for relation in relations:
                forward_block(
                    what,
                    refs[kind.__name__],
                    kind,
                    zs,
                    relation,
                    jnp.minimum(sub, kind.subs - 1),
                    sems,
                    sub < kind.subs,
                )


def launch(refs, kinds, sems):
    z = place()[0]

    def go(sub):
        for kind in kinds:
            forward_block(
                "launch",
                refs[kind.__name__],
                kind,
                z,
                "own",
                jnp.minimum(sub, kind.subs - 1),
                sems,
                sub < kind.subs,
            )

    repeat(max(kind.subs for kind in kinds), go)


NEAR_LOW = ((1, 2), (1, 2), (2, 1), (2, 1))
ONLY_ONE = ((1,),) * PLANES
ONLY_LAST = ((3,),) * PLANES
NEAR = ((0, 1, 2, 3), (1, 0, 2, 3), (2, 3, 1, 0), (3, 2, 1, 0))
PLAN_LOW = ((Broad, NEAR_LOW), (Narrow, ONLY_ONE))
PLAN_UP = ((Broad, ONLY_LAST),)
PLAN_DOWN = ((Down, NEAR),)
PLAN_ALL = PLAN_LOW + PLAN_UP + PLAN_DOWN


BF16 = jnp.bfloat16
F32 = jnp.float32
PLAIN = (((1,), (0,)), ((), ()))
BOTH_LAST = (((1,), (1,)), ((), ()))
BOTH_FIRST = (((0,), (0,)), ((), ()))
LANES = 128
PAIRS = HEADS // 2
TOKENS_HERE = 512


def multiply(left, right, dims=PLAIN):
    return lax.dot_general(left, right, dims, preferred_element_type=F32)


def two_heads(block):
    lanes = lax.broadcasted_iota(jnp.int32, block.shape, 1)
    zero = jnp.zeros_like(block)
    return (jnp.where(lanes < HEAD_DIM, block, zero), jnp.where(lanes < HEAD_DIM, zero, block))


def attend_pair(pair, queries, keys, values, mixed, log_totals):
    columns = pl.ds(pl.multiple_of(pair * LANES, LANES), LANES)
    key_block = keys[:, columns]
    value_flat = values[:, columns].T
    parts = []
    for head, query_block in enumerate(two_heads(queries[:, columns])):
        scores = multiply(key_block, query_block, BOTH_LAST)
        largest = jnp.max(scores, axis=0, keepdims=True)
        weights = jnp.exp((scores - largest) * HEAD_DIM**-0.5)
        total = jnp.sum(weights, axis=0, keepdims=True)
        parts.append(multiply(value_flat, weights.astype(BF16)) * (1.0 / total))
        log_totals[2 * pair + head] = largest * HEAD_DIM**-0.5 + jnp.log(total)
    joined = jnp.concatenate([parts[0][:HEAD_DIM], parts[1][HEAD_DIM:]], axis=0)
    mixed[:, columns] = joined.T.astype(BF16)


def normalize(values):
    center = values - jnp.mean(values, axis=-1, keepdims=True)
    return center * lax.rsqrt(jnp.mean(center * center, axis=-1, keepdims=True) + norm_eps)


def from_weights(left, whole, start, width):
    columns = pl.ds(pl.multiple_of(start, LANES), width)
    return multiply(left[:, :HALF], whole[0, :HALF, columns]) + multiply(
        left[:, HALF:], whole[1, :HALF, columns]
    )


def bias_of(whole, start, width):
    columns = pl.ds(pl.multiple_of(start, LANES), width)
    both = whole[0, HALF:TALL, columns].astype(F32) + whole[1, HALF:TALL, columns].astype(F32)
    return both[:1]


def forward_kernel(
    low_in,
    low_down,
    hidden_in,
    cotangent,
    condition,
    whole_in,
    whole_down,
    hidden_out,
    grad_out_out,
    cond_all,
    modulation,
    input_one_out,
    queries_out,
    keys_out,
    values_out,
    mixed_out,
    log_totals,
    attn_out_out,
    middle_out,
    input_two_out,
    slope,
    grad_branch_out,
    row_grads,
    block_out,
    grad_down,
    own_in,
    own_down,
    ada_weights,
    ada_part,
    mod_parts,
    up_stage,
    wide,
    active,
    flat_branch,
    flat_mate,
    wide_mate,
    down_stage,
    send_sem,
    recv_sem,
    core_sem,
    local_sem,
    cond_send,
    cond_recv,
    mod_send,
    mod_recv,
    swap_sem,
    pair_sem,
    up_sem,
    down_sem,
    rows_sem,
    wide_sem,
    hidden,
    grad_out,
    input_one,
    queries,
    keys,
    values,
    mixed,
    attn_out,
    middle,
    input_two,
    grad_branch,
    keep_sem,
):
    z, x, c, y = place()
    dp = (z * 2 + x) * 2 + c
    near = neighbours()
    sems = (send_sem, recv_sem, core_sem)
    refs = {"Broad": (own_in, low_in), "Narrow": (own_in, low_in), "Down": (own_down, low_down)}
    at_home = c == y

    def remote(source, target, sent, arrived, device):
        return pltpu.make_async_remote_copy(
            src_ref=source,
            dst_ref=target,
            send_sem=sent,
            recv_sem=arrived,
            device_id=device,
            device_id_type=MESH,
        )

    kept = {
        name: pltpu.make_async_copy(source, target, keep_sem.at[index])
        for index, (name, source, target) in enumerate(
            (
                ("hidden", hidden, hidden_out),
                ("grad_out", grad_out, grad_out_out),
                ("input_one", input_one, input_one_out),
                ("queries", queries, queries_out),
                ("keys", keys, keys_out),
                ("values", values, values_out),
                ("mixed", mixed, mixed_out),
                ("attn_out", attn_out, attn_out_out),
                ("middle", middle, middle_out),
                ("input_two", input_two, input_two_out),
                ("grad_branch", grad_branch, grad_branch_out),
            )
        )
    }

    def keep(*which):
        for name in which:
            kept[name].start()

    broad = pltpu.make_async_copy(
        low_in,
        own_in.at[y, :, pl.ds(pl.multiple_of(jnp.maximum(dp, 7) * WIDE - LOW, LANES), WIDE)],
        local_sem.at[0],
    )
    narrow = pltpu.make_async_copy(
        low_in.at[:, pl.ds(WIDE - 128, 128)], own_in.at[y, :, pl.ds(0, 128)], local_sem.at[0]
    )
    down = pltpu.make_async_copy(
        low_down,
        own_down.at[
            pl.ds(pl.multiple_of(dp * 64, 64), 64),
            pl.ds(pl.multiple_of(y * FF_PART, LANES), FF_PART),
        ],
        local_sem.at[1],
    )
    ada = pltpu.make_async_copy(low_in, ada_weights, local_sem.at[2])
    ada.start()
    down.start()

    @pl.when(dp >= 7)
    def _():
        broad.start()

    @pl.when(dp == 6)
    def _():
        narrow.start()

    greet_all()

    cond_all[dp] = condition[...].astype(F32)

    def cond_copy(at):
        there = lax.rem(dp + at + 1, DP)
        return remote(
            cond_all.at[dp], cond_all.at[dp], cond_send.at[at], cond_recv.at[dp], (there, y)
        )

    repeat(DP - 1, lambda at: cond_copy(at).start())

    swaps = []
    for index, (source, target) in enumerate(((hidden_in, hidden), (cotangent, grad_out))):
        swaps.append(
            (
                pltpu.make_async_copy(source, target, swap_sem.at[index, 0]),
                remote(
                    source, target, swap_sem.at[index, 1], swap_sem.at[index, 2], near["swap"]
                ),
            )
        )

    def trade(index):
        @pl.when(at_home)
        def _():
            swaps[index][0].start()

        @pl.when(jnp.logical_not(at_home))
        def _():
            swaps[index][1].start()

    def traded(index):
        @pl.when(at_home)
        def _():
            swaps[index][0].wait()

        @pl.when(jnp.logical_not(at_home))
        def _():
            swaps[index][1].wait()

    trade(0)
    launch(refs, (Broad, Narrow), sems)

    @pl.when((z == 0) | (z == PLANES - 1))
    def _():
        launch(refs, (Down,), sems)

    def pass_on(plan, relations):
        subs = max(kind.subs for kind, _ in plan)
        repeat(subs, lambda sub: forward_step("tick", refs, plan, relations, sems, sub))

    pass_on(PLAN_LOW, ("own",))

    def cond_arrived(at):
        there = lax.rem(dp + at + 1, DP)
        remote(
            cond_all.at[dp], cond_all.at[there], cond_send.at[at], cond_recv.at[there], (there, y)
        ).wait_recv()

    repeat(DP - 1, cond_arrived)
    raw = jnp.concatenate([cond_all[index] for index in range(DP)], axis=0)
    active[...] = (raw / (1.0 + jnp.exp(-raw))).astype(BF16)
    ada.wait()
    partial = (
        multiply(
            active[:, pl.ds(pl.multiple_of(y * HALF, LANES), HALF)],
            ada_weights[:HALF],
        )
        + ada_weights[HALF:].astype(F32)[:1]
    )
    for index in range(DP):
        ada_part[index] = partial[index : index + 1]

    def mod_target(at):
        latent, core = at // 2, lax.rem(at, 2)
        return (latent // 2 * 2 + core, lax.rem(latent, 2))

    def mod_copy(at):
        return remote(
            ada_part.at[at // 2],
            mod_parts.at[dp * 2 + y],
            mod_send.at[at],
            mod_recv.at[dp * 2 + y],
            mod_target(at),
        )

    def elsewhere(at):
        there = mod_target(at)
        return (there[0] != dp) | (there[1] != y)

    @pl.when(dp < 7)
    def _():
        def send(at):
            @pl.when(elsewhere(at))
            def _():
                mod_copy(at).start()

            @pl.when(jnp.logical_not(elsewhere(at)))
            def _():
                mod_parts[dp * 2 + y] = ada_part[at // 2]

        repeat(2 * DP, send)

    pass_on(PLAN_LOW, ("x", "y"))

    @pl.when((z > 0) & (z < PLANES - 1))
    def _():
        launch(refs, (Down,), sems)

    pass_on(PLAN_UP, ("own",))
    trade(1)
    traded(0)

    def mod_arrived(at):
        @pl.when(at != dp * 2 + y)
        def _():
            remote(
                ada_part.at[0], mod_parts.at[at], mod_send.at[0], mod_recv.at[at], near["x"]
            ).wait_recv()

    repeat(14, mod_arrived)
    for index in range(7):
        modulation[:, index * WIDE : (index + 1) * WIDE] = (
            mod_parts[2 * index] + mod_parts[2 * index + 1]
        )

    def vector(index):
        return modulation[:, index * D : (index + 1) * D]

    def shape_one(at):
        rows = pl.ds(pl.multiple_of(at * 128, 128), 128)
        normed = normalize(hidden[rows].astype(F32))
        input_one[rows] = (normed * (1.0 + vector(1)) + vector(0)).astype(BF16)

    repeat(4, shape_one)
    keep("hidden", "input_one")

    pass_on(PLAN_LOW, ("xy",))
    repeat(SUBS, lambda at: forward_step("core", refs, PLAN_LOW, RELATIONS, sems, at))

    @pl.when(dp >= 7)
    def _():
        broad.wait()

    @pl.when(dp == 6)
    def _():
        narrow.wait()

    def project(at):
        columns = pl.ds(pl.multiple_of(at * 256, LANES), 256)
        keys[:HALF, columns] = from_weights(input_one, own_in, D + at * 256, 256).astype(BF16)
        values[:HALF, columns] = (
            from_weights(input_one, own_in, 2 * D + at * 256, 256)
            + bias_of(own_in, D + at * 256, 256)
        ).astype(BF16)

    repeat(D // 256, project)
    mates = [
        remote(
            one.at[:HALF], one.at[HALF:], pair_sem.at[index, 0], pair_sem.at[index, 1], near["core"]
        )
        for index, one in enumerate((keys, values))
    ]
    for mate in mates:
        mate.start()

    def project_queries(at):
        columns = pl.ds(pl.multiple_of(at * 256, LANES), 256)
        queries[:, columns] = (
            from_weights(input_one, own_in, at * 256, 256) + bias_of(own_in, at * 256, 256)
        ).astype(BF16)

    repeat(D // 256, project_queries)
    for mate in mates:
        mate.wait()
    keep("queries", "keys", "values")

    def attention(pair):
        attend_pair(pair, queries, keys, values, mixed, log_totals)

        @pl.when(pair < SUBS)
        def _():
            forward_step("tick", refs, PLAN_UP, ("x", "y"), sems, pair)

        @pl.when(pair == SUBS)
        def _():
            forward_step("tick", refs, PLAN_DOWN, ("own",), sems, 0)

        @pl.when((pair > SUBS) & (pair <= 2 * SUBS))
        def _():
            forward_step("tick", refs, PLAN_UP, ("xy",), sems, pair - SUBS - 1)

    repeat(PAIRS, attention)
    keep("mixed")

    def project_out(at):
        columns = pl.ds(pl.multiple_of(at * 256, LANES), 256)
        attn_out[:, columns] = from_weights(mixed, own_in, 3 * D + at * 256, 256) + bias_of(
            own_in, 2 * D + at * 256, 256
        )

    repeat(D // 256, project_out)

    def shape_two(at):
        rows = pl.ds(pl.multiple_of(at * 128, 128), 128)
        mid = hidden[rows].astype(F32) + vector(2) * attn_out[rows]
        middle[rows] = mid
        input_two[rows] = (normalize(mid) * (1.0 + vector(4)) + vector(3)).astype(BF16)

    repeat(4, shape_two)
    keep("attn_out", "middle", "input_two")
    repeat(SUBS, lambda at: forward_step("core", refs, PLAN_UP, RELATIONS, sems, at))
    whole_copies = [
        pltpu.make_async_copy(
            own_in.at[half, pl.ds(0, HALF)],
            whole_in.at[pl.ds(half * HALF, HALF)],
            local_sem.at[3 + half],
        )
        for half in range(2)
    ]
    for whole_copy in whole_copies:
        whole_copy.start()
    tile = 512

    def up_copy(at, slot):
        return pltpu.make_async_copy(
            up_stage.at[slot],
            slope.at[:, pl.ds(pl.multiple_of(at * tile, LANES), tile)],
            up_sem.at[slot],
        )

    def down_grad_copy(at, slot):
        return pltpu.make_async_copy(
            down_stage.at[slot],
            grad_down.at[:, pl.ds(pl.multiple_of(at * tile, LANES), tile)],
            down_sem.at[slot],
        )

    traded(1)

    def shape_branch(at):
        columns = pl.ds(pl.multiple_of(at * 256, LANES), 256)
        gate = modulation[:, pl.ds(pl.multiple_of(5 * D + at * 256, LANES), 256)]
        scaled = (grad_out[:, columns].astype(F32) * gate).astype(BF16)
        grad_branch[:, columns] = scaled
        flat = scaled.T
        for part in range(4):
            rows = pl.ds(pl.multiple_of((2 * at + part // 2) * 64, 64), 64)
            flat_branch[part % 2, rows] = flat[part * 64 : (part + 1) * 64]
        row_grads[1:2, columns] = jnp.sum(scaled.astype(F32), axis=0, keepdims=True)

    repeat(D // 256, shape_branch)
    keep("grad_out", "grad_branch")
    rows_away = remote(
        flat_branch.at[1 - c], flat_mate, rows_sem.at[0], rows_sem.at[1], near["core"]
    )
    rows_away.start()

    def wide_copy(at):
        columns = pl.ds(pl.multiple_of(at * tile, LANES), tile)
        return remote(
            wide.at[:, columns],
            wide_mate.at[:, columns],
            wide_sem.at[at, 0],
            wide_sem.at[at, 1],
            near["core"],
        )

    def grow_down(at):
        slot = lax.rem(at, 2)

        @pl.when(at >= 2)
        def _():
            down_grad_copy(at - 2, slot).wait()

        wide_copy(at).wait_recv()
        for side in range(2):
            columns = pl.ds(pl.multiple_of(at * tile + side * 256, LANES), 256)
            down_stage[slot, :, side * 256 : (side + 1) * 256] = (
                multiply(flat_branch[c], wide[:, columns])
                + multiply(flat_mate[...], wide_mate[:, columns])
            ).astype(BF16)
        down_grad_copy(at, slot).start()

    def widen(at):
        slot = lax.rem(at, 2)

        @pl.when(at >= 2)
        def _():
            up_copy(at - 2, slot).wait()

        factor = math.sqrt(2.0 / math.pi)
        for side in range(2):
            start = at * tile + side * 256
            value = from_weights(input_two, own_in, 4 * D + start, 256) + bias_of(
                own_in, 3 * D + start, 256
            )
            square = value * value
            bent = jnp.tanh(factor * value * (1.0 + 0.044715 * square))
            half_up = 0.5 + 0.5 * bent
            up_stage[slot, :, side * 256 : (side + 1) * 256] = (
                half_up
                + 0.5
                * value
                * (1.0 - bent * bent)
                * (factor + 3.0 * 0.044715 * factor * square)
            ).astype(BF16)
            wide[:, pl.ds(pl.multiple_of(start, LANES), 256)] = (value * half_up).astype(BF16)
        up_copy(at, slot).start()
        wide_copy(at).start()

        @pl.when(at >= 1)
        def _():
            grow_down(at - 1)

        @pl.when(at == 1)
        def _():
            forward_step("tick", refs, PLAN_DOWN, ("x", "y"), sems, 0)

        @pl.when(at == FF // tile - 1)
        def _():
            forward_step("tick", refs, PLAN_DOWN, ("xy",), sems, 0)

    rows_away.wait_recv()
    repeat(FF // tile, widen)
    grow_down(FF // tile - 1)
    for at in (FF // tile - 2, FF // tile - 1):
        up_copy(at, at % 2).wait()
        down_grad_copy(at, at % 2).wait()
    down.wait()

    def narrow_down(at):
        columns = pl.ds(pl.multiple_of(at * 256, LANES), 256)
        value = bias_of(own_in, 7 * D + at * 256, 256)
        for side in range(2):
            value += multiply(
                wide[:, side * FF_PART : (side + 1) * FF_PART],
                own_down[columns, side * FF_PART : (side + 1) * FF_PART],
                BOTH_LAST,
            )
        gate = modulation[:, pl.ds(pl.multiple_of(5 * D + at * 256, LANES), 256)]
        block_out[:, columns] = (middle[:, columns] + gate * value).astype(BF16)
        towards = grad_out[:, columns].astype(F32)
        row_grads[0:1, columns] = jnp.sum(towards * value, axis=0, keepdims=True)

    forward_step("core", refs, PLAN_DOWN, RELATIONS, sems, 0)
    down_copy = pltpu.make_async_copy(own_down, whole_down, local_sem.at[5])
    down_copy.start()
    repeat(PLANES, narrow_down)

    repeat(SUBS, lambda at: forward_step("drain", refs, PLAN_ALL, RELATIONS, sems, at))
    repeat(DP - 1, lambda at: cond_copy(at).wait_send())

    @pl.when(dp < 7)
    def _():
        def sent(at):
            @pl.when(elsewhere(at))
            def _():
                mod_copy(at).wait_send()

        repeat(2 * DP, sent)

    for whole_copy in whole_copies:
        whole_copy.wait()
    down_copy.wait()
    rows_away.wait_send()
    repeat(FF // tile, lambda at: wide_copy(at).wait_send())
    for one in kept.values():
        one.wait()


def run_forward(low_in, low_down, hidden_in, cotangent, condition):
    shape = jax.ShapeDtypeStruct
    rows = TOKENS_HERE
    wide, flat = shape((rows, D), BF16), shape((rows, D), F32)
    both = shape((2 * rows, D), BF16)
    outs = [
        (shape((D, KEPT), BF16), pl.ANY),
        (shape((D, FF), BF16), pl.ANY),
        (wide, pl.ANY),
        (wide, pl.ANY),
        (shape((DP, 1, D), F32), pltpu.VMEM),
        (shape((1, 7 * WIDE), F32), pltpu.VMEM),
        (wide, pl.ANY),
        (wide, pl.ANY),
        (both, pl.ANY),
        (both, pl.ANY),
        (wide, pl.ANY),
        (shape((HEADS, 1, rows), F32), pltpu.VMEM),
        (flat, pl.ANY),
        (flat, pl.ANY),
        (wide, pl.ANY),
        (shape((rows, FF), BF16), pl.ANY),
        (wide, pl.ANY),
        (shape((8, D), F32), pltpu.VMEM),
        (wide, pltpu.VMEM),
        (shape((D // 2, FF), BF16), pl.ANY),
    ]
    kept = (wide, wide, wide, wide, both, both, wide, flat, flat, wide, wide)
    dma = pltpu.SemaphoreType.DMA
    return pl.pallas_call(
        forward_kernel,
        out_shape=[one for one, _ in outs],
        in_specs=[pl.BlockSpec(memory_space=pl.ANY)] * 4
        + [pl.BlockSpec(memory_space=pltpu.VMEM)],
        out_specs=[pl.BlockSpec(memory_space=where) for _, where in outs],
        scratch_shapes=[
            pltpu.VMEM((2, TALL, KEPT), BF16),
            pltpu.VMEM((D, FF), BF16),
            pltpu.VMEM((TALL, WIDE), BF16),
            pltpu.VMEM((DP, 1, WIDE), F32),
            pltpu.VMEM((14, 1, WIDE), F32),
            pltpu.VMEM((2, rows, 512), BF16),
            pltpu.VMEM((rows, FF), BF16),
            pltpu.VMEM((DP, D), BF16),
            pltpu.VMEM((2, D // 2, rows), BF16),
            pltpu.VMEM((D // 2, rows), BF16),
            pltpu.VMEM((rows, FF), BF16),
            pltpu.VMEM((2, D // 2, 512), BF16),
            dma((SLOTS, 5)),
            dma((SLOTS, 2)),
            dma((SLOTS,)),
            dma((6,)),
            dma((DP,)),
            dma((DP,)),
            dma((2 * DP,)),
            dma((14,)),
            dma((2, 3)),
            dma((2, 2)),
            dma((2,)),
            dma((2,)),
            dma((2,)),
            dma((FF // 512, 2)),
        ]
        + [pltpu.VMEM(one.shape, one.dtype) for one in kept]
        + [dma((len(kept),))],
        compiler_params=pltpu.CompilerParams(
            collective_id=0, has_side_effects=True, vmem_limit_bytes=62 * 2**20
        ),
        name="forward",
    )(low_in, low_down, hidden_in, cotangent, condition)


GRAD_SUBS = 8
GRAD_ROWS = HALF // GRAD_SUBS


class BroadGrad:
    height, width, subs, source_column = GRAD_ROWS, WIDE, GRAD_SUBS, 0
    split = GRAD_ROWS // 2
    lag = 1

    @staticmethod
    def holds(zs, xs, cs):
        return (zs * 2 + xs) * 2 + cs >= 7

    @staticmethod
    def corner(zs, xs, ys, cs, sub):
        column = jnp.maximum(((zs * 2 + xs) * 2 + cs) * WIDE - LOW, 128)
        return (
            pl.multiple_of(ys * HALF + sub * GRAD_ROWS, GRAD_ROWS),
            pl.multiple_of(column, 128),
        )


class HighGrad(BroadGrad):
    split = 48
    lag = 2


class NarrowGrad:
    height, width, subs, source_column = HALF, 128, 1, WIDE - 128
    split = HALF // 2
    lag = 1

    @staticmethod
    def holds(zs, xs, cs):
        return (zs * 2 + xs) * 2 + cs == 6

    @staticmethod
    def corner(zs, xs, ys, cs, sub):
        return (pl.multiple_of(ys * HALF, HALF), 0)


def reduce_block(what, refs, kind, zs, plane_at, planes, relation, sub, sems, valid):
    grads, first_column, owned, buffers = refs
    from_core, from_x, from_y, from_low, from_high, half_a, half_b = buffers
    send_sem, recv_sem = sems
    z, x, c, y = place()
    near = neighbours()
    xs = 1 - x if "x" in relation else x
    ys = 1 - y if "y" in relation else y
    flat = plane_at * kind.subs + sub
    count = planes * kind.subs
    kin = RELATIONS.index(relation)
    slot = kin * count + flat
    rows, half_rows = kind.height, kind.split

    def remote(source, target, index, arrival, key):
        return pltpu.make_async_remote_copy(
            src_ref=source,
            dst_ref=target,
            send_sem=send_sem.at[slot, index],
            recv_sem=recv_sem.at[arrival, flat],
            device_id=near[key],
            device_id_type=MESH,
        )

    def share(cs):
        row, column = kind.corner(zs, xs, ys, cs, sub)
        column = jnp.clip(column - first_column, 0, grads.shape[1] - kind.width)
        return (pl.ds(row, rows), pl.ds(pl.multiple_of(column, 128), kind.width))

    total = from_core.at[slot]
    across = remote(grads.at[share(1 - c)], total, 2, kin, "core")
    other = valid & kind.holds(zs, xs, 1 - c)
    if what == "across":
        pl.when(other)(across.start)
        return
    if what == "drain":
        pl.when(other)(across.wait_send)
    valid = valid & kind.holds(zs, xs, c)
    part_a = from_core.at[slot, pl.ds(0, half_rows)]
    part_b = from_core.at[slot, pl.ds(half_rows, rows - half_rows)]
    if relation == "xy":
        sends = [
            (valid, remote(part_a, half_a.at[flat], 0, 4, "y")),
            (valid, remote(part_b, half_b.at[flat], 1, 5, "x")),
        ]
    elif relation == "x":
        sends = [(valid, remote(total, from_x.at[flat], 0, 6, "x"))]
    elif relation == "y":
        sends = [(valid, remote(total, from_y.at[flat], 0, 7, "y"))]
    else:
        sends = [
            (valid & (z < zs), remote(total, from_low.at[flat], 0, 8, "up")),
            (valid & (z > zs), remote(total, from_high.at[flat], 1, 9, "down")),
        ]
    if what == "drain":
        for condition, descriptor in sends:
            pl.when(condition)(descriptor.wait_send)
        return

    @pl.when(valid)
    def _():
        remote(total, total, 2, kin, "core").wait_recv()
        value = from_core[slot].astype(F32) + grads[share(c)].astype(F32)
        if relation == "xy":
            from_core[slot] = value.astype(BF16)
        elif relation == "x":
            remote(half_a.at[flat], half_a.at[flat], 0, 4, "y").wait_recv()
            from_core[slot, pl.ds(half_rows, rows - half_rows)] = value[half_rows:].astype(BF16)
            from_core[slot, pl.ds(0, half_rows)] = (
                value[:half_rows] + half_a[flat].astype(F32)
            ).astype(BF16)
        elif relation == "y":
            remote(half_b.at[flat], half_b.at[flat], 1, 5, "x").wait_recv()
            from_core[slot, pl.ds(0, half_rows)] = value[:half_rows].astype(BF16)
            from_core[slot, pl.ds(half_rows, rows - half_rows)] = (
                value[half_rows:] + half_b[flat].astype(F32)
            ).astype(BF16)
        else:
            remote(from_x.at[flat], from_x.at[flat], 0, 6, "x").wait_recv()
            remote(from_y.at[flat], from_y.at[flat], 0, 7, "y").wait_recv()
            value += from_x[flat].astype(F32) + from_y[flat].astype(F32)

            @pl.when((z <= zs) & (z > 0))
            def _():
                remote(from_low.at[flat], from_low.at[flat], 0, 8, "up").wait_recv()

            @pl.when((z >= zs) & (z < PLANES - 1))
            def _():
                remote(from_high.at[flat], from_high.at[flat], 1, 9, "down").wait_recv()

            def low():
                return jnp.where(z > 0, from_low[flat].astype(F32), 0.0)

            def high():
                return jnp.where(z < PLANES - 1, from_high[flat].astype(F32), 0.0)

            @pl.when(z < zs)
            def _():
                from_core[slot] = (value + low()).astype(BF16)

            @pl.when(z > zs)
            def _():
                from_core[slot] = (value + high()).astype(BF16)

            @pl.when(z == zs)
            def _():
                owned[
                    pl.ds(pl.multiple_of(sub * rows, rows), rows),
                    pl.ds(kind.source_column, kind.width),
                ] = value + low() + high()

    for condition, descriptor in sends:
        pl.when(condition)(descriptor.start)


def reduce_step(what, refs, plan, sems, at):
    z = place()[0]
    for kind, planes in plan:
        name = kind.__name__
        for plane_at, zs in enumerate(planes):
            for relation in ("xy", "x", "y", "own"):
                sub = at
                if what == "tick":
                    depth = 0
                    if relation == "own":
                        depth = by_plane(
                            z,
                            [
                                place_z
                                if place_z < zs
                                else max(place_z, 3 - place_z)
                                if place_z == zs
                                else 3 - place_z
                                for place_z in range(PLANES)
                            ],
                        )
                    sub = at - kind.lag * (2 - HOPS[relation] + depth)
                reduce_block(
                    what,
                    refs[name],
                    kind,
                    zs,
                    plane_at,
                    len(planes),
                    relation,
                    jnp.clip(sub, 0, kind.subs - 1),
                    sems[name],
                    (sub >= 0) & (sub < kind.subs),
                )


def landing(kind, planes):
    count = planes * kind.subs
    full = pltpu.VMEM((count, kind.height, kind.width), BF16)
    half_a = pltpu.VMEM((count, kind.split, kind.width), BF16)
    half_b = pltpu.VMEM((count, kind.height - kind.split, kind.width), BF16)
    sums = pltpu.VMEM((4 * count, kind.height, kind.width), BF16)
    return [sums] + [full] * 4 + [half_a, half_b]


def landing_signals(kind, planes):
    count = planes * kind.subs
    return [pltpu.SemaphoreType.DMA((4 * count, 3)), pltpu.SemaphoreType.DMA((10, count))]


def greet_near():
    z, x, c, y = place()
    near = neighbours()
    barrier = pltpu.get_barrier_semaphore()
    for key in ("x", "y", "core"):
        pl.semaphore_signal(barrier, inc=1, device_id=near[key], device_id_type=MESH)

    @pl.when(z < PLANES - 1)
    def _():
        pl.semaphore_signal(barrier, inc=1, device_id=near["up"], device_id_type=MESH)

    @pl.when(z > 0)
    def _():
        pl.semaphore_signal(barrier, inc=1, device_id=near["down"], device_id_type=MESH)

    middle = (z > 0) & (z < PLANES - 1)

    @pl.when(middle)
    def _():
        pl.semaphore_wait(barrier, 5)

    @pl.when(jnp.logical_not(middle))
    def _():
        pl.semaphore_wait(barrier, 4)


REDUCE_HIGH = ((HighGrad, (3,)),)
REDUCE_LOW = ((BroadGrad, (1, 2)), (NarrowGrad, (1,)))
HIGH_STEPS = GRAD_SUBS + 5 * HighGrad.lag
LOW_STEPS = GRAD_SUBS + 4
HIGH_FIRST = FF // 8


def attend_back(
    pair, queries, keys, values, mixed, grad_mixed, log_totals, grad_query, grad_key, grad_value
):
    columns = pl.ds(pl.multiple_of(pair * LANES, LANES), LANES)
    key_block = keys[:, columns]
    value_block = values[:, columns]
    key_flat = key_block.T
    key_sum, value_sum = None, None
    step = 256
    for part in range(TOKENS_HERE // step):
        rows = pl.ds(part * step, step)
        grad_block = grad_mixed[rows, columns]
        product = (grad_block.astype(F32) * mixed[rows, columns].astype(F32)).T
        query_parts = []
        heads = zip(two_heads(queries[rows, columns]), two_heads(grad_block))
        for head, (query_head, grad_head) in enumerate(heads):
            scores = multiply(key_block, query_head, BOTH_LAST)
            weights = jnp.exp(scores * HEAD_DIM**-0.5 - log_totals[2 * pair + head, :, rows])
            grad_weights = multiply(value_block, grad_head, BOTH_LAST)
            inner = jnp.sum(
                product[HEAD_DIM * head : HEAD_DIM * (head + 1)], axis=0, keepdims=True
            )
            grad_scores = (weights * (grad_weights - inner)).astype(BF16)
            value_term = multiply(weights.astype(BF16), grad_head)
            key_term = multiply(grad_scores, query_head)
            value_sum = value_term if value_sum is None else value_sum + value_term
            key_sum = key_term if key_sum is None else key_sum + key_term
            query_parts.append(multiply(key_flat, grad_scores))
        joined = jnp.concatenate([query_parts[0][:HEAD_DIM], query_parts[1][HEAD_DIM:]], axis=0)
        grad_query[rows, columns] = (joined * HEAD_DIM**-0.5).T.astype(BF16)
    grad_key[:, columns] = (key_sum * HEAD_DIM**-0.5).astype(BF16)
    grad_value[:, columns] = value_sum.astype(BF16)


def backward_kernel(
    queries_in,
    keys_in,
    values_in,
    mixed_in,
    grad_mixed_in,
    log_totals_in,
    grads_in,
    input_one_in,
    hidden_in,
    grad_middle_in,
    grad_attn_in,
    scale_one,
    gate_one_sum,
    shift_two_sum,
    scale_two_sum,
    row_grads,
    bias_out_sum,
    bias_up_sum,
    whole_in,
    owned,
    input_grad,
    input_low,
    sums,
    grad_low,
    queries,
    keys,
    values,
    mixed,
    grad_mixed,
    log_totals,
    grads,
    input_one,
    hidden,
    grad_middle,
    grad_attn,
    load_sem,
    grad_query,
    grad_key,
    grad_value,
    row_sums,
    key_all,
    value_all,
    key_mate,
    value_mate,
    flat_one,
    weight_stage,
    grad_stage,
    grad_one,
    mate_sem,
    weight_sem,
    grad_sem,
    *scratch,
):
    dp = lax.axis_index("dp")
    near = neighbours()
    refs = {"HighGrad": (grads, 4 * D, owned, scratch[:7])}
    sems = {"HighGrad": scratch[7:9]}
    tile = 512
    tiles = 3 * D // tile
    loads = [
        pltpu.make_async_copy(source, target, load_sem.at[index])
        for index, (source, target) in enumerate(
            (
                (grads_in, grads),
                (input_one_in, input_one),
                (queries_in, queries),
                (keys_in, keys),
                (values_in, values),
                (mixed_in, mixed),
                (grad_mixed_in, grad_mixed),
                (log_totals_in, log_totals),
                (hidden_in, hidden),
                (grad_middle_in, grad_middle),
                (grad_attn_in, grad_attn),
            )
        )
    ]
    for load in loads:
        load.start()

    def weight_copy(at, slot):
        return pltpu.make_async_copy(
            whole_in.at[:, pl.ds(pl.multiple_of(at * tile, LANES), tile)],
            weight_stage.at[slot],
            weight_sem.at[slot],
        )

    def grad_copy(at, slot):
        return pltpu.make_async_copy(
            grad_stage.at[slot],
            grad_low.at[:, pl.ds(pl.multiple_of(at * tile, LANES), tile)],
            grad_sem.at[slot],
        )

    weight_copy(0, 0).start()
    greet_near()
    loads[0].wait()
    repeat(GRAD_SUBS, lambda at: reduce_step("across", refs, REDUCE_HIGH, sems, at))
    ahead = HighGrad.lag
    repeat(ahead, lambda at: reduce_step("tick", refs, REDUCE_HIGH, sems, at))

    @pl.when(dp < 12)
    def _():
        owned[...] = jnp.zeros_like(owned)

    for load in loads[1:]:
        load.wait()

    def flatten(source):
        def go(at):
            columns = pl.ds(pl.multiple_of(at * 256, LANES), 256)
            flat_one[pl.ds(pl.multiple_of(at * 256, 256), 256)] = source[:, columns].T

        repeat(D // 256, go)

    flatten(input_one)

    def mates(pair):
        columns = pl.ds(pl.multiple_of(pair * LANES, LANES), LANES)
        return [
            pltpu.make_async_remote_copy(
                src_ref=source.at[HALF:, columns],
                dst_ref=target.at[:, columns],
                send_sem=mate_sem.at[pair, 2 * index],
                recv_sem=mate_sem.at[pair, 2 * index + 1],
                device_id=near["core"],
                device_id_type=MESH,
            )
            for index, (source, target) in enumerate(((key_all, key_mate), (value_all, value_mate)))
        ]

    def attention(pair):
        attend_back(
            pair,
            queries,
            keys,
            values,
            mixed,
            grad_mixed,
            log_totals,
            grad_query,
            key_all,
            value_all,
        )
        for mate in mates(pair):
            mate.start()
        reduce_step("tick", refs, REDUCE_HIGH, sems, pair + ahead)

    repeat(PAIRS, attention)
    for source, target, total, index in (
        (key_all, key_mate, grad_key, 0),
        (value_all, value_mate, grad_value, 1),
    ):
        repeat(PAIRS, lambda pair: mates(pair)[index].wait())
        total[...] = (source[:HALF].astype(F32) + target[...].astype(F32)).astype(BF16)

    grad_one[...] = jnp.zeros_like(grad_one)

    def project_back(source, base):
        def go(at):
            slot = lax.rem(at, 2)
            weight_copy(at, slot).wait()

            @pl.when(at + 1 < tiles)
            def _():
                weight_copy(at + 1, 1 - slot).start()

            @pl.when(at >= 2)
            def _():
                grad_copy(at - 2, slot).wait()

            columns = pl.ds(pl.multiple_of((at - base) * tile, LANES), tile)
            for side in range(2):
                part = slice(side * 512, (side + 1) * 512)
                grad_one[:, part] += multiply(
                    source[:, columns], weight_stage[slot, part], BOTH_LAST
                )
                narrow = pl.ds(pl.multiple_of((at - base) * tile + side * 256, LANES), 256)
                grad_stage[slot, :, side * 256 : (side + 1) * 256] = multiply(
                    flat_one[...], source[:, narrow]
                ).astype(BF16)
            grad_copy(at, slot).start()

            reduce_step("tick", refs, REDUCE_HIGH, sems, at + ahead + PAIRS)

        def run(at, carried):
            go(at + base)
            return carried

        lax.fori_loop(0, D // tile, run, 0)

    project_back(grad_query, 0)
    project_back(grad_key, D // tile)
    project_back(grad_value, 2 * D // tile)

    flatten(mixed)

    def project_out_back(part):
        at = part + tiles
        slot = lax.rem(at, 2)
        grad_copy(at - 2, slot).wait()
        for side in range(2):
            narrow = pl.ds(pl.multiple_of(part * tile + side * 256, LANES), 256)
            grad_stage[slot, :, side * 256 : (side + 1) * 256] = multiply(
                flat_one[...], grad_attn[:, narrow]
            ).astype(BF16)
        grad_copy(at, slot).start()
        reduce_step("tick", refs, REDUCE_HIGH, sems, at + ahead + PAIRS)

    repeat(D // tile, project_out_back)
    row_sums[...] = jnp.zeros_like(row_sums)

    def shape_back(at):
        rows = pl.ds(pl.multiple_of(at * 128, 128), 128)
        value = hidden[rows].astype(F32)
        center = value - jnp.mean(value, axis=-1, keepdims=True)
        inverse = lax.rsqrt(jnp.mean(center * center, axis=-1, keepdims=True) + norm_eps)
        normed = center * inverse
        towards = grad_one[rows]
        row_sums[0:1] += jnp.sum(towards, axis=0, keepdims=True)
        row_sums[1:2] += jnp.sum(towards * normed, axis=0, keepdims=True)
        row_sums[2:3] += jnp.sum(grad_query[rows].astype(F32), axis=0, keepdims=True)
        row_sums[3:4] += jnp.sum(grad_value[rows].astype(F32), axis=0, keepdims=True)
        scaled = towards * (1.0 + scale_one[...])
        result = grad_middle[rows] + inverse * (
            scaled
            - jnp.mean(scaled, axis=-1, keepdims=True)
            - normed * jnp.mean(scaled * normed, axis=-1, keepdims=True)
        )
        input_grad[rows] = result
        input_low[rows] = result.astype(BF16)
        reduce_step("tick", refs, REDUCE_HIGH, sems, at + ahead + PAIRS + tiles + D // tile)

    repeat(4, shape_back)
    for index in range(2):
        sums[:, index * D : (index + 1) * D] = row_sums[index : index + 1]
        start = 6 * D + WIDE + index * D
        sums[:, start : start + D] = row_sums[index + 2 : index + 3]
    sums[:, 2 * D : 3 * D] = gate_one_sum[...]
    sums[:, 3 * D : 4 * D] = shift_two_sum[...]
    sums[:, 4 * D : 5 * D] = scale_two_sum[...]
    sums[:, 5 * D : 6 * D] = row_grads[0:1]
    sums[:, 6 * D : 6 * D + WIDE] = jnp.zeros((1, WIDE), F32)
    sums[:, 8 * D + WIDE : 9 * D + WIDE] = bias_out_sum[...]
    sums[:, 9 * D + WIDE : 9 * D + WIDE + FF] = bias_up_sum[...]
    sums[:, 9 * D + WIDE + FF :] = row_grads[1:2]
    for at in (tiles + D // tile - 2, tiles + D // tile - 1):
        grad_copy(at, at % 2).wait()
    repeat(GRAD_SUBS, lambda at: reduce_step("drain", refs, REDUCE_HIGH, sems, at))


def run_backward(*given):
    shape = jax.ShapeDtypeStruct
    rows = TOKENS_HERE
    vmem = pl.BlockSpec(memory_space=pltpu.VMEM)
    hbm = pl.BlockSpec(memory_space=pl.ANY)
    dma = pltpu.SemaphoreType.DMA
    return pl.pallas_call(
        backward_kernel,
        out_shape=[
            shape((HALF, WIDE), F32),
            shape((rows, D), F32),
            shape((rows, D), BF16),
            shape((1, VECTOR), F32),
            shape((D, 4 * D), BF16),
        ],
        in_specs=[hbm] * 11 + [vmem] * 7 + [hbm],
        out_specs=[vmem] * 4 + [hbm],
        scratch_shapes=[pltpu.VMEM(one.shape, one.dtype) for one in given[:11]]
        + [dma((11,))]
        + [pltpu.VMEM((rows, D), BF16)] * 3
        + [pltpu.VMEM((8, D), F32)]
        + [pltpu.VMEM((2 * rows, D), BF16)] * 2
        + [pltpu.VMEM((rows, D), BF16)] * 2
        + [
            pltpu.VMEM((D, rows), BF16),
            pltpu.VMEM((2, D, 512), BF16),
            pltpu.VMEM((2, D, 512), BF16),
            pltpu.VMEM((rows, D), F32),
            dma((PAIRS, 4)),
            dma((2,)),
            dma((2,)),
        ]
        + landing(HighGrad, 1)
        + landing_signals(HighGrad, 1),
        compiler_params=pltpu.CompilerParams(
            collective_id=1, has_side_effects=True, vmem_limit_bytes=62 * 2**20
        ),
        cost_estimate=pl.CostEstimate(
            flops=12 * 2 * 512 * 1024 * 1024, bytes_accessed=60 * 2**20, transcendentals=2**23
        ),
        name="backward",
    )(*given)


VECTOR = 17 * WIDE


def finish_kernel(
    grad_low,
    grad_up,
    low_in,
    active_rows,
    condition,
    sums,
    owned_high,
    down_sum,
    owned,
    cond_grad,
    bias_grad,
    owned_down,
    grads,
    ada_weights,
    sum_mate,
    sum_pieces,
    ada_in,
    cond_piece,
    cond_in,
    down_mate,
    bias_parts,
    local_sem,
    mate_sem,
    down_sem,
    piece_send,
    ada_recv,
    bias_recv,
    cond_send,
    cond_recv,
    *scratch,
):
    z, x, c, y = place()
    dp = (z * 2 + x) * 2 + c
    near = neighbours()
    refs = {
        "BroadGrad": (grads, 0, owned, scratch[0:7]),
        "NarrowGrad": (grads, 0, owned, scratch[7:14]),
    }
    sems = {"BroadGrad": scratch[14:16], "NarrowGrad": scratch[16:18]}

    def remote(source, target, sent, arrived, device):
        return pltpu.make_async_remote_copy(
            src_ref=source,
            dst_ref=target,
            send_sem=sent,
            recv_sem=arrived,
            device_id=device,
            device_id_type=MESH,
        )

    loads = [
        pltpu.make_async_copy(grad_low, grads.at[:, : 4 * D], local_sem.at[0]),
        pltpu.make_async_copy(
            grad_up.at[:, :HIGH_FIRST], grads.at[:, 4 * D : 4 * D + HIGH_FIRST], local_sem.at[1]
        ),
        pltpu.make_async_copy(low_in.at[pl.ds(0, HALF)], ada_weights, local_sem.at[2]),
    ]
    for load in loads:
        load.start()
    owned[...] = owned_high[...]
    greet_all()
    mate = remote(sums, sum_mate, mate_sem.at[0], mate_sem.at[1], near["core"])
    mate.start()
    down_away = remote(
        down_sum.at[:, pl.ds(pl.multiple_of((1 - y) * FF_PART, LANES), FF_PART)],
        down_mate,
        down_sem.at[0],
        down_sem.at[1],
        near["y"],
    )
    down_away.start()

    for load in loads[:2]:
        load.wait()
    repeat(GRAD_SUBS, lambda at: reduce_step("across", refs, REDUCE_LOW, sems, at))
    repeat(2, lambda at: reduce_step("tick", refs, REDUCE_LOW, sems, at))

    mate.wait()
    for index in range(17):
        columns = slice(index * WIDE, (index + 1) * WIDE)
        piece = sums[:, columns] + sum_mate[:, columns]
        if index < 7:
            piece = piece.astype(BF16).astype(F32)
        sum_pieces[index] = piece
    latent = (z * 2 + x) * 2 + y

    def piece_target(at):
        return jnp.where(at < 7, at, at - 1)

    def piece_copy(at, target, arrived):
        return remote(
            sum_pieces.at[at], target, piece_send.at[at], arrived, (piece_target(at), c)
        )

    def each_piece(act, keep):
        def go(at):
            mine = (piece_target(at) == dp) & (y == c)

            @pl.when(jnp.logical_not(mine) & (at < 7))
            def _():
                act(piece_copy(at, ada_in.at[latent], ada_recv.at[latent]))

            @pl.when(jnp.logical_not(mine) & (at >= 7))
            def _():
                act(piece_copy(at, bias_parts.at[latent], bias_recv.at[latent]))

            if keep:

                @pl.when(mine & (at < 7))
                def _():
                    ada_in[latent] = sum_pieces[at]

                @pl.when(mine & (at >= 7))
                def _():
                    bias_parts[latent] = sum_pieces[at]

        repeat(17, go)

    each_piece(lambda copy: copy.start(), True)
    repeat(3, lambda at: reduce_step("tick", refs, REDUCE_LOW, sems, at + 2))

    def from_latent(at, target, arrived):
        mine = (at // 2 == z * 2 + x) & (lax.rem(at, 2) == y) & (c == y)

        @pl.when(jnp.logical_not(mine))
        def _():
            remote(
                sum_pieces.at[0], target.at[at], piece_send.at[0], arrived.at[at], near["x"]
            ).wait_recv()

    loads[2].wait()

    @pl.when(dp < 7)
    def _():
        repeat(DP, lambda at: from_latent(at, ada_in, ada_recv))
        gathered = jnp.concatenate([ada_in[index] for index in range(DP)], axis=0)
        bias_grad[...] = jnp.sum(gathered, axis=0, keepdims=True)
        narrow = gathered.astype(BF16)
        owned[...] += multiply(active_rows[...], narrow, BOTH_FIRST)
        part = multiply(narrow, ada_weights[...], BOTH_LAST)
        for index in range(DP):
            cond_piece[index] = part[index : index + 1]

    @pl.when(dp >= 7)
    def _():
        bias_grad[...] = jnp.zeros_like(bias_grad)

    def cond_copy(at):
        return remote(
            cond_piece.at[at // 2],
            cond_in.at[dp * 2 + y],
            cond_send.at[at],
            cond_recv.at[dp * 2 + y],
            (at // 2, lax.rem(at, 2)),
        )

    def each_cond(act, keep):
        def go(at):
            mine = at == dp * 2 + y

            @pl.when(jnp.logical_not(mine))
            def _():
                act(cond_copy(at))

            if keep:

                @pl.when(mine)
                def _():
                    cond_in[dp * 2 + y] = cond_piece[at // 2]

        repeat(2 * DP, go)

    @pl.when(dp < 7)
    def _():
        each_cond(lambda copy: copy.start(), True)

    repeat(LOW_STEPS - 5, lambda at: reduce_step("tick", refs, REDUCE_LOW, sems, at + 5))

    def cond_arrived(at):
        @pl.when(at != dp * 2 + y)
        def _():
            remote(
                cond_piece.at[0], cond_in.at[at], cond_send.at[0], cond_recv.at[at], near["x"]
            ).wait_recv()

    repeat(14, cond_arrived)
    sides = []
    for side in range(2):
        total = cond_in[side]
        for index in range(1, 7):
            total = total + cond_in[2 * index + side]
        sides.append(total)
    value = condition[...].astype(F32)
    logistic = 1.0 / (1.0 + jnp.exp(-value))
    cond_grad[...] = jnp.concatenate(sides, axis=1) * (
        logistic * (1.0 + value * (1.0 - logistic))
    )

    @pl.when(dp >= 6)
    def _():
        repeat(DP, lambda at: from_latent(at, bias_parts, bias_recv))
        total = bias_parts[0]
        for index in range(1, DP):
            total = total + bias_parts[index]
        bias_grad[...] += total

    down_away.wait()
    owned_down[...] = down_sum[
        :, pl.ds(pl.multiple_of(y * FF_PART, LANES), FF_PART)
    ].astype(F32) + down_mate[...].astype(F32)
    each_piece(lambda copy: copy.wait_send(), False)

    @pl.when(dp < 7)
    def _():
        each_cond(lambda copy: copy.wait_send(), False)

    repeat(GRAD_SUBS, lambda at: reduce_step("drain", refs, REDUCE_LOW, sems, at))


def run_finish(
    grad_low,
    grad_up,
    low_in,
    active_rows,
    condition,
    sums,
    owned_high,
    down_sum,
):
    shape = jax.ShapeDtypeStruct
    dma = pltpu.SemaphoreType.DMA
    vmem = pl.BlockSpec(memory_space=pltpu.VMEM)
    hbm = pl.BlockSpec(memory_space=pl.ANY)
    return pl.pallas_call(
        finish_kernel,
        out_shape=[
            shape((HALF, WIDE), F32),
            shape((1, D), F32),
            shape((1, WIDE), F32),
            shape((64, FF_PART), F32),
        ],
        in_specs=[hbm] * 3 + [vmem] * 5,
        out_specs=[vmem] * 4,
        scratch_shapes=[
            pltpu.VMEM((D, 4 * D + HIGH_FIRST), BF16),
            pltpu.VMEM((HALF, WIDE), BF16),
            pltpu.VMEM((1, VECTOR), F32),
            pltpu.VMEM((17, 1, WIDE), F32),
            pltpu.VMEM((DP, 1, WIDE), F32),
            pltpu.VMEM((DP, 1, HALF), F32),
            pltpu.VMEM((14, 1, HALF), F32),
            pltpu.VMEM((64, FF_PART), BF16),
            pltpu.VMEM((DP, 1, WIDE), F32),
            dma((3,)),
            dma((2,)),
            dma((2,)),
            dma((17,)),
            dma((DP,)),
            dma((DP,)),
            dma((2 * DP,)),
            dma((14,)),
        ]
        + landing(BroadGrad, 2)
        + landing(NarrowGrad, 1)
        + landing_signals(BroadGrad, 2)
        + landing_signals(NarrowGrad, 1),
        compiler_params=pltpu.CompilerParams(
            collective_id=2, has_side_effects=True, vmem_limit_bytes=60 * 2**20
        ),
        name="finish",
    )(
        grad_low,
        grad_up,
        low_in,
        active_rows,
        condition,
        sums,
        owned_high,
        down_sum,
    )


def swap_away(values):
    pairs = []
    for index in range(2 * DP):
        y, c = index % 2, index // 2 % 2
        if y != c:
            pairs.append((index, index // 4 * 4 + y * 2 + c))
    return lax.ppermute(values, ("dp", "seq"), pairs)


def local(
    hidden_in,
    condition,
    cotangent,
    weights_in,
    weights_down,
    biases,
    moment_in,
    moment_down,
    moment_bias,
    square_in,
    square_down,
    square_bias,
):
    dp = lax.axis_index("dp")
    y = lax.axis_index("seq")
    side = WIDE // 2
    bias_row = jnp.pad(biases.astype(BF16)[None], ((0, 15), (0, side)))
    bias_row = jnp.where(y == 0, bias_row, jnp.roll(bias_row, side, axis=1))
    low_in = jnp.concatenate([weights_in.astype(BF16), bias_row], axis=0)
    (
        whole_in,
        whole_down,
        hidden,
        grad_out,
        cond_all,
        modulation,
        input_one,
        queries,
        keys,
        values,
        mixed,
        log_totals,
        attn_out,
        middle,
        input_two,
        slope,
        grad_branch,
        row_grads,
        block_out,
        grad_down,
    ) = run_forward(
        low_in,
        weights_down.astype(BF16).T,
        hidden_in[0],
        cotangent[0],
        condition,
    )
    at_home = lax.rem(dp, 2) == y
    block_swapped = swap_away(block_out)
    grad_out = grad_out.astype(F32)
    pieces = [modulation[:, part * D : (part + 1) * D] for part in range(6)]
    shift_one, scale_one, gate_one, shift_two, scale_two, gate_two = pieces

    def back_through(gradients, start, width):
        return lax.dot_general(
            gradients,
            whole_in[:, start : start + width],
            BOTH_LAST,
            preferred_element_type=F32,
        )

    def outer(left, right):
        return lax.dot_general(left, right, BOTH_FIRST, preferred_element_type=F32)

    def down_rows(total):
        return jnp.sum(total.astype(F32), axis=0, keepdims=True)

    down_sum = lax.psum_scatter(
        grad_down,
        "dp",
        scatter_dimension=0,
        axis_index_groups=[list(range(core, DP, 2)) for core in range(2)],
        tiled=True,
    )
    grad_act = jnp.dot(grad_branch, whole_down, preferred_element_type=F32)
    grad_upward = (grad_act * slope).astype(BF16)
    grad_up = outer(input_two, grad_upward).astype(BF16)
    grad_input_two = back_through(grad_upward, 4 * D, FF)
    normed_two, norm_pull_two = jax.vjp(layer_norm, middle)
    shift_two_grad = down_rows(grad_input_two)
    scale_two_grad = down_rows(grad_input_two * normed_two)
    grad_middle = grad_out + norm_pull_two(grad_input_two * (1.0 + scale_two))[0]
    grad_attn = (grad_middle * gate_one).astype(BF16)
    gate_one_grad = down_rows(grad_middle * attn_out)
    grad_mixed = back_through(grad_attn, 3 * D, D).astype(BF16)
    owned_high, input_grad, input_low, sums, grad_low = run_backward(
        queries,
        keys,
        values,
        mixed,
        grad_mixed,
        log_totals,
        grad_up,
        input_one,
        hidden,
        grad_middle,
        grad_attn,
        scale_one,
        gate_one_grad,
        shift_two_grad,
        scale_two_grad,
        row_grads,
        down_rows(grad_attn),
        down_rows(grad_upward),
        whole_in,
    )
    active_rows = lax.dynamic_slice_in_dim(
        jax.nn.silu(cond_all[:, 0]).astype(BF16), y * HALF, HALF, 1
    )
    owned_in, cond_grad, bias_grad, owned_down = run_finish(
        grad_low,
        grad_up,
        low_in,
        active_rows,
        condition,
        sums,
        owned_high,
        down_sum,
    )
    owned_down = owned_down.T
    input_low, owned_in = lax.optimization_barrier((input_low, owned_in))
    input_swapped = swap_away(input_low)
    input_grad = jnp.where(at_home, input_grad, input_swapped.astype(F32))
    block_out = jnp.where(at_home, block_out, block_swapped)
    owned_bias = lax.dynamic_slice_in_dim(bias_grad[0], y * side, side, 0)
    moments_in, squares_in, master_in = adamw_step(
        weights_in, moment_in, square_in, owned_in, rate_in
    )
    moments_down, squares_down, master_down = adamw_step(
        weights_down, moment_down, square_down, owned_down, rate_down
    )
    moments_bias, squares_bias, master_bias = adamw_step(
        biases, moment_bias, square_bias, owned_bias, rate_bias
    )
    return (
        block_out[None],
        input_grad[None],
        cond_grad,
        moments_in,
        moments_down,
        moments_bias,
        squares_in,
        squares_down,
        squares_bias,
        master_in,
        master_down,
        master_bias,
        master_in.astype(BF16),
        master_down.astype(BF16),
        master_bias.astype(BF16),
    )


def solution(mesh):
    return jax.shard_map(
        local if dict(mesh.shape) == {"dp": 16, "seq": 2} else local_general,
        mesh=mesh,
        in_specs=(
            P("dp", "seq", None),
            P("dp", None),
            P("dp", "seq", None),
            P("seq", "dp"),
            P("seq", "dp"),
            P(("dp", "seq")),
            P("seq", "dp"),
            P("seq", "dp"),
            P(("dp", "seq")),
            P("seq", "dp"),
            P("seq", "dp"),
            P(("dp", "seq")),
        ),
        out_specs=(
            P("dp", "seq", None),
            P("dp", "seq", None),
            P("dp", None),
            P("seq", "dp"),
            P("seq", "dp"),
            P(("dp", "seq")),
            P("seq", "dp"),
            P("seq", "dp"),
            P(("dp", "seq")),
            P("seq", "dp"),
            P("seq", "dp"),
            P(("dp", "seq")),
            P("seq", "dp"),
            P("seq", "dp"),
            P(("dp", "seq")),
        ),
        check_vma=False,
    )
```
